32 devices in a mesh: seq: 4 (over z), fsdp: 8 (over y, x, core).
Axes of the slice: x: 2, y: 2, z: 4, core: 2. Of those that a mesh axis runs over, the one named last changes fastest.
Arguments:
- block_input: bfloat16 [8, 1024, 2048], P('fsdp', 'seq'), may hold values from -6 to 6
- query_weight: bfloat16 [2048, 2048], P('fsdp'), may hold values from -0.125 to 0.125
- key_weight: bfloat16 [2048, 2048], P('fsdp'), may hold values from -0.125 to 0.125
- value_weight: bfloat16 [2048, 2048], P('fsdp'), may hold values from -0.125 to 0.125
- out_weight: bfloat16 [2048, 2048], P('fsdp'), may hold values from -0.125 to 0.125
- gate_weight: bfloat16 [2048, 8192], P('fsdp'), may hold values from -0.125 to 0.125
- up_weight: bfloat16 [2048, 8192], P('fsdp'), may hold values from -0.125 to 0.125
- down_weight: bfloat16 [8192, 2048], P('fsdp'), may hold values from -0.0625 to 0.0625
- query_gain: float32 [2048], replicated, may hold values from 1 to 2
- key_gain: float32 [2048], replicated, may hold values from 1 to 2
- attention_gain: float32 [2048], replicated, may hold values from 0.25 to 1.75
- swiglu_gain: float32 [2048], replicated, may hold values from 0.25 to 1.75
- cotangent: bfloat16 [8, 1024, 2048], P('fsdp', 'seq'), may hold values from -6 to 6
Outputs:
- output: float32 [8, 1024, 2048], P('fsdp', 'seq')
- input_grad: float32 [8, 1024, 2048], P('fsdp', 'seq')
- query_weight_grad: float32 [2048, 2048], P('fsdp')
- key_weight_grad: float32 [2048, 2048], P('fsdp')
- value_weight_grad: float32 [2048, 2048], P('fsdp')
- out_weight_grad: float32 [2048, 2048], P('fsdp')
- gate_weight_grad: float32 [2048, 8192], P('fsdp')
- up_weight_grad: float32 [2048, 8192], P('fsdp')
- down_weight_grad: float32 [8192, 2048], P('fsdp')
- query_gain_grad: float32 [2048], replicated
- key_gain_grad: float32 [2048], replicated
- attention_gain_grad: float32 [2048], replicated
- swiglu_gain_grad: float32 [2048], replicated
The draws below stay inside these ranges and needn't reach their ends.
All inputs are finite; a program needn't handle non-finite values.
Results may differ from the reference program's by a relative error of at most 0.023.
Values may be sent and summed in bfloat16 or wider, within the bound.
A program may use at most 512 MiB of HBM per device.

```python
import math
import jax
import jax.numpy as jnp
from jax import lax

D = 2048
HEADS = 16
HEAD_DIM = 128
FF = 8192
LENGTH = 1024
SEQS = 8


def level_of(rng, dims, shards, least, high):
    def one(dim, blocks):
        heights = jax.random.uniform(jax.random.fold_in(jax.random.fold_in(rng, 6), dim), (blocks,), jnp.float32, least / len(shards), high / len(shards))
        return jnp.repeat(jnp.exp(heights), dims[dim] // blocks).reshape((-1,) + (1,) * (len(dims) - dim - 1))

    gain = one(*shards[0])
    for cut in shards[1:]:
        gain = gain * one(*cut)
    return gain


def centred(stream_key, dims, spread, most, pieces=(), kind=jnp.bfloat16):
    values = spread * jax.random.normal(stream_key, dims, jnp.float32)
    if pieces:
        values = values * level_of(stream_key, dims, pieces, -0.22, 0.18)
    return jnp.clip(values, -most, most).astype(kind)


def setup_inputs(seed: int = 0) -> dict:
    splits = jax.random.split(jax.random.key(seed), 14)
    block_input = centred(splits[0], (SEQS, LENGTH, D), 1.0, 6.0, ((0, 8), (1, 4)))
    query_weight = centred(splits[1], (D, D), D ** -0.5, 0.125, ((0, 8),))
    key_weight = centred(splits[2], (D, D), D ** -0.5, 0.125, ((0, 8),))
    value_weight = centred(splits[3], (D, D), D ** -0.5, 0.125, ((0, 8),))
    out_weight = centred(splits[4], (D, D), D ** -0.5, 0.125, ((0, 8),))
    gate_weight = centred(splits[5], (D, FF), D ** -0.5, 0.125, ((0, 8),))
    up_weight = centred(splits[6], (D, FF), D ** -0.5, 0.125, ((0, 8),))
    down_weight = centred(splits[7], (FF, D), FF ** -0.5, 0.0625, ((0, 8),))
    query_gain = jnp.clip(jnp.exp(jax.random.uniform(splits[8], (D,), jnp.float32, math.log(1.0), math.log(2.0))), 1.0, 2.0)
    key_gain = jnp.clip(jnp.exp(jax.random.uniform(splits[9], (D,), jnp.float32, math.log(1.0), math.log(2.0))), 1.0, 2.0)
    attention_gain = jnp.clip(1.0 + 0.15 * jax.random.normal(splits[10], (D,), jnp.float32), 0.25, 1.75)
    swiglu_gain = jnp.clip(1.0 + 0.15 * jax.random.normal(splits[11], (D,), jnp.float32), 0.25, 1.75)
    cotangent = centred(splits[12], (SEQS, LENGTH, D), 1.0, 6.0, ((0, 8), (1, 4)))
    return {"block_input": block_input, "query_weight": query_weight, "key_weight": key_weight, "value_weight": value_weight, "out_weight": out_weight, "gate_weight": gate_weight, "up_weight": up_weight, "down_weight": down_weight, "query_gain": query_gain, "key_gain": key_gain, "attention_gain": attention_gain, "swiglu_gain": swiglu_gain, "cotangent": cotangent}


epsilon = 1e-06
rotary_base = 500000.0
masked_value = -1e+30

@jax.custom_vjp
def low(v):
    return lax.optimization_barrier(v.astype(jnp.bfloat16)).astype(jnp.float32)

@jax.custom_vjp
def low_back(v):
    return v

def low_keep(v):
    return (low(v), None)

def low_pass(kept, grad):
    return (grad,)

def back_keep(v):
    return (v, None)

def back_low(kept, grad):
    return (low(grad),)
low.defvjp(low_keep, low_pass)
low_back.defvjp(back_keep, back_low)

def matmul(operand, matrix):
    return jnp.dot(operand, matrix, precision=lax.Precision.HIGHEST)

def root_norm(values, gain_vector):
    factor = lax.rsqrt(lax.optimization_barrier(jnp.mean(values * values, axis=-1, keepdims=True)) + epsilon)
    return values * factor * gain_vector

def rotary_tables(count):
    positions = jnp.arange(count, dtype=jnp.int32).astype(jnp.float32)
    middle = HEAD_DIM // 2
    frequency = rotary_base ** (-2.0 * jnp.arange(middle, dtype=jnp.float32) / HEAD_DIM)
    angles = positions[:, None] * frequency[None, :]
    return (jnp.cos(angles)[:, None, :], jnp.sin(angles)[:, None, :])

def rotate(values, cosine, sine_table):
    middle = values.shape[-1] // 2
    leading = values[..., :middle]
    trailing = values[..., middle:]
    return jnp.concatenate([leading * cosine - trailing * sine_table, trailing * cosine + leading * sine_table], axis=-1)

def attend(queries, keys, values):
    length = queries.shape[0]
    block_rows = min(512, length)
    blocks = length // block_rows
    score_scale = HEAD_DIM ** (-0.5)
    grouped = queries.reshape(blocks, block_rows, HEADS, HEAD_DIM)
    starts = jnp.arange(blocks, dtype=jnp.int32) * block_rows
    key_positions = jnp.arange(length, dtype=jnp.int32)

    def one_block(operands):
        query_block, row_start = operands
        products = jnp.einsum('qhd,khd->hqk', query_block, keys, precision=lax.Precision.HIGHEST)
        scores = low_back(products * score_scale)
        query_positions = row_start + jnp.arange(block_rows, dtype=jnp.int32)
        allowed = key_positions[None, :] <= query_positions[:, None]
        scores = jnp.where(allowed[None], scores, masked_value)
        maximum = lax.optimization_barrier(jnp.max(scores, axis=-1, keepdims=True))
        exponent = jnp.exp(scores - maximum)
        probabilities = exponent / lax.optimization_barrier(jnp.sum(exponent, axis=-1, keepdims=True))
        return jnp.einsum('hqk,khd->qhd', low(probabilities), values, precision=lax.Precision.HIGHEST)
    outputs = lax.map(jax.checkpoint(one_block), (grouped, starts))
    return outputs.reshape(length, HEADS * HEAD_DIM)

def layer(sequence, params):
    query_weight, key_weight, value_weight, out_weight, gate_weight, up_weight, down_weight, query_gain, key_gain, attention_gain, swiglu_gain = params
    length = sequence.shape[0]
    cosine, sine_table = rotary_tables(length)
    query_raw = low_back(matmul(sequence, query_weight))
    key_raw = low_back(matmul(sequence, key_weight))
    value_raw = matmul(sequence, value_weight)
    queries = low_back(low(rotate(root_norm(query_raw, query_gain).reshape(length, HEADS, HEAD_DIM), cosine, sine_table)))
    keys_rot = low_back(low(rotate(root_norm(key_raw, key_gain).reshape(length, HEADS, HEAD_DIM), cosine, sine_table)))
    values_low = low_back(low(value_raw)).reshape(length, HEADS, HEAD_DIM)
    attended = low_back(low(attend(queries, keys_rot, values_low)))
    branch = low_back(matmul(attended, out_weight))
    residual = sequence + root_norm(branch, attention_gain)
    residual_low = low(residual)
    gate_value = low_back(matmul(residual_low, gate_weight))
    upward = low_back(matmul(residual_low, up_weight))
    hidden = low(gate_value * jax.nn.sigmoid(gate_value) * upward)
    mixed_out = low_back(matmul(hidden, down_weight))
    return residual + root_norm(mixed_out, swiglu_gain)

def forward(block_input, params):

    def step(carried, sequence):
        return (carried, jax.checkpoint(layer)(sequence, params))
    carried, outputs = lax.scan(step, jnp.zeros((), jnp.float32), block_input)
    return outputs

def reference(block_input, query_weight, key_weight, value_weight, out_weight, gate_weight, up_weight, down_weight, query_gain, key_gain, attention_gain, swiglu_gain, cotangent):
    params = tuple((matrix.astype(jnp.float32) for matrix in (query_weight, key_weight, value_weight, out_weight, gate_weight, up_weight, down_weight, query_gain, key_gain, attention_gain, swiglu_gain)))
    output, pullback = jax.vjp(forward, block_input.astype(jnp.float32), params)
    input_grad, param_grads = pullback(cotangent.astype(jnp.float32))
    return (output, input_grad, param_grads[0], param_grads[1], param_grads[2], param_grads[3], param_grads[4], param_grads[5], param_grads[6], param_grads[7], param_grads[8], param_grads[9], param_grads[10])
```

```python
import jax
import jax.numpy as jnp
from jax import lax
from jax.experimental import pallas as pl
from jax.experimental.pallas import tpu as pltpu
from jax.sharding import PartitionSpec as P

HEADS = 16


epsilon = 1e-06
rotary_base = 500000.0
masked_value = -1e30


def norm_factor(values):
    return lax.rsqrt(jnp.mean(values * values, axis=-1, keepdims=True) + epsilon)


def norm_backward(values, factor, gain_vector, upstream):
    scaled = upstream * gain_vector
    inner_mean = jnp.mean(scaled * values, axis=-1, keepdims=True)
    value_grad = factor * scaled - values * factor * factor * factor * inner_mean
    gain_grad = jnp.sum(upstream * values * factor, axis=0)
    return (value_grad, gain_grad)


def rotary_tables(count, offset, head_size):
    positions = (offset + jnp.arange(count, dtype=jnp.int32)).astype(jnp.float32)
    middle = head_size // 2
    frequency = rotary_base ** (-2.0 * jnp.arange(middle, dtype=jnp.float32) / head_size)
    angles = positions[:, None] * frequency[None, :]
    return (jnp.cos(angles)[:, None, :], jnp.sin(angles)[:, None, :])


def rotate(values, cosine, sine_table, direction_sign):
    middle = values.shape[-1] // 2
    leading = values[..., :middle]
    trailing = values[..., middle:]
    signed = sine_table * direction_sign
    return jnp.concatenate(
        [leading * cosine - trailing * signed, trailing * cosine + leading * signed], axis=-1
    )


def times_transposed(operand, matrix):
    return lax.dot_general(
        operand, matrix, (((1,), (1,)), ((), ())), preferred_element_type=jnp.float32
    )


def transposed_times(operand, matrix):
    return lax.dot_general(
        operand, matrix, (((0,), (0,)), ((), ())), preferred_element_type=jnp.float32
    )


def masked_scores(query_block, keys, row_start, block_rows, score_scale):
    length = keys.shape[0]
    scores = (
        jnp.einsum("qhd,khd->hqk", query_block, keys, preferred_element_type=jnp.float32)
        * score_scale
    )
    query_positions = row_start + jnp.arange(block_rows, dtype=jnp.int32)
    key_positions = jnp.arange(length, dtype=jnp.int32)
    allowed = key_positions[None, :] <= query_positions[:, None]
    return jnp.where(allowed[None], scores, masked_value)


def attention_forward(queries, keys, values):
    length = queries.shape[0]
    block_rows = min(512, length)
    blocks = length // block_rows
    score_scale = queries.shape[-1] ** (-0.5)

    def one_block(block_index):
        row_start = block_index * block_rows
        query_block = lax.dynamic_slice_in_dim(queries, row_start, block_rows, 0)
        scores = masked_scores(query_block, keys, row_start, block_rows, score_scale)
        maximum = jnp.max(scores, axis=-1, keepdims=True)
        exponent = jnp.exp(scores - maximum)
        row_total = jnp.sum(exponent, axis=-1, keepdims=True)
        log_total = maximum[..., 0] + jnp.log(row_total[..., 0])
        weights_low = (exponent / row_total).astype(jnp.bfloat16)
        attended = jnp.einsum(
            "hqk,khd->qhd", weights_low, values, preferred_element_type=jnp.float32
        )
        return (attended.astype(jnp.bfloat16), log_total)

    attended, log_total = lax.map(one_block, jnp.arange(blocks, dtype=jnp.int32))
    return (attended.reshape(length, -1), log_total)


def attention_backward(queries, keys, values, attended_grad, log_total):
    length = queries.shape[0]
    block_rows = min(512, length)
    blocks = length // block_rows
    score_scale = queries.shape[-1] ** (-0.5)
    empty = jnp.zeros(keys.shape, jnp.float32)

    def one_block(carried, operands):
        key_sum, value_sum = carried
        block_index, block_total = operands
        row_start = block_index * block_rows
        query_block = lax.dynamic_slice_in_dim(queries, row_start, block_rows, 0)
        grad_block = lax.dynamic_slice_in_dim(attended_grad, row_start, block_rows, 0)
        scores = masked_scores(query_block, keys, row_start, block_rows, score_scale)
        probabilities = jnp.exp(scores - block_total[..., None])
        weights_low = probabilities.astype(jnp.bfloat16)
        value_sum = value_sum + jnp.einsum(
            "hqk,qhd->khd", weights_low, grad_block, preferred_element_type=jnp.float32
        )
        probability_grad = jnp.einsum(
            "qhd,khd->hqk", grad_block, values, preferred_element_type=jnp.float32
        )
        inner_sum = jnp.sum(probabilities * probability_grad, axis=-1, keepdims=True)
        score_grad = (probabilities * (probability_grad - inner_sum)).astype(jnp.bfloat16)
        query_grad = (
            jnp.einsum("hqk,khd->qhd", score_grad, keys, preferred_element_type=jnp.float32)
            * score_scale
        )
        key_sum = (
            key_sum
            + jnp.einsum(
                "hqk,qhd->khd", score_grad, query_block, preferred_element_type=jnp.float32
            )
            * score_scale
        )
        return ((key_sum, value_sum), query_grad.astype(jnp.bfloat16))

    (key_sum, value_sum), query_grads = lax.scan(
        one_block, (empty, empty), (jnp.arange(blocks, dtype=jnp.int32), log_total)
    )
    return (
        query_grads.reshape(keys.shape),
        key_sum.astype(jnp.bfloat16),
        value_sum.astype(jnp.bfloat16),
    )


def local(
    block_input,
    query_weight,
    key_weight,
    value_weight,
    out_weight,
    gate_weight,
    up_weight,
    down_weight,
    query_gain,
    key_gain,
    attention_gain,
    swiglu_gain,
    cotangent,
):
    tokens = block_input.shape[1]
    model_width = block_input.shape[2]
    head_size = model_width // HEADS
    groups = lax.axis_size("seq")
    local_heads = HEADS // groups
    sequence = block_input.reshape(tokens, model_width)
    query_full, key_full, value_full, out_full = (
        lax.all_gather(query_weight, "fsdp", axis=0, tiled=True),
        lax.all_gather(key_weight, "fsdp", axis=0, tiled=True),
        lax.all_gather(value_weight, "fsdp", axis=0, tiled=True),
        lax.all_gather(out_weight, "fsdp", axis=0, tiled=True),
    )
    query_raw = jnp.dot(sequence, query_full, preferred_element_type=jnp.float32)
    key_raw = jnp.dot(sequence, key_full, preferred_element_type=jnp.float32)
    value_raw = jnp.dot(sequence, value_full, preferred_element_type=jnp.float32)
    query_factor = norm_factor(query_raw)
    key_factor = norm_factor(key_raw)
    cosine, sine_table = rotary_tables(tokens, lax.axis_index("seq") * tokens, head_size)
    query_rot = rotate(
        (query_raw * query_factor * query_gain).reshape(tokens, HEADS, head_size),
        cosine,
        sine_table,
        1.0,
    )
    key_rot = rotate(
        (key_raw * key_factor * key_gain).reshape(tokens, HEADS, head_size), cosine, sine_table, 1.0
    )
    stacked = jnp.stack(
        [
            query_rot.reshape(tokens, model_width).astype(jnp.bfloat16),
            key_rot.reshape(tokens, model_width).astype(jnp.bfloat16),
            value_raw.astype(jnp.bfloat16),
        ]
    )
    grouped = lax.all_to_all(stacked, "seq", split_axis=2, concat_axis=1, tiled=True)
    length = grouped.shape[1]
    head_queries = grouped[0].reshape(length, local_heads, head_size)
    head_keys = grouped[1].reshape(length, local_heads, head_size)
    head_values = grouped[2].reshape(length, local_heads, head_size)
    attended_heads, log_total = attention_forward(head_queries, head_keys, head_values)
    attended = lax.all_to_all(attended_heads, "seq", split_axis=0, concat_axis=1, tiled=True)
    branch = jnp.dot(attended, out_full, preferred_element_type=jnp.float32)
    branch_factor = norm_factor(branch)
    residual = sequence.astype(jnp.float32) + branch * branch_factor * attention_gain
    residual_low = residual.astype(jnp.bfloat16)
    gate_full, up_full, down_full = (
        lax.all_gather(gate_weight, "fsdp", axis=0, tiled=True),
        lax.all_gather(up_weight, "fsdp", axis=0, tiled=True),
        lax.all_gather(down_weight, "fsdp", axis=0, tiled=True),
    )
    gate_value = jnp.dot(residual_low, gate_full, preferred_element_type=jnp.float32)
    upward = jnp.dot(residual_low, up_full, preferred_element_type=jnp.float32)
    sigmoid_gate = jax.nn.sigmoid(gate_value)
    activated = gate_value * sigmoid_gate
    hidden = (activated * upward).astype(jnp.bfloat16)
    mixed_out = jnp.dot(hidden, down_full, preferred_element_type=jnp.float32)
    mixed_factor = norm_factor(mixed_out)
    output = residual + mixed_out * mixed_factor * swiglu_gain
    upstream = cotangent.reshape(tokens, model_width).astype(jnp.float32)
    mixed_float, swiglu_gain_grad = norm_backward(mixed_out, mixed_factor, swiglu_gain, upstream)
    mixed_grad = mixed_float.astype(jnp.bfloat16)
    gate_back, up_back, down_back = (
        lax.all_gather(gate_weight, "fsdp", axis=0, tiled=True),
        lax.all_gather(up_weight, "fsdp", axis=0, tiled=True),
        lax.all_gather(down_weight, "fsdp", axis=0, tiled=True),
    )
    hidden_grad = times_transposed(mixed_grad, down_back)
    gate_grad = (
        hidden_grad * upward * sigmoid_gate * (1.0 + gate_value * (1.0 - sigmoid_gate))
    ).astype(jnp.bfloat16)
    up_grad = (hidden_grad * activated).astype(jnp.bfloat16)
    residual_grad = (
        upstream + times_transposed(gate_grad, gate_back) + times_transposed(up_grad, up_back)
    )
    joined = jnp.concatenate([gate_grad, up_grad], axis=1)
    branch_float, attention_gain_grad = norm_backward(
        branch, branch_factor, attention_gain, residual_grad
    )
    branch_grad = branch_float.astype(jnp.bfloat16)
    query_back, key_back, value_back, out_back = (
        lax.all_gather(query_weight, "fsdp", axis=0, tiled=True),
        lax.all_gather(key_weight, "fsdp", axis=0, tiled=True),
        lax.all_gather(value_weight, "fsdp", axis=0, tiled=True),
        lax.all_gather(out_weight, "fsdp", axis=0, tiled=True),
    )
    attended_grad = times_transposed(branch_grad, out_back).astype(jnp.bfloat16)
    head_grad = lax.all_to_all(attended_grad, "seq", split_axis=1, concat_axis=0, tiled=True)
    query_grads, key_grads, value_grads = attention_backward(
        head_queries,
        head_keys,
        head_values,
        head_grad.reshape(length, local_heads, head_size),
        log_total,
    )
    back_stack = jnp.stack([query_grads, key_grads, value_grads]).reshape(
        3, length, local_heads * head_size
    )
    token_grads = lax.all_to_all(back_stack, "seq", split_axis=1, concat_axis=2, tiled=True)
    query_norm_grad = rotate(
        token_grads[0].astype(jnp.float32).reshape(tokens, HEADS, head_size),
        cosine,
        sine_table,
        -1.0,
    )
    key_norm_grad = rotate(
        token_grads[1].astype(jnp.float32).reshape(tokens, HEADS, head_size),
        cosine,
        sine_table,
        -1.0,
    )
    query_float, query_gain_grad = norm_backward(
        query_raw, query_factor, query_gain, query_norm_grad.reshape(tokens, model_width)
    )
    key_float, key_gain_grad = norm_backward(
        key_raw, key_factor, key_gain, key_norm_grad.reshape(tokens, model_width)
    )
    query_raw_grad = query_float.astype(jnp.bfloat16)
    key_raw_grad = key_float.astype(jnp.bfloat16)
    value_tokens = token_grads[2]
    input_grad = (
        residual_grad
        + times_transposed(query_raw_grad, query_back)
        + times_transposed(key_raw_grad, key_back)
        + times_transposed(value_tokens, value_back)
    )
    projected = jnp.concatenate([query_raw_grad, key_raw_grad, value_tokens], axis=1)
    hidden_width = gate_weight.shape[1]
    columns = hidden
    down_shard = lax.psum_scatter(
        transposed_times(columns, mixed_grad).astype(jnp.bfloat16),
        "fsdp",
        scatter_dimension=0,
        tiled=True,
    )
    columns = residual_low
    gate_up_shard = lax.psum_scatter(
        transposed_times(columns, joined).astype(jnp.bfloat16),
        "fsdp",
        scatter_dimension=0,
        tiled=True,
    )
    attention_shard = lax.psum_scatter(
        jnp.concatenate(
            [transposed_times(sequence, projected), transposed_times(attended, branch_grad)], axis=1
        ).astype(jnp.bfloat16),
        "fsdp",
        scatter_dimension=0,
        tiled=True,
    )
    attention_total, gate_up_total, down_total = (
        lax.psum(attention_shard, "seq").astype(jnp.float32),
        lax.psum(gate_up_shard, "seq").astype(jnp.float32),
        lax.psum(down_shard, "seq").astype(jnp.float32),
    )
    gain_totals = lax.psum(
        jnp.stack([query_gain_grad, key_gain_grad, attention_gain_grad, swiglu_gain_grad]),
        ("seq", "fsdp"),
    )
    return (
        output.reshape(1, tokens, model_width),
        input_grad.reshape(1, tokens, model_width),
        attention_total[:, :model_width],
        attention_total[:, model_width : 2 * model_width],
        attention_total[:, 2 * model_width : 3 * model_width],
        attention_total[:, 3 * model_width :],
        gate_up_total[:, :hidden_width],
        gate_up_total[:, hidden_width:],
        down_total,
        gain_totals[0],
        gain_totals[1],
        gain_totals[2],
        gain_totals[3],
    )


MESH = pl.DeviceIdType.MESH
VMEM_LIMIT = 48 * 1024 * 1024


def flip(value, bit):
    return value + bit - 2 * bit * lax.rem(lax.div(value, bit), 2)


def flip_mask(value, mask):
    for bit in (1, 2, 4):
        if mask & bit:
            value = flip(value, bit)
    return value


def place():
    seq, shard = lax.axis_index("seq"), lax.axis_index("fsdp")
    return seq, shard


def greet(targets):
    barrier = pltpu.get_barrier_semaphore()
    for target in targets:
        pl.semaphore_signal(barrier, inc=1, device_id=target, device_id_type=MESH)
    pl.semaphore_wait(barrier, len(targets))


def remote(source, target_ref, send, receive, device):
    return pltpu.make_async_remote_copy(
        src_ref=source,
        dst_ref=target_ref,
        send_sem=send,
        recv_sem=receive,
        device_id=device,
        device_id_type=MESH,
    )


def column_others(seq, shard):
    mate = flip(shard, 1)
    others = [(lax.rem(seq + step, 4), shard) for step in (1, 2, 3)]
    return others + [(lax.rem(seq + step, 4), mate) for step in (0, 1, 2, 3)]


def ordered(kernel, inputs, after):
    count, extra = len(inputs), len(after)
    return lambda *refs: kernel(*refs[:count], *refs[count + extra :])


def comm_call(kernel, out_shape, inputs, in_specs, out_specs, scratch, name, number, after=()):
    return pl.pallas_call(
        ordered(kernel, inputs, after),
        out_shape=out_shape,
        in_specs=list(in_specs) + [ANY] * len(after),
        out_specs=out_specs,
        scratch_shapes=scratch,
        name=name,
        compiler_params=pltpu.CompilerParams(
            collective_id=number, has_side_effects=True, vmem_limit_bytes=VMEM_LIMIT
        ),
    )(*inputs, *after)


def keep_kernel(x, out):
    out[...] = x[...]


def keep_number(x, out):
    out[0] = x[0]


def keep(x, after, space=pltpu.VMEM):
    return pl.pallas_call(
        ordered(keep_number if space == pltpu.SMEM else keep_kernel, (x,), after),
        out_shape=jax.ShapeDtypeStruct(x.shape, x.dtype),
        in_specs=[pl.BlockSpec(memory_space=space)] + [ANY] * len(after),
        out_specs=pl.BlockSpec(memory_space=space),
        name="keep",
    )(x, *after)


ANY = pl.BlockSpec(memory_space=pl.ANY)
VM = pl.BlockSpec(memory_space=pltpu.VMEM)
DMA = pltpu.SemaphoreType.DMA


def entry_kernel(
    x, wq, wk, wv, xo, wo, local, x_send, x_recv, fwd_send, w_send, w_recv
):
    seq, shard = place()
    core, half = lax.rem(shard, 2), lax.div(seq, 2)
    quarter = lax.rem(seq, 2)
    rows, width = wq.shape[0], wo.shape[1] // 3
    weights = (wq, wk, wv)
    greet(
        [(seq, flip_mask(shard, mask)) for mask in range(1, 8)]
        + [(lax.rem(seq + step, 4), shard) for step in (1, 2, 3)]
    )
    mine = pl.ds(pl.multiple_of(shard * rows, rows), rows)

    def columns(index):
        return slice(index * width, (index + 1) * width)

    def block(index, target):
        group = 2 * quarter + lax.rem(target, 2)
        return weights[index].at[:, pl.ds(pl.multiple_of(group * width, width), width)]

    x_copies = []
    for which in (0, 1):
        target = 2 * core + which
        copy = remote(x, xo.at[seq], x_send.at[which], x_recv.at[seq], (target, shard))

        @pl.when(target != seq)
        def _():
            copy.start()

        @pl.when(target == seq)
        def _():
            pltpu.make_async_copy(x, xo.at[seq], local.at[3]).start()

        x_copies.append((target, copy))
    copies = []
    for index in range(3):
        for mask in (2, 4, 3, 5, 1):
            target = flip_mask(shard, mask)
            copy = remote(
                block(index, target),
                wo.at[mine, columns(index)],
                w_send.at[index, mask - 1],
                w_recv.at[index, mask - 1],
                (seq, target),
            )
            copy.start()
            copies.append(copy)
    own = [
        pltpu.make_async_copy(block(index, shard), wo.at[mine, columns(index)], local.at[index])
        for index in range(3)
    ]
    for copy in own:
        copy.start()

    mate = (seq, flip(shard, 1))
    for turn in range(4):
        source = lax.rem(seq + turn, 4)
        forward = remote(
            xo.at[source], xo.at[source], fwd_send.at[turn], x_recv.at[source], mate
        )

        @pl.when(core == half)
        def _():
            if turn == 0:
                pltpu.make_async_copy(x, xo.at[seq], local.at[3]).wait()
            else:
                forward.wait_recv()
            forward.start()

    for turn in range(4):
        source = lax.rem(seq + turn, 4)
        forward = remote(
            xo.at[source], xo.at[source], fwd_send.at[turn], x_recv.at[source], mate
        )

        @pl.when(core == half)
        def _():
            forward.wait_send()

        @pl.when(core != half)
        def _():
            forward.wait_recv()

    def arrival(index, origin, mask):
        spot = wo.at[pl.ds(pl.multiple_of(origin * rows, rows), rows), columns(index)]
        return remote(spot, spot, w_send.at[index, 0], w_recv.at[index, mask - 1], mate)

    base = shard - core
    side, above = flip(base, 2), flip(base, 4)
    onward = []
    for index in range(3):
        for origin, mask, slot, target in (
            (side, 2 + core, 6 + core, flip(shard, 4)),
            (above + 1, 5 - core, 7 - core, flip(shard, 2)),
        ):
            arrival(index, origin, mask).wait_recv()
            spot = wo.at[pl.ds(pl.multiple_of(origin * rows, rows), rows), columns(index)]
            copy = remote(
                spot,
                spot,
                w_send.at[index, 5 + len(onward) % 2],
                w_recv.at[index, slot - 1],
                (seq, target),
            )
            copy.start()
            onward.append(copy)
    for target, copy in x_copies:

        @pl.when(target != seq)
        def _():
            copy.wait_send()

    for copy in own:
        copy.wait()
    for copy in copies + onward:
        copy.wait_send()
    far = flip_mask(base, 6)
    for index in range(3):
        arrival(index, flip(shard, 1), 1).wait_recv()
        arrival(index, side + 1, 3 - core).wait_recv()
        arrival(index, above, 4 + core).wait_recv()
        arrival(index, far, 6 + core).wait_recv()
        arrival(index, far + 1, 7 - core).wait_recv()


def entry(x, wq, wk, wv, number):
    rows, width = wq.shape
    group = width // 4
    return comm_call(
        entry_kernel,
        (
            jax.ShapeDtypeStruct((4,) + x.shape, x.dtype),
            jax.ShapeDtypeStruct((8 * rows, 3 * group), wq.dtype),
        ),
        (x, wq, wk, wv),
        [ANY] * 4,
        (ANY, ANY),
        [DMA((4,)), DMA((2,)), DMA((4,)), DMA((4,)), DMA((3, 7)), DMA((3, 7))],
        "entry",
        number,
    )


def stats_kernel(part, total, held, send, receive):
    seq, shard = place()
    partners = [
        (seq, flip(shard, 1)),
        (flip(seq, 1), shard),
        (flip(seq, 1), flip(shard, 1)),
    ]
    greet(partners)
    copies = [
        remote(part, held.at[index], send.at[index], receive.at[index], partner)
        for index, partner in enumerate(partners)
    ]
    for copy in copies:
        copy.start()
    for copy in copies:
        copy.wait()
    total[...] = (part[...] + held[0]) + (held[1] + held[2])


def stats_sum(part, number, after=()):
    return comm_call(
        stats_kernel,
        jax.ShapeDtypeStruct(part.shape, part.dtype),
        (part,),
        [VM],
        VM,
        [pltpu.VMEM((3,) + part.shape, part.dtype), DMA((3,)), DMA((3,))],
        "stats",
        number,
        after,
    )


def to_tokens_kernel(heads, tokens, local, send, receive):
    seq, shard = place()
    core, half = lax.rem(shard, 2), lax.div(seq, 2)
    base = shard - core
    width = heads.shape[2]
    group = 2 * lax.rem(seq, 2) + core
    greet(column_others(seq, shard))
    mine = tokens.at[:, pl.ds(pl.multiple_of(group * width, width), width)]
    steps = []
    for turn in range(4):
        target = lax.rem(seq + turn, 4)
        remote_copy = remote(
            heads.at[target], mine, send.at[turn], receive.at[group], (target, base + half)
        )
        if turn == 0:
            here = core == half
            own = pltpu.make_async_copy(heads.at[target], mine, local)

            @pl.when(here)
            def _():
                own.start()

            @pl.when(jnp.logical_not(here))
            def _():
                remote_copy.start()

        else:
            remote_copy.start()
        steps.append(remote_copy)
    for turn in range(4):
        if turn == 0:

            @pl.when(here)
            def _():
                own.wait()

            @pl.when(jnp.logical_not(here))
            def _():
                steps[0].wait_send()

        else:
            steps[turn].wait_send()
    for source in range(4):
        slot = tokens.at[:, source * width : (source + 1) * width]
        arrival = remote(heads.at[0], slot, send.at[0], receive.at[source], (seq, shard))

        @pl.when(jnp.logical_not(jnp.logical_and(here, group == source)))
        def _():
            arrival.wait_recv()


def to_tokens(heads, number, after=()):
    blocks, rows, width = heads.shape
    return comm_call(
        to_tokens_kernel,
        jax.ShapeDtypeStruct((rows, 4 * width), heads.dtype),
        (heads,),
        [ANY],
        ANY,
        [DMA, DMA((4,)), DMA((4,))],
        "to_tokens",
        number,
        after,
    )


def to_heads_kernel(tokens, heads, local, send, receive):
    seq, shard = place()
    core, half = lax.rem(shard, 2), lax.div(seq, 2)
    base = shard - core
    width = heads.shape[2]
    greet(column_others(seq, shard))
    here = core == half
    mine = 2 * lax.rem(seq, 2) + core
    copies = []
    for group in range(4):
        target = (2 * core + group // 2, base + group % 2)
        source = tokens.at[:, group * width : (group + 1) * width]
        copy = remote(source, heads.at[seq], send.at[group], receive.at[seq], target)
        own = pltpu.make_async_copy(source, heads.at[seq], local)
        self_copy = jnp.logical_and(here, mine == group)

        @pl.when(self_copy)
        def _():
            own.start()

        @pl.when(jnp.logical_not(self_copy))
        def _():
            copy.start()

        copies.append((self_copy, own, copy))
    for self_copy, own, copy in copies:

        @pl.when(self_copy)
        def _():
            own.wait()

        @pl.when(jnp.logical_not(self_copy))
        def _():
            copy.wait_send()

    for source in range(4):
        arrival = remote(
            tokens.at[:, 0:width], heads.at[source], send.at[0], receive.at[source], (seq, shard)
        )

        @pl.when(jnp.logical_not(jnp.logical_and(here, seq == source)))
        def _():
            arrival.wait_recv()


def to_heads(tokens, number, after=()):
    rows, width = tokens.shape
    return comm_call(
        to_heads_kernel,
        jax.ShapeDtypeStruct((4, rows, width // 4), tokens.dtype),
        (tokens,),
        [ANY],
        ANY,
        [DMA, DMA((4,)), DMA((4,))],
        "to_heads",
        number,
        after,
    )


def plane_gather_kernel(x, out, local, send, receive):
    seq, shard = place()
    core = lax.rem(shard, 2)
    near = [(seq, flip(shard, bit)) for bit in (2, 4, 1)]
    greet(near)
    own = pltpu.make_async_copy(x, out.at[shard], local)
    own.start()
    firsts = [
        remote(x, out.at[shard], send.at[index], receive.at[index], device)
        for index, device in enumerate(near)
    ]
    for copy in firsts:
        copy.start()
    mate = near[2]

    def pass_on(slot, index, device):
        return remote(out.at[slot], out.at[slot], send.at[index], receive.at[index], device)

    first_bit = 2 + 2 * core
    second_bit = 4 - 2 * core
    first, second = flip_bit(shard, first_bit), flip_bit(shard, second_bit)
    diagonal = flip_mask(shard, 6)

    def arrival(slot, index):
        return remote(out.at[slot], out.at[slot], send.at[0], receive.at[index], mate)

    arrival(first, core).wait_recv()
    across = pass_on(first, 3, (seq, second))
    across.start()
    one = remote(out.at[first], out.at[first], send.at[4], receive.at[4 + core], mate)
    one.start()
    arrival(second, 1 - core).wait_recv()
    two = remote(out.at[second], out.at[second], send.at[5], receive.at[5 - core], mate)
    two.start()
    arrival(diagonal, 3).wait_recv()
    three = pass_on(diagonal, 6, mate)
    three.start()
    own.wait()
    for copy in firsts:
        copy.wait_send()
    for copy in (across, one, two, three):
        copy.wait_send()
    mate_shard = flip(shard, 1)
    arrival(mate_shard, 2).wait_recv()
    arrival(flip(mate_shard, 2), 4).wait_recv()
    arrival(flip(mate_shard, 4), 5).wait_recv()
    arrival(flip_mask(mate_shard, 6), 6).wait_recv()


def flip_bit(value, bit):
    return value + bit - 2 * bit * lax.rem(lax.div(value, bit), 2)


def plane_gather(x, number, after=()):
    return comm_call(
        plane_gather_kernel,
        jax.ShapeDtypeStruct((8,) + x.shape, x.dtype),
        (x,),
        [ANY],
        ANY,
        [DMA, DMA((7,)), DMA((7,))],
        "plane_gather",
        number,
        after,
    )


PIECES = 2


def add_rows(rows, body):
    step = 32

    def one(index, carry):
        body(pl.ds(pl.multiple_of(index * step, step), step))
        return carry

    lax.fori_loop(0, rows // step, one, 0)


def plane_scatter_kernel(part, out, mated, first_in, second_in, sums, sem_s, sem_r):
    seq, shard = place()
    core, chip = lax.rem(shard, 2), lax.div(shard, 2)
    rows = out.shape[0] // PIECES
    mate = (seq, flip(shard, 1))
    bit = 1 + core
    first, second = flip_bit(chip, bit), flip_bit(chip, 3 - bit)
    diagonal = 3 - chip
    first_device, second_device = (seq, 2 * first + core), (seq, 2 * second + core)
    greet([mate, first_device, second_device])

    def piece(index):
        return pl.ds(index * rows, rows)

    order = (diagonal, first, second, chip)
    swaps = {}
    for slot, target in enumerate(order):
        for index in range(PIECES):
            copy = remote(
                part.at[2 * target + 1 - core, piece(index)],
                mated.at[target, piece(index)],
                sem_s.at[0, slot, index],
                sem_r.at[0, target, index],
                mate,
            )
            copy.start()
            swaps[slot, index] = copy

    def came(target, index):
        remote(
            part.at[0, piece(index)],
            mated.at[target, piece(index)],
            sem_s.at[0, 0, index],
            sem_r.at[0, target, index],
            mate,
        ).wait_recv()

    sends = []
    for index in range(PIECES):
        for slot, target in ((0, diagonal), (1, first)):
            came(target, index)

            def add(span, slot=slot, target=target, index=index):
                span = pl.ds(span.start + index * rows, span.size)
                sums[slot, span] = (
                    part[2 * target + core, span].astype(jnp.float32)
                    + mated[target, span].astype(jnp.float32)
                ).astype(jnp.bfloat16)

            add_rows(rows, add)
            copy = remote(
                sums.at[slot, piece(index)],
                first_in.at[slot, piece(index)],
                sem_s.at[1, slot, index],
                sem_r.at[1, slot, index],
                first_device,
            )
            copy.start()
            sends.append(copy)
    finals = []
    for index in range(PIECES):
        came(second, index)
        sends[2 * index].wait_recv()

        def add(span, index=index):
            span = pl.ds(span.start + index * rows, span.size)
            sums[2, span] = (
                part[2 * second + core, span].astype(jnp.float32)
                + mated[second, span].astype(jnp.float32)
                + first_in[0, span].astype(jnp.float32)
            ).astype(jnp.bfloat16)

        add_rows(rows, add)
        copy = remote(
            sums.at[2, piece(index)],
            second_in.at[piece(index)],
            sem_s.at[2, 0, index],
            sem_r.at[2, 0, index],
            second_device,
        )
        copy.start()
        finals.append(copy)
    for index in range(PIECES):
        came(chip, index)
        sends[2 * index + 1].wait_recv()
        finals[index].wait_recv()

        def add(span, index=index):
            span = pl.ds(span.start + index * rows, span.size)
            out[span] = (
                part[shard, span].astype(jnp.float32) + mated[chip, span].astype(jnp.float32)
            ) + (first_in[1, span].astype(jnp.float32) + second_in[span].astype(jnp.float32))

        add_rows(rows, add)
    for copy in list(swaps.values()) + sends + finals:
        copy.wait_send()


def plane_scatter(part, number, after=()):
    _, rows, width = part.shape
    low = part.dtype
    return comm_call(
        plane_scatter_kernel,
        jax.ShapeDtypeStruct((rows, width), jnp.float32),
        (part,),
        [VM],
        VM,
        [
            pltpu.VMEM((4, rows, width), low),
            pltpu.VMEM((2, rows, width), low),
            pltpu.VMEM((rows, width), low),
            pltpu.VMEM((3, rows, width), low),
            DMA((3, 4, PIECES)),
            DMA((3, 4, PIECES)),
        ],
        "plane_scatter",
        number,
        after,
    )


def finish_kernel(
    part, grads, out_grad, out, placed,
    mated, sums, landed, first_in, second_in, onward, total, swapped,
    local, sem_s, sem_r, grad_s, grad_r
):
    seq, shard = place()
    core, half, quarter = lax.rem(shard, 2), lax.div(seq, 2), lax.rem(seq, 2)
    chip = lax.div(shard, 2)
    base = shard - core
    rows = out.shape[0] // 2
    mate = (seq, flip(shard, 1))
    bit = 1 + core
    first, second, diagonal = flip_bit(chip, bit), flip_bit(chip, 3 - bit), 3 - chip
    first_device, second_device = (seq, 2 * first + core), (seq, 2 * second + core)
    greet(column_others(seq, shard) + [first_device, second_device])
    mine = pl.ds(pl.multiple_of(core * rows, rows), rows)
    other = pl.ds(pl.multiple_of((1 - core) * rows, rows), rows)
    here = core == half
    order = [2 * (1 - half) + 1 - quarter, 2 * (1 - half) + quarter, flip(seq, 1), seq]
    swaps = []
    for slot, block in enumerate(order):
        copy = remote(
            part.at[block, other], mated.at[slot], sem_s.at[0, slot], sem_r.at[0, slot], mate
        )
        copy.start()
        swaps.append(copy)
    long = grads.shape[1] // 2
    firsts = []
    for index in range(2):
        span = slice(index * long, (index + 1) * long)
        for slot, target in ((0, diagonal), (1, first)):
            copy = remote(
                grads.at[target, span],
                first_in.at[slot, span],
                grad_s.at[slot, index],
                grad_r.at[slot, index],
                first_device,
            )
            copy.start()
            firsts.append(copy)
    placed[...] = jnp.zeros_like(placed)
    width = out_grad.shape[1]
    placed[:, 3 * width :] = out_grad[...]

    sends = []
    for slot, block in enumerate(order):
        swaps[slot].wait_recv()

        def add(span, slot=slot, block=block):
            source = pl.ds(pl.multiple_of(span.start + core * rows, 32), span.size)
            sums[slot, span] = (
                part[block, source].astype(jnp.float32) + mated[slot, span].astype(jnp.float32)
            ).astype(jnp.bfloat16)

        add_rows(rows, add)
        copy = remote(
            sums.at[slot],
            landed.at[quarter, core],
            sem_s.at[1, slot],
            sem_r.at[1, 2 * quarter + core],
            (block, base + half),
        )
        if slot < 3:
            copy.start()
        else:
            own = pltpu.make_async_copy(sums.at[slot], landed.at[quarter, core], local)

            @pl.when(here)
            def _():
                own.start()

            @pl.when(jnp.logical_not(here))
            def _():
                copy.start()

        sends.append(copy)

    seconds = []
    for index in range(2):
        firsts[2 * index].wait_recv()

        def add(span, index=index):
            span = pl.ds(span.start + index * long, span.size)
            onward[span] = (
                grads[second, span].astype(jnp.float32) + first_in[0, span].astype(jnp.float32)
            ).astype(jnp.bfloat16)

        add_rows(long, add)
        span = slice(index * long, (index + 1) * long)
        copy = remote(
            onward.at[span], second_in.at[span], grad_s.at[2, index], grad_r.at[2, index],
            second_device,
        )
        copy.start()
        seconds.append(copy)
    for turn in range(2):
        start = pl.multiple_of((1 - core if turn == 0 else core) * long, long)
        if turn == 0:
            for copy in (firsts[1], firsts[3], seconds[0], seconds[1]):
                copy.wait_recv()

        def add(span, start=start):
            span = pl.ds(pl.multiple_of(span.start + start, 32), span.size)
            total[span] = (
                (grads[chip, span].astype(jnp.float32) + first_in[1, span].astype(jnp.float32))
                + second_in[span].astype(jnp.float32)
            ).astype(jnp.bfloat16)

        add_rows(long, add)
        if turn == 0:
            swap = remote(
                total.at[pl.ds(start, long)], swapped, grad_s.at[3, 0], grad_r.at[3, 0], mate
            )
            swap.start()
    group = 2 * quarter + core
    part_width = width // 4
    own_rows = pl.ds(pl.multiple_of(core * long, long), long)
    for index in range(3):
        spot = pl.multiple_of(index * width + group * part_width, part_width)
        placed[:, pl.ds(spot, part_width)] = total[
            own_rows, index * part_width : (index + 1) * part_width
        ]
    swap.wait_recv()
    for index in range(3):
        spot = pl.multiple_of(
            index * width + (2 * quarter + 1 - core) * part_width, part_width
        )
        placed[:, pl.ds(spot, part_width)] = swapped[
            :, index * part_width : (index + 1) * part_width
        ]

    for slot in range(3):
        sends[slot].wait_send()

    @pl.when(here)
    def _():
        own.wait()

    @pl.when(jnp.logical_not(here))
    def _():
        sends[3].wait_send()

    for source in range(4):
        arrival = remote(
            sums.at[0],
            landed.at[source // 2, source % 2],
            sem_s.at[1, 0],
            sem_r.at[1, source],
            mate,
        )

        @pl.when(jnp.logical_not(jnp.logical_and(here, 2 * quarter + core == source)))
        def _():
            arrival.wait_recv()

    for side in range(2):

        def add(span, side=side):
            target = pl.ds(span.start + side * rows, span.size)
            out[target] = landed[0, side, span].astype(jnp.float32) + landed[
                1, side, span
            ].astype(jnp.float32)

        add_rows(rows, add)
    for copy in swaps + firsts + seconds + [swap]:
        copy.wait_send()


def finish(part, grads, out_grad, number, after=()):
    _, rows, width = part.shape
    _, long, joined = grads.shape
    low = part.dtype
    return comm_call(
        finish_kernel,
        (
            jax.ShapeDtypeStruct((rows, width), jnp.float32),
            jax.ShapeDtypeStruct((long // 2, 4 * width), low),
        ),
        (part, grads, out_grad),
        [VM] * 3,
        (VM, VM),
        [
            pltpu.VMEM((4, rows // 2, width), low),
            pltpu.VMEM((4, rows // 2, width), low),
            pltpu.VMEM((2, 2, rows // 2, width), low),
            pltpu.VMEM((2, long, joined), low),
            pltpu.VMEM((long, joined), low),
            pltpu.VMEM((long, joined), low),
            pltpu.VMEM((long, joined), low),
            pltpu.VMEM((long // 2, joined), low),
            DMA,
            DMA((2, 4)),
            DMA((2, 4)),
            DMA((4, 2)),
            DMA((4, 2)),
        ],
        "finish",
        number,
        after,
    )


def turn_heads(values, cosine, signed):
    middle = values.shape[-1] // 2
    return values * cosine + jnp.concatenate(
        [values[:, middle:], values[:, :middle]], axis=1
    ) * signed


def dot_nt(a, b):
    return lax.dot_general(a, b, (((1,), (1,)), ((), ())), preferred_element_type=jnp.float32)


def dot_tn(a, b):
    return lax.dot_general(a, b, (((0,), (0,)), ((), ())), preferred_element_type=jnp.float32)


def dot_nn(a, b):
    return jnp.dot(a, b, preferred_element_type=jnp.float32)


ATTENTION_ROWS = 256


def causal(scores, start):
    query = start + lax.broadcasted_iota(jnp.int32, scores.shape, 0)
    key = lax.broadcasted_iota(jnp.int32, scores.shape, 1)
    return jnp.where(key <= query, scores, masked_value)


def attend_kernel(
    q_raw, k_raw, v_raw, q_factor, k_factor, q_gain, k_gain, cosine, signed,
    q_out, k_out, v_out, attended, log_total
):
    length, size = q_raw.shape
    scale = size ** (-0.5)
    cos, sin = cosine[...], signed[...]
    q_out[...] = turn_heads(
        q_raw[...] * q_factor[...] * q_gain[...], cos, sin
    ).astype(jnp.bfloat16)
    k_out[...] = turn_heads(
        k_raw[...] * k_factor[...] * k_gain[...], cos, sin
    ).astype(jnp.bfloat16)
    v_out[...] = v_raw[...].astype(jnp.bfloat16)
    rows = min(ATTENTION_ROWS, length)
    for start in range(0, length, rows):
        stop = start + rows
        scores = dot_nt(q_out[start:stop], k_out[:stop]) * scale
        scores = causal(scores, start)
        maximum = jnp.max(scores, axis=-1, keepdims=True)
        exponent = jnp.exp(scores - maximum)
        total = jnp.sum(exponent, axis=-1, keepdims=True)
        weights = (exponent * (1.0 / total)).astype(jnp.bfloat16)
        attended[start:stop] = dot_nn(weights, v_out[:stop]).astype(jnp.bfloat16)
        log_total[0, start:stop] = maximum + jnp.log(total)


def attend(raw, q_factor, k_factor, q_gain, k_gain, cosine, signed, size, after=()):
    length, width = raw.shape[0], raw.shape[1] // 3
    heads = width // size
    by_head = pl.BlockSpec((length, size), lambda h: (0, h))
    parts = [
        pl.BlockSpec((length, size), lambda h, start=index * heads: (0, start + h))
        for index in range(3)
    ]
    fixed = pl.BlockSpec((length, size), lambda h: (0, 0))
    factor = pl.BlockSpec((length, 1), lambda h: (0, 0))
    gain = pl.BlockSpec((1, size), lambda h: (0, h))
    low = jax.ShapeDtypeStruct((length, width), jnp.bfloat16)
    flops = heads * length * length * size * 2
    inputs = (raw, raw, raw, q_factor, k_factor, q_gain, k_gain, cosine, signed)
    return pl.pallas_call(
        ordered(attend_kernel, inputs, after),
        grid=(heads,),
        out_shape=(low, low, low, low, jax.ShapeDtypeStruct((heads, length, 1), jnp.float32)),
        in_specs=parts + [factor] * 2 + [gain] * 2 + [fixed] * 2 + [ANY] * len(after),
        out_specs=[by_head] * 4 + [pl.BlockSpec((1, length, 1), lambda h: (h, 0, 0))],
        name="attend",
        compiler_params=pltpu.CompilerParams(vmem_limit_bytes=VMEM_LIMIT),
        cost_estimate=pl.CostEstimate(
            flops=flops, bytes_accessed=20 * length * width, transcendentals=flops // (4 * size)
        ),
    )(*inputs, *after)


def attend_back_kernel(
    queries, keys, values, grads, log_total, cosine, signed, q_grad, k_grad, v_grad, k_sum, v_sum
):
    length, size = queries.shape
    scale = size ** (-0.5)
    rows = min(ATTENTION_ROWS, length)
    k_sum[...] = jnp.zeros_like(k_sum)
    v_sum[...] = jnp.zeros_like(v_sum)
    for start in range(0, length, rows):
        stop = start + rows
        query, grad = queries[start:stop], grads[start:stop]
        scores = causal(dot_nt(query, keys[:stop]) * scale, start)
        weights = jnp.exp(scores - log_total[0, start:stop])
        v_sum[:stop] += dot_tn(weights.astype(jnp.bfloat16), grad)
        weight_grad = dot_nt(grad, values[:stop])
        inner = jnp.sum(weights * weight_grad, axis=-1, keepdims=True)
        score_grad = (weights * (weight_grad - inner)).astype(jnp.bfloat16)
        q_low = (dot_nn(score_grad, keys[:stop]) * scale).astype(jnp.bfloat16)
        q_grad[start:stop] = turn_heads(
            q_low.astype(jnp.float32), cosine[start:stop], -signed[start:stop]
        )
        k_sum[:stop] += dot_tn(score_grad, query)
    k_low = (k_sum[...] * scale).astype(jnp.bfloat16)
    k_grad[...] = turn_heads(k_low.astype(jnp.float32), cosine[...], -signed[...])
    v_grad[...] = v_sum[...].astype(jnp.bfloat16)


def attend_back(queries, keys, values, grads, log_total, cosine, signed, size, after=()):
    length, width = queries.shape
    heads = width // size
    by_head = pl.BlockSpec((length, size), lambda h: (0, h))
    fixed = pl.BlockSpec((length, size), lambda h: (0, 0))
    wide = jax.ShapeDtypeStruct((length, width), jnp.float32)
    flops = heads * length * length * size * 5
    inputs = (queries, keys, values, grads, log_total, cosine, signed)
    return pl.pallas_call(
        ordered(attend_back_kernel, inputs, after),
        grid=(heads,),
        out_shape=(wide, wide, jax.ShapeDtypeStruct((length, width), jnp.bfloat16)),
        in_specs=[by_head] * 4
        + [pl.BlockSpec((1, length, 1), lambda h: (h, 0, 0))]
        + [fixed] * 2
        + [ANY] * len(after),
        out_specs=[by_head] * 3,
        scratch_shapes=[pltpu.VMEM((length, size), jnp.float32)] * 2,
        name="attend_back",
        compiler_params=pltpu.CompilerParams(vmem_limit_bytes=VMEM_LIMIT),
        cost_estimate=pl.CostEstimate(
            flops=flops, bytes_accessed=20 * length * width, transcendentals=flops // (10 * size)
        ),
    )(*inputs, *after)


class LineGather:
    def __init__(self, block):
        self.seq = lax.axis_index("seq")
        self.block = block
        self.up, self.down = [block], [block]

    def step(self):
        done = len(self.up)
        up = [(i, i + 1) for i in range(done - 1, 3)]
        down = [(3 - i, 3 - j) for i, j in up]
        self.up.append(lax.ppermute(self.up[-1], "seq", up))
        self.down.append(lax.ppermute(self.down[-1], "seq", down))
        return (self.up[-1], self.down[-1])

    def blocks(self):
        while len(self.up) < 4:
            self.step()
        seq = self.seq
        found = [(seq, self.block)]
        for back in (1, 2, 3):
            came = jnp.where(seq >= back, self.up[back], self.down[4 - back])
            found.append((lax.rem(seq + 4 - back, 4), came))
        return found


def line_total(part):
    for route in ([(0, 1), (3, 2)], [(1, 2), (2, 1)]):
        part = part + lax.ppermute(part, "seq", route)
    seq = lax.axis_index("seq")
    inner = jnp.logical_or(seq == 1, seq == 2)
    return jnp.where(inner, part, lax.ppermute(part, "seq", [(1, 0), (2, 3)]))


def gain_sums(part):
    for mask in (1, 2, 4):
        part = part + lax.ppermute(part, "fsdp", [(i, i ^ mask) for i in range(8)])
    return line_total(part)


def split_layer(
    block_input, query_weight, key_weight, value_weight, out_weight, gate_weight, up_weight,
    down_weight, query_gain, key_gain, attention_gain, swiglu_gain, cotangent
):
    tokens, width = block_input.shape[1:]
    head_size = width // HEADS
    seq, shard = lax.axis_index("seq"), lax.axis_index("fsdp")
    core, chip = lax.rem(shard, 2), lax.div(shard, 2)
    half, quarter = lax.div(seq, 2), lax.rem(seq, 2)
    rows = query_weight.shape[0]
    hidden_width = gate_weight.shape[1] // 8
    group_width = width // 4
    group = 2 * quarter + core
    length = 4 * tokens
    low = jnp.bfloat16
    sequence = block_input.reshape(tokens, width)

    whole, qkv = entry(sequence, query_weight, key_weight, value_weight, 1)
    whole = whole.reshape(length, width)
    out_full = lax.all_gather(
        keep(out_weight, (qkv,)), "fsdp", axis=0, tiled=True
    )
    shard_later = keep(shard.reshape(1), (qkv,), pltpu.SMEM)[0]

    def columns_of(weight):
        pieces = {}
        for mask in (1, 2, 4, 3, 5, 6, 7, 0):
            partner = flip_mask(shard_later, mask)
            piece = lax.dynamic_slice_in_dim(weight, partner * hidden_width, hidden_width, 1)
            if mask:
                piece = lax.ppermute(piece, "fsdp", [(i, i ^ mask) for i in range(8)])
            pieces[mask] = piece
        return pieces

    def joined_columns(pieces):
        cols = jnp.zeros((8, rows, hidden_width), low)
        for mask, piece in pieces.items():
            cols = lax.dynamic_update_index_in_dim(cols, piece, flip_mask(shard, mask), 0)
        return cols.reshape(width, hidden_width)

    gate_pieces, up_pieces = columns_of(gate_weight), columns_of(up_weight)
    gate_cols, up_cols = joined_columns(gate_pieces), joined_columns(up_pieces)

    raw = dot_nn(whole, qkv)
    q_raw, k_raw = raw[:, :group_width], raw[:, group_width : 2 * group_width]

    def reduced(first, second, number, after=()):
        part = jnp.stack([first, second]).reshape(2 * length // 128, 128)
        total = stats_sum(part, number, after).reshape(2, length, 1)
        return total[0] / width, total[1] / width

    q_mean, k_mean = reduced(
        jnp.sum(q_raw * q_raw, axis=-1), jnp.sum(k_raw * k_raw, axis=-1), 2
    )
    q_factor, k_factor = lax.rsqrt(q_mean + epsilon), lax.rsqrt(k_mean + epsilon)
    cosine, sine = rotary_tables(length, 0, head_size)
    cosine = jnp.concatenate([cosine[:, 0], cosine[:, 0]], axis=1)
    signed = jnp.concatenate([-sine[:, 0], sine[:, 0]], axis=1)
    q_gain_part = lax.dynamic_slice_in_dim(query_gain, group * group_width, group_width)[None]
    k_gain_part = lax.dynamic_slice_in_dim(key_gain, group * group_width, group_width)[None]
    queries, keys, values, attended_heads, log_total = attend(
        raw, q_factor, k_factor, q_gain_part, k_gain_part, cosine, signed, head_size,
        tuple(gate_pieces[mask] for mask in (1, 2, 4, 3)),
    )
    attended = to_tokens(
        attended_heads.reshape(4, tokens, group_width),
        3,
        tuple(gate_pieces[mask] for mask in (5, 6, 7)) + (up_pieces[1], up_pieces[2]),
    )
    branch = dot_nn(attended, out_full)
    branch_factor = norm_factor(branch)
    residual = sequence.astype(jnp.float32) + branch * branch_factor * attention_gain

    plane = plane_gather(
        residual.astype(low), 4, tuple(up_pieces[mask] for mask in (4, 3, 5, 6, 7))
    ).reshape(8 * tokens, width)
    gate_value = dot_nn(plane, gate_cols)
    upward = dot_nn(plane, up_cols)
    sigmoid_gate = jax.nn.sigmoid(gate_value)
    hidden = (gate_value * sigmoid_gate * upward).astype(low)
    mixed_part = dot_nn(hidden, down_weight).astype(low)
    mixed_out = plane_scatter(mixed_part.reshape(8, tokens, width), 5)
    mixed_factor = norm_factor(mixed_out)
    output = residual + mixed_out * mixed_factor * swiglu_gain
    upstream = cotangent.reshape(tokens, width).astype(jnp.float32)
    mixed_float, swiglu_gain_grad = norm_backward(mixed_out, mixed_factor, swiglu_gain, upstream)
    mixed_plane = plane_gather(mixed_float.astype(low), 6).reshape(8 * tokens, width)
    down_grad = transposed_times(hidden, mixed_plane).astype(low)
    down_block = lax.psum_scatter(down_grad, "seq", scatter_dimension=0, tiled=True)
    hidden_grad = times_transposed(mixed_plane, down_weight)
    gate_grad = (
        hidden_grad * upward * sigmoid_gate * (1.0 + gate_value * (1.0 - sigmoid_gate))
    ).astype(low)
    up_grad = (hidden_grad * (gate_value * sigmoid_gate)).astype(low)
    residual_part = (
        times_transposed(gate_grad, gate_cols) + times_transposed(up_grad, up_cols)
    ).astype(low)
    gate_sum = transposed_times(plane, gate_grad).astype(low).reshape(8, rows, hidden_width)
    gate_block = lax.psum_scatter(gate_sum, "seq", scatter_dimension=1, tiled=True)
    up_sum = transposed_times(plane, up_grad).astype(low).reshape(8, rows, hidden_width)
    up_block = lax.psum_scatter(up_sum, "seq", scatter_dimension=1, tiled=True)
    residual_grad = upstream + plane_scatter(
        residual_part.reshape(8, tokens, width), 7, (down_block, gate_sum, up_sum)
    )

    down_line = LineGather(down_block)

    branch_float, attention_gain_grad = norm_backward(
        branch, branch_factor, attention_gain, residual_grad
    )
    branch_grad = branch_float.astype(low)
    attended_grad = times_transposed(branch_grad, out_full).astype(low)
    head_grad = to_heads(attended_grad, 8).reshape(length, group_width)
    out_grad = lax.psum_scatter(
        transposed_times(attended, branch_grad).astype(low), "fsdp", scatter_dimension=0, tiled=True
    )
    q_norm_grad, k_norm_grad, value_grad = attend_back(
        queries, keys, values, head_grad, log_total, cosine, signed, head_size,
        (gate_block,),
    )
    q_scaled, k_scaled = q_norm_grad * q_gain_part, k_norm_grad * k_gain_part
    q_inner, k_inner = reduced(
        jnp.sum(q_scaled * q_raw, axis=-1), jnp.sum(k_scaled * k_raw, axis=-1), 9
    )
    q_gain_sum = jnp.sum(q_norm_grad * q_raw * q_factor, axis=0)
    k_gain_sum = jnp.sum(k_norm_grad * k_raw * k_factor, axis=0)
    q_raw_grad = (q_factor * q_scaled - q_raw * (q_factor * q_factor * q_factor * q_inner)).astype(low)
    k_raw_grad = (k_factor * k_scaled - k_raw * (k_factor * k_factor * k_factor * k_inner)).astype(low)
    joined = jnp.concatenate([q_raw_grad, k_raw_grad, value_grad], axis=1)
    input_part = times_transposed(joined, qkv).astype(low)
    qkv_grad = transposed_times(whole, joined).astype(low)
    input_sum, attention_part = finish(
        input_part.reshape(4, tokens, width),
        qkv_grad.reshape(4, 2 * rows, 3 * group_width),
        out_grad,
        10,
        (up_block,) + down_line.step() + down_line.step() + down_line.step(),
    )
    input_grad = residual_grad + input_sum

    share = rows // 4

    def owned(block):
        full = jnp.zeros((share, 8 * hidden_width), low)
        for mask in (1, 2, 4, 3, 5, 6, 7, 0):
            partner = flip_mask(shard, mask)
            piece = lax.dynamic_index_in_dim(block, partner, 0, keepdims=False)
            if mask:
                piece = lax.ppermute(piece, "fsdp", [(i, i ^ mask) for i in range(8)])
            full = lax.dynamic_update_slice(full, piece, (0, partner * hidden_width))
        return full

    gate_line, up_line = LineGather(owned(gate_block)), LineGather(owned(up_block))
    attention_line = LineGather(
        lax.psum_scatter(attention_part, "seq", scatter_dimension=0, tiled=True)
    )

    def whole_line(line):
        blocks = line.blocks()
        count, columns = line.block.shape
        total = jnp.zeros((4 * count, columns), jnp.float32)
        for slot, block in blocks:
            total = lax.dynamic_update_slice(
                total, block.astype(jnp.float32), (slot * count, 0)
            )
        return total

    down_total, gate_total, up_total = map(whole_line, (down_line, gate_line, up_line))
    attention_total = whole_line(attention_line)
    query_total, key_total, value_total, out_total = (
        attention_total[:, index * width : (index + 1) * width] for index in range(4)
    )

    def widen(part):
        return lax.dynamic_update_slice(
            jnp.zeros((width,), jnp.float32), part, (group * group_width,)
        )

    gain_totals = gain_sums(
        jnp.stack([widen(q_gain_sum), widen(k_gain_sum), attention_gain_grad, swiglu_gain_grad])
    )
    return (
        output.reshape(1, tokens, width),
        input_grad.reshape(1, tokens, width),
        query_total,
        key_total,
        value_total,
        out_total,
        gate_total,
        up_total,
        down_total,
        gain_totals[0],
        gain_totals[1],
        gain_totals[2],
        gain_totals[3],
    )


def fits(mesh):
    return mesh.shape["seq"] == 4 and mesh.shape["fsdp"] == 8


def solution(mesh):
    placed = (
        P("fsdp", "seq", None),
        P("fsdp", None),
        P("fsdp", None),
        P("fsdp", None),
        P("fsdp", None),
        P("fsdp", None),
        P("fsdp", None),
        P("fsdp", None),
        P(),
        P(),
        P(),
        P(),
        P("fsdp", "seq", None),
    )
    return jax.shard_map(
        split_layer if fits(mesh) else local,
        mesh=mesh,
        in_specs=placed,
        out_specs=(
            P("fsdp", "seq", None),
            P("fsdp", "seq", None),
            P("fsdp", None),
            P("fsdp", None),
            P("fsdp", None),
            P("fsdp", None),
            P("fsdp", None),
            P("fsdp", None),
            P("fsdp", None),
            P(),
            P(),
            P(),
            P(),
        ),
        check_vma=False,
    )
```

```python
import jax
import jax.numpy as jnp
from jax import lax
from jax.experimental import pallas as pl
from jax.experimental.pallas import tpu as pltpu
from jax.sharding import PartitionSpec as P

HEADS = 16


epsilon = 1e-06
rotary_base = 500000.0
masked_value = -1e30


def norm_factor(values):
    return lax.rsqrt(jnp.mean(values * values, axis=-1, keepdims=True) + epsilon)


def norm_backward(values, factor, gain_vector, upstream):
    scaled = upstream * gain_vector
    inner_mean = jnp.mean(scaled * values, axis=-1, keepdims=True)
    value_grad = factor * scaled - values * factor * factor * factor * inner_mean
    gain_grad = jnp.sum(upstream * values * factor, axis=0)
    return (value_grad, gain_grad)


def rotary_tables(count, offset, head_size):
    positions = (offset + jnp.arange(count, dtype=jnp.int32)).astype(jnp.float32)
    middle = head_size // 2
    frequency = rotary_base ** (-2.0 * jnp.arange(middle, dtype=jnp.float32) / head_size)
    angles = positions[:, None] * frequency[None, :]
    return (jnp.cos(angles)[:, None, :], jnp.sin(angles)[:, None, :])


def rotate(values, cosine, sine_table, direction_sign):
    middle = values.shape[-1] // 2
    leading = values[..., :middle]
    trailing = values[..., middle:]
    signed = sine_table * direction_sign
    return jnp.concatenate(
        [leading * cosine - trailing * signed, trailing * cosine + leading * signed], axis=-1
    )


def times_transposed(operand, matrix):
    return lax.dot_general(
        operand, matrix, (((1,), (1,)), ((), ())), preferred_element_type=jnp.float32
    )


def transposed_times(operand, matrix):
    return lax.dot_general(
        operand, matrix, (((0,), (0,)), ((), ())), preferred_element_type=jnp.float32
    )


def masked_scores(query_block, keys, row_start, block_rows, score_scale):
    length = keys.shape[0]
    scores = (
        jnp.einsum("qhd,khd->hqk", query_block, keys, preferred_element_type=jnp.float32)
        * score_scale
    )
    query_positions = row_start + jnp.arange(block_rows, dtype=jnp.int32)
    key_positions = jnp.arange(length, dtype=jnp.int32)
    allowed = key_positions[None, :] <= query_positions[:, None]
    return jnp.where(allowed[None], scores, masked_value)


def attention_forward(queries, keys, values):
    length = queries.shape[0]
    block_rows = min(512, length)
    blocks = length // block_rows
    score_scale = queries.shape[-1] ** (-0.5)

    def one_block(block_index):
        row_start = block_index * block_rows
        query_block = lax.dynamic_slice_in_dim(queries, row_start, block_rows, 0)
        scores = masked_scores(query_block, keys, row_start, block_rows, score_scale)
        maximum = jnp.max(scores, axis=-1, keepdims=True)
        exponent = jnp.exp(scores - maximum)
        row_total = jnp.sum(exponent, axis=-1, keepdims=True)
        log_total = maximum[..., 0] + jnp.log(row_total[..., 0])
        weights_low = (exponent / row_total).astype(jnp.bfloat16)
        attended = jnp.einsum(
            "hqk,khd->qhd", weights_low, values, preferred_element_type=jnp.float32
        )
        return (attended.astype(jnp.bfloat16), log_total)

    attended, log_total = lax.map(one_block, jnp.arange(blocks, dtype=jnp.int32))
    return (attended.reshape(length, -1), log_total)


def attention_backward(queries, keys, values, attended_grad, log_total):
    length = queries.shape[0]
    block_rows = min(512, length)
    blocks = length // block_rows
    score_scale = queries.shape[-1] ** (-0.5)
    empty = jnp.zeros(keys.shape, jnp.float32)

    def one_block(carried, operands):
        key_sum, value_sum = carried
        block_index, block_total = operands
        row_start = block_index * block_rows
        query_block = lax.dynamic_slice_in_dim(queries, row_start, block_rows, 0)
        grad_block = lax.dynamic_slice_in_dim(attended_grad, row_start, block_rows, 0)
        scores = masked_scores(query_block, keys, row_start, block_rows, score_scale)
        probabilities = jnp.exp(scores - block_total[..., None])
        weights_low = probabilities.astype(jnp.bfloat16)
        value_sum = value_sum + jnp.einsum(
            "hqk,qhd->khd", weights_low, grad_block, preferred_element_type=jnp.float32
        )
        probability_grad = jnp.einsum(
            "qhd,khd->hqk", grad_block, values, preferred_element_type=jnp.float32
        )
        inner_sum = jnp.sum(probabilities * probability_grad, axis=-1, keepdims=True)
        score_grad = (probabilities * (probability_grad - inner_sum)).astype(jnp.bfloat16)
        query_grad = (
            jnp.einsum("hqk,khd->qhd", score_grad, keys, preferred_element_type=jnp.float32)
            * score_scale
        )
        key_sum = (
            key_sum
            + jnp.einsum(
                "hqk,qhd->khd", score_grad, query_block, preferred_element_type=jnp.float32
            )
            * score_scale
        )
        return ((key_sum, value_sum), query_grad.astype(jnp.bfloat16))

    (key_sum, value_sum), query_grads = lax.scan(
        one_block, (empty, empty), (jnp.arange(blocks, dtype=jnp.int32), log_total)
    )
    return (
        query_grads.reshape(keys.shape),
        key_sum.astype(jnp.bfloat16),
        value_sum.astype(jnp.bfloat16),
    )


def local(
    block_input,
    query_weight,
    key_weight,
    value_weight,
    out_weight,
    gate_weight,
    up_weight,
    down_weight,
    query_gain,
    key_gain,
    attention_gain,
    swiglu_gain,
    cotangent,
):
    tokens = block_input.shape[1]
    model_width = block_input.shape[2]
    head_size = model_width // HEADS
    groups = lax.axis_size("seq")
    local_heads = HEADS // groups
    sequence = block_input.reshape(tokens, model_width)
    query_full, key_full, value_full, out_full = (
        lax.all_gather(query_weight, "fsdp", axis=0, tiled=True),
        lax.all_gather(key_weight, "fsdp", axis=0, tiled=True),
        lax.all_gather(value_weight, "fsdp", axis=0, tiled=True),
        lax.all_gather(out_weight, "fsdp", axis=0, tiled=True),
    )
    query_raw = jnp.dot(sequence, query_full, preferred_element_type=jnp.float32)
    key_raw = jnp.dot(sequence, key_full, preferred_element_type=jnp.float32)
    value_raw = jnp.dot(sequence, value_full, preferred_element_type=jnp.float32)
    query_factor = norm_factor(query_raw)
    key_factor = norm_factor(key_raw)
    cosine, sine_table = rotary_tables(tokens, lax.axis_index("seq") * tokens, head_size)
    query_rot = rotate(
        (query_raw * query_factor * query_gain).reshape(tokens, HEADS, head_size),
        cosine,
        sine_table,
        1.0,
    )
    key_rot = rotate(
        (key_raw * key_factor * key_gain).reshape(tokens, HEADS, head_size), cosine, sine_table, 1.0
    )
    stacked = jnp.stack(
        [
            query_rot.reshape(tokens, model_width).astype(jnp.bfloat16),
            key_rot.reshape(tokens, model_width).astype(jnp.bfloat16),
            value_raw.astype(jnp.bfloat16),
        ]
    )
    grouped = lax.all_to_all(stacked, "seq", split_axis=2, concat_axis=1, tiled=True)
    length = grouped.shape[1]
    head_queries = grouped[0].reshape(length, local_heads, head_size)
    head_keys = grouped[1].reshape(length, local_heads, head_size)
    head_values = grouped[2].reshape(length, local_heads, head_size)
    attended_heads, log_total = attention_forward(head_queries, head_keys, head_values)
    attended = lax.all_to_all(attended_heads, "seq", split_axis=0, concat_axis=1, tiled=True)
    branch = jnp.dot(attended, out_full, preferred_element_type=jnp.float32)
    branch_factor = norm_factor(branch)
    residual = sequence.astype(jnp.float32) + branch * branch_factor * attention_gain
    residual_low = residual.astype(jnp.bfloat16)
    gate_full, up_full, down_full = (
        lax.all_gather(gate_weight, "fsdp", axis=0, tiled=True),
        lax.all_gather(up_weight, "fsdp", axis=0, tiled=True),
        lax.all_gather(down_weight, "fsdp", axis=0, tiled=True),
    )
    gate_value = jnp.dot(residual_low, gate_full, preferred_element_type=jnp.float32)
    upward = jnp.dot(residual_low, up_full, preferred_element_type=jnp.float32)
    sigmoid_gate = jax.nn.sigmoid(gate_value)
    activated = gate_value * sigmoid_gate
    hidden = (activated * upward).astype(jnp.bfloat16)
    mixed_out = jnp.dot(hidden, down_full, preferred_element_type=jnp.float32)
    mixed_factor = norm_factor(mixed_out)
    output = residual + mixed_out * mixed_factor * swiglu_gain
    upstream = cotangent.reshape(tokens, model_width).astype(jnp.float32)
    mixed_float, swiglu_gain_grad = norm_backward(mixed_out, mixed_factor, swiglu_gain, upstream)
    mixed_grad = mixed_float.astype(jnp.bfloat16)
    gate_back, up_back, down_back = (
        lax.all_gather(gate_weight, "fsdp", axis=0, tiled=True),
        lax.all_gather(up_weight, "fsdp", axis=0, tiled=True),
        lax.all_gather(down_weight, "fsdp", axis=0, tiled=True),
    )
    hidden_grad = times_transposed(mixed_grad, down_back)
    gate_grad = (
        hidden_grad * upward * sigmoid_gate * (1.0 + gate_value * (1.0 - sigmoid_gate))
    ).astype(jnp.bfloat16)
    up_grad = (hidden_grad * activated).astype(jnp.bfloat16)
    residual_grad = (
        upstream + times_transposed(gate_grad, gate_back) + times_transposed(up_grad, up_back)
    )
    joined = jnp.concatenate([gate_grad, up_grad], axis=1)
    branch_float, attention_gain_grad = norm_backward(
        branch, branch_factor, attention_gain, residual_grad
    )
    branch_grad = branch_float.astype(jnp.bfloat16)
    query_back, key_back, value_back, out_back = (
        lax.all_gather(query_weight, "fsdp", axis=0, tiled=True),
        lax.all_gather(key_weight, "fsdp", axis=0, tiled=True),
        lax.all_gather(value_weight, "fsdp", axis=0, tiled=True),
        lax.all_gather(out_weight, "fsdp", axis=0, tiled=True),
    )
    attended_grad = times_transposed(branch_grad, out_back).astype(jnp.bfloat16)
    head_grad = lax.all_to_all(attended_grad, "seq", split_axis=1, concat_axis=0, tiled=True)
    query_grads, key_grads, value_grads = attention_backward(
        head_queries,
        head_keys,
        head_values,
        head_grad.reshape(length, local_heads, head_size),
        log_total,
    )
    back_stack = jnp.stack([query_grads, key_grads, value_grads]).reshape(
        3, length, local_heads * head_size
    )
    token_grads = lax.all_to_all(back_stack, "seq", split_axis=1, concat_axis=2, tiled=True)
    query_norm_grad = rotate(
        token_grads[0].astype(jnp.float32).reshape(tokens, HEADS, head_size),
        cosine,
        sine_table,
        -1.0,
    )
    key_norm_grad = rotate(
        token_grads[1].astype(jnp.float32).reshape(tokens, HEADS, head_size),
        cosine,
        sine_table,
        -1.0,
    )
    query_float, query_gain_grad = norm_backward(
        query_raw, query_factor, query_gain, query_norm_grad.reshape(tokens, model_width)
    )
    key_float, key_gain_grad = norm_backward(
        key_raw, key_factor, key_gain, key_norm_grad.reshape(tokens, model_width)
    )
    query_raw_grad = query_float.astype(jnp.bfloat16)
    key_raw_grad = key_float.astype(jnp.bfloat16)
    value_tokens = token_grads[2]
    input_grad = (
        residual_grad
        + times_transposed(query_raw_grad, query_back)
        + times_transposed(key_raw_grad, key_back)
        + times_transposed(value_tokens, value_back)
    )
    projected = jnp.concatenate([query_raw_grad, key_raw_grad, value_tokens], axis=1)
    hidden_width = gate_weight.shape[1]
    columns = hidden
    down_shard = lax.psum_scatter(
        transposed_times(columns, mixed_grad).astype(jnp.bfloat16),
        "fsdp",
        scatter_dimension=0,
        tiled=True,
    )
    columns = residual_low
    gate_up_shard = lax.psum_scatter(
        transposed_times(columns, joined).astype(jnp.bfloat16),
        "fsdp",
        scatter_dimension=0,
        tiled=True,
    )
    attention_shard = lax.psum_scatter(
        jnp.concatenate(
            [transposed_times(sequence, projected), transposed_times(attended, branch_grad)], axis=1
        ).astype(jnp.bfloat16),
        "fsdp",
        scatter_dimension=0,
        tiled=True,
    )
    attention_total, gate_up_total, down_total = (
        lax.psum(attention_shard, "seq").astype(jnp.float32),
        lax.psum(gate_up_shard, "seq").astype(jnp.float32),
        lax.psum(down_shard, "seq").astype(jnp.float32),
    )
    gain_totals = lax.psum(
        jnp.stack([query_gain_grad, key_gain_grad, attention_gain_grad, swiglu_gain_grad]),
        ("seq", "fsdp"),
    )
    return (
        output.reshape(1, tokens, model_width),
        input_grad.reshape(1, tokens, model_width),
        attention_total[:, :model_width],
        attention_total[:, model_width : 2 * model_width],
        attention_total[:, 2 * model_width : 3 * model_width],
        attention_total[:, 3 * model_width :],
        gate_up_total[:, :hidden_width],
        gate_up_total[:, hidden_width:],
        down_total,
        gain_totals[0],
        gain_totals[1],
        gain_totals[2],
        gain_totals[3],
    )


MESH = pl.DeviceIdType.MESH
ANY = pl.BlockSpec(memory_space=pl.ANY)
VM = pl.BlockSpec(memory_space=pltpu.VMEM)
DMA = pltpu.SemaphoreType.DMA
VMEM_LIMIT = 56 * 1024 * 1024


def flip(value, bit):
    return value + bit - 2 * bit * lax.rem(lax.div(value, bit), 2)


def flip_mask(value, mask):
    for bit in (1, 2, 4):
        if mask & bit:
            value = flip(value, bit)
    return value


def place():
    seq, shard = lax.axis_index("seq"), lax.axis_index("fsdp")
    return seq, shard


def greet(targets):
    barrier = pltpu.get_barrier_semaphore()
    for target in targets:
        pl.semaphore_signal(barrier, inc=1, device_id=target, device_id_type=MESH)
    pl.semaphore_wait(barrier, len(targets))


def remote(source, target_ref, send, receive, device):
    return pltpu.make_async_remote_copy(
        src_ref=source,
        dst_ref=target_ref,
        send_sem=send,
        recv_sem=receive,
        device_id=device,
        device_id_type=MESH,
    )


def column_others(seq, shard):
    mate = flip(shard, 1)
    others = [(lax.rem(seq + step, 4), shard) for step in (1, 2, 3)]
    return others + [(lax.rem(seq + step, 4), mate) for step in (0, 1, 2, 3)]


def ordered(kernel, inputs, after):
    count, extra = len(inputs), len(after)
    return lambda *refs: kernel(*refs[:count], *refs[count + extra :])


def comm_call(kernel, out_shape, inputs, in_specs, out_specs, scratch, name, number, after=()):
    return pl.pallas_call(
        ordered(kernel, inputs, after),
        out_shape=out_shape,
        in_specs=list(in_specs) + [ANY] * len(after),
        out_specs=out_specs,
        scratch_shapes=scratch,
        name=name,
        compiler_params=pltpu.CompilerParams(
            collective_id=number, has_side_effects=True, vmem_limit_bytes=VMEM_LIMIT
        ),
        cost_estimate=pl.CostEstimate(flops=1, bytes_accessed=1, transcendentals=0),
    )(*inputs, *after)


def keep_kernel(x, out):
    out[...] = x[...]


def hold_kernel(x, out):
    pass


def hold(x, after):
    return pl.pallas_call(
        ordered(hold_kernel, (x,), after),
        out_shape=jax.ShapeDtypeStruct(x.shape, x.dtype),
        in_specs=[ANY] * (1 + len(after)),
        out_specs=ANY,
        input_output_aliases={0: 0},
        name="hold",
    )(x, *after)


def keep(x, after):
    return pl.pallas_call(
        ordered(keep_kernel, (x,), after),
        out_shape=jax.ShapeDtypeStruct(x.shape, x.dtype),
        in_specs=[VM] + [ANY] * len(after),
        out_specs=VM,
        name="keep",
    )(x, *after)


def entry_kernel(
    x, wq, wk, wv, xo, wo, local, x_send, x_recv, fwd_send, w_send, w_recv
):
    seq, shard = place()
    core, half = lax.rem(shard, 2), lax.div(seq, 2)
    quarter = lax.rem(seq, 2)
    rows, width = wq.shape[0], wo.shape[1] // 3
    weights = (wq, wk, wv)
    greet(
        [(seq, flip_mask(shard, mask)) for mask in range(1, 8)]
        + [(lax.rem(seq + step, 4), shard) for step in (1, 2, 3)]
    )
    mine = pl.ds(pl.multiple_of(shard * rows, rows), rows)

    def columns(index):
        return slice(index * width, (index + 1) * width)

    def block(index, target):
        group = 2 * quarter + lax.rem(target, 2)
        return weights[index].at[:, pl.ds(pl.multiple_of(group * width, width), width)]

    x_copies = []
    for which in (0, 1):
        target = 2 * core + which
        copy = remote(x, xo.at[seq], x_send.at[which], x_recv.at[seq], (target, shard))

        @pl.when(target != seq)
        def _():
            copy.start()

        @pl.when(target == seq)
        def _():
            pltpu.make_async_copy(x, xo.at[seq], local.at[3]).start()

        x_copies.append((target, copy))
    copies = []
    for index in range(3):
        for mask in (2, 4, 3, 5, 1):
            target = flip_mask(shard, mask)
            copy = remote(
                block(index, target),
                wo.at[mine, columns(index)],
                w_send.at[index, mask - 1],
                w_recv.at[index, mask - 1],
                (seq, target),
            )
            copy.start()
            copies.append(copy)
    own = [
        pltpu.make_async_copy(block(index, shard), wo.at[mine, columns(index)], local.at[index])
        for index in range(3)
    ]
    for copy in own:
        copy.start()

    mate = (seq, flip(shard, 1))
    for turn in range(4):
        source = lax.rem(seq + turn, 4)
        forward = remote(
            xo.at[source], xo.at[source], fwd_send.at[turn], x_recv.at[source], mate
        )

        @pl.when(core == half)
        def _():
            if turn == 0:
                pltpu.make_async_copy(x, xo.at[seq], local.at[3]).wait()
            else:
                forward.wait_recv()
            forward.start()

    for turn in range(4):
        source = lax.rem(seq + turn, 4)
        forward = remote(
            xo.at[source], xo.at[source], fwd_send.at[turn], x_recv.at[source], mate
        )

        @pl.when(core == half)
        def _():
            forward.wait_send()

        @pl.when(core != half)
        def _():
            forward.wait_recv()

    def arrival(index, origin, mask):
        spot = wo.at[pl.ds(pl.multiple_of(origin * rows, rows), rows), columns(index)]
        return remote(spot, spot, w_send.at[index, 0], w_recv.at[index, mask - 1], mate)

    base = shard - core
    side, above = flip(base, 2), flip(base, 4)
    onward = []
    for index in range(3):
        for origin, mask, slot, target in (
            (side, 2 + core, 6 + core, flip(shard, 4)),
            (above + 1, 5 - core, 7 - core, flip(shard, 2)),
        ):
            arrival(index, origin, mask).wait_recv()
            spot = wo.at[pl.ds(pl.multiple_of(origin * rows, rows), rows), columns(index)]
            copy = remote(
                spot,
                spot,
                w_send.at[index, 5 + len(onward) % 2],
                w_recv.at[index, slot - 1],
                (seq, target),
            )
            copy.start()
            onward.append(copy)
    for target, copy in x_copies:

        @pl.when(target != seq)
        def _():
            copy.wait_send()

    for copy in own:
        copy.wait()
    for copy in copies + onward:
        copy.wait_send()
    far = flip_mask(base, 6)
    for index in range(3):
        arrival(index, flip(shard, 1), 1).wait_recv()
        arrival(index, side + 1, 3 - core).wait_recv()
        arrival(index, above, 4 + core).wait_recv()
        arrival(index, far, 6 + core).wait_recv()
        arrival(index, far + 1, 7 - core).wait_recv()


def entry(x, wq, wk, wv, number):
    rows, width = wq.shape
    group = width // 4
    return comm_call(
        entry_kernel,
        (
            jax.ShapeDtypeStruct((4,) + x.shape, x.dtype),
            jax.ShapeDtypeStruct((8 * rows, 3 * group), wq.dtype),
        ),
        (x, wq, wk, wv),
        [ANY] * 4,
        (ANY, ANY),
        [DMA((4,)), DMA((2,)), DMA((4,)), DMA((4,)), DMA((3, 7)), DMA((3, 7))],
        "entry",
        number,
    )


def stats_kernel(part, total, held, send, receive):
    seq, shard = place()
    partners = [
        (seq, flip(shard, 1)),
        (flip(seq, 1), shard),
        (flip(seq, 1), flip(shard, 1)),
    ]
    greet(partners)
    copies = [
        remote(part, held.at[index], send.at[index], receive.at[index], partner)
        for index, partner in enumerate(partners)
    ]
    for copy in copies:
        copy.start()
    for copy in copies:
        copy.wait()
    total[...] = (part[...] + held[0]) + (held[1] + held[2])


def stats_sum(part, number, after=()):
    return comm_call(
        stats_kernel,
        jax.ShapeDtypeStruct(part.shape, part.dtype),
        (part,),
        [VM],
        VM,
        [pltpu.VMEM((3,) + part.shape, part.dtype), DMA((3,)), DMA((3,))],
        "stats",
        number,
        after,
    )


def plane_others(seq, shard):
    return [(seq, flip_mask(shard, mask)) for mask in range(1, 8)]


class ColumnExchange:
    def __init__(self, weight, cols, local, send, receive):
        self.parts = (weight, cols, local, send, receive)
        self.seq, self.shard = place()
        self.width = cols.shape[2]

    def block(self, target):
        weight = self.parts[0]
        return weight.at[:, pl.ds(pl.multiple_of(target * self.width, self.width), self.width)]

    def copies(self):
        _, cols, local, send, receive = self.parts
        spot = cols.at[self.shard]
        for mask in (2, 4, 3, 5, 6, 7, 1):
            target = flip_mask(self.shard, mask)
            yield remote(
                self.block(target), spot, send.at[mask], receive.at[mask], (self.seq, target)
            )

    def start(self):
        _, cols, local, _, _ = self.parts
        self.started = list(self.copies())
        for copy in self.started:
            copy.start()
        self.own = pltpu.make_async_copy(self.block(self.shard), cols.at[self.shard], local)
        self.own.start()

    def wait(self):
        self.own.wait()
        for copy in self.started:
            copy.wait()


EXCHANGE = [DMA, DMA((8,)), DMA((8,))]


def columns_shape(weight):
    rows, width = weight.shape
    return jax.ShapeDtypeStruct((8, rows, width // 8), weight.dtype)


def to_tokens_kernel(
    heads, weight, tokens, cols, local, send, receive, cols_local, cols_send, cols_receive
):
    seq, shard = place()
    core, half = lax.rem(shard, 2), lax.div(seq, 2)
    base = shard - core
    width = heads.shape[2]
    group = 2 * lax.rem(seq, 2) + core
    greet(column_others(seq, shard) + plane_others(seq, shard)[1:])
    mine = tokens.at[:, pl.ds(pl.multiple_of(group * width, width), width)]
    steps = []
    for turn in range(4):
        target = lax.rem(seq + turn, 4)
        remote_copy = remote(
            heads.at[target], mine, send.at[turn], receive.at[group], (target, base + half)
        )
        if turn == 0:
            here = core == half
            own = pltpu.make_async_copy(heads.at[target], mine, local)

            @pl.when(here)
            def _():
                own.start()

            @pl.when(jnp.logical_not(here))
            def _():
                remote_copy.start()

        else:
            remote_copy.start()
        steps.append(remote_copy)
    exchange = ColumnExchange(weight, cols, cols_local, cols_send, cols_receive)
    exchange.start()
    for turn in range(4):
        if turn == 0:

            @pl.when(here)
            def _():
                own.wait()

            @pl.when(jnp.logical_not(here))
            def _():
                steps[0].wait_send()

        else:
            steps[turn].wait_send()
    for source in range(4):
        slot = tokens.at[:, source * width : (source + 1) * width]
        arrival = remote(heads.at[0], slot, send.at[0], receive.at[source], (seq, shard))

        @pl.when(jnp.logical_not(jnp.logical_and(here, group == source)))
        def _():
            arrival.wait_recv()

    exchange.wait()


def to_tokens(heads, weight, number, after=()):
    blocks, rows, width = heads.shape
    return comm_call(
        to_tokens_kernel,
        (jax.ShapeDtypeStruct((rows, 4 * width), heads.dtype), columns_shape(weight)),
        (heads, weight),
        [ANY] * 2,
        (ANY, ANY),
        [DMA, DMA((4,)), DMA((4,))] + EXCHANGE,
        "to_tokens",
        number,
        after,
    )


def to_heads_kernel(tokens, heads, local, send, receive):
    seq, shard = place()
    core, half = lax.rem(shard, 2), lax.div(seq, 2)
    base = shard - core
    width = heads.shape[2]
    greet(column_others(seq, shard))
    here = core == half
    mine = 2 * lax.rem(seq, 2) + core
    copies = []
    for group in range(4):
        target = (2 * core + group // 2, base + group % 2)
        source = tokens.at[:, group * width : (group + 1) * width]
        copy = remote(source, heads.at[seq], send.at[group], receive.at[seq], target)
        own = pltpu.make_async_copy(source, heads.at[seq], local)
        self_copy = jnp.logical_and(here, mine == group)

        @pl.when(self_copy)
        def _():
            own.start()

        @pl.when(jnp.logical_not(self_copy))
        def _():
            copy.start()

        copies.append((self_copy, own, copy))
    for self_copy, own, copy in copies:

        @pl.when(self_copy)
        def _():
            own.wait()

        @pl.when(jnp.logical_not(self_copy))
        def _():
            copy.wait_send()

    for source in range(4):
        arrival = remote(
            tokens.at[:, 0:width], heads.at[source], send.at[0], receive.at[source], (seq, shard)
        )

        @pl.when(jnp.logical_not(jnp.logical_and(here, seq == source)))
        def _():
            arrival.wait_recv()


def to_heads(tokens, number, after=()):
    rows, width = tokens.shape
    return comm_call(
        to_heads_kernel,
        jax.ShapeDtypeStruct((4, rows, width // 4), tokens.dtype),
        (tokens,),
        [ANY],
        ANY,
        [DMA, DMA((4,)), DMA((4,))],
        "to_heads",
        number,
        after,
    )


def gather_plane(x, out, local, send, receive, ready, exchange=None):
    seq, shard = place()
    core = lax.rem(shard, 2)
    near = [(seq, flip(shard, bit)) for bit in (2, 4, 1)]
    greet(plane_others(seq, shard) if exchange else near)
    own = pltpu.make_async_copy(x, out.at[shard], local)
    own.start()
    firsts = [
        remote(x, out.at[shard], send.at[index], receive.at[index], device)
        for index, device in enumerate(near)
    ]
    for copy in firsts:
        copy.start()
    if exchange:
        exchange.start()
    mate = near[2]
    mate_shard = flip(shard, 1)

    def pass_on(slot, index, device):
        return remote(out.at[slot], out.at[slot], send.at[index], receive.at[index], device)

    first_bit = 2 + 2 * core
    second_bit = 4 - 2 * core
    first, second = flip_bit(shard, first_bit), flip_bit(shard, second_bit)
    diagonal = flip_mask(shard, 6)

    def arrival(slot, index):
        return remote(out.at[slot], out.at[slot], send.at[0], receive.at[index], mate)

    own.wait()
    ready(shard)
    arrival(mate_shard, 2).wait_recv()
    ready(mate_shard)
    arrival(first, core).wait_recv()
    across = pass_on(first, 3, (seq, second))
    across.start()
    one = remote(out.at[first], out.at[first], send.at[4], receive.at[4 + core], mate)
    one.start()
    arrival(second, 1 - core).wait_recv()
    two = remote(out.at[second], out.at[second], send.at[5], receive.at[5 - core], mate)
    two.start()
    ready(first)
    ready(second)
    arrival(flip(mate_shard, 2), 4).wait_recv()
    ready(flip(mate_shard, 2))
    arrival(diagonal, 3).wait_recv()
    three = pass_on(diagonal, 6, mate)
    three.start()
    arrival(flip(mate_shard, 4), 5).wait_recv()
    ready(flip(mate_shard, 4))
    ready(diagonal)
    arrival(flip_mask(mate_shard, 6), 6).wait_recv()
    ready(flip_mask(mate_shard, 6))
    for copy in firsts + [across, one, two, three]:
        copy.wait_send()


class Stores:
    def __init__(self, pairs, sems):
        self.pairs, self.sems = pairs, sems

    def copies(self, slot):
        return [
            pltpu.make_async_copy(source.at[slot], target.at[slot], self.sems.at[index, slot])
            for index, (source, target) in enumerate(self.pairs)
        ]

    def start(self, slot):
        for copy in self.copies(slot):
            copy.start()

    def wait(self):
        def one(slot, carry):
            for copy in self.copies(slot):
                copy.wait()
            return carry

        lax.fori_loop(0, 8, one, 0)


TILE = 512


def tiles(width, body):
    def one(index, carry):
        body(pl.ds(pl.multiple_of(index * TILE, TILE), TILE))
        return carry

    lax.fori_loop(0, width // TILE, one, 0)


def hidden_kernel(
    x, weight, gate_cols, plane, up_cols, gate, upward, hidden,
    plane_in, up_in, gate_wide, gate_low, up_low, hidden_low, local, send, receive, store,
    up_store, cols_local, cols_send, cols_receive
):
    exchange = ColumnExchange(weight, up_in, cols_local, cols_send, cols_receive)
    width = gate_wide.shape[2]
    early = Stores([(plane_in, plane), (gate_low, gate)], store.at[0])
    late = Stores([(up_low, upward), (hidden_low, hidden)], store.at[1])

    def ready(slot):
        def tile(at):
            value = dot_nn(plane_in[slot], gate_cols[:, at])
            gate_wide[slot, :, at] = value
            gate_low[slot, :, at] = value.astype(jnp.bfloat16)

        tiles(width, tile)
        early.start(slot)

    gather_plane(x, plane_in, local, send, receive, ready, exchange)
    exchange.wait()
    kept = pltpu.make_async_copy(up_in, up_cols, up_store)
    kept.start()

    def last(slot, carry):
        def tile(at):
            value = dot_nn(plane_in[slot], up_in[:, :, at].reshape(-1, TILE))
            gated = gate_wide[slot, :, at]
            up_low[slot, :, at] = value.astype(jnp.bfloat16)
            hidden_low[slot, :, at] = (
                gated * (1.0 / (1.0 + jnp.exp(-gated))) * value
            ).astype(jnp.bfloat16)

        tiles(width, tile)
        late.start(slot)
        return carry

    lax.fori_loop(0, 8, last, 0)
    early.wait()
    late.wait()
    kept.wait()


def gather_hidden(x, gate_cols, weight, number, after=()):
    rows, wide = x.shape
    width = weight.shape[1] // 8
    low = x.dtype
    narrow = (8, rows, width)
    result = jax.ShapeDtypeStruct(narrow, low)
    return comm_call(
        hidden_kernel,
        (jax.ShapeDtypeStruct((8, rows, wide), low), columns_shape(weight)) + (result,) * 3,
        (x, weight, gate_cols),
        [VM, ANY, VM],
        (ANY,) * 5,
        [
            pltpu.VMEM((8, rows, wide), low),
            pltpu.VMEM(columns_shape(weight).shape, low),
            pltpu.VMEM(narrow, jnp.float32),
        ]
        + [pltpu.VMEM(narrow, low)] * 3
        + [DMA, DMA((7,)), DMA((7,)), DMA((2, 2, 8)), DMA]
        + EXCHANGE,
        "gather_hidden",
        number,
        after,
    )


def hidden_grad_kernel(
    x, down, gate, upward, plane, gate_grad, up_grad,
    plane_in, gate_low, up_low, local, send, receive, store
):
    width = gate.shape[2]
    stores = Stores([(plane_in, plane), (gate_low, gate_grad), (up_low, up_grad)], store)

    def ready(slot):
        def tile(at):
            grad = dot_nt(plane_in[slot], down[at])
            gated = gate[slot, :, at].astype(jnp.float32)
            sigmoid = 1.0 / (1.0 + jnp.exp(-gated))
            part = grad * sigmoid
            gate_low[slot, :, at] = (
                part * upward[slot, :, at].astype(jnp.float32) * (1.0 + gated * (1.0 - sigmoid))
            ).astype(jnp.bfloat16)
            up_low[slot, :, at] = (part * gated).astype(jnp.bfloat16)

        tiles(width, tile)
        stores.start(slot)

    gather_plane(x, plane_in, local, send, receive, ready)
    stores.wait()


def gather_hidden_grad(x, down, gate, upward, number, after=()):
    rows, wide = x.shape
    low = x.dtype
    narrow = gate.shape
    result = jax.ShapeDtypeStruct(narrow, low)
    return comm_call(
        hidden_grad_kernel,
        (jax.ShapeDtypeStruct((8, rows, wide), low), result, result),
        (x, down, gate, upward),
        [VM] * 4,
        (ANY,) * 3,
        [pltpu.VMEM((8, rows, wide), low)]
        + [pltpu.VMEM(narrow, low)] * 2
        + [DMA, DMA((7,)), DMA((7,)), DMA((3, 8))],
        "gather_hidden_grad",
        number,
        after,
    )


def flip_bit(value, bit):
    return value + bit - 2 * bit * lax.rem(lax.div(value, bit), 2)


PIECES = 2


def add_rows(rows, body):
    step = 32

    def one(index, carry):
        body(pl.ds(pl.multiple_of(index * step, step), step))
        return carry

    lax.fori_loop(0, rows // step, one, 0)


def scatter_products(produce, part, out, mated, first_in, second_in, sums, sem_s, sem_r):
    seq, shard = place()
    core, chip = lax.rem(shard, 2), lax.div(shard, 2)
    rows = out.shape[0] // PIECES
    mate = (seq, flip(shard, 1))
    bit = 1 + core
    first, second = flip_bit(chip, bit), flip_bit(chip, 3 - bit)
    diagonal = 3 - chip
    first_device, second_device = (seq, 2 * first + core), (seq, 2 * second + core)
    greet([mate, first_device, second_device])

    def piece(index):
        return pl.ds(index * rows, rows)

    order, mate_order = (diagonal, first, second, chip), (diagonal, second, first, chip)
    swaps = {}

    def make(slot):
        target = mate_order[slot]
        produce(2 * target + 1 - core)
        for index in range(PIECES):
            copy = remote(
                part.at[2 * target + 1 - core, piece(index)],
                mated.at[target, piece(index)],
                sem_s.at[0, slot, index],
                sem_r.at[0, target, index],
                mate,
            )
            copy.start()
            swaps[slot, index] = copy
        produce(2 * order[slot] + core)

    make(0)
    make(1)

    def came(target, index):
        remote(
            part.at[0, piece(index)],
            mated.at[target, piece(index)],
            sem_s.at[0, 0, index],
            sem_r.at[0, target, index],
            mate,
        ).wait_recv()

    sends = []
    for index in range(PIECES):
        for slot, target in ((0, diagonal), (1, first)):
            came(target, index)

            def add(span, slot=slot, target=target, index=index):
                span = pl.ds(span.start + index * rows, span.size)
                sums[slot, span] = (
                    part[2 * target + core, span].astype(jnp.float32)
                    + mated[target, span].astype(jnp.float32)
                ).astype(jnp.bfloat16)

            add_rows(rows, add)
            copy = remote(
                sums.at[slot, piece(index)],
                first_in.at[slot, piece(index)],
                sem_s.at[1, slot, index],
                sem_r.at[1, slot, index],
                first_device,
            )
            copy.start()
            sends.append(copy)
    make(2)
    make(3)
    finals = []
    for index in range(PIECES):
        came(second, index)
        sends[2 * index].wait_recv()

        def add(span, index=index):
            span = pl.ds(span.start + index * rows, span.size)
            sums[2, span] = (
                part[2 * second + core, span].astype(jnp.float32)
                + mated[second, span].astype(jnp.float32)
                + first_in[0, span].astype(jnp.float32)
            ).astype(jnp.bfloat16)

        add_rows(rows, add)
        copy = remote(
            sums.at[2, piece(index)],
            second_in.at[piece(index)],
            sem_s.at[2, 0, index],
            sem_r.at[2, 0, index],
            second_device,
        )
        copy.start()
        finals.append(copy)
    for index in range(PIECES):
        came(chip, index)
        sends[2 * index + 1].wait_recv()
        finals[index].wait_recv()

        def add(span, index=index):
            span = pl.ds(span.start + index * rows, span.size)
            out[span] = (
                part[shard, span].astype(jnp.float32) + mated[chip, span].astype(jnp.float32)
            ) + (first_in[1, span].astype(jnp.float32) + second_in[span].astype(jnp.float32))

        add_rows(rows, add)
    for copy in list(swaps.values()) + sends + finals:
        copy.wait_send()


def out_scatter_kernel(hidden, down, out, part, *scratch):
    def produce(block):
        def tile(at):
            part[block, :, at] = dot_nn(hidden[block], down[:, at]).astype(jnp.bfloat16)

        tiles(down.shape[1], tile)

    scatter_products(produce, part, out, *scratch)


def back_scatter_kernel(gate_grad, up_grad, gate_cols, up_cols, out, part, *scratch):
    def produce(block):
        def tile(at):
            part[block, :, at] = (
                dot_nt(gate_grad[block], gate_cols[at]) + dot_nt(up_grad[block], up_cols[at])
            ).astype(jnp.bfloat16)

        tiles(gate_cols.shape[0], tile)

    scatter_products(produce, part, out, *scratch)


def plane_scatter(kernel, inputs, rows, width, name, number, after=()):
    low = jnp.bfloat16
    return comm_call(
        kernel,
        jax.ShapeDtypeStruct((rows, width), jnp.float32),
        inputs,
        [VM] * len(inputs),
        VM,
        [
            pltpu.VMEM((8, rows, width), low),
            pltpu.VMEM((4, rows, width), low),
            pltpu.VMEM((2, rows, width), low),
            pltpu.VMEM((rows, width), low),
            pltpu.VMEM((3, rows, width), low),
            DMA((3, 4, PIECES)),
            DMA((3, 4, PIECES)),
        ],
        name,
        number,
        after,
    )


def finish_kernel(
    part, grads, out, placed,
    mated, sums, landed, first_in, second_in, onward, total, swapped,
    local, sem_s, sem_r, grad_s, grad_r
):
    seq, shard = place()
    core, half, quarter = lax.rem(shard, 2), lax.div(seq, 2), lax.rem(seq, 2)
    chip = lax.div(shard, 2)
    base = shard - core
    rows = out.shape[0] // 2
    mate = (seq, flip(shard, 1))
    bit = 1 + core
    first, second, diagonal = flip_bit(chip, bit), flip_bit(chip, 3 - bit), 3 - chip
    first_device, second_device = (seq, 2 * first + core), (seq, 2 * second + core)
    greet(column_others(seq, shard) + [first_device, second_device])
    mine = pl.ds(pl.multiple_of(core * rows, rows), rows)
    other = pl.ds(pl.multiple_of((1 - core) * rows, rows), rows)
    here = core == half
    order = [2 * (1 - half) + 1 - quarter, 2 * (1 - half) + quarter, flip(seq, 1), seq]
    swaps = []
    for slot, block in enumerate(order):
        copy = remote(
            part.at[block, other], mated.at[slot], sem_s.at[0, slot], sem_r.at[0, slot], mate
        )
        copy.start()
        swaps.append(copy)
    long = grads.shape[1] // 2
    firsts = []
    for index in range(2):
        span = slice(index * long, (index + 1) * long)
        for slot, target in ((0, diagonal), (1, first)):
            copy = remote(
                grads.at[target, span],
                first_in.at[slot, span],
                grad_s.at[slot, index],
                grad_r.at[slot, index],
                first_device,
            )
            copy.start()
            firsts.append(copy)
    placed[...] = jnp.zeros_like(placed)

    sends = []
    for slot, block in enumerate(order):
        swaps[slot].wait_recv()

        def add(span, slot=slot, block=block):
            source = pl.ds(pl.multiple_of(span.start + core * rows, 32), span.size)
            sums[slot, span] = (
                part[block, source].astype(jnp.float32) + mated[slot, span].astype(jnp.float32)
            ).astype(jnp.bfloat16)

        add_rows(rows, add)
        copy = remote(
            sums.at[slot],
            landed.at[quarter, core],
            sem_s.at[1, slot],
            sem_r.at[1, 2 * quarter + core],
            (block, base + half),
        )
        if slot < 3:
            copy.start()
        else:
            own = pltpu.make_async_copy(sums.at[slot], landed.at[quarter, core], local)

            @pl.when(here)
            def _():
                own.start()

            @pl.when(jnp.logical_not(here))
            def _():
                copy.start()

        sends.append(copy)

    seconds = []
    for index in range(2):
        firsts[2 * index].wait_recv()

        def add(span, index=index):
            span = pl.ds(span.start + index * long, span.size)
            onward[span] = (
                grads[second, span].astype(jnp.float32) + first_in[0, span].astype(jnp.float32)
            ).astype(jnp.bfloat16)

        add_rows(long, add)
        span = slice(index * long, (index + 1) * long)
        copy = remote(
            onward.at[span], second_in.at[span], grad_s.at[2, index], grad_r.at[2, index],
            second_device,
        )
        copy.start()
        seconds.append(copy)
    for turn in range(2):
        start = pl.multiple_of((1 - core if turn == 0 else core) * long, long)
        if turn == 0:
            for copy in (firsts[1], firsts[3], seconds[0], seconds[1]):
                copy.wait_recv()

        def add(span, start=start):
            span = pl.ds(pl.multiple_of(span.start + start, 32), span.size)
            total[span] = (
                (grads[chip, span].astype(jnp.float32) + first_in[1, span].astype(jnp.float32))
                + second_in[span].astype(jnp.float32)
            ).astype(jnp.bfloat16)

        add_rows(long, add)
        if turn == 0:
            swap = remote(
                total.at[pl.ds(start, long)], swapped, grad_s.at[3, 0], grad_r.at[3, 0], mate
            )
            swap.start()
    group = 2 * quarter + core
    part_width = out.shape[1] // 4
    own_rows = pl.ds(pl.multiple_of(core * long, long), long)
    for index in range(3):
        spot = pl.multiple_of(group * part_width, part_width)
        placed[index, :, pl.ds(spot, part_width)] = total[
            own_rows, index * part_width : (index + 1) * part_width
        ]
    swap.wait_recv()
    for index in range(3):
        spot = pl.multiple_of((2 * quarter + 1 - core) * part_width, part_width)
        placed[index, :, pl.ds(spot, part_width)] = swapped[
            :, index * part_width : (index + 1) * part_width
        ]

    for slot in range(3):
        sends[slot].wait_send()

    @pl.when(here)
    def _():
        own.wait()

    @pl.when(jnp.logical_not(here))
    def _():
        sends[3].wait_send()

    for source in range(4):
        arrival = remote(
            sums.at[0],
            landed.at[source // 2, source % 2],
            sem_s.at[1, 0],
            sem_r.at[1, source],
            mate,
        )

        @pl.when(jnp.logical_not(jnp.logical_and(here, 2 * quarter + core == source)))
        def _():
            arrival.wait_recv()

    for side in range(2):

        def add(span, side=side):
            target = pl.ds(span.start + side * rows, span.size)
            out[target] = landed[0, side, span].astype(jnp.float32) + landed[
                1, side, span
            ].astype(jnp.float32)

        add_rows(rows, add)
    for copy in swaps + firsts + seconds + [swap]:
        copy.wait_send()


def finish(part, grads, number, after=()):
    _, rows, width = part.shape
    _, long, joined = grads.shape
    low = part.dtype
    return comm_call(
        finish_kernel,
        (
            jax.ShapeDtypeStruct((rows, width), jnp.float32),
            jax.ShapeDtypeStruct((3, long // 2, width), low),
        ),
        (part, grads),
        [VM] * 2,
        (VM, VM),
        [
            pltpu.VMEM((4, rows // 2, width), low),
            pltpu.VMEM((4, rows // 2, width), low),
            pltpu.VMEM((2, 2, rows // 2, width), low),
            pltpu.VMEM((2, long, joined), low),
            pltpu.VMEM((long, joined), low),
            pltpu.VMEM((long, joined), low),
            pltpu.VMEM((long, joined), low),
            pltpu.VMEM((long // 2, joined), low),
            DMA,
            DMA((2, 4)),
            DMA((2, 4)),
            DMA((4, 2)),
            DMA((4, 2)),
        ],
        "finish",
        number,
        after,
    )


def turn_heads(values, cosine, signed):
    middle = values.shape[-1] // 2
    return values * cosine + jnp.concatenate(
        [values[:, middle:], values[:, :middle]], axis=1
    ) * signed


def dot_nt(a, b):
    return lax.dot_general(a, b, (((1,), (1,)), ((), ())), preferred_element_type=jnp.float32)


def dot_tn(a, b):
    return lax.dot_general(a, b, (((0,), (0,)), ((), ())), preferred_element_type=jnp.float32)


def dot_nn(a, b):
    return jnp.dot(a, b, preferred_element_type=jnp.float32)


ATTENTION_ROWS = 256


def causal(scores, start):
    query = start + lax.broadcasted_iota(jnp.int32, scores.shape, 0)
    key = lax.broadcasted_iota(jnp.int32, scores.shape, 1)
    return jnp.where(key <= query, scores, masked_value)


def attend_kernel(
    q_raw, k_raw, v_raw, q_factor, k_factor, q_gain, k_gain, cosine, signed,
    q_out, k_out, v_out, attended, log_total
):
    length, size = q_raw.shape
    scale = size ** (-0.5)
    cos, sin = cosine[...], signed[...]
    q_out[...] = turn_heads(
        q_raw[...] * q_factor[...] * q_gain[...], cos, sin
    ).astype(jnp.bfloat16)
    k_out[...] = turn_heads(
        k_raw[...] * k_factor[...] * k_gain[...], cos, sin
    ).astype(jnp.bfloat16)
    v_out[...] = v_raw[...].astype(jnp.bfloat16)
    rows = min(ATTENTION_ROWS, length)
    for start in range(0, length, rows):
        stop = start + rows
        scores = dot_nt(q_out[start:stop], k_out[:stop]) * scale
        scores = causal(scores, start)
        maximum = jnp.max(scores, axis=-1, keepdims=True)
        exponent = jnp.exp(scores - maximum)
        total = jnp.sum(exponent, axis=-1, keepdims=True)
        weights = (exponent * (1.0 / total)).astype(jnp.bfloat16)
        attended[start:stop] = dot_nn(weights, v_out[:stop]).astype(jnp.bfloat16)
        log_total[0, start:stop] = maximum + jnp.log(total)


def attend(raw, q_factor, k_factor, q_gain, k_gain, cosine, signed, size, after=()):
    length, width = raw.shape[0], raw.shape[1] // 3
    heads = width // size
    by_head = pl.BlockSpec((length, size), lambda h: (0, h))
    parts = [
        pl.BlockSpec((length, size), lambda h, start=index * heads: (0, start + h))
        for index in range(3)
    ]
    fixed = pl.BlockSpec((length, size), lambda h: (0, 0))
    factor = pl.BlockSpec((length, 1), lambda h: (0, 0))
    gain = pl.BlockSpec((1, size), lambda h: (0, h))
    low = jax.ShapeDtypeStruct((length, width), jnp.bfloat16)
    flops = heads * length * length * size * 2
    inputs = (raw, raw, raw, q_factor, k_factor, q_gain, k_gain, cosine, signed)
    return pl.pallas_call(
        ordered(attend_kernel, inputs, after),
        grid=(heads,),
        out_shape=(low, low, low, low, jax.ShapeDtypeStruct((heads, length, 1), jnp.float32)),
        in_specs=parts + [factor] * 2 + [gain] * 2 + [fixed] * 2 + [ANY] * len(after),
        out_specs=[by_head] * 4 + [pl.BlockSpec((1, length, 1), lambda h: (h, 0, 0))],
        name="attend",
        compiler_params=pltpu.CompilerParams(vmem_limit_bytes=VMEM_LIMIT),
        cost_estimate=pl.CostEstimate(
            flops=flops, bytes_accessed=20 * length * width, transcendentals=flops // (4 * size)
        ),
    )(*inputs, *after)


def attend_back_kernel(
    queries, keys, values, grads, log_total, cosine, signed, q_grad, k_grad, v_grad, k_sum, v_sum
):
    length, size = queries.shape
    scale = size ** (-0.5)
    rows = min(ATTENTION_ROWS, length)
    k_sum[...] = jnp.zeros_like(k_sum)
    v_sum[...] = jnp.zeros_like(v_sum)
    for start in range(0, length, rows):
        stop = start + rows
        query, grad = queries[start:stop], grads[start:stop]
        scores = causal(dot_nt(query, keys[:stop]) * scale, start)
        weights = jnp.exp(scores - log_total[0, start:stop])
        v_sum[:stop] += dot_tn(weights.astype(jnp.bfloat16), grad)
        weight_grad = dot_nt(grad, values[:stop])
        inner = jnp.sum(weights * weight_grad, axis=-1, keepdims=True)
        score_grad = (weights * (weight_grad - inner)).astype(jnp.bfloat16)
        q_low = (dot_nn(score_grad, keys[:stop]) * scale).astype(jnp.bfloat16)
        q_grad[start:stop] = turn_heads(
            q_low.astype(jnp.float32), cosine[start:stop], -signed[start:stop]
        )
        k_sum[:stop] += dot_tn(score_grad, query)
    k_low = (k_sum[...] * scale).astype(jnp.bfloat16)
    k_grad[...] = turn_heads(k_low.astype(jnp.float32), cosine[...], -signed[...])
    v_grad[...] = v_sum[...].astype(jnp.bfloat16)


def attend_back(queries, keys, values, grads, log_total, cosine, signed, size, after=()):
    length, width = queries.shape
    heads = width // size
    by_head = pl.BlockSpec((length, size), lambda h: (0, h))
    fixed = pl.BlockSpec((length, size), lambda h: (0, 0))
    wide = jax.ShapeDtypeStruct((length, width), jnp.float32)
    flops = heads * length * length * size * 5
    inputs = (queries, keys, values, grads, log_total, cosine, signed)
    return pl.pallas_call(
        ordered(attend_back_kernel, inputs, after),
        grid=(heads,),
        out_shape=(wide, wide, jax.ShapeDtypeStruct((length, width), jnp.bfloat16)),
        in_specs=[by_head] * 4
        + [pl.BlockSpec((1, length, 1), lambda h: (h, 0, 0))]
        + [fixed] * 2
        + [ANY] * len(after),
        out_specs=[by_head] * 3,
        scratch_shapes=[pltpu.VMEM((length, size), jnp.float32)] * 2,
        name="attend_back",
        compiler_params=pltpu.CompilerParams(vmem_limit_bytes=VMEM_LIMIT),
        cost_estimate=pl.CostEstimate(
            flops=flops, bytes_accessed=20 * length * width, transcendentals=flops // (10 * size)
        ),
    )(*inputs, *after)


LINE_ROWS = 128


def flip_by(value, mask):
    for bit in (1, 2, 4):
        here, there = lax.rem(lax.div(value, bit), 2), lax.rem(lax.div(mask, bit), 2)
        value = value + bit * (lax.rem(here + there, 2) - here)
    return value


def line_kernel(
    gate, up, out_part, rest, gate_rows, up_rows, out,
    first, second, held, total, load_sem, send, receive, spread_send, spread_receive
):
    seq, shard = place()
    inner = jnp.logical_or(seq == 1, seq == 2)
    outer = jnp.logical_not(inner)
    beside = (seq + 1 - 2 * lax.rem(seq, 2), shard)
    across = (3 - seq, shard)
    greet([beside, across] + plane_others(seq, shard))
    rows, width = gate_rows.shape[0], gate.shape[1]
    cuts = rows // LINE_ROWS
    early = 8 * cuts
    late = [
        part.at[start : start + LINE_ROWS]
        for part in (out_part, rest)
        for start in range(0, part.shape[0], LINE_ROWS)
    ]
    count = early + len(late)

    def owner(index):
        return flip_by(shard, 7 - lax.div(index, cuts))

    def sources(index):
        start = owner(index) * rows + lax.rem(index, cuts) * LINE_ROWS
        span = pl.ds(pl.multiple_of(start, LINE_ROWS), LINE_ROWS)
        return gate.at[span], up.at[span]

    halves = (slice(0, width), slice(width, 2 * width))

    def inward(index, side, source):
        return remote(
            source,
            first.at[index, :, halves[side]],
            send.at[side, index],
            receive.at[side, index],
            beside,
        )

    def inward_late(index, source):
        return remote(source, first.at[index], send.at[0, index], receive.at[0, index], beside)

    def swap(index):
        return remote(
            first.at[index], second.at[index], send.at[2, index], receive.at[2, index], across
        )

    def outward(index):
        return remote(
            total.at[index], total.at[index], send.at[3, index], receive.at[3, index], beside
        )

    def outward_late(index, place_in_out):
        here = out.at[place_in_out * LINE_ROWS : (place_in_out + 1) * LINE_ROWS]
        return remote(here, here, send.at[3, index], receive.at[3, index], beside)

    def spread(index, side, away=True):
        target = (gate_rows, up_rows)[side]
        down = pl.ds(pl.multiple_of(lax.rem(index, cuts) * LINE_ROWS, LINE_ROWS), LINE_ROWS)
        along = pl.ds(pl.multiple_of(shard * width, width), width)
        source, spot = total.at[index, :, halves[side]], target.at[down, along]
        if not away:
            return pltpu.make_async_copy(source, spot, spread_send.at[side, index])
        return remote(
            source,
            spot,
            spread_send.at[side, index],
            spread_receive.at[side, index],
            (seq, owner(index)),
        )

    away = 7 * cuts

    def each(start, stop, body):
        def one(index, carry):
            body(index)
            return carry

        lax.fori_loop(start, stop, one, 0)

    def spread_start(index):
        for side in range(2):

            @pl.when(index < away)
            def _():
                spread(index, side).start()

            @pl.when(index >= away)
            def _():
                spread(index, side, False).start()

    @pl.when(outer)
    def _():
        def start(index):
            for side, source in enumerate(sources(index)):
                inward(index, side, source).start()

        each(0, early, start)
        for spot, part in enumerate(late):
            inward_late(early + spot, part).start()

        def finish_one(index):
            outward(index).wait_recv()
            spread_start(index)

        each(0, early, finish_one)
        for spot in range(len(late)):
            outward_late(early + spot, spot).wait_recv()

        def sent(index):
            for side, source in enumerate(sources(index)):
                inward(index, side, source).wait_send()

        each(0, early, sent)
        for spot, part in enumerate(late):
            inward_late(early + spot, part).wait_send()

    @pl.when(inner)
    def _():
        def loads(index):
            slot = lax.rem(index, 2)
            for side, source in enumerate(sources(index)):
                yield pltpu.make_async_copy(
                    source, held.at[slot, :, halves[side]], load_sem.at[slot, side]
                )

        def load(index):
            for copy in loads(index):
                copy.start()

        def add_in(index, own):
            def add(at):
                first[index, at] = (
                    first[index, at].astype(jnp.float32) + own(at).astype(jnp.float32)
                ).astype(jnp.bfloat16)

            add_rows(LINE_ROWS, add)
            swap(index).start()

        def add_up(index, store):
            swap(index).wait_recv()

            def add(at):
                store(
                    at,
                    (
                        first[index, at].astype(jnp.float32)
                        + second[index, at].astype(jnp.float32)
                    ).astype(jnp.bfloat16),
                )

            add_rows(LINE_ROWS, add)

        def total_store(index):
            def store(at, value):
                total[index, at] = value

            return store

        def close(index):
            add_up(index, total_store(index))
            outward(index).start()
            spread_start(index)

        def step(index):
            @pl.when(index + 1 < early)
            def _():
                load(index + 1)

            for copy in loads(index):
                copy.wait()
            for side, source in enumerate(sources(index)):
                inward(index, side, source).wait_recv()
            slot = lax.rem(index, 2)
            add_in(index, lambda at: held[slot, at])

            @pl.when(index > 0)
            def _():
                close(index - 1)

        load(0)
        each(0, early, step)

        def close_late(spot):
            def store(at, value):
                out[pl.ds(at.start + spot * LINE_ROWS, at.size)] = value

            add_up(early + spot, store)
            outward_late(early + spot, spot).start()

        for spot, part in enumerate(late):
            inward_late(early + spot, part).wait_recv()
            add_in(early + spot, lambda at, part=part: part[at])
            if spot:
                close_late(spot - 1)
            else:
                close(early - 1)
        close_late(len(late) - 1)

        def sent(index):
            swap(index).wait_send()
            outward(index).wait_send()

        each(0, early, sent)
        for spot in range(len(late)):
            swap(early + spot).wait_send()
            outward_late(early + spot, spot).wait_send()

    def spread_wait(index):
        for side in range(2):

            @pl.when(index < away)
            def _():
                spread(index, side).wait()

            @pl.when(index >= away)
            def _():
                spread(index, side, False).wait()

    each(0, early, spread_wait)


def line_sums(gate, up, out_part, rest, number, after=()):
    rows, width = gate.shape[0] // 8, gate.shape[1]
    low = gate.dtype
    tail = (out_part.shape[0] + rest.shape[0], rest.shape[1])
    early, late = gate.shape[0] // LINE_ROWS, tail[0] // LINE_ROWS
    block = (LINE_ROWS, 2 * width)
    owned = jax.ShapeDtypeStruct((rows, 8 * width), low)
    return comm_call(
        line_kernel,
        (owned, owned, jax.ShapeDtypeStruct(tail, low)),
        (gate, up, out_part, rest),
        [ANY, ANY, VM, VM],
        (ANY, ANY, VM),
        [
            pltpu.VMEM((early + late,) + block, low),
            pltpu.VMEM((early + late,) + block, low),
            pltpu.VMEM((2,) + block, low),
            pltpu.VMEM((early,) + block, low),
            DMA((2, 2)),
            DMA((4, early + late)),
            DMA((4, early + late)),
            DMA((2, early)),
            DMA((2, early)),
        ],
        "line_sums",
        number,
        after,
    )


def line_total(part):
    for route in ([(0, 1), (3, 2)], [(1, 2), (2, 1)]):
        part = part + lax.ppermute(part, "seq", route)
    seq = lax.axis_index("seq")
    inner = jnp.logical_or(seq == 1, seq == 2)
    return jnp.where(inner, part, lax.ppermute(part, "seq", [(1, 0), (2, 3)]))


def gain_sums(part):
    for mask in (1, 2, 4):
        part = part + lax.ppermute(part, "fsdp", [(i, i ^ mask) for i in range(8)])
    return line_total(part)


def split_layer(
    block_input, query_weight, key_weight, value_weight, out_weight, gate_weight, up_weight,
    down_weight, query_gain, key_gain, attention_gain, swiglu_gain, cotangent
):
    tokens, width = block_input.shape[1:]
    head_size = width // HEADS
    seq, shard = lax.axis_index("seq"), lax.axis_index("fsdp")
    core, chip = lax.rem(shard, 2), lax.div(shard, 2)
    half, quarter = lax.div(seq, 2), lax.rem(seq, 2)
    rows = query_weight.shape[0]
    hidden_width = gate_weight.shape[1] // 8
    group_width = width // 4
    group = 2 * quarter + core
    length = 4 * tokens
    low = jnp.bfloat16
    sequence = block_input.reshape(tokens, width)

    whole, qkv = entry(sequence, query_weight, key_weight, value_weight, 1)
    whole = whole.reshape(length, width)
    out_full = lax.all_gather(
        keep(out_weight, (qkv,)), "fsdp", axis=0, tiled=True
    )
    raw = dot_nn(whole, qkv)
    q_raw, k_raw = raw[:, :group_width], raw[:, group_width : 2 * group_width]

    def reduced(first, second, number, after=()):
        part = jnp.stack([first, second]).reshape(2 * length // 128, 128)
        total = stats_sum(part, number, after).reshape(2, length, 1)
        return total[0] / width, total[1] / width

    q_mean, k_mean = reduced(
        jnp.sum(q_raw * q_raw, axis=-1), jnp.sum(k_raw * k_raw, axis=-1), 2
    )
    q_factor, k_factor = lax.rsqrt(q_mean + epsilon), lax.rsqrt(k_mean + epsilon)
    cosine, sine = rotary_tables(length, 0, head_size)
    cosine = jnp.concatenate([cosine[:, 0], cosine[:, 0]], axis=1)
    signed = jnp.concatenate([-sine[:, 0], sine[:, 0]], axis=1)
    q_gain_part = lax.dynamic_slice_in_dim(query_gain, group * group_width, group_width)[None]
    k_gain_part = lax.dynamic_slice_in_dim(key_gain, group * group_width, group_width)[None]
    queries, keys, values, attended_heads, log_total = attend(
        raw, q_factor, k_factor, q_gain_part, k_gain_part, cosine, signed, head_size
    )
    attended, gate_cols = to_tokens(
        attended_heads.reshape(4, tokens, group_width), gate_weight, 3
    )
    gate_cols = gate_cols.reshape(width, hidden_width)
    branch = dot_nn(attended, out_full)
    branch_factor = norm_factor(branch)
    residual = sequence.astype(jnp.float32) + branch * branch_factor * attention_gain

    plane, up_cols, gate, upward, hidden = gather_hidden(
        residual.astype(low), gate_cols, up_weight, 4
    )
    plane, up_cols = plane.reshape(8 * tokens, width), up_cols.reshape(width, hidden_width)
    mixed_out = plane_scatter(
        out_scatter_kernel, (hidden, down_weight), tokens, width, "out_scatter", 5
    )
    mixed_factor = norm_factor(mixed_out)
    output = residual + mixed_out * mixed_factor * swiglu_gain
    upstream = cotangent.reshape(tokens, width).astype(jnp.float32)
    mixed_float, swiglu_gain_grad = norm_backward(mixed_out, mixed_factor, swiglu_gain, upstream)
    mixed_plane, gate_grad, up_grad = gather_hidden_grad(
        mixed_float.astype(low), down_weight, gate, upward, 6
    )
    mixed_plane = mixed_plane.reshape(8 * tokens, width)
    down_grad = transposed_times(
        hidden.reshape(8 * tokens, hidden_width), mixed_plane
    ).astype(low)
    down_sum = lax.psum(down_grad, "seq")
    gate_sum = transposed_times(plane, gate_grad.reshape(8 * tokens, hidden_width)).astype(low)
    up_sum = transposed_times(plane, up_grad.reshape(8 * tokens, hidden_width)).astype(low)

    residual_grad = upstream + plane_scatter(
        back_scatter_kernel,
        (gate_grad, up_grad, gate_cols, up_cols),
        tokens,
        width,
        "back_scatter",
        7,
        (gate_sum, up_sum),
    )

    branch_float, attention_gain_grad = norm_backward(
        branch, branch_factor, attention_gain, residual_grad
    )
    branch_grad = branch_float.astype(low)
    attended_grad = times_transposed(branch_grad, out_full).astype(low)
    head_grad = to_heads(attended_grad, 8).reshape(length, group_width)
    out_grad = lax.psum_scatter(
        transposed_times(attended, branch_grad).astype(low), "fsdp", scatter_dimension=0, tiled=True
    )
    q_norm_grad, k_norm_grad, value_grad = attend_back(
        queries, keys, values, head_grad, log_total, cosine, signed, head_size, (down_sum,)
    )
    q_scaled, k_scaled = q_norm_grad * q_gain_part, k_norm_grad * k_gain_part
    q_inner, k_inner = reduced(
        jnp.sum(q_scaled * q_raw, axis=-1), jnp.sum(k_scaled * k_raw, axis=-1), 9
    )
    q_gain_sum = jnp.sum(q_norm_grad * q_raw * q_factor, axis=0)
    k_gain_sum = jnp.sum(k_norm_grad * k_raw * k_factor, axis=0)
    q_raw_grad = (q_factor * q_scaled - q_raw * (q_factor * q_factor * q_factor * q_inner)).astype(low)
    k_raw_grad = (k_factor * k_scaled - k_raw * (k_factor * k_factor * k_factor * k_inner)).astype(low)
    joined = jnp.concatenate([q_raw_grad, k_raw_grad, value_grad], axis=1)
    input_part = times_transposed(joined, qkv).astype(low)
    qkv_grad = transposed_times(whole, joined).astype(low)
    input_sum, attention_part = finish(
        input_part.reshape(4, tokens, width),
        qkv_grad.reshape(4, 2 * rows, 3 * group_width),
        10,
    )
    input_grad = residual_grad + input_sum

    gate_rows, up_rows, late = line_sums(
        gate_sum, up_sum, out_grad, attention_part.reshape(3 * rows, width), 11
    )
    down_total = down_sum.astype(jnp.float32)
    gate_total, up_total = gate_rows.astype(jnp.float32), up_rows.astype(jnp.float32)
    out_total, query_total, key_total, value_total = (
        late[index * rows : (index + 1) * rows].astype(jnp.float32) for index in range(4)
    )

    def widen(part):
        return lax.dynamic_update_slice(
            jnp.zeros((width,), jnp.float32), part, (group * group_width,)
        )

    gain_totals = gain_sums(
        jnp.stack([widen(q_gain_sum), widen(k_gain_sum), attention_gain_grad, swiglu_gain_grad])
    )
    return (
        output.reshape(1, tokens, width),
        input_grad.reshape(1, tokens, width),
        query_total,
        key_total,
        value_total,
        out_total,
        gate_total,
        up_total,
        down_total,
        gain_totals[0],
        gain_totals[1],
        gain_totals[2],
        gain_totals[3],
    )


def fits(mesh):
    return mesh.shape["seq"] == 4 and mesh.shape["fsdp"] == 8


def solution(mesh):
    placed = (
        P("fsdp", "seq", None),
        P("fsdp", None),
        P("fsdp", None),
        P("fsdp", None),
        P("fsdp", None),
        P("fsdp", None),
        P("fsdp", None),
        P("fsdp", None),
        P(),
        P(),
        P(),
        P(),
        P("fsdp", "seq", None),
    )
    return jax.shard_map(
        split_layer if fits(mesh) else local,
        mesh=mesh,
        in_specs=placed,
        out_specs=(
            P("fsdp", "seq", None),
            P("fsdp", "seq", None),
            P("fsdp", None),
            P("fsdp", None),
            P("fsdp", None),
            P("fsdp", None),
            P("fsdp", None),
            P("fsdp", None),
            P("fsdp", None),
            P(),
            P(),
            P(),
            P(),
        ),
        check_vma=False,
    )
```

```python
import jax
import jax.numpy as jnp
from jax import lax
from jax.experimental import pallas as pl
from jax.experimental.pallas import tpu as pltpu
from jax.sharding import PartitionSpec as P

HEADS = 16


epsilon = 1e-06
rotary_base = 500000.0
masked_value = -1e30


def norm_factor(values):
    return lax.rsqrt(jnp.mean(values * values, axis=-1, keepdims=True) + epsilon)


def norm_backward(values, factor, gain_vector, upstream):
    scaled = upstream * gain_vector
    inner_mean = jnp.mean(scaled * values, axis=-1, keepdims=True)
    value_grad = factor * scaled - values * factor * factor * factor * inner_mean
    gain_grad = jnp.sum(upstream * values * factor, axis=0)
    return (value_grad, gain_grad)


def rotary_tables(count, offset, head_size):
    positions = (offset + jnp.arange(count, dtype=jnp.int32)).astype(jnp.float32)
    middle = head_size // 2
    frequency = rotary_base ** (-2.0 * jnp.arange(middle, dtype=jnp.float32) / head_size)
    angles = positions[:, None] * frequency[None, :]
    return (jnp.cos(angles)[:, None, :], jnp.sin(angles)[:, None, :])


def rotate(values, cosine, sine_table, direction_sign):
    middle = values.shape[-1] // 2
    leading = values[..., :middle]
    trailing = values[..., middle:]
    signed = sine_table * direction_sign
    return jnp.concatenate(
        [leading * cosine - trailing * signed, trailing * cosine + leading * signed], axis=-1
    )


def times_transposed(operand, matrix):
    return lax.dot_general(
        operand, matrix, (((1,), (1,)), ((), ())), preferred_element_type=jnp.float32
    )


def transposed_times(operand, matrix):
    return lax.dot_general(
        operand, matrix, (((0,), (0,)), ((), ())), preferred_element_type=jnp.float32
    )


def masked_scores(query_block, keys, row_start, block_rows, score_scale):
    length = keys.shape[0]
    scores = (
        jnp.einsum("qhd,khd->hqk", query_block, keys, preferred_element_type=jnp.float32)
        * score_scale
    )
    query_positions = row_start + jnp.arange(block_rows, dtype=jnp.int32)
    key_positions = jnp.arange(length, dtype=jnp.int32)
    allowed = key_positions[None, :] <= query_positions[:, None]
    return jnp.where(allowed[None], scores, masked_value)


def attention_forward(queries, keys, values):
    length = queries.shape[0]
    block_rows = min(512, length)
    blocks = length // block_rows
    score_scale = queries.shape[-1] ** (-0.5)

    def one_block(block_index):
        row_start = block_index * block_rows
        query_block = lax.dynamic_slice_in_dim(queries, row_start, block_rows, 0)
        scores = masked_scores(query_block, keys, row_start, block_rows, score_scale)
        maximum = jnp.max(scores, axis=-1, keepdims=True)
        exponent = jnp.exp(scores - maximum)
        row_total = jnp.sum(exponent, axis=-1, keepdims=True)
        log_total = maximum[..., 0] + jnp.log(row_total[..., 0])
        weights_low = (exponent / row_total).astype(jnp.bfloat16)
        attended = jnp.einsum(
            "hqk,khd->qhd", weights_low, values, preferred_element_type=jnp.float32
        )
        return (attended.astype(jnp.bfloat16), log_total)

    attended, log_total = lax.map(one_block, jnp.arange(blocks, dtype=jnp.int32))
    return (attended.reshape(length, -1), log_total)


def attention_backward(queries, keys, values, attended_grad, log_total):
    length = queries.shape[0]
    block_rows = min(512, length)
    blocks = length // block_rows
    score_scale = queries.shape[-1] ** (-0.5)
    empty = jnp.zeros(keys.shape, jnp.float32)

    def one_block(carried, operands):
        key_sum, value_sum = carried
        block_index, block_total = operands
        row_start = block_index * block_rows
        query_block = lax.dynamic_slice_in_dim(queries, row_start, block_rows, 0)
        grad_block = lax.dynamic_slice_in_dim(attended_grad, row_start, block_rows, 0)
        scores = masked_scores(query_block, keys, row_start, block_rows, score_scale)
        probabilities = jnp.exp(scores - block_total[..., None])
        weights_low = probabilities.astype(jnp.bfloat16)
        value_sum = value_sum + jnp.einsum(
            "hqk,qhd->khd", weights_low, grad_block, preferred_element_type=jnp.float32
        )
        probability_grad = jnp.einsum(
            "qhd,khd->hqk", grad_block, values, preferred_element_type=jnp.float32
        )
        inner_sum = jnp.sum(probabilities * probability_grad, axis=-1, keepdims=True)
        score_grad = (probabilities * (probability_grad - inner_sum)).astype(jnp.bfloat16)
        query_grad = (
            jnp.einsum("hqk,khd->qhd", score_grad, keys, preferred_element_type=jnp.float32)
            * score_scale
        )
        key_sum = (
            key_sum
            + jnp.einsum(
                "hqk,qhd->khd", score_grad, query_block, preferred_element_type=jnp.float32
            )
            * score_scale
        )
        return ((key_sum, value_sum), query_grad.astype(jnp.bfloat16))

    (key_sum, value_sum), query_grads = lax.scan(
        one_block, (empty, empty), (jnp.arange(blocks, dtype=jnp.int32), log_total)
    )
    return (
        query_grads.reshape(keys.shape),
        key_sum.astype(jnp.bfloat16),
        value_sum.astype(jnp.bfloat16),
    )


def local(
    block_input,
    query_weight,
    key_weight,
    value_weight,
    out_weight,
    gate_weight,
    up_weight,
    down_weight,
    query_gain,
    key_gain,
    attention_gain,
    swiglu_gain,
    cotangent,
):
    tokens = block_input.shape[1]
    model_width = block_input.shape[2]
    head_size = model_width // HEADS
    groups = lax.axis_size("seq")
    local_heads = HEADS // groups
    sequence = block_input.reshape(tokens, model_width)
    query_full, key_full, value_full, out_full = (
        lax.all_gather(query_weight, "fsdp", axis=0, tiled=True),
        lax.all_gather(key_weight, "fsdp", axis=0, tiled=True),
        lax.all_gather(value_weight, "fsdp", axis=0, tiled=True),
        lax.all_gather(out_weight, "fsdp", axis=0, tiled=True),
    )
    query_raw = jnp.dot(sequence, query_full, preferred_element_type=jnp.float32)
    key_raw = jnp.dot(sequence, key_full, preferred_element_type=jnp.float32)
    value_raw = jnp.dot(sequence, value_full, preferred_element_type=jnp.float32)
    query_factor = norm_factor(query_raw)
    key_factor = norm_factor(key_raw)
    cosine, sine_table = rotary_tables(tokens, lax.axis_index("seq") * tokens, head_size)
    query_rot = rotate(
        (query_raw * query_factor * query_gain).reshape(tokens, HEADS, head_size),
        cosine,
        sine_table,
        1.0,
    )
    key_rot = rotate(
        (key_raw * key_factor * key_gain).reshape(tokens, HEADS, head_size), cosine, sine_table, 1.0
    )
    stacked = jnp.stack(
        [
            query_rot.reshape(tokens, model_width).astype(jnp.bfloat16),
            key_rot.reshape(tokens, model_width).astype(jnp.bfloat16),
            value_raw.astype(jnp.bfloat16),
        ]
    )
    grouped = lax.all_to_all(stacked, "seq", split_axis=2, concat_axis=1, tiled=True)
    length = grouped.shape[1]
    head_queries = grouped[0].reshape(length, local_heads, head_size)
    head_keys = grouped[1].reshape(length, local_heads, head_size)
    head_values = grouped[2].reshape(length, local_heads, head_size)
    attended_heads, log_total = attention_forward(head_queries, head_keys, head_values)
    attended = lax.all_to_all(attended_heads, "seq", split_axis=0, concat_axis=1, tiled=True)
    branch = jnp.dot(attended, out_full, preferred_element_type=jnp.float32)
    branch_factor = norm_factor(branch)
    residual = sequence.astype(jnp.float32) + branch * branch_factor * attention_gain
    residual_low = residual.astype(jnp.bfloat16)
    gate_full, up_full, down_full = (
        lax.all_gather(gate_weight, "fsdp", axis=0, tiled=True),
        lax.all_gather(up_weight, "fsdp", axis=0, tiled=True),
        lax.all_gather(down_weight, "fsdp", axis=0, tiled=True),
    )
    gate_value = jnp.dot(residual_low, gate_full, preferred_element_type=jnp.float32)
    upward = jnp.dot(residual_low, up_full, preferred_element_type=jnp.float32)
    sigmoid_gate = jax.nn.sigmoid(gate_value)
    activated = gate_value * sigmoid_gate
    hidden = (activated * upward).astype(jnp.bfloat16)
    mixed_out = jnp.dot(hidden, down_full, preferred_element_type=jnp.float32)
    mixed_factor = norm_factor(mixed_out)
    output = residual + mixed_out * mixed_factor * swiglu_gain
    upstream = cotangent.reshape(tokens, model_width).astype(jnp.float32)
    mixed_float, swiglu_gain_grad = norm_backward(mixed_out, mixed_factor, swiglu_gain, upstream)
    mixed_grad = mixed_float.astype(jnp.bfloat16)
    gate_back, up_back, down_back = (
        lax.all_gather(gate_weight, "fsdp", axis=0, tiled=True),
        lax.all_gather(up_weight, "fsdp", axis=0, tiled=True),
        lax.all_gather(down_weight, "fsdp", axis=0, tiled=True),
    )
    hidden_grad = times_transposed(mixed_grad, down_back)
    gate_grad = (
        hidden_grad * upward * sigmoid_gate * (1.0 + gate_value * (1.0 - sigmoid_gate))
    ).astype(jnp.bfloat16)
    up_grad = (hidden_grad * activated).astype(jnp.bfloat16)
    residual_grad = (
        upstream + times_transposed(gate_grad, gate_back) + times_transposed(up_grad, up_back)
    )
    joined = jnp.concatenate([gate_grad, up_grad], axis=1)
    branch_float, attention_gain_grad = norm_backward(
        branch, branch_factor, attention_gain, residual_grad
    )
    branch_grad = branch_float.astype(jnp.bfloat16)
    query_back, key_back, value_back, out_back = (
        lax.all_gather(query_weight, "fsdp", axis=0, tiled=True),
        lax.all_gather(key_weight, "fsdp", axis=0, tiled=True),
        lax.all_gather(value_weight, "fsdp", axis=0, tiled=True),
        lax.all_gather(out_weight, "fsdp", axis=0, tiled=True),
    )
    attended_grad = times_transposed(branch_grad, out_back).astype(jnp.bfloat16)
    head_grad = lax.all_to_all(attended_grad, "seq", split_axis=1, concat_axis=0, tiled=True)
    query_grads, key_grads, value_grads = attention_backward(
        head_queries,
        head_keys,
        head_values,
        head_grad.reshape(length, local_heads, head_size),
        log_total,
    )
    back_stack = jnp.stack([query_grads, key_grads, value_grads]).reshape(
        3, length, local_heads * head_size
    )
    token_grads = lax.all_to_all(back_stack, "seq", split_axis=1, concat_axis=2, tiled=True)
    query_norm_grad = rotate(
        token_grads[0].astype(jnp.float32).reshape(tokens, HEADS, head_size),
        cosine,
        sine_table,
        -1.0,
    )
    key_norm_grad = rotate(
        token_grads[1].astype(jnp.float32).reshape(tokens, HEADS, head_size),
        cosine,
        sine_table,
        -1.0,
    )
    query_float, query_gain_grad = norm_backward(
        query_raw, query_factor, query_gain, query_norm_grad.reshape(tokens, model_width)
    )
    key_float, key_gain_grad = norm_backward(
        key_raw, key_factor, key_gain, key_norm_grad.reshape(tokens, model_width)
    )
    query_raw_grad = query_float.astype(jnp.bfloat16)
    key_raw_grad = key_float.astype(jnp.bfloat16)
    value_tokens = token_grads[2]
    input_grad = (
        residual_grad
        + times_transposed(query_raw_grad, query_back)
        + times_transposed(key_raw_grad, key_back)
        + times_transposed(value_tokens, value_back)
    )
    projected = jnp.concatenate([query_raw_grad, key_raw_grad, value_tokens], axis=1)
    hidden_width = gate_weight.shape[1]
    columns = hidden
    down_shard = lax.psum_scatter(
        transposed_times(columns, mixed_grad).astype(jnp.bfloat16),
        "fsdp",
        scatter_dimension=0,
        tiled=True,
    )
    columns = residual_low
    gate_up_shard = lax.psum_scatter(
        transposed_times(columns, joined).astype(jnp.bfloat16),
        "fsdp",
        scatter_dimension=0,
        tiled=True,
    )
    attention_shard = lax.psum_scatter(
        jnp.concatenate(
            [transposed_times(sequence, projected), transposed_times(attended, branch_grad)], axis=1
        ).astype(jnp.bfloat16),
        "fsdp",
        scatter_dimension=0,
        tiled=True,
    )
    attention_total, gate_up_total, down_total = (
        lax.psum(attention_shard, "seq").astype(jnp.float32),
        lax.psum(gate_up_shard, "seq").astype(jnp.float32),
        lax.psum(down_shard, "seq").astype(jnp.float32),
    )
    gain_totals = lax.psum(
        jnp.stack([query_gain_grad, key_gain_grad, attention_gain_grad, swiglu_gain_grad]),
        ("seq", "fsdp"),
    )
    return (
        output.reshape(1, tokens, model_width),
        input_grad.reshape(1, tokens, model_width),
        attention_total[:, :model_width],
        attention_total[:, model_width : 2 * model_width],
        attention_total[:, 2 * model_width : 3 * model_width],
        attention_total[:, 3 * model_width :],
        gate_up_total[:, :hidden_width],
        gate_up_total[:, hidden_width:],
        down_total,
        gain_totals[0],
        gain_totals[1],
        gain_totals[2],
        gain_totals[3],
    )


MESH = pl.DeviceIdType.MESH
ANY = pl.BlockSpec(memory_space=pl.ANY)
VM = pl.BlockSpec(memory_space=pltpu.VMEM)
DMA = pltpu.SemaphoreType.DMA
VMEM_LIMIT = 56 * 1024 * 1024


def flip(value, bit):
    return value + bit - 2 * bit * lax.rem(lax.div(value, bit), 2)


def flip_mask(value, mask):
    for bit in (1, 2, 4):
        if mask & bit:
            value = flip(value, bit)
    return value


def place():
    seq, shard = lax.axis_index("seq"), lax.axis_index("fsdp")
    return seq, shard


def greet(targets):
    barrier = pltpu.get_barrier_semaphore()
    for target in targets:
        pl.semaphore_signal(barrier, inc=1, device_id=target, device_id_type=MESH)
    pl.semaphore_wait(barrier, len(targets))


def remote(source, target_ref, send, receive, device):
    return pltpu.make_async_remote_copy(
        src_ref=source,
        dst_ref=target_ref,
        send_sem=send,
        recv_sem=receive,
        device_id=device,
        device_id_type=MESH,
    )


def column_others(seq, shard):
    mate = flip(shard, 1)
    others = [(lax.rem(seq + step, 4), shard) for step in (1, 2, 3)]
    return others + [(lax.rem(seq + step, 4), mate) for step in (0, 1, 2, 3)]


def ordered(kernel, inputs, after):
    count, extra = len(inputs), len(after)
    return lambda *refs: kernel(*refs[:count], *refs[count + extra :])


def comm_call(kernel, out_shape, inputs, in_specs, out_specs, scratch, name, number, after=()):
    return pl.pallas_call(
        ordered(kernel, inputs, after),
        out_shape=out_shape,
        in_specs=list(in_specs) + [ANY] * len(after),
        out_specs=out_specs,
        scratch_shapes=scratch,
        name=name,
        compiler_params=pltpu.CompilerParams(
            collective_id=number, has_side_effects=True, vmem_limit_bytes=VMEM_LIMIT
        ),
        cost_estimate=pl.CostEstimate(flops=1, bytes_accessed=1, transcendentals=0),
    )(*inputs, *after)


def keep_kernel(x, out):
    out[...] = x[...]


def hold_kernel(x, out):
    pass


def hold(x, after):
    return pl.pallas_call(
        ordered(hold_kernel, (x,), after),
        out_shape=jax.ShapeDtypeStruct(x.shape, x.dtype),
        in_specs=[ANY] * (1 + len(after)),
        out_specs=ANY,
        input_output_aliases={0: 0},
        name="hold",
    )(x, *after)


def keep(x, after):
    return pl.pallas_call(
        ordered(keep_kernel, (x,), after),
        out_shape=jax.ShapeDtypeStruct(x.shape, x.dtype),
        in_specs=[VM] + [ANY] * len(after),
        out_specs=VM,
        name="keep",
    )(x, *after)


def entry_kernel(
    x, wq, wk, wv, xo, wo, local, x_send, x_recv, fwd_send, w_send, w_recv
):
    seq, shard = place()
    core, half = lax.rem(shard, 2), lax.div(seq, 2)
    quarter = lax.rem(seq, 2)
    rows, width = wq.shape[0], wo.shape[1] // 3
    weights = (wq, wk, wv)
    greet(
        [(seq, flip_mask(shard, mask)) for mask in range(1, 8)]
        + [(lax.rem(seq + step, 4), shard) for step in (1, 2, 3)]
    )
    mine = pl.ds(pl.multiple_of(shard * rows, rows), rows)

    def columns(index):
        return slice(index * width, (index + 1) * width)

    def block(index, target):
        group = 2 * quarter + lax.rem(target, 2)
        return weights[index].at[:, pl.ds(pl.multiple_of(group * width, width), width)]

    x_copies = []
    for which in (0, 1):
        target = 2 * core + which
        copy = remote(x, xo.at[seq], x_send.at[which], x_recv.at[seq], (target, shard))

        @pl.when(target != seq)
        def _():
            copy.start()

        @pl.when(target == seq)
        def _():
            pltpu.make_async_copy(x, xo.at[seq], local.at[3]).start()

        x_copies.append((target, copy))
    copies = []
    for index in range(3):
        for mask in (2, 4, 3, 5, 1):
            target = flip_mask(shard, mask)
            copy = remote(
                block(index, target),
                wo.at[mine, columns(index)],
                w_send.at[index, mask - 1],
                w_recv.at[index, mask - 1],
                (seq, target),
            )
            copy.start()
            copies.append(copy)
    own = [
        pltpu.make_async_copy(block(index, shard), wo.at[mine, columns(index)], local.at[index])
        for index in range(3)
    ]
    for copy in own:
        copy.start()

    mate = (seq, flip(shard, 1))
    for turn in range(4):
        source = lax.rem(seq + turn, 4)
        forward = remote(
            xo.at[source], xo.at[source], fwd_send.at[turn], x_recv.at[source], mate
        )

        @pl.when(core == half)
        def _():
            if turn == 0:
                pltpu.make_async_copy(x, xo.at[seq], local.at[3]).wait()
            else:
                forward.wait_recv()
            forward.start()

    for turn in range(4):
        source = lax.rem(seq + turn, 4)
        forward = remote(
            xo.at[source], xo.at[source], fwd_send.at[turn], x_recv.at[source], mate
        )

        @pl.when(core == half)
        def _():
            forward.wait_send()

        @pl.when(core != half)
        def _():
            forward.wait_recv()

    def arrival(index, origin, mask):
        spot = wo.at[pl.ds(pl.multiple_of(origin * rows, rows), rows), columns(index)]
        return remote(spot, spot, w_send.at[index, 0], w_recv.at[index, mask - 1], mate)

    base = shard - core
    side, above = flip(base, 2), flip(base, 4)
    onward = []
    for index in range(3):
        for origin, mask, slot, target in (
            (side, 2 + core, 6 + core, flip(shard, 4)),
            (above + 1, 5 - core, 7 - core, flip(shard, 2)),
        ):
            arrival(index, origin, mask).wait_recv()
            spot = wo.at[pl.ds(pl.multiple_of(origin * rows, rows), rows), columns(index)]
            copy = remote(
                spot,
                spot,
                w_send.at[index, 5 + len(onward) % 2],
                w_recv.at[index, slot - 1],
                (seq, target),
            )
            copy.start()
            onward.append(copy)
    for target, copy in x_copies:

        @pl.when(target != seq)
        def _():
            copy.wait_send()

    for copy in own:
        copy.wait()
    for copy in copies + onward:
        copy.wait_send()
    far = flip_mask(base, 6)
    for index in range(3):
        arrival(index, flip(shard, 1), 1).wait_recv()
        arrival(index, side + 1, 3 - core).wait_recv()
        arrival(index, above, 4 + core).wait_recv()
        arrival(index, far, 6 + core).wait_recv()
        arrival(index, far + 1, 7 - core).wait_recv()


def entry(x, wq, wk, wv, number):
    rows, width = wq.shape
    group = width // 4
    return comm_call(
        entry_kernel,
        (
            jax.ShapeDtypeStruct((4,) + x.shape, x.dtype),
            jax.ShapeDtypeStruct((8 * rows, 3 * group), wq.dtype),
        ),
        (x, wq, wk, wv),
        [ANY] * 4,
        (ANY, ANY),
        [DMA((4,)), DMA((2,)), DMA((4,)), DMA((4,)), DMA((3, 7)), DMA((3, 7))],
        "entry",
        number,
    )


def stats_kernel(part, total, held, send, receive):
    seq, shard = place()
    partners = [
        (seq, flip(shard, 1)),
        (flip(seq, 1), shard),
        (flip(seq, 1), flip(shard, 1)),
    ]
    greet(partners)
    copies = [
        remote(part, held.at[index], send.at[index], receive.at[index], partner)
        for index, partner in enumerate(partners)
    ]
    for copy in copies:
        copy.start()
    for copy in copies:
        copy.wait()
    total[...] = (part[...] + held[0]) + (held[1] + held[2])


def stats_sum(part, number, after=()):
    return comm_call(
        stats_kernel,
        jax.ShapeDtypeStruct(part.shape, part.dtype),
        (part,),
        [VM],
        VM,
        [pltpu.VMEM((3,) + part.shape, part.dtype), DMA((3,)), DMA((3,))],
        "stats",
        number,
        after,
    )


def plane_others(seq, shard):
    return [(seq, flip_mask(shard, mask)) for mask in range(1, 8)]


class ColumnExchange:
    def __init__(self, weight, cols, local, send, receive):
        self.parts = (weight, cols, local, send, receive)
        self.seq, self.shard = place()
        self.width = cols.shape[2]

    def block(self, target):
        weight = self.parts[0]
        return weight.at[:, pl.ds(pl.multiple_of(target * self.width, self.width), self.width)]

    def copies(self):
        _, cols, local, send, receive = self.parts
        spot = cols.at[self.shard]
        for mask in (2, 4, 3, 5, 6, 7, 1):
            target = flip_mask(self.shard, mask)
            yield remote(
                self.block(target), spot, send.at[mask], receive.at[mask], (self.seq, target)
            )

    def start(self):
        _, cols, local, _, _ = self.parts
        self.started = list(self.copies())
        for copy in self.started:
            copy.start()
        self.own = pltpu.make_async_copy(self.block(self.shard), cols.at[self.shard], local)
        self.own.start()

    def wait(self):
        self.own.wait()
        for copy in self.started:
            copy.wait()


EXCHANGE = [DMA, DMA((8,)), DMA((8,))]


class PairExchange(ColumnExchange):
    def start(self):
        _, cols, local, send, receive = self.parts
        seq, shard = self.seq, self.shard
        self.sender = lax.rem(shard, 2) == lax.rem(seq, 2)
        copies = {
            mask: remote(
                self.block(flip_mask(shard, mask)),
                cols.at[shard],
                send.at[mask],
                receive.at[mask],
                (seq, flip_mask(shard, mask)),
            )
            for mask in range(1, 8)
        }
        copies[1].start()
        self.started = [copies[1]]
        self.sent = [copies[mask] for mask in (2, 4, 3, 5, 6, 7)]

        @pl.when(self.sender)
        def _():
            for copy in self.sent:
                copy.start()

        self.own = pltpu.make_async_copy(self.block(shard), cols.at[shard], local)
        self.own.start()

    def turn(self, bits):
        _, cols, _, send, receive = self.parts
        parity = lax.rem(lax.rem(self.shard, 2) + lax.rem(self.seq, 2), 2)
        here, there = bits + parity, bits + 1 - parity
        spot, came = cols.at[flip_by(self.shard, here)], cols.at[flip_by(self.shard, there)]
        pair = (flip(self.seq, 1), self.shard)
        arrival = remote(spot, spot, send.at[here], receive.at[here], pair)
        onward = remote(spot, spot, send.at[8 + bits // 2], receive.at[here], pair)
        swapped = remote(came, came, send.at[8 + bits // 2], receive.at[there], pair)
        return arrival, onward, swapped

    def relay(self, bits):
        arrival, onward, _ = self.turn(bits)
        arrival.wait_recv()
        onward.start()

    def wait(self):
        self.own.wait()
        for copy in self.started:
            copy.wait()

        @pl.when(self.sender)
        def _():
            for copy in self.sent:
                copy.wait_send()

        for bits in (2, 4, 6):
            _, onward, swapped = self.turn(bits)
            onward.wait_send()
            swapped.wait_recv()


PAIR_EXCHANGE = [DMA, DMA((12,)), DMA((8,))]


def columns_shape(weight):
    rows, width = weight.shape
    return jax.ShapeDtypeStruct((8, rows, width // 8), weight.dtype)


def to_tokens_kernel(
    heads, weight, tokens, cols, local, send, receive, cols_local, cols_send, cols_receive
):
    seq, shard = place()
    core, half = lax.rem(shard, 2), lax.div(seq, 2)
    base = shard - core
    width = heads.shape[2]
    group = 2 * lax.rem(seq, 2) + core
    greet(column_others(seq, shard) + plane_others(seq, shard)[1:])
    mine = tokens.at[:, pl.ds(pl.multiple_of(group * width, width), width)]
    steps = []
    for turn in range(4):
        target = lax.rem(seq + turn, 4)
        remote_copy = remote(
            heads.at[target], mine, send.at[turn], receive.at[group], (target, base + half)
        )
        if turn == 0:
            here = core == half
            own = pltpu.make_async_copy(heads.at[target], mine, local)

            @pl.when(here)
            def _():
                own.start()

            @pl.when(jnp.logical_not(here))
            def _():
                remote_copy.start()

        else:
            remote_copy.start()
        steps.append(remote_copy)
    exchange = ColumnExchange(weight, cols, cols_local, cols_send, cols_receive)
    exchange.start()
    for turn in range(4):
        if turn == 0:

            @pl.when(here)
            def _():
                own.wait()

            @pl.when(jnp.logical_not(here))
            def _():
                steps[0].wait_send()

        else:
            steps[turn].wait_send()
    for source in range(4):
        slot = tokens.at[:, source * width : (source + 1) * width]
        arrival = remote(heads.at[0], slot, send.at[0], receive.at[source], (seq, shard))

        @pl.when(jnp.logical_not(jnp.logical_and(here, group == source)))
        def _():
            arrival.wait_recv()

    exchange.wait()


def to_tokens(heads, weight, number, after=()):
    blocks, rows, width = heads.shape
    return comm_call(
        to_tokens_kernel,
        (jax.ShapeDtypeStruct((rows, 4 * width), heads.dtype), columns_shape(weight)),
        (heads, weight),
        [ANY] * 2,
        (ANY, ANY),
        [DMA, DMA((4,)), DMA((4,))] + EXCHANGE,
        "to_tokens",
        number,
        after,
    )


def to_heads_kernel(
    tokens, attended, grads, heads, out, part, *scratch
):
    local, send, receive = scratch[-3:]
    scratch = scratch[:-3]
    seq, shard = place()
    greet(column_others(seq, shard) + plane_others(seq, shard)[1:])
    core, half = lax.rem(shard, 2), lax.div(seq, 2)
    base = shard - core
    width = heads.shape[2]
    here = core == half
    mine = 2 * lax.rem(seq, 2) + core
    copies = []
    for group in range(4):
        target = (2 * core + group // 2, base + group % 2)
        source = tokens.at[:, group * width : (group + 1) * width]
        copy = remote(source, heads.at[seq], send.at[group], receive.at[seq], target)
        own = pltpu.make_async_copy(source, heads.at[seq], local)
        self_copy = jnp.logical_and(here, mine == group)

        @pl.when(self_copy)
        def _():
            own.start()

        @pl.when(jnp.logical_not(self_copy))
        def _():
            copy.start()

        copies.append((self_copy, own, copy))
    def produce(block):
        rows = out.shape[0]
        span = pl.ds(pl.multiple_of(block * rows, rows), rows)

        def tile(at):
            part[block, :, at] = dot_tn(attended[:, span], grads[:, at]).astype(jnp.bfloat16)

        tiles(grads.shape[1], tile)

    scatter_products(produce, part, out, *scratch, meet=False)
    for self_copy, own, copy in copies:

        @pl.when(self_copy)
        def _():
            own.wait()

        @pl.when(jnp.logical_not(self_copy))
        def _():
            copy.wait_send()

    for source in range(4):
        arrival = remote(
            tokens.at[:, 0:width], heads.at[source], send.at[0], receive.at[source], (seq, shard)
        )

        @pl.when(jnp.logical_not(jnp.logical_and(here, seq == source)))
        def _():
            arrival.wait_recv()


def to_heads(tokens, attended, grads, number, after=()):
    rows, width = tokens.shape
    low = tokens.dtype
    return comm_call(
        to_heads_kernel,
        (
            jax.ShapeDtypeStruct((4, rows, width // 4), low),
            jax.ShapeDtypeStruct((rows, width), jnp.float32),
        ),
        (tokens, attended, grads),
        [ANY, VM, VM],
        (ANY, VM),
        scatter_scratch(rows, width) + [DMA, DMA((4,)), DMA((4,))],
        "to_heads",
        number,
        after,
    )


def gather_plane(x, out, local, send, receive, ready, exchange=None):
    seq, shard = place()
    core = lax.rem(shard, 2)
    near = [(seq, flip(shard, bit)) for bit in (2, 4, 1)]
    greet(plane_others(seq, shard) + [(flip(seq, 1), shard)] if exchange else near)
    own = pltpu.make_async_copy(x, out.at[shard], local)
    own.start()
    firsts = [
        remote(x, out.at[shard], send.at[index], receive.at[index], device)
        for index, device in enumerate(near)
    ]
    for copy in firsts:
        copy.start()
    if exchange:
        exchange.start()
    mate = near[2]
    mate_shard = flip(shard, 1)

    def pass_on(slot, index, device):
        return remote(out.at[slot], out.at[slot], send.at[index], receive.at[index], device)

    first_bit = 2 + 2 * core
    second_bit = 4 - 2 * core
    first, second = flip_bit(shard, first_bit), flip_bit(shard, second_bit)
    diagonal = flip_mask(shard, 6)

    def arrival(slot, index):
        return remote(out.at[slot], out.at[slot], send.at[0], receive.at[index], mate)

    own.wait()
    ready(shard)
    arrival(mate_shard, 2).wait_recv()
    ready(mate_shard)
    arrival(first, core).wait_recv()
    across = pass_on(first, 3, (seq, second))
    across.start()
    one = remote(out.at[first], out.at[first], send.at[4], receive.at[4 + core], mate)
    one.start()
    arrival(second, 1 - core).wait_recv()
    two = remote(out.at[second], out.at[second], send.at[5], receive.at[5 - core], mate)
    two.start()
    ready(first)
    ready(second)
    if exchange:
        exchange.relay(2)
        exchange.relay(4)
    arrival(flip(mate_shard, 2), 4).wait_recv()
    ready(flip(mate_shard, 2))
    arrival(diagonal, 3).wait_recv()
    three = pass_on(diagonal, 6, mate)
    three.start()
    arrival(flip(mate_shard, 4), 5).wait_recv()
    ready(flip(mate_shard, 4))
    ready(diagonal)
    arrival(flip_mask(mate_shard, 6), 6).wait_recv()
    ready(flip_mask(mate_shard, 6))
    if exchange:
        exchange.relay(6)
    for copy in firsts + [across, one, two, three]:
        copy.wait_send()


class Stores:
    def __init__(self, pairs, sems):
        self.pairs, self.sems = pairs, sems

    def copies(self, slot):
        return [
            pltpu.make_async_copy(source.at[slot], target.at[slot], self.sems.at[index, slot])
            for index, (source, target) in enumerate(self.pairs)
        ]

    def start(self, slot):
        for copy in self.copies(slot):
            copy.start()

    def wait(self):
        def one(slot, carry):
            for copy in self.copies(slot):
                copy.wait()
            return carry

        lax.fori_loop(0, 8, one, 0)


TILE = 512


def tiles(width, body):
    def one(index, carry):
        body(pl.ds(pl.multiple_of(index * TILE, TILE), TILE))
        return carry

    lax.fori_loop(0, width // TILE, one, 0)


def hidden_kernel(
    x, weight, gate_cols, plane, up_cols, gate, upward, hidden,
    plane_in, up_in, gate_wide, gate_low, up_low, hidden_low, local, send, receive, store,
    up_store, cols_local, cols_send, cols_receive
):
    exchange = PairExchange(weight, up_in, cols_local, cols_send, cols_receive)
    width = gate_wide.shape[2]
    early = Stores([(plane_in, plane), (gate_low, gate)], store.at[0])
    late = Stores([(up_low, upward), (hidden_low, hidden)], store.at[1])

    def ready(slot):
        def tile(at):
            value = dot_nn(plane_in[slot], gate_cols[:, at])
            gate_wide[slot, :, at] = value
            gate_low[slot, :, at] = value.astype(jnp.bfloat16)

        tiles(width, tile)
        early.start(slot)

    gather_plane(x, plane_in, local, send, receive, ready, exchange)
    exchange.wait()
    kept = pltpu.make_async_copy(up_in, up_cols, up_store)
    kept.start()

    def last(slot, carry):
        def tile(at):
            value = dot_nn(plane_in[slot], up_in[:, :, at].reshape(-1, TILE))
            gated = gate_wide[slot, :, at]
            up_low[slot, :, at] = value.astype(jnp.bfloat16)
            hidden_low[slot, :, at] = (
                gated * (1.0 / (1.0 + jnp.exp(-gated))) * value
            ).astype(jnp.bfloat16)

        tiles(width, tile)
        late.start(slot)
        return carry

    lax.fori_loop(0, 8, last, 0)
    early.wait()
    late.wait()
    kept.wait()


def gather_hidden(x, gate_cols, weight, number, after=()):
    rows, wide = x.shape
    width = weight.shape[1] // 8
    low = x.dtype
    narrow = (8, rows, width)
    result = jax.ShapeDtypeStruct(narrow, low)
    return comm_call(
        hidden_kernel,
        (jax.ShapeDtypeStruct((8, rows, wide), low), columns_shape(weight)) + (result,) * 3,
        (x, weight, gate_cols),
        [VM, ANY, VM],
        (ANY,) * 5,
        [
            pltpu.VMEM((8, rows, wide), low),
            pltpu.VMEM(columns_shape(weight).shape, low),
            pltpu.VMEM(narrow, jnp.float32),
        ]
        + [pltpu.VMEM(narrow, low)] * 3
        + [DMA, DMA((7,)), DMA((7,)), DMA((2, 2, 8)), DMA]
        + PAIR_EXCHANGE,
        "gather_hidden",
        number,
        after,
    )


def hidden_grad_kernel(
    x, down, gate, upward, plane, gate_grad, up_grad,
    plane_in, gate_low, up_low, local, send, receive, store
):
    width = gate.shape[2]
    stores = Stores([(plane_in, plane), (gate_low, gate_grad), (up_low, up_grad)], store)

    def ready(slot):
        def tile(at):
            grad = dot_nt(plane_in[slot], down[at])
            gated = gate[slot, :, at].astype(jnp.float32)
            sigmoid = 1.0 / (1.0 + jnp.exp(-gated))
            part = grad * sigmoid
            gate_low[slot, :, at] = (
                part * upward[slot, :, at].astype(jnp.float32) * (1.0 + gated * (1.0 - sigmoid))
            ).astype(jnp.bfloat16)
            up_low[slot, :, at] = (part * gated).astype(jnp.bfloat16)

        tiles(width, tile)
        stores.start(slot)

    gather_plane(x, plane_in, local, send, receive, ready)
    stores.wait()


def gather_hidden_grad(x, down, gate, upward, number, after=()):
    rows, wide = x.shape
    low = x.dtype
    narrow = gate.shape
    result = jax.ShapeDtypeStruct(narrow, low)
    return comm_call(
        hidden_grad_kernel,
        (jax.ShapeDtypeStruct((8, rows, wide), low), result, result),
        (x, down, gate, upward),
        [VM] * 4,
        (ANY,) * 3,
        [pltpu.VMEM((8, rows, wide), low)]
        + [pltpu.VMEM(narrow, low)] * 2
        + [DMA, DMA((7,)), DMA((7,)), DMA((3, 8))],
        "gather_hidden_grad",
        number,
        after,
    )


def flip_bit(value, bit):
    return value + bit - 2 * bit * lax.rem(lax.div(value, bit), 2)


PIECES = 2


def add_rows(rows, body):
    step = 32

    def one(index, carry):
        body(pl.ds(pl.multiple_of(index * step, step), step))
        return carry

    lax.fori_loop(0, rows // step, one, 0)


def scatter_products(
    produce, part, out, mated, first_in, second_in, sums, sem_s, sem_r, meet=True
):
    seq, shard = place()
    core, chip = lax.rem(shard, 2), lax.div(shard, 2)
    rows = out.shape[0] // PIECES
    mate = (seq, flip(shard, 1))
    bit = 1 + core
    first, second = flip_bit(chip, bit), flip_bit(chip, 3 - bit)
    diagonal = 3 - chip
    first_device, second_device = (seq, 2 * first + core), (seq, 2 * second + core)
    if meet:
        greet([mate, first_device, second_device])

    def piece(index):
        return pl.ds(index * rows, rows)

    order, mate_order = (diagonal, first, second, chip), (diagonal, second, first, chip)
    swaps = {}

    def make(slot):
        target = mate_order[slot]
        produce(2 * target + 1 - core)
        for index in range(PIECES):
            copy = remote(
                part.at[2 * target + 1 - core, piece(index)],
                mated.at[target, piece(index)],
                sem_s.at[0, slot, index],
                sem_r.at[0, target, index],
                mate,
            )
            copy.start()
            swaps[slot, index] = copy
        produce(2 * order[slot] + core)

    make(0)
    make(1)

    def came(target, index):
        remote(
            part.at[0, piece(index)],
            mated.at[target, piece(index)],
            sem_s.at[0, 0, index],
            sem_r.at[0, target, index],
            mate,
        ).wait_recv()

    sends = []
    for index in range(PIECES):
        for slot, target in ((0, diagonal), (1, first)):
            came(target, index)

            def add(span, slot=slot, target=target, index=index):
                span = pl.ds(span.start + index * rows, span.size)
                sums[slot, span] = (
                    part[2 * target + core, span].astype(jnp.float32)
                    + mated[target, span].astype(jnp.float32)
                ).astype(jnp.bfloat16)

            add_rows(rows, add)
            copy = remote(
                sums.at[slot, piece(index)],
                first_in.at[slot, piece(index)],
                sem_s.at[1, slot, index],
                sem_r.at[1, slot, index],
                first_device,
            )
            copy.start()
            sends.append(copy)
    make(2)
    make(3)
    finals = []
    for index in range(PIECES):
        came(second, index)
        sends[2 * index].wait_recv()

        def add(span, index=index):
            span = pl.ds(span.start + index * rows, span.size)
            sums[2, span] = (
                part[2 * second + core, span].astype(jnp.float32)
                + mated[second, span].astype(jnp.float32)
                + first_in[0, span].astype(jnp.float32)
            ).astype(jnp.bfloat16)

        add_rows(rows, add)
        copy = remote(
            sums.at[2, piece(index)],
            second_in.at[piece(index)],
            sem_s.at[2, 0, index],
            sem_r.at[2, 0, index],
            second_device,
        )
        copy.start()
        finals.append(copy)
    for index in range(PIECES):
        came(chip, index)
        sends[2 * index + 1].wait_recv()
        finals[index].wait_recv()

        def add(span, index=index):
            span = pl.ds(span.start + index * rows, span.size)
            out[span] = (
                part[shard, span].astype(jnp.float32) + mated[chip, span].astype(jnp.float32)
            ) + (first_in[1, span].astype(jnp.float32) + second_in[span].astype(jnp.float32))

        add_rows(rows, add)
    for copy in list(swaps.values()) + sends + finals:
        copy.wait_send()


def out_scatter_kernel(hidden, down, out, part, *scratch):
    def produce(block):
        def tile(at):
            part[block, :, at] = dot_nn(hidden[block], down[:, at]).astype(jnp.bfloat16)

        tiles(down.shape[1], tile)

    scatter_products(produce, part, out, *scratch)


def back_scatter_kernel(gate_grad, up_grad, gate_cols, up_cols, out, part, *scratch):
    def produce(block):
        def tile(at):
            part[block, :, at] = (
                dot_nt(gate_grad[block], gate_cols[at]) + dot_nt(up_grad[block], up_cols[at])
            ).astype(jnp.bfloat16)

        tiles(gate_cols.shape[0], tile)

    scatter_products(produce, part, out, *scratch)


def scatter_scratch(rows, width):
    low = jnp.bfloat16
    return [
        pltpu.VMEM((8, rows, width), low),
        pltpu.VMEM((4, rows, width), low),
        pltpu.VMEM((2, rows, width), low),
        pltpu.VMEM((rows, width), low),
        pltpu.VMEM((3, rows, width), low),
        DMA((3, 4, PIECES)),
        DMA((3, 4, PIECES)),
    ]


def plane_scatter(kernel, inputs, rows, width, name, number, after=()):
    return comm_call(
        kernel,
        jax.ShapeDtypeStruct((rows, width), jnp.float32),
        inputs,
        [VM] * len(inputs),
        VM,
        scatter_scratch(rows, width),
        name,
        number,
        after,
    )


LINE_ROWS = 128
RING = 4


def flip_by(value, mask):
    for bit in (1, 2, 4):
        here, there = lax.rem(lax.div(value, bit), 2), lax.rem(lax.div(mask, bit), 2)
        value = value + bit * (lax.rem(here + there, 2) - here)
    return value


class LineSums:
    def __init__(self, gate, up, late, gate_rows, up_rows, out, landed, scratch):
        self.gate, self.up, self.late = gate, up, late
        self.rows_out, self.out = (gate_rows, up_rows), out
        self.first_in, self.second_in, self.total_in = landed
        (
            self.own, self.sums, self.others, self.totals,
            self.own_sem, self.load_sem, self.keep_sem, self.send, self.receive,
            self.spread_send, self.spread_receive,
        ) = scratch
        self.seq, self.shard = place()
        self.inner = jnp.logical_or(self.seq == 1, self.seq == 2)
        self.outer = jnp.logical_not(self.inner)
        self.beside = (self.seq + 1 - 2 * lax.rem(self.seq, 2), self.shard)
        self.across = (3 - self.seq, self.shard)
        self.rows, self.width = gate_rows.shape[0], gate.shape[1]
        self.cuts = self.rows // LINE_ROWS
        self.early = 8 * self.cuts
        self.count = self.early + len(late)
        self.away = 7 * self.cuts
        self.halves = (slice(0, self.width), slice(self.width, 2 * self.width))

    def is_late(self, index):
        return isinstance(index, int) and index >= self.early

    def owner(self, index):
        return flip_by(self.shard, 7 - lax.div(index, self.cuts))

    def sources(self, index):
        if self.is_late(index):
            return [(self.late[index - self.early], slice(0, 2 * self.width))]
        start = self.owner(index) * self.rows + lax.rem(index, self.cuts) * LINE_ROWS
        span = pl.ds(pl.multiple_of(start, LINE_ROWS), LINE_ROWS)
        return list(zip((self.gate.at[span], self.up.at[span]), self.halves))

    def inward(self, index):
        return [
            remote(
                source,
                self.first_in.at[index, :, half],
                self.send.at[side, index],
                self.receive.at[side, index],
                self.beside,
            )
            for side, (source, half) in enumerate(self.sources(index))
        ]

    def swap(self, index):
        return remote(
            self.sums.at[lax.rem(index, RING)],
            self.second_in.at[index],
            self.send.at[2, index],
            self.receive.at[2, index],
            self.across,
        )

    def result(self, index):
        if self.is_late(index):
            start = (index - self.early) * LINE_ROWS
            return self.out.at[start : start + LINE_ROWS]
        return self.total_in.at[index]

    def outward(self, index):
        return remote(
            self.totals.at[lax.rem(index, RING)],
            self.result(index),
            self.send.at[3, index],
            self.receive.at[3, index],
            self.beside,
        )

    def keep(self, index):
        return pltpu.make_async_copy(
            self.totals.at[lax.rem(index, RING)], self.result(index), self.keep_sem.at[index]
        )

    def own_loads(self, index):
        slot = lax.rem(index, 2)
        return [
            pltpu.make_async_copy(
                source, self.own.at[slot, :, half], self.own_sem.at[slot, side]
            )
            for side, (source, half) in enumerate(self.sources(index))
        ]

    def spread(self, index, side, source, away):
        down = pl.ds(
            pl.multiple_of(lax.rem(index, self.cuts) * LINE_ROWS, LINE_ROWS), LINE_ROWS
        )
        along = pl.ds(pl.multiple_of(self.shard * self.width, self.width), self.width)
        source = source.at[:, self.halves[side]]
        spot = self.rows_out[side].at[down, along]
        if not away:
            return pltpu.make_async_copy(source, spot, self.spread_send.at[side, index])
        return remote(
            source,
            spot,
            self.spread_send.at[side, index],
            self.spread_receive.at[side, index],
            (self.seq, self.owner(index)),
        )

    def spread_each(self, index, source, there, here):
        for side in range(2):

            @pl.when(index < self.away)
            def _():
                there(self.spread(index, side, source, True))

            @pl.when(index >= self.away)
            def _():
                here(self.spread(index, side, source, False))

    def spread_start(self, index, source):
        self.spread_each(index, source, lambda copy: copy.start(), lambda copy: copy.start())

    def spread_sent(self, index, source):
        self.spread_each(index, source, lambda copy: copy.wait_send(), lambda copy: copy.wait())

    def add_up(self, target, first, second):
        def add(at):
            target[at] = (
                first[at].astype(jnp.float32) + second[at].astype(jnp.float32)
            ).astype(jnp.bfloat16)

        add_rows(LINE_ROWS, add)

    def begin(self):
        @pl.when(self.outer)
        def _():
            for copy in self.inward(0):
                copy.start()

        @pl.when(self.inner)
        def _():
            for copy in self.own_loads(0):
                copy.start()

    def retire(self, index):
        self.outward(index).wait_send()
        if self.is_late(index):
            self.keep(index).wait()
        else:
            self.spread_sent(index, self.totals.at[lax.rem(index, RING)])

    def close(self, index):
        slot = lax.rem(index, RING)
        self.swap(index).wait_recv()
        load = pltpu.make_async_copy(
            self.second_in.at[index], self.others, self.load_sem.at[1]
        )
        load.start()
        if isinstance(index, int):
            self.retire(index - RING)
        else:

            @pl.when(index >= RING)
            def _():
                self.retire(index - RING)

        load.wait()
        self.add_up(self.totals.at[slot], self.sums.at[slot], self.others)
        self.outward(index).start()
        if self.is_late(index):
            self.keep(index).start()
        else:
            self.spread_start(index, self.totals.at[slot])

    def inner_step(self, index, following):
        slot = lax.rem(index, RING)
        if following:
            for copy in self.own_loads(index + 1):
                copy.start()
        for copy in self.inward(index):
            copy.wait_recv()
        if isinstance(index, int):
            self.swap(index - RING).wait_send()
        else:

            @pl.when(index >= RING)
            def _():
                self.swap(index - RING).wait_send()

        load = pltpu.make_async_copy(
            self.first_in.at[index], self.sums.at[slot], self.load_sem.at[0]
        )
        load.start()
        for copy in self.own_loads(index):
            copy.wait()
        load.wait()
        self.add_up(self.sums.at[slot], self.sums.at[slot], self.own.at[lax.rem(index, 2)])
        self.swap(index).start()
        if isinstance(index, int):
            self.close(index - 1)
        else:

            @pl.when(index > 0)
            def _():
                self.close(index - 1)

    def outer_take(self, index):
        self.outward(index).wait_recv()
        if not self.is_late(index):
            self.spread_start(index, self.total_in.at[index])

    def outer_step(self, index, following):
        if following:
            for copy in self.inward(index + 1):
                copy.start()
        if isinstance(index, int):
            self.outer_take(index - 3)
        else:

            @pl.when(index >= 3)
            def _():
                self.outer_take(index - 3)

    def step(self, index, following=True):
        @pl.when(self.inner)
        def _():
            self.inner_step(index, following)

        @pl.when(self.outer)
        def _():
            self.outer_step(index, following)

    def run(self, start, stop):
        def one(index, carry):
            self.step(index)
            return carry

        lax.fori_loop(start, min(stop, self.early - 1), one, 0)

    def finish(self):
        early, count = self.early, self.count
        for index in range(early - 1, count):
            self.step(index, index + 1 < count)

        @pl.when(self.inner)
        def _():
            self.close(count - 1)
            for index in range(count - RING, count):
                self.swap(index).wait_send()
                self.retire(index)

        def each(body):
            def one(index, carry):
                body(index)
                return carry

            lax.fori_loop(0, early, one, 0)

        @pl.when(self.outer)
        def _():
            for index in range(count - 3, count):
                self.outer_take(index)

            def sent(index):
                for copy in self.inward(index):
                    copy.wait_send()
                self.spread_sent(index, self.total_in.at[index])

            each(sent)
            for index in range(early, count):
                for copy in self.inward(index):
                    copy.wait_send()

        def received(index):
            for side in range(2):

                @pl.when(index < self.away)
                def _():
                    self.spread(index, side, self.total_in.at[index], True).wait_recv()

        each(received)


def finish_kernel(
    joined, weight, whole, gate, up, out_grad,
    out, gate_rows, up_rows, line_out, first_chunks, second_chunks, total_chunks,
    part, grads, placed,
    mated, sums, landed, first_in, second_in, onward, total, swapped,
    local, sem_s, sem_r, grad_s, grad_r, *line_scratch
):
    seq, shard = place()
    core, half, quarter = lax.rem(shard, 2), lax.div(seq, 2), lax.rem(seq, 2)
    chip = lax.div(shard, 2)
    base = shard - core
    rows = out.shape[0] // 2
    mate = (seq, flip(shard, 1))
    bit = 1 + core
    first, second, diagonal = flip_bit(chip, bit), flip_bit(chip, 3 - bit), 3 - chip
    first_device, second_device = (seq, 2 * first + core), (seq, 2 * second + core)
    greet(column_others(seq, shard) + plane_others(seq, shard)[1:])
    late = [
        out_grad.at[start : start + LINE_ROWS] for start in range(0, out_grad.shape[0], LINE_ROWS)
    ] + [
        placed.at[index, start : start + LINE_ROWS]
        for index in range(3)
        for start in range(0, placed.shape[1], LINE_ROWS)
    ]
    line = LineSums(
        gate, up, late, gate_rows, up_rows, line_out,
        (first_chunks, second_chunks, total_chunks), line_scratch,
    )
    line.begin()

    mine = pl.ds(pl.multiple_of(core * rows, rows), rows)
    other = pl.ds(pl.multiple_of((1 - core) * rows, rows), rows)
    here = core == half
    order = [2 * (1 - half) + 1 - quarter, 2 * (1 - half) + quarter, flip(seq, 1), seq]
    long = grads.shape[1] // 2

    def project(target):
        span = pl.ds(pl.multiple_of(target * 2 * long, 2 * long), 2 * long)

        def tile(at):
            grads[target, :, at] = dot_tn(whole[:, span], joined[:, at]).astype(jnp.bfloat16)

        tiles(grads.shape[2], tile)

    firsts = []
    for slot, target in ((0, diagonal), (1, first)):
        project(target)
        for index in range(2):
            span = slice(index * long, (index + 1) * long)
            copy = remote(
                grads.at[target, span],
                first_in.at[slot, span],
                grad_s.at[slot, index],
                grad_r.at[slot, index],
                first_device,
            )
            copy.start()
            firsts.append(copy)
    swaps = []
    for slot, block in enumerate(order):
        tokens = pl.ds(pl.multiple_of(block * 2 * rows, 2 * rows), 2 * rows)

        def tile(at):
            part[block, :, at] = dot_nt(joined[tokens], weight[at]).astype(jnp.bfloat16)

        tiles(part.shape[2], tile)
        copy = remote(
            part.at[block, other], mated.at[slot], sem_s.at[0, slot], sem_r.at[0, slot], mate
        )
        copy.start()
        swaps.append(copy)
    line.run(0, 1)
    project(second)
    project(chip)
    placed[...] = jnp.zeros_like(placed)

    sends = []
    for slot, block in enumerate(order):
        swaps[slot].wait_recv()

        def add(span, slot=slot, block=block):
            source = pl.ds(pl.multiple_of(span.start + core * rows, 32), span.size)
            sums[slot, span] = (
                part[block, source].astype(jnp.float32) + mated[slot, span].astype(jnp.float32)
            ).astype(jnp.bfloat16)

        add_rows(rows, add)
        copy = remote(
            sums.at[slot],
            landed.at[quarter, core],
            sem_s.at[1, slot],
            sem_r.at[1, 2 * quarter + core],
            (block, base + half),
        )
        if slot < 3:
            copy.start()
        else:
            own = pltpu.make_async_copy(sums.at[slot], landed.at[quarter, core], local)

            @pl.when(here)
            def _():
                own.start()

            @pl.when(jnp.logical_not(here))
            def _():
                copy.start()

        sends.append(copy)
    line.run(1, 3)

    seconds = []
    for index in range(2):
        firsts[index].wait_recv()

        def add(span, index=index):
            span = pl.ds(span.start + index * long, span.size)
            onward[span] = (
                grads[second, span].astype(jnp.float32) + first_in[0, span].astype(jnp.float32)
            ).astype(jnp.bfloat16)

        add_rows(long, add)
        span = slice(index * long, (index + 1) * long)
        copy = remote(
            onward.at[span], second_in.at[span], grad_s.at[2, index], grad_r.at[2, index],
            second_device,
        )
        copy.start()
        seconds.append(copy)
    line.run(3, 6)
    for turn in range(2):
        start = pl.multiple_of((1 - core if turn == 0 else core) * long, long)
        if turn == 0:
            for copy in (firsts[2], firsts[3], seconds[0], seconds[1]):
                copy.wait_recv()

        def add(span, start=start):
            span = pl.ds(pl.multiple_of(span.start + start, 32), span.size)
            total[span] = (
                (grads[chip, span].astype(jnp.float32) + first_in[1, span].astype(jnp.float32))
                + second_in[span].astype(jnp.float32)
            ).astype(jnp.bfloat16)

        add_rows(long, add)
        if turn == 0:
            swap = remote(
                total.at[pl.ds(start, long)], swapped, grad_s.at[3, 0], grad_r.at[3, 0], mate
            )
            swap.start()
    group = 2 * quarter + core
    part_width = out.shape[1] // 4
    own_rows = pl.ds(pl.multiple_of(core * long, long), long)
    for index in range(3):
        spot = pl.multiple_of(group * part_width, part_width)
        placed[index, :, pl.ds(spot, part_width)] = total[
            own_rows, index * part_width : (index + 1) * part_width
        ]
    swap.wait_recv()
    for index in range(3):
        spot = pl.multiple_of((2 * quarter + 1 - core) * part_width, part_width)
        placed[index, :, pl.ds(spot, part_width)] = swapped[
            :, index * part_width : (index + 1) * part_width
        ]
    line.run(6, 8)

    for slot in range(3):
        sends[slot].wait_send()

    @pl.when(here)
    def _():
        own.wait()

    @pl.when(jnp.logical_not(here))
    def _():
        sends[3].wait_send()

    for source in range(4):
        arrival = remote(
            sums.at[0],
            landed.at[source // 2, source % 2],
            sem_s.at[1, 0],
            sem_r.at[1, source],
            mate,
        )

        @pl.when(jnp.logical_not(jnp.logical_and(here, 2 * quarter + core == source)))
        def _():
            arrival.wait_recv()

    for side in range(2):

        def add(span, side=side):
            target = pl.ds(span.start + side * rows, span.size)
            out[target] = landed[0, side, span].astype(jnp.float32) + landed[
                1, side, span
            ].astype(jnp.float32)

        add_rows(rows, add)
    for copy in swaps + firsts + seconds + [swap]:
        copy.wait_send()
    line.run(8, line.early)
    line.finish()


def finish(joined, weight, whole, gate, up, out_grad, number, after=()):
    length, width = whole.shape
    rows, long, wide = length // 4, weight.shape[0] // 4, weight.shape[1]
    low = joined.dtype
    hidden_width = gate.shape[1]
    tail = out_grad.shape[0] + 3 * long // 2
    early, late = gate.shape[0] // LINE_ROWS, tail // LINE_ROWS
    count = early + late
    block = (LINE_ROWS, 2 * hidden_width)
    owned = jax.ShapeDtypeStruct((gate.shape[0] // 8, 8 * hidden_width), low)
    chunks = jax.ShapeDtypeStruct((count,) + block, low)
    results = comm_call(
        finish_kernel,
        (
            jax.ShapeDtypeStruct((rows, width), jnp.float32),
            owned,
            owned,
            jax.ShapeDtypeStruct((tail, width), low),
            chunks,
            chunks,
            chunks,
        ),
        (joined, weight, whole, gate, up, out_grad),
        [VM] * 3 + [ANY] * 3,
        (VM,) + (ANY,) * 6,
        [
            pltpu.VMEM((4, rows, width), low),
            pltpu.VMEM((4, long, wide), low),
            pltpu.VMEM((3, long // 2, width), low),
            pltpu.VMEM((4, rows // 2, width), low),
            pltpu.VMEM((4, rows // 2, width), low),
            pltpu.VMEM((2, 2, rows // 2, width), low),
            pltpu.VMEM((2, long, wide), low),
            pltpu.VMEM((long, wide), low),
            pltpu.VMEM((long, wide), low),
            pltpu.VMEM((long, wide), low),
            pltpu.VMEM((long // 2, wide), low),
            DMA,
            DMA((2, 4)),
            DMA((2, 4)),
            DMA((4, 2)),
            DMA((4, 2)),
            pltpu.VMEM((2,) + block, low),
            pltpu.VMEM((RING,) + block, low),
            pltpu.VMEM(block, low),
            pltpu.VMEM((RING,) + block, low),
            DMA((2, 2)),
            DMA((2,)),
            DMA((count,)),
            DMA((4, count)),
            DMA((4, count)),
            DMA((2, early)),
            DMA((2, early)),
        ],
        "finish",
        number,
        after,
    )
    return results[:4]


def turn_heads(values, cosine, signed):
    middle = values.shape[-1] // 2
    return values * cosine + jnp.concatenate(
        [values[:, middle:], values[:, :middle]], axis=1
    ) * signed


def dot_nt(a, b):
    return lax.dot_general(a, b, (((1,), (1,)), ((), ())), preferred_element_type=jnp.float32)


def dot_tn(a, b):
    return lax.dot_general(a, b, (((0,), (0,)), ((), ())), preferred_element_type=jnp.float32)


def dot_nn(a, b):
    return jnp.dot(a, b, preferred_element_type=jnp.float32)


ATTENTION_ROWS = 256


def causal(scores, start):
    query = start + lax.broadcasted_iota(jnp.int32, scores.shape, 0)
    key = lax.broadcasted_iota(jnp.int32, scores.shape, 1)
    return jnp.where(key <= query, scores, masked_value)


def attend_kernel(
    q_raw, k_raw, v_raw, q_factor, k_factor, q_gain, k_gain, cosine, signed,
    q_out, k_out, v_out, attended, log_total
):
    length, size = q_raw.shape
    scale = size ** (-0.5)
    cos, sin = cosine[...], signed[...]
    q_out[...] = turn_heads(
        q_raw[...] * q_factor[...] * q_gain[...], cos, sin
    ).astype(jnp.bfloat16)
    k_out[...] = turn_heads(
        k_raw[...] * k_factor[...] * k_gain[...], cos, sin
    ).astype(jnp.bfloat16)
    v_out[...] = v_raw[...].astype(jnp.bfloat16)
    rows = min(ATTENTION_ROWS, length)
    for start in range(0, length, rows):
        stop = start + rows
        scores = dot_nt(q_out[start:stop], k_out[:stop]) * scale
        scores = causal(scores, start)
        maximum = jnp.max(scores, axis=-1, keepdims=True)
        exponent = jnp.exp(scores - maximum)
        total = jnp.sum(exponent, axis=-1, keepdims=True)
        weights = (exponent * (1.0 / total)).astype(jnp.bfloat16)
        attended[start:stop] = dot_nn(weights, v_out[:stop]).astype(jnp.bfloat16)
        log_total[0, start:stop] = maximum + jnp.log(total)


def attend(raw, q_factor, k_factor, q_gain, k_gain, cosine, signed, size, after=()):
    length, width = raw.shape[0], raw.shape[1] // 3
    heads = width // size
    by_head = pl.BlockSpec((length, size), lambda h: (0, h))
    parts = [
        pl.BlockSpec((length, size), lambda h, start=index * heads: (0, start + h))
        for index in range(3)
    ]
    fixed = pl.BlockSpec((length, size), lambda h: (0, 0))
    factor = pl.BlockSpec((length, 1), lambda h: (0, 0))
    gain = pl.BlockSpec((1, size), lambda h: (0, h))
    low = jax.ShapeDtypeStruct((length, width), jnp.bfloat16)
    flops = heads * length * length * size * 2
    inputs = (raw, raw, raw, q_factor, k_factor, q_gain, k_gain, cosine, signed)
    return pl.pallas_call(
        ordered(attend_kernel, inputs, after),
        grid=(heads,),
        out_shape=(low, low, low, low, jax.ShapeDtypeStruct((heads, length, 1), jnp.float32)),
        in_specs=parts + [factor] * 2 + [gain] * 2 + [fixed] * 2 + [ANY] * len(after),
        out_specs=[by_head] * 4 + [pl.BlockSpec((1, length, 1), lambda h: (h, 0, 0))],
        name="attend",
        compiler_params=pltpu.CompilerParams(vmem_limit_bytes=VMEM_LIMIT),
        cost_estimate=pl.CostEstimate(
            flops=flops, bytes_accessed=20 * length * width, transcendentals=flops // (4 * size)
        ),
    )(*inputs, *after)


def attend_back_kernel(
    queries, keys, values, grads, log_total, cosine, signed, q_grad, k_grad, v_grad, k_sum, v_sum
):
    length, size = queries.shape
    scale = size ** (-0.5)
    rows = min(ATTENTION_ROWS, length)
    k_sum[...] = jnp.zeros_like(k_sum)
    v_sum[...] = jnp.zeros_like(v_sum)
    for start in range(0, length, rows):
        stop = start + rows
        query, grad = queries[start:stop], grads[start:stop]
        scores = causal(dot_nt(query, keys[:stop]) * scale, start)
        weights = jnp.exp(scores - log_total[0, start:stop])
        v_sum[:stop] += dot_tn(weights.astype(jnp.bfloat16), grad)
        weight_grad = dot_nt(grad, values[:stop])
        inner = jnp.sum(weights * weight_grad, axis=-1, keepdims=True)
        score_grad = (weights * (weight_grad - inner)).astype(jnp.bfloat16)
        q_low = (dot_nn(score_grad, keys[:stop]) * scale).astype(jnp.bfloat16)
        q_grad[start:stop] = turn_heads(
            q_low.astype(jnp.float32), cosine[start:stop], -signed[start:stop]
        )
        k_sum[:stop] += dot_tn(score_grad, query)
    k_low = (k_sum[...] * scale).astype(jnp.bfloat16)
    k_grad[...] = turn_heads(k_low.astype(jnp.float32), cosine[...], -signed[...])
    v_grad[...] = v_sum[...].astype(jnp.bfloat16)


def attend_back(queries, keys, values, grads, log_total, cosine, signed, size, after=()):
    length, width = queries.shape
    heads = width // size
    by_head = pl.BlockSpec((length, size), lambda h: (0, h))
    fixed = pl.BlockSpec((length, size), lambda h: (0, 0))
    wide = jax.ShapeDtypeStruct((length, width), jnp.float32)
    flops = heads * length * length * size * 5
    inputs = (queries, keys, values, grads, log_total, cosine, signed)
    return pl.pallas_call(
        ordered(attend_back_kernel, inputs, after),
        grid=(heads,),
        out_shape=(wide, wide, jax.ShapeDtypeStruct((length, width), jnp.bfloat16)),
        in_specs=[by_head] * 4
        + [pl.BlockSpec((1, length, 1), lambda h: (h, 0, 0))]
        + [fixed] * 2
        + [ANY] * len(after),
        out_specs=[by_head] * 3,
        scratch_shapes=[pltpu.VMEM((length, size), jnp.float32)] * 2,
        name="attend_back",
        compiler_params=pltpu.CompilerParams(vmem_limit_bytes=VMEM_LIMIT),
        cost_estimate=pl.CostEstimate(
            flops=flops, bytes_accessed=20 * length * width, transcendentals=flops // (10 * size)
        ),
    )(*inputs, *after)


def line_total(part):
    for route in ([(0, 1), (3, 2)], [(1, 2), (2, 1)]):
        part = part + lax.ppermute(part, "seq", route)
    seq = lax.axis_index("seq")
    inner = jnp.logical_or(seq == 1, seq == 2)
    return jnp.where(inner, part, lax.ppermute(part, "seq", [(1, 0), (2, 3)]))


def gain_sums(part):
    for mask in (1, 2, 4):
        part = part + lax.ppermute(part, "fsdp", [(i, i ^ mask) for i in range(8)])
    return line_total(part)


def split_layer(
    block_input, query_weight, key_weight, value_weight, out_weight, gate_weight, up_weight,
    down_weight, query_gain, key_gain, attention_gain, swiglu_gain, cotangent
):
    tokens, width = block_input.shape[1:]
    head_size = width // HEADS
    seq, shard = lax.axis_index("seq"), lax.axis_index("fsdp")
    core, chip = lax.rem(shard, 2), lax.div(shard, 2)
    half, quarter = lax.div(seq, 2), lax.rem(seq, 2)
    rows = query_weight.shape[0]
    hidden_width = gate_weight.shape[1] // 8
    group_width = width // 4
    group = 2 * quarter + core
    length = 4 * tokens
    low = jnp.bfloat16
    sequence = block_input.reshape(tokens, width)

    whole, qkv = entry(sequence, query_weight, key_weight, value_weight, 1)
    whole = whole.reshape(length, width)
    out_full = lax.all_gather(
        keep(out_weight, (qkv,)), "fsdp", axis=0, tiled=True
    )
    raw = dot_nn(whole, qkv)
    q_raw, k_raw = raw[:, :group_width], raw[:, group_width : 2 * group_width]

    def reduced(first, second, number, after=()):
        part = jnp.stack([first, second]).reshape(2 * length // 128, 128)
        total = stats_sum(part, number, after).reshape(2, length, 1)
        return total[0] / width, total[1] / width

    q_mean, k_mean = reduced(
        jnp.sum(q_raw * q_raw, axis=-1), jnp.sum(k_raw * k_raw, axis=-1), 2
    )
    q_factor, k_factor = lax.rsqrt(q_mean + epsilon), lax.rsqrt(k_mean + epsilon)
    cosine, sine = rotary_tables(length, 0, head_size)
    cosine = jnp.concatenate([cosine[:, 0], cosine[:, 0]], axis=1)
    signed = jnp.concatenate([-sine[:, 0], sine[:, 0]], axis=1)
    q_gain_part = lax.dynamic_slice_in_dim(query_gain, group * group_width, group_width)[None]
    k_gain_part = lax.dynamic_slice_in_dim(key_gain, group * group_width, group_width)[None]
    queries, keys, values, attended_heads, log_total = attend(
        raw, q_factor, k_factor, q_gain_part, k_gain_part, cosine, signed, head_size
    )
    attended, gate_cols = to_tokens(
        attended_heads.reshape(4, tokens, group_width), gate_weight, 3
    )
    gate_cols = gate_cols.reshape(width, hidden_width)
    branch = dot_nn(attended, out_full)
    branch_factor = norm_factor(branch)
    residual = sequence.astype(jnp.float32) + branch * branch_factor * attention_gain

    plane, up_cols, gate, upward, hidden = gather_hidden(
        residual.astype(low), gate_cols, up_weight, 4
    )
    plane, up_cols = plane.reshape(8 * tokens, width), up_cols.reshape(width, hidden_width)
    mixed_out = plane_scatter(
        out_scatter_kernel, (hidden, down_weight), tokens, width, "out_scatter", 5
    )
    mixed_factor = norm_factor(mixed_out)
    output = residual + mixed_out * mixed_factor * swiglu_gain
    upstream = cotangent.reshape(tokens, width).astype(jnp.float32)
    mixed_float, swiglu_gain_grad = norm_backward(mixed_out, mixed_factor, swiglu_gain, upstream)
    mixed_plane, gate_grad, up_grad = gather_hidden_grad(
        mixed_float.astype(low), down_weight, gate, upward, 6
    )
    mixed_plane = mixed_plane.reshape(8 * tokens, width)
    down_grad = transposed_times(
        hidden.reshape(8 * tokens, hidden_width), mixed_plane
    ).astype(low)
    down_sum = lax.psum(down_grad, "seq")
    gate_sum = transposed_times(plane, gate_grad.reshape(8 * tokens, hidden_width)).astype(low)
    up_sum = transposed_times(plane, up_grad.reshape(8 * tokens, hidden_width)).astype(low)

    residual_grad = upstream + plane_scatter(
        back_scatter_kernel,
        (gate_grad, up_grad, gate_cols, up_cols),
        tokens,
        width,
        "back_scatter",
        7,
        (gate_sum, up_sum),
    )

    branch_float, attention_gain_grad = norm_backward(
        branch, branch_factor, attention_gain, residual_grad
    )
    branch_grad = branch_float.astype(low)
    attended_grad = times_transposed(branch_grad, out_full).astype(low)
    head_grad, out_grad = to_heads(attended_grad, attended, branch_grad, 8)
    head_grad, out_grad = head_grad.reshape(length, group_width), out_grad.astype(low)
    q_norm_grad, k_norm_grad, value_grad = attend_back(
        queries, keys, values, head_grad, log_total, cosine, signed, head_size, (down_sum,)
    )
    q_scaled, k_scaled = q_norm_grad * q_gain_part, k_norm_grad * k_gain_part
    q_inner, k_inner = reduced(
        jnp.sum(q_scaled * q_raw, axis=-1), jnp.sum(k_scaled * k_raw, axis=-1), 9
    )
    q_gain_sum = jnp.sum(q_norm_grad * q_raw * q_factor, axis=0)
    k_gain_sum = jnp.sum(k_norm_grad * k_raw * k_factor, axis=0)
    q_raw_grad = (q_factor * q_scaled - q_raw * (q_factor * q_factor * q_factor * q_inner)).astype(low)
    k_raw_grad = (k_factor * k_scaled - k_raw * (k_factor * k_factor * k_factor * k_inner)).astype(low)
    joined = jnp.concatenate([q_raw_grad, k_raw_grad, value_grad], axis=1)
    input_sum, gate_rows, up_rows, late = finish(
        joined, qkv, whole, gate_sum, up_sum, out_grad, 10
    )
    input_grad = residual_grad + input_sum

    down_total = down_sum.astype(jnp.float32)
    gate_total, up_total = gate_rows.astype(jnp.float32), up_rows.astype(jnp.float32)
    out_total, query_total, key_total, value_total = (
        late[index * rows : (index + 1) * rows].astype(jnp.float32) for index in range(4)
    )

    def widen(part):
        return lax.dynamic_update_slice(
            jnp.zeros((width,), jnp.float32), part, (group * group_width,)
        )

    gain_totals = gain_sums(
        jnp.stack([widen(q_gain_sum), widen(k_gain_sum), attention_gain_grad, swiglu_gain_grad])
    )
    return (
        output.reshape(1, tokens, width),
        input_grad.reshape(1, tokens, width),
        query_total,
        key_total,
        value_total,
        out_total,
        gate_total,
        up_total,
        down_total,
        gain_totals[0],
        gain_totals[1],
        gain_totals[2],
        gain_totals[3],
    )


def fits(mesh):
    return mesh.shape["seq"] == 4 and mesh.shape["fsdp"] == 8


def solution(mesh):
    placed = (
        P("fsdp", "seq", None),
        P("fsdp", None),
        P("fsdp", None),
        P("fsdp", None),
        P("fsdp", None),
        P("fsdp", None),
        P("fsdp", None),
        P("fsdp", None),
        P(),
        P(),
        P(),
        P(),
        P("fsdp", "seq", None),
    )
    return jax.shard_map(
        split_layer if fits(mesh) else local,
        mesh=mesh,
        in_specs=placed,
        out_specs=(
            P("fsdp", "seq", None),
            P("fsdp", "seq", None),
            P("fsdp", None),
            P("fsdp", None),
            P("fsdp", None),
            P("fsdp", None),
            P("fsdp", None),
            P("fsdp", None),
            P("fsdp", None),
            P(),
            P(),
            P(),
            P(),
        ),
        check_vma=False,
    )
```

```python
import jax
import jax.numpy as jnp
from jax import lax
from jax.experimental import pallas as pl
from jax.experimental.pallas import tpu as pltpu
from jax.sharding import PartitionSpec as P

HEADS = 16


epsilon = 1e-06
rotary_base = 500000.0
masked_value = -1e30


def norm_factor(values):
    return lax.rsqrt(jnp.mean(values * values, axis=-1, keepdims=True) + epsilon)


def norm_backward(values, factor, gain_vector, upstream):
    scaled = upstream * gain_vector
    inner_mean = jnp.mean(scaled * values, axis=-1, keepdims=True)
    value_grad = factor * scaled - values * factor * factor * factor * inner_mean
    gain_grad = jnp.sum(upstream * values * factor, axis=0)
    return (value_grad, gain_grad)


def rotary_tables(count, offset, head_size):
    positions = (offset + jnp.arange(count, dtype=jnp.int32)).astype(jnp.float32)
    middle = head_size // 2
    frequency = rotary_base ** (-2.0 * jnp.arange(middle, dtype=jnp.float32) / head_size)
    angles = positions[:, None] * frequency[None, :]
    return (jnp.cos(angles)[:, None, :], jnp.sin(angles)[:, None, :])


def rotate(values, cosine, sine_table, direction_sign):
    middle = values.shape[-1] // 2
    leading = values[..., :middle]
    trailing = values[..., middle:]
    signed = sine_table * direction_sign
    return jnp.concatenate(
        [leading * cosine - trailing * signed, trailing * cosine + leading * signed], axis=-1
    )


def times_transposed(operand, matrix):
    return lax.dot_general(
        operand, matrix, (((1,), (1,)), ((), ())), preferred_element_type=jnp.float32
    )


def transposed_times(operand, matrix):
    return lax.dot_general(
        operand, matrix, (((0,), (0,)), ((), ())), preferred_element_type=jnp.float32
    )


def masked_scores(query_block, keys, row_start, block_rows, score_scale):
    length = keys.shape[0]
    scores = (
        jnp.einsum("qhd,khd->hqk", query_block, keys, preferred_element_type=jnp.float32)
        * score_scale
    )
    query_positions = row_start + jnp.arange(block_rows, dtype=jnp.int32)
    key_positions = jnp.arange(length, dtype=jnp.int32)
    allowed = key_positions[None, :] <= query_positions[:, None]
    return jnp.where(allowed[None], scores, masked_value)


def attention_forward(queries, keys, values):
    length = queries.shape[0]
    block_rows = min(512, length)
    blocks = length // block_rows
    score_scale = queries.shape[-1] ** (-0.5)

    def one_block(block_index):
        row_start = block_index * block_rows
        query_block = lax.dynamic_slice_in_dim(queries, row_start, block_rows, 0)
        scores = masked_scores(query_block, keys, row_start, block_rows, score_scale)
        maximum = jnp.max(scores, axis=-1, keepdims=True)
        exponent = jnp.exp(scores - maximum)
        row_total = jnp.sum(exponent, axis=-1, keepdims=True)
        log_total = maximum[..., 0] + jnp.log(row_total[..., 0])
        weights_low = (exponent / row_total).astype(jnp.bfloat16)
        attended = jnp.einsum(
            "hqk,khd->qhd", weights_low, values, preferred_element_type=jnp.float32
        )
        return (attended.astype(jnp.bfloat16), log_total)

    attended, log_total = lax.map(one_block, jnp.arange(blocks, dtype=jnp.int32))
    return (attended.reshape(length, -1), log_total)


def attention_backward(queries, keys, values, attended_grad, log_total):
    length = queries.shape[0]
    block_rows = min(512, length)
    blocks = length // block_rows
    score_scale = queries.shape[-1] ** (-0.5)
    empty = jnp.zeros(keys.shape, jnp.float32)

    def one_block(carried, operands):
        key_sum, value_sum = carried
        block_index, block_total = operands
        row_start = block_index * block_rows
        query_block = lax.dynamic_slice_in_dim(queries, row_start, block_rows, 0)
        grad_block = lax.dynamic_slice_in_dim(attended_grad, row_start, block_rows, 0)
        scores = masked_scores(query_block, keys, row_start, block_rows, score_scale)
        probabilities = jnp.exp(scores - block_total[..., None])
        weights_low = probabilities.astype(jnp.bfloat16)
        value_sum = value_sum + jnp.einsum(
            "hqk,qhd->khd", weights_low, grad_block, preferred_element_type=jnp.float32
        )
        probability_grad = jnp.einsum(
            "qhd,khd->hqk", grad_block, values, preferred_element_type=jnp.float32
        )
        inner_sum = jnp.sum(probabilities * probability_grad, axis=-1, keepdims=True)
        score_grad = (probabilities * (probability_grad - inner_sum)).astype(jnp.bfloat16)
        query_grad = (
            jnp.einsum("hqk,khd->qhd", score_grad, keys, preferred_element_type=jnp.float32)
            * score_scale
        )
        key_sum = (
            key_sum
            + jnp.einsum(
                "hqk,qhd->khd", score_grad, query_block, preferred_element_type=jnp.float32
            )
            * score_scale
        )
        return ((key_sum, value_sum), query_grad.astype(jnp.bfloat16))

    (key_sum, value_sum), query_grads = lax.scan(
        one_block, (empty, empty), (jnp.arange(blocks, dtype=jnp.int32), log_total)
    )
    return (
        query_grads.reshape(keys.shape),
        key_sum.astype(jnp.bfloat16),
        value_sum.astype(jnp.bfloat16),
    )


def local(
    block_input,
    query_weight,
    key_weight,
    value_weight,
    out_weight,
    gate_weight,
    up_weight,
    down_weight,
    query_gain,
    key_gain,
    attention_gain,
    swiglu_gain,
    cotangent,
):
    tokens = block_input.shape[1]
    model_width = block_input.shape[2]
    head_size = model_width // HEADS
    groups = lax.axis_size("seq")
    local_heads = HEADS // groups
    sequence = block_input.reshape(tokens, model_width)
    query_full, key_full, value_full, out_full = (
        lax.all_gather(query_weight, "fsdp", axis=0, tiled=True),
        lax.all_gather(key_weight, "fsdp", axis=0, tiled=True),
        lax.all_gather(value_weight, "fsdp", axis=0, tiled=True),
        lax.all_gather(out_weight, "fsdp", axis=0, tiled=True),
    )
    query_raw = jnp.dot(sequence, query_full, preferred_element_type=jnp.float32)
    key_raw = jnp.dot(sequence, key_full, preferred_element_type=jnp.float32)
    value_raw = jnp.dot(sequence, value_full, preferred_element_type=jnp.float32)
    query_factor = norm_factor(query_raw)
    key_factor = norm_factor(key_raw)
    cosine, sine_table = rotary_tables(tokens, lax.axis_index("seq") * tokens, head_size)
    query_rot = rotate(
        (query_raw * query_factor * query_gain).reshape(tokens, HEADS, head_size),
        cosine,
        sine_table,
        1.0,
    )
    key_rot = rotate(
        (key_raw * key_factor * key_gain).reshape(tokens, HEADS, head_size), cosine, sine_table, 1.0
    )
    stacked = jnp.stack(
        [
            query_rot.reshape(tokens, model_width).astype(jnp.bfloat16),
            key_rot.reshape(tokens, model_width).astype(jnp.bfloat16),
            value_raw.astype(jnp.bfloat16),
        ]
    )
    grouped = lax.all_to_all(stacked, "seq", split_axis=2, concat_axis=1, tiled=True)
    length = grouped.shape[1]
    head_queries = grouped[0].reshape(length, local_heads, head_size)
    head_keys = grouped[1].reshape(length, local_heads, head_size)
    head_values = grouped[2].reshape(length, local_heads, head_size)
    attended_heads, log_total = attention_forward(head_queries, head_keys, head_values)
    attended = lax.all_to_all(attended_heads, "seq", split_axis=0, concat_axis=1, tiled=True)
    branch = jnp.dot(attended, out_full, preferred_element_type=jnp.float32)
    branch_factor = norm_factor(branch)
    residual = sequence.astype(jnp.float32) + branch * branch_factor * attention_gain
    residual_low = residual.astype(jnp.bfloat16)
    gate_full, up_full, down_full = (
        lax.all_gather(gate_weight, "fsdp", axis=0, tiled=True),
        lax.all_gather(up_weight, "fsdp", axis=0, tiled=True),
        lax.all_gather(down_weight, "fsdp", axis=0, tiled=True),
    )
    gate_value = jnp.dot(residual_low, gate_full, preferred_element_type=jnp.float32)
    upward = jnp.dot(residual_low, up_full, preferred_element_type=jnp.float32)
    sigmoid_gate = jax.nn.sigmoid(gate_value)
    activated = gate_value * sigmoid_gate
    hidden = (activated * upward).astype(jnp.bfloat16)
    mixed_out = jnp.dot(hidden, down_full, preferred_element_type=jnp.float32)
    mixed_factor = norm_factor(mixed_out)
    output = residual + mixed_out * mixed_factor * swiglu_gain
    upstream = cotangent.reshape(tokens, model_width).astype(jnp.float32)
    mixed_float, swiglu_gain_grad = norm_backward(mixed_out, mixed_factor, swiglu_gain, upstream)
    mixed_grad = mixed_float.astype(jnp.bfloat16)
    gate_back, up_back, down_back = (
        lax.all_gather(gate_weight, "fsdp", axis=0, tiled=True),
        lax.all_gather(up_weight, "fsdp", axis=0, tiled=True),
        lax.all_gather(down_weight, "fsdp", axis=0, tiled=True),
    )
    hidden_grad = times_transposed(mixed_grad, down_back)
    gate_grad = (
        hidden_grad * upward * sigmoid_gate * (1.0 + gate_value * (1.0 - sigmoid_gate))
    ).astype(jnp.bfloat16)
    up_grad = (hidden_grad * activated).astype(jnp.bfloat16)
    residual_grad = (
        upstream + times_transposed(gate_grad, gate_back) + times_transposed(up_grad, up_back)
    )
    joined = jnp.concatenate([gate_grad, up_grad], axis=1)
    branch_float, attention_gain_grad = norm_backward(
        branch, branch_factor, attention_gain, residual_grad
    )
    branch_grad = branch_float.astype(jnp.bfloat16)
    query_back, key_back, value_back, out_back = (
        lax.all_gather(query_weight, "fsdp", axis=0, tiled=True),
        lax.all_gather(key_weight, "fsdp", axis=0, tiled=True),
        lax.all_gather(value_weight, "fsdp", axis=0, tiled=True),
        lax.all_gather(out_weight, "fsdp", axis=0, tiled=True),
    )
    attended_grad = times_transposed(branch_grad, out_back).astype(jnp.bfloat16)
    head_grad = lax.all_to_all(attended_grad, "seq", split_axis=1, concat_axis=0, tiled=True)
    query_grads, key_grads, value_grads = attention_backward(
        head_queries,
        head_keys,
        head_values,
        head_grad.reshape(length, local_heads, head_size),
        log_total,
    )
    back_stack = jnp.stack([query_grads, key_grads, value_grads]).reshape(
        3, length, local_heads * head_size
    )
    token_grads = lax.all_to_all(back_stack, "seq", split_axis=1, concat_axis=2, tiled=True)
    query_norm_grad = rotate(
        token_grads[0].astype(jnp.float32).reshape(tokens, HEADS, head_size),
        cosine,
        sine_table,
        -1.0,
    )
    key_norm_grad = rotate(
        token_grads[1].astype(jnp.float32).reshape(tokens, HEADS, head_size),
        cosine,
        sine_table,
        -1.0,
    )
    query_float, query_gain_grad = norm_backward(
        query_raw, query_factor, query_gain, query_norm_grad.reshape(tokens, model_width)
    )
    key_float, key_gain_grad = norm_backward(
        key_raw, key_factor, key_gain, key_norm_grad.reshape(tokens, model_width)
    )
    query_raw_grad = query_float.astype(jnp.bfloat16)
    key_raw_grad = key_float.astype(jnp.bfloat16)
    value_tokens = token_grads[2]
    input_grad = (
        residual_grad
        + times_transposed(query_raw_grad, query_back)
        + times_transposed(key_raw_grad, key_back)
        + times_transposed(value_tokens, value_back)
    )
    projected = jnp.concatenate([query_raw_grad, key_raw_grad, value_tokens], axis=1)
    hidden_width = gate_weight.shape[1]
    columns = hidden
    down_shard = lax.psum_scatter(
        transposed_times(columns, mixed_grad).astype(jnp.bfloat16),
        "fsdp",
        scatter_dimension=0,
        tiled=True,
    )
    columns = residual_low
    gate_up_shard = lax.psum_scatter(
        transposed_times(columns, joined).astype(jnp.bfloat16),
        "fsdp",
        scatter_dimension=0,
        tiled=True,
    )
    attention_shard = lax.psum_scatter(
        jnp.concatenate(
            [transposed_times(sequence, projected), transposed_times(attended, branch_grad)], axis=1
        ).astype(jnp.bfloat16),
        "fsdp",
        scatter_dimension=0,
        tiled=True,
    )
    attention_total, gate_up_total, down_total = (
        lax.psum(attention_shard, "seq").astype(jnp.float32),
        lax.psum(gate_up_shard, "seq").astype(jnp.float32),
        lax.psum(down_shard, "seq").astype(jnp.float32),
    )
    gain_totals = lax.psum(
        jnp.stack([query_gain_grad, key_gain_grad, attention_gain_grad, swiglu_gain_grad]),
        ("seq", "fsdp"),
    )
    return (
        output.reshape(1, tokens, model_width),
        input_grad.reshape(1, tokens, model_width),
        attention_total[:, :model_width],
        attention_total[:, model_width : 2 * model_width],
        attention_total[:, 2 * model_width : 3 * model_width],
        attention_total[:, 3 * model_width :],
        gate_up_total[:, :hidden_width],
        gate_up_total[:, hidden_width:],
        down_total,
        gain_totals[0],
        gain_totals[1],
        gain_totals[2],
        gain_totals[3],
    )


MESH = pl.DeviceIdType.MESH
ANY = pl.BlockSpec(memory_space=pl.ANY)
VM = pl.BlockSpec(memory_space=pltpu.VMEM)
DMA = pltpu.SemaphoreType.DMA
VMEM_LIMIT = 60 * 1024 * 1024


def flip(value, bit):
    return value + bit - 2 * bit * lax.rem(lax.div(value, bit), 2)


def flip_mask(value, mask):
    for bit in (1, 2, 4):
        if mask & bit:
            value = flip(value, bit)
    return value


def place():
    seq, shard = lax.axis_index("seq"), lax.axis_index("fsdp")
    return seq, shard


def greet(targets):
    barrier = pltpu.get_barrier_semaphore()
    for target in targets:
        pl.semaphore_signal(barrier, inc=1, device_id=target, device_id_type=MESH)
    pl.semaphore_wait(barrier, len(targets))


def remote(source, target_ref, send, receive, device):
    return pltpu.make_async_remote_copy(
        src_ref=source,
        dst_ref=target_ref,
        send_sem=send,
        recv_sem=receive,
        device_id=device,
        device_id_type=MESH,
    )


def column_others(seq, shard):
    mate = flip(shard, 1)
    others = [(lax.rem(seq + step, 4), shard) for step in (1, 2, 3)]
    return others + [(lax.rem(seq + step, 4), mate) for step in (0, 1, 2, 3)]


def ordered(kernel, inputs, after):
    count, extra = len(inputs), len(after)
    return lambda *refs: kernel(*refs[:count], *refs[count + extra :])


def comm_call(kernel, out_shape, inputs, in_specs, out_specs, scratch, name, number, after=()):
    return pl.pallas_call(
        ordered(kernel, inputs, after),
        out_shape=out_shape,
        in_specs=list(in_specs) + [ANY] * len(after),
        out_specs=out_specs,
        scratch_shapes=scratch,
        name=name,
        compiler_params=pltpu.CompilerParams(
            collective_id=number, has_side_effects=True, vmem_limit_bytes=VMEM_LIMIT
        ),
        cost_estimate=pl.CostEstimate(flops=1, bytes_accessed=1, transcendentals=0),
    )(*inputs, *after)


def keep_kernel(x, out):
    out[...] = x[...]


def hold_kernel(x, out):
    pass


def hold(x, after):
    return pl.pallas_call(
        ordered(hold_kernel, (x,), after),
        out_shape=jax.ShapeDtypeStruct(x.shape, x.dtype),
        in_specs=[ANY] * (1 + len(after)),
        out_specs=ANY,
        input_output_aliases={0: 0},
        name="hold",
    )(x, *after)


def keep(x, after):
    return pl.pallas_call(
        ordered(keep_kernel, (x,), after),
        out_shape=jax.ShapeDtypeStruct(x.shape, x.dtype),
        in_specs=[VM] + [ANY] * len(after),
        out_specs=VM,
        name="keep",
    )(x, *after)


def entry_kernel(
    x, wq, wk, wv, xo, wo, local, x_send, x_recv, fwd_send, w_send, w_recv
):
    seq, shard = place()
    core, half = lax.rem(shard, 2), lax.div(seq, 2)
    quarter = lax.rem(seq, 2)
    rows, width = wq.shape[0], wo.shape[1] // 3
    weights = (wq, wk, wv)
    greet(
        [(seq, flip_mask(shard, mask)) for mask in range(1, 8)]
        + [(lax.rem(seq + step, 4), shard) for step in (1, 2, 3)]
    )
    mine = pl.ds(pl.multiple_of(shard * rows, rows), rows)

    def columns(index):
        return slice(index * width, (index + 1) * width)

    def block(index, target):
        group = 2 * quarter + lax.rem(target, 2)
        return weights[index].at[:, pl.ds(pl.multiple_of(group * width, width), width)]

    x_copies = []
    for which in (0, 1):
        target = 2 * core + which
        copy = remote(x, xo.at[seq], x_send.at[which], x_recv.at[seq], (target, shard))

        @pl.when(target != seq)
        def _():
            copy.start()

        @pl.when(target == seq)
        def _():
            pltpu.make_async_copy(x, xo.at[seq], local.at[3]).start()

        x_copies.append((target, copy))
    copies = []
    for index in range(3):
        for mask in (2, 4, 3, 5, 1):
            target = flip_mask(shard, mask)
            copy = remote(
                block(index, target),
                wo.at[mine, columns(index)],
                w_send.at[index, mask - 1],
                w_recv.at[index, mask - 1],
                (seq, target),
            )
            copy.start()
            copies.append(copy)
    own = [
        pltpu.make_async_copy(block(index, shard), wo.at[mine, columns(index)], local.at[index])
        for index in range(3)
    ]
    for copy in own:
        copy.start()

    mate = (seq, flip(shard, 1))
    for turn in range(4):
        source = lax.rem(seq + turn, 4)
        forward = remote(
            xo.at[source], xo.at[source], fwd_send.at[turn], x_recv.at[source], mate
        )

        @pl.when(core == half)
        def _():
            if turn == 0:
                pltpu.make_async_copy(x, xo.at[seq], local.at[3]).wait()
            else:
                forward.wait_recv()
            forward.start()

    for turn in range(4):
        source = lax.rem(seq + turn, 4)
        forward = remote(
            xo.at[source], xo.at[source], fwd_send.at[turn], x_recv.at[source], mate
        )

        @pl.when(core == half)
        def _():
            forward.wait_send()

        @pl.when(core != half)
        def _():
            forward.wait_recv()

    def arrival(index, origin, mask):
        spot = wo.at[pl.ds(pl.multiple_of(origin * rows, rows), rows), columns(index)]
        return remote(spot, spot, w_send.at[index, 0], w_recv.at[index, mask - 1], mate)

    base = shard - core
    side, above = flip(base, 2), flip(base, 4)
    onward = []
    for index in range(3):
        for origin, mask, slot, target in (
            (side, 2 + core, 6 + core, flip(shard, 4)),
            (above + 1, 5 - core, 7 - core, flip(shard, 2)),
        ):
            arrival(index, origin, mask).wait_recv()
            spot = wo.at[pl.ds(pl.multiple_of(origin * rows, rows), rows), columns(index)]
            copy = remote(
                spot,
                spot,
                w_send.at[index, 5 + len(onward) % 2],
                w_recv.at[index, slot - 1],
                (seq, target),
            )
            copy.start()
            onward.append(copy)
    for target, copy in x_copies:

        @pl.when(target != seq)
        def _():
            copy.wait_send()

    for copy in own:
        copy.wait()
    for copy in copies + onward:
        copy.wait_send()
    far = flip_mask(base, 6)
    for index in range(3):
        arrival(index, flip(shard, 1), 1).wait_recv()
        arrival(index, side + 1, 3 - core).wait_recv()
        arrival(index, above, 4 + core).wait_recv()
        arrival(index, far, 6 + core).wait_recv()
        arrival(index, far + 1, 7 - core).wait_recv()


def entry(x, wq, wk, wv, number):
    rows, width = wq.shape
    group = width // 4
    return comm_call(
        entry_kernel,
        (
            jax.ShapeDtypeStruct((4,) + x.shape, x.dtype),
            jax.ShapeDtypeStruct((8 * rows, 3 * group), wq.dtype),
        ),
        (x, wq, wk, wv),
        [ANY] * 4,
        (ANY, ANY),
        [DMA((4,)), DMA((2,)), DMA((4,)), DMA((4,)), DMA((3, 7)), DMA((3, 7))],
        "entry",
        number,
    )


def stats_kernel(part, total, held, send, receive):
    seq, shard = place()
    partners = [
        (seq, flip(shard, 1)),
        (flip(seq, 1), shard),
        (flip(seq, 1), flip(shard, 1)),
    ]
    greet(partners)
    copies = [
        remote(part, held.at[index], send.at[index], receive.at[index], partner)
        for index, partner in enumerate(partners)
    ]
    for copy in copies:
        copy.start()
    for copy in copies:
        copy.wait()
    total[...] = (part[...] + held[0]) + (held[1] + held[2])


def stats_sum(part, number, after=()):
    return comm_call(
        stats_kernel,
        jax.ShapeDtypeStruct(part.shape, part.dtype),
        (part,),
        [VM],
        VM,
        [pltpu.VMEM((3,) + part.shape, part.dtype), DMA((3,)), DMA((3,))],
        "stats",
        number,
        after,
    )


def plane_others(seq, shard):
    return [(seq, flip_mask(shard, mask)) for mask in range(1, 8)]


class ColumnExchange:
    def __init__(self, weight, cols, local, send, receive):
        self.parts = (weight, cols, local, send, receive)
        self.seq, self.shard = place()
        self.width = cols.shape[2]

    def block(self, target):
        weight = self.parts[0]
        return weight.at[:, pl.ds(pl.multiple_of(target * self.width, self.width), self.width)]

    def copies(self):
        _, cols, local, send, receive = self.parts
        spot = cols.at[self.shard]
        for mask in (2, 4, 3, 5, 6, 7, 1):
            target = flip_mask(self.shard, mask)
            yield remote(
                self.block(target), spot, send.at[mask], receive.at[mask], (self.seq, target)
            )

    def start(self):
        _, cols, local, _, _ = self.parts
        self.started = list(self.copies())
        for copy in self.started:
            copy.start()
        self.own = pltpu.make_async_copy(self.block(self.shard), cols.at[self.shard], local)
        self.own.start()

    def wait(self):
        self.own.wait()
        for copy in self.started:
            copy.wait()


EXCHANGE = [DMA, DMA((8,)), DMA((8,))]


class PairExchange(ColumnExchange):
    def start(self):
        _, cols, local, send, receive = self.parts
        seq, shard = self.seq, self.shard
        self.sender = lax.rem(shard, 2) == lax.rem(seq, 2)
        copies = {
            mask: remote(
                self.block(flip_mask(shard, mask)),
                cols.at[shard],
                send.at[mask],
                receive.at[mask],
                (seq, flip_mask(shard, mask)),
            )
            for mask in range(1, 8)
        }
        copies[1].start()
        self.started = [copies[1]]
        self.sent = [copies[mask] for mask in (2, 4, 3, 5, 6, 7)]

        @pl.when(self.sender)
        def _():
            for copy in self.sent:
                copy.start()

        self.own = pltpu.make_async_copy(self.block(shard), cols.at[shard], local)
        self.own.start()

    def turn(self, bits):
        _, cols, _, send, receive = self.parts
        parity = lax.rem(lax.rem(self.shard, 2) + lax.rem(self.seq, 2), 2)
        here, there = bits + parity, bits + 1 - parity
        spot, came = cols.at[flip_by(self.shard, here)], cols.at[flip_by(self.shard, there)]
        pair = (flip(self.seq, 1), self.shard)
        arrival = remote(spot, spot, send.at[here], receive.at[here], pair)
        onward = remote(spot, spot, send.at[8 + bits // 2], receive.at[here], pair)
        swapped = remote(came, came, send.at[8 + bits // 2], receive.at[there], pair)
        return arrival, onward, swapped

    def relay(self, bits):
        arrival, onward, _ = self.turn(bits)
        arrival.wait_recv()
        onward.start()

    def wait(self):
        self.own.wait()
        for copy in self.started:
            copy.wait()

        @pl.when(self.sender)
        def _():
            for copy in self.sent:
                copy.wait_send()

        for bits in (2, 4, 6):
            _, onward, swapped = self.turn(bits)
            onward.wait_send()
            swapped.wait_recv()


PAIR_EXCHANGE = [DMA, DMA((12,)), DMA((8,))]


def columns_shape(weight):
    rows, width = weight.shape
    return jax.ShapeDtypeStruct((8, rows, width // 8), weight.dtype)


def to_tokens_kernel(
    heads, weight, tokens, cols, local, send, receive, cols_local, cols_send, cols_receive
):
    seq, shard = place()
    core, half = lax.rem(shard, 2), lax.div(seq, 2)
    base = shard - core
    width = heads.shape[2]
    group = 2 * lax.rem(seq, 2) + core
    greet(column_others(seq, shard) + plane_others(seq, shard)[1:])
    mine = tokens.at[:, pl.ds(pl.multiple_of(group * width, width), width)]
    steps = []
    for turn in range(4):
        target = lax.rem(seq + turn, 4)
        remote_copy = remote(
            heads.at[target], mine, send.at[turn], receive.at[group], (target, base + half)
        )
        if turn == 0:
            here = core == half
            own = pltpu.make_async_copy(heads.at[target], mine, local)

            @pl.when(here)
            def _():
                own.start()

            @pl.when(jnp.logical_not(here))
            def _():
                remote_copy.start()

        else:
            remote_copy.start()
        steps.append(remote_copy)
    exchange = ColumnExchange(weight, cols, cols_local, cols_send, cols_receive)
    exchange.start()
    for turn in range(4):
        if turn == 0:

            @pl.when(here)
            def _():
                own.wait()

            @pl.when(jnp.logical_not(here))
            def _():
                steps[0].wait_send()

        else:
            steps[turn].wait_send()
    for source in range(4):
        slot = tokens.at[:, source * width : (source + 1) * width]
        arrival = remote(heads.at[0], slot, send.at[0], receive.at[source], (seq, shard))

        @pl.when(jnp.logical_not(jnp.logical_and(here, group == source)))
        def _():
            arrival.wait_recv()

    exchange.wait()


def to_tokens(heads, weight, number, after=()):
    blocks, rows, width = heads.shape
    return comm_call(
        to_tokens_kernel,
        (jax.ShapeDtypeStruct((rows, 4 * width), heads.dtype), columns_shape(weight)),
        (heads, weight),
        [ANY] * 2,
        (ANY, ANY),
        [DMA, DMA((4,)), DMA((4,))] + EXCHANGE,
        "to_tokens",
        number,
        after,
    )


def to_heads_kernel(
    tokens, attended, grads, heads, out, part, *scratch
):
    local, send, receive = scratch[-3:]
    scratch = scratch[:-3]
    seq, shard = place()
    greet(column_others(seq, shard) + plane_others(seq, shard)[1:])
    core, half = lax.rem(shard, 2), lax.div(seq, 2)
    base = shard - core
    width = heads.shape[2]
    here = core == half
    mine = 2 * lax.rem(seq, 2) + core
    copies = []
    for group in range(4):
        target = (2 * core + group // 2, base + group % 2)
        source = tokens.at[:, group * width : (group + 1) * width]
        copy = remote(source, heads.at[seq], send.at[group], receive.at[seq], target)
        own = pltpu.make_async_copy(source, heads.at[seq], local)
        self_copy = jnp.logical_and(here, mine == group)

        @pl.when(self_copy)
        def _():
            own.start()

        @pl.when(jnp.logical_not(self_copy))
        def _():
            copy.start()

        copies.append((self_copy, own, copy))
    def produce(block):
        rows = out.shape[0]
        span = pl.ds(pl.multiple_of(block * rows, rows), rows)

        def tile(at):
            part[block, :, at] = dot_tn(attended[:, span], grads[:, at]).astype(jnp.bfloat16)

        tiles(grads.shape[1], tile)

    scatter_products(produce, part, out, *scratch, meet=False)
    for self_copy, own, copy in copies:

        @pl.when(self_copy)
        def _():
            own.wait()

        @pl.when(jnp.logical_not(self_copy))
        def _():
            copy.wait_send()

    for source in range(4):
        arrival = remote(
            tokens.at[:, 0:width], heads.at[source], send.at[0], receive.at[source], (seq, shard)
        )

        @pl.when(jnp.logical_not(jnp.logical_and(here, seq == source)))
        def _():
            arrival.wait_recv()


def to_heads(tokens, attended, grads, number, after=()):
    rows, width = tokens.shape
    low = tokens.dtype
    return comm_call(
        to_heads_kernel,
        (
            jax.ShapeDtypeStruct((4, rows, width // 4), low),
            jax.ShapeDtypeStruct((rows, width), jnp.float32),
        ),
        (tokens, attended, grads),
        [ANY, VM, VM],
        (ANY, VM),
        scatter_scratch(rows, width) + [DMA, DMA((4,)), DMA((4,))],
        "to_heads",
        number,
        after,
    )


def gather_plane(x, out, local, send, receive, ready, exchange=None):
    seq, shard = place()
    core = lax.rem(shard, 2)
    near = [(seq, flip(shard, bit)) for bit in (2, 4, 1)]
    greet(plane_others(seq, shard) + [(flip(seq, 1), shard)] if exchange else near)
    own = pltpu.make_async_copy(x, out.at[shard], local)
    own.start()
    firsts = [
        remote(x, out.at[shard], send.at[index], receive.at[index], device)
        for index, device in enumerate(near)
    ]
    for copy in firsts:
        copy.start()
    if exchange:
        exchange.start()
    mate = near[2]
    mate_shard = flip(shard, 1)

    def pass_on(slot, index, device):
        return remote(out.at[slot], out.at[slot], send.at[index], receive.at[index], device)

    first_bit = 2 + 2 * core
    second_bit = 4 - 2 * core
    first, second = flip_bit(shard, first_bit), flip_bit(shard, second_bit)
    diagonal = flip_mask(shard, 6)

    def arrival(slot, index):
        return remote(out.at[slot], out.at[slot], send.at[0], receive.at[index], mate)

    own.wait()
    ready(shard)
    arrival(mate_shard, 2).wait_recv()
    ready(mate_shard)
    arrival(first, core).wait_recv()
    across = pass_on(first, 3, (seq, second))
    across.start()
    one = remote(out.at[first], out.at[first], send.at[4], receive.at[4 + core], mate)
    one.start()
    arrival(second, 1 - core).wait_recv()
    two = remote(out.at[second], out.at[second], send.at[5], receive.at[5 - core], mate)
    two.start()
    ready(first)
    ready(second)
    if exchange:
        exchange.relay(2)
        exchange.relay(4)
    arrival(flip(mate_shard, 2), 4).wait_recv()
    ready(flip(mate_shard, 2))
    arrival(diagonal, 3).wait_recv()
    three = pass_on(diagonal, 6, mate)
    three.start()
    arrival(flip(mate_shard, 4), 5).wait_recv()
    ready(flip(mate_shard, 4))
    ready(diagonal)
    arrival(flip_mask(mate_shard, 6), 6).wait_recv()
    ready(flip_mask(mate_shard, 6))
    if exchange:
        exchange.relay(6)
    for copy in firsts + [across, one, two, three]:
        copy.wait_send()


class Stores:
    def __init__(self, pairs, sems):
        self.pairs, self.sems = pairs, sems

    def copies(self, slot):
        return [
            pltpu.make_async_copy(source.at[slot], target.at[slot], self.sems.at[index, slot])
            for index, (source, target) in enumerate(self.pairs)
        ]

    def start(self, slot):
        for copy in self.copies(slot):
            copy.start()

    def wait(self):
        def one(slot, carry):
            for copy in self.copies(slot):
                copy.wait()
            return carry

        lax.fori_loop(0, 8, one, 0)


TILE = 512


def tiles(width, body):
    def one(index, carry):
        body(pl.ds(pl.multiple_of(index * TILE, TILE), TILE))
        return carry

    lax.fori_loop(0, width // TILE, one, 0)


def hidden_kernel(
    x, weight, gate_cols, plane, up_cols, gate, upward, hidden,
    plane_in, up_in, gate_wide, gate_low, up_low, hidden_low, local, send, receive, store,
    up_store, cols_local, cols_send, cols_receive
):
    exchange = PairExchange(weight, up_in, cols_local, cols_send, cols_receive)
    width = gate_wide.shape[2]
    early = Stores([(plane_in, plane), (gate_low, gate)], store.at[0])
    late = Stores([(up_low, upward), (hidden_low, hidden)], store.at[1])

    def ready(slot):
        def tile(at):
            value = dot_nn(plane_in[slot], gate_cols[:, at])
            gate_wide[slot, :, at] = value
            gate_low[slot, :, at] = value.astype(jnp.bfloat16)

        tiles(width, tile)
        early.start(slot)

    gather_plane(x, plane_in, local, send, receive, ready, exchange)
    exchange.wait()
    kept = pltpu.make_async_copy(up_in, up_cols, up_store)
    kept.start()

    def last(slot, carry):
        def tile(at):
            value = dot_nn(plane_in[slot], up_in[:, :, at].reshape(-1, TILE))
            gated = gate_wide[slot, :, at]
            up_low[slot, :, at] = value.astype(jnp.bfloat16)
            hidden_low[slot, :, at] = (
                gated * (1.0 / (1.0 + jnp.exp(-gated))) * value
            ).astype(jnp.bfloat16)

        tiles(width, tile)
        late.start(slot)
        return carry

    lax.fori_loop(0, 8, last, 0)
    early.wait()
    late.wait()
    kept.wait()


def gather_hidden(x, gate_cols, weight, number, after=()):
    rows, wide = x.shape
    width = weight.shape[1] // 8
    low = x.dtype
    narrow = (8, rows, width)
    result = jax.ShapeDtypeStruct(narrow, low)
    return comm_call(
        hidden_kernel,
        (jax.ShapeDtypeStruct((8, rows, wide), low), columns_shape(weight)) + (result,) * 3,
        (x, weight, gate_cols),
        [VM, ANY, VM],
        (ANY,) * 5,
        [
            pltpu.VMEM((8, rows, wide), low),
            pltpu.VMEM(columns_shape(weight).shape, low),
            pltpu.VMEM(narrow, jnp.float32),
        ]
        + [pltpu.VMEM(narrow, low)] * 3
        + [DMA, DMA((7,)), DMA((7,)), DMA((2, 2, 8)), DMA]
        + PAIR_EXCHANGE,
        "gather_hidden",
        number,
        after,
    )


def hidden_grad_kernel(
    x, down, gate, upward, plane, gate_grad, up_grad,
    plane_in, gate_low, up_low, local, send, receive, store
):
    width = gate.shape[2]
    stores = Stores([(plane_in, plane), (gate_low, gate_grad), (up_low, up_grad)], store)

    def ready(slot):
        def tile(at):
            grad = dot_nt(plane_in[slot], down[at])
            gated = gate[slot, :, at].astype(jnp.float32)
            sigmoid = 1.0 / (1.0 + jnp.exp(-gated))
            part = grad * sigmoid
            gate_low[slot, :, at] = (
                part * upward[slot, :, at].astype(jnp.float32) * (1.0 + gated * (1.0 - sigmoid))
            ).astype(jnp.bfloat16)
            up_low[slot, :, at] = (part * gated).astype(jnp.bfloat16)

        tiles(width, tile)
        stores.start(slot)

    gather_plane(x, plane_in, local, send, receive, ready)
    stores.wait()


def gather_hidden_grad(x, down, gate, upward, number, after=()):
    rows, wide = x.shape
    low = x.dtype
    narrow = gate.shape
    result = jax.ShapeDtypeStruct(narrow, low)
    return comm_call(
        hidden_grad_kernel,
        (jax.ShapeDtypeStruct((8, rows, wide), low), result, result),
        (x, down, gate, upward),
        [VM] * 4,
        (ANY,) * 3,
        [pltpu.VMEM((8, rows, wide), low)]
        + [pltpu.VMEM(narrow, low)] * 2
        + [DMA, DMA((7,)), DMA((7,)), DMA((3, 8))],
        "gather_hidden_grad",
        number,
        after,
    )


def flip_bit(value, bit):
    return value + bit - 2 * bit * lax.rem(lax.div(value, bit), 2)


PIECES = 2


def add_rows(rows, body):
    step = 32

    def one(index, carry):
        body(pl.ds(pl.multiple_of(index * step, step), step))
        return carry

    lax.fori_loop(0, rows // step, one, 0)


def scatter_products(
    produce, part, out, mated, first_in, second_in, sums, sem_s, sem_r, meet=True
):
    seq, shard = place()
    core, chip = lax.rem(shard, 2), lax.div(shard, 2)
    rows = out.shape[0] // PIECES
    mate = (seq, flip(shard, 1))
    bit = 1 + core
    first, second = flip_bit(chip, bit), flip_bit(chip, 3 - bit)
    diagonal = 3 - chip
    first_device, second_device = (seq, 2 * first + core), (seq, 2 * second + core)
    if meet:
        greet([mate, first_device, second_device])

    def piece(index):
        return pl.ds(index * rows, rows)

    order, mate_order = (diagonal, first, second, chip), (diagonal, second, first, chip)
    swaps = {}

    def make(slot):
        target = mate_order[slot]
        produce(2 * target + 1 - core)
        for index in range(PIECES):
            copy = remote(
                part.at[2 * target + 1 - core, piece(index)],
                mated.at[target, piece(index)],
                sem_s.at[0, slot, index],
                sem_r.at[0, target, index],
                mate,
            )
            copy.start()
            swaps[slot, index] = copy
        produce(2 * order[slot] + core)

    make(0)
    make(1)

    def came(target, index):
        remote(
            part.at[0, piece(index)],
            mated.at[target, piece(index)],
            sem_s.at[0, 0, index],
            sem_r.at[0, target, index],
            mate,
        ).wait_recv()

    sends = []
    for index in range(PIECES):
        for slot, target in ((0, diagonal), (1, first)):
            came(target, index)

            def add(span, slot=slot, target=target, index=index):
                span = pl.ds(span.start + index * rows, span.size)
                sums[slot, span] = (
                    part[2 * target + core, span].astype(jnp.float32)
                    + mated[target, span].astype(jnp.float32)
                ).astype(jnp.bfloat16)

            add_rows(rows, add)
            copy = remote(
                sums.at[slot, piece(index)],
                first_in.at[slot, piece(index)],
                sem_s.at[1, slot, index],
                sem_r.at[1, slot, index],
                first_device,
            )
            copy.start()
            sends.append(copy)
    make(2)
    make(3)
    finals = []
    for index in range(PIECES):
        came(second, index)
        sends[2 * index].wait_recv()

        def add(span, index=index):
            span = pl.ds(span.start + index * rows, span.size)
            sums[2, span] = (
                part[2 * second + core, span].astype(jnp.float32)
                + mated[second, span].astype(jnp.float32)
                + first_in[0, span].astype(jnp.float32)
            ).astype(jnp.bfloat16)

        add_rows(rows, add)
        copy = remote(
            sums.at[2, piece(index)],
            second_in.at[piece(index)],
            sem_s.at[2, 0, index],
            sem_r.at[2, 0, index],
            second_device,
        )
        copy.start()
        finals.append(copy)
    for index in range(PIECES):
        came(chip, index)
        sends[2 * index + 1].wait_recv()
        finals[index].wait_recv()

        def add(span, index=index):
            span = pl.ds(span.start + index * rows, span.size)
            out[span] = (
                part[shard, span].astype(jnp.float32) + mated[chip, span].astype(jnp.float32)
            ) + (first_in[1, span].astype(jnp.float32) + second_in[span].astype(jnp.float32))

        add_rows(rows, add)
    for copy in list(swaps.values()) + sends + finals:
        copy.wait_send()


def out_scatter_kernel(hidden, down, out, part, *scratch):
    def produce(block):
        def tile(at):
            part[block, :, at] = dot_nn(hidden[block], down[:, at]).astype(jnp.bfloat16)

        tiles(down.shape[1], tile)

    scatter_products(produce, part, out, *scratch)


def back_scatter_kernel(gate_grad, up_grad, gate_cols, up_cols, out, part, *scratch):
    def produce(block):
        def tile(at):
            part[block, :, at] = (
                dot_nt(gate_grad[block], gate_cols[at]) + dot_nt(up_grad[block], up_cols[at])
            ).astype(jnp.bfloat16)

        tiles(gate_cols.shape[0], tile)

    scatter_products(produce, part, out, *scratch)


def scatter_scratch(rows, width):
    low = jnp.bfloat16
    return [
        pltpu.VMEM((8, rows, width), low),
        pltpu.VMEM((4, rows, width), low),
        pltpu.VMEM((2, rows, width), low),
        pltpu.VMEM((rows, width), low),
        pltpu.VMEM((3, rows, width), low),
        DMA((3, 4, PIECES)),
        DMA((3, 4, PIECES)),
    ]


def plane_scatter(kernel, inputs, rows, width, name, number, after=()):
    return comm_call(
        kernel,
        jax.ShapeDtypeStruct((rows, width), jnp.float32),
        inputs,
        [VM] * len(inputs),
        VM,
        scatter_scratch(rows, width),
        name,
        number,
        after,
    )


LINE_ROWS = 128
RING = 4
CLOSE_LAG = 2
TAKE_LAG = 5


def flip_by(value, mask):
    for bit in (1, 2, 4):
        here, there = lax.rem(lax.div(value, bit), 2), lax.rem(lax.div(mask, bit), 2)
        value = value + bit * (lax.rem(here + there, 2) - here)
    return value


class LineSums:
    def __init__(self, gate, up, late, gate_rows, up_rows, out, landed, scratch):
        self.gate, self.up, self.late = gate, up, late
        self.rows_out, self.out = (gate_rows, up_rows), out
        self.first_in, self.second_in, self.total_in = landed
        (
            self.own, self.sums, self.others, self.totals,
            self.own_sem, self.load_sem, self.keep_sem, self.send, self.receive,
            self.spread_send, self.spread_receive,
        ) = scratch
        self.seq, self.shard = place()
        self.inner = jnp.logical_or(self.seq == 1, self.seq == 2)
        self.outer = jnp.logical_not(self.inner)
        self.beside = (self.seq + 1 - 2 * lax.rem(self.seq, 2), self.shard)
        self.across = (3 - self.seq, self.shard)
        self.rows, self.width = gate_rows.shape[0], gate.shape[1]
        self.cuts = self.rows // LINE_ROWS
        self.early = 8 * self.cuts
        self.count = self.early + len(late)
        self.away = 7 * self.cuts
        self.halves = (slice(0, self.width), slice(self.width, 2 * self.width))

    def is_late(self, index):
        return isinstance(index, int) and index >= self.early

    def owner(self, index):
        return flip_by(self.shard, 7 - lax.div(index, self.cuts))

    def sources(self, index):
        if self.is_late(index):
            return [(self.late[index - self.early], slice(0, 2 * self.width))]
        start = self.owner(index) * self.rows + lax.rem(index, self.cuts) * LINE_ROWS
        span = pl.ds(pl.multiple_of(start, LINE_ROWS), LINE_ROWS)
        return list(zip((self.gate.at[span], self.up.at[span]), self.halves))

    def inward(self, index):
        return [
            remote(
                source,
                self.first_in.at[index, :, half],
                self.send.at[side, index],
                self.receive.at[side, index],
                self.beside,
            )
            for side, (source, half) in enumerate(self.sources(index))
        ]

    def swap(self, index):
        return remote(
            self.sums.at[lax.rem(index, RING)],
            self.second_in.at[index],
            self.send.at[2, index],
            self.receive.at[2, index],
            self.across,
        )

    def result(self, index):
        if self.is_late(index):
            start = (index - self.early) * LINE_ROWS
            return self.out.at[start : start + LINE_ROWS]
        return self.total_in.at[index]

    def outward(self, index):
        return remote(
            self.totals.at[lax.rem(index, RING)],
            self.result(index),
            self.send.at[3, index],
            self.receive.at[3, index],
            self.beside,
        )

    def keep(self, index):
        return pltpu.make_async_copy(
            self.totals.at[lax.rem(index, RING)], self.result(index), self.keep_sem.at[index]
        )

    def own_loads(self, index):
        slot = lax.rem(index, 2)
        return [
            pltpu.make_async_copy(
                source, self.own.at[slot, :, half], self.own_sem.at[slot, side]
            )
            for side, (source, half) in enumerate(self.sources(index))
        ]

    def spread(self, index, side, source, away):
        down = pl.ds(
            pl.multiple_of(lax.rem(index, self.cuts) * LINE_ROWS, LINE_ROWS), LINE_ROWS
        )
        along = pl.ds(pl.multiple_of(self.shard * self.width, self.width), self.width)
        source = source.at[:, self.halves[side]]
        spot = self.rows_out[side].at[down, along]
        if not away:
            return pltpu.make_async_copy(source, spot, self.spread_send.at[side, index])
        return remote(
            source,
            spot,
            self.spread_send.at[side, index],
            self.spread_receive.at[side, index],
            (self.seq, self.owner(index)),
        )

    def spread_each(self, index, source, there, here):
        for side in range(2):

            @pl.when(index < self.away)
            def _():
                there(self.spread(index, side, source, True))

            @pl.when(index >= self.away)
            def _():
                here(self.spread(index, side, source, False))

    def spread_start(self, index, source):
        self.spread_each(index, source, lambda copy: copy.start(), lambda copy: copy.start())

    def spread_sent(self, index, source):
        self.spread_each(index, source, lambda copy: copy.wait_send(), lambda copy: copy.wait())

    def add_up(self, target, first, second):
        def add(at):
            target[at] = (
                first[at].astype(jnp.float32) + second[at].astype(jnp.float32)
            ).astype(jnp.bfloat16)

        add_rows(LINE_ROWS, add)

    def begin(self):
        @pl.when(self.outer)
        def _():
            for copy in self.inward(0):
                copy.start()

        @pl.when(self.inner)
        def _():
            for copy in self.own_loads(0):
                copy.start()

    def retire(self, index):
        self.outward(index).wait_send()
        if self.is_late(index):
            self.keep(index).wait()
        else:
            self.spread_sent(index, self.totals.at[lax.rem(index, RING)])

    def close(self, index):
        slot = lax.rem(index, RING)
        self.swap(index).wait_recv()
        load = pltpu.make_async_copy(
            self.second_in.at[index], self.others, self.load_sem.at[1]
        )
        load.start()
        if isinstance(index, int):
            self.retire(index - RING)
        else:

            @pl.when(index >= RING)
            def _():
                self.retire(index - RING)

        load.wait()
        self.add_up(self.totals.at[slot], self.sums.at[slot], self.others)
        self.outward(index).start()
        if self.is_late(index):
            self.keep(index).start()
        else:
            self.spread_start(index, self.totals.at[slot])

    def inner_step(self, index, following):
        slot = lax.rem(index, RING)
        if following:
            for copy in self.own_loads(index + 1):
                copy.start()
        for copy in self.inward(index):
            copy.wait_recv()
        if isinstance(index, int):
            self.swap(index - RING).wait_send()
        else:

            @pl.when(index >= RING)
            def _():
                self.swap(index - RING).wait_send()

        load = pltpu.make_async_copy(
            self.first_in.at[index], self.sums.at[slot], self.load_sem.at[0]
        )
        load.start()
        for copy in self.own_loads(index):
            copy.wait()
        load.wait()
        self.add_up(self.sums.at[slot], self.sums.at[slot], self.own.at[lax.rem(index, 2)])
        self.swap(index).start()
        if isinstance(index, int):
            self.close(index - CLOSE_LAG)
        else:

            @pl.when(index >= CLOSE_LAG)
            def _():
                self.close(index - CLOSE_LAG)

    def outer_take(self, index):
        self.outward(index).wait_recv()
        if not self.is_late(index):
            self.spread_start(index, self.total_in.at[index])

    def outer_step(self, index, following):
        if following:
            for copy in self.inward(index + 1):
                copy.start()
        if isinstance(index, int):
            self.outer_take(index - TAKE_LAG)
        else:

            @pl.when(index >= TAKE_LAG)
            def _():
                self.outer_take(index - TAKE_LAG)

    def step(self, index, following=True):
        @pl.when(self.inner)
        def _():
            self.inner_step(index, following)

        @pl.when(self.outer)
        def _():
            self.outer_step(index, following)

    def run(self, start, stop):
        def one(index, carry):
            self.step(index)
            return carry

        lax.fori_loop(start, min(stop, self.early - 1), one, 0)

    def finish(self):
        early, count = self.early, self.count
        for index in range(early - 1, count):
            self.step(index, index + 1 < count)

        @pl.when(self.inner)
        def _():
            for index in range(count - CLOSE_LAG, count):
                self.close(index)
            for index in range(count - RING, count):
                self.swap(index).wait_send()
                self.retire(index)

        def each(body):
            def one(index, carry):
                body(index)
                return carry

            lax.fori_loop(0, early, one, 0)

        @pl.when(self.outer)
        def _():
            for index in range(count - TAKE_LAG, count):
                self.outer_take(index)

            def sent(index):
                for copy in self.inward(index):
                    copy.wait_send()
                self.spread_sent(index, self.total_in.at[index])

            each(sent)
            for index in range(early, count):
                for copy in self.inward(index):
                    copy.wait_send()

        def received(index):
            for side in range(2):

                @pl.when(index < self.away)
                def _():
                    self.spread(index, side, self.total_in.at[index], True).wait_recv()

        each(received)


class HeadLoads:
    def __init__(self, sources, log_total, raw, low, logs, wide, sems):
        self.sources, self.log_total, self.raw = sources, log_total, raw
        self.low, self.logs, self.wide, self.sems = low, logs, wide, sems
        self.size = low.shape[3]

    def raws(self, head):
        slot, size = lax.rem(head, 2), self.size
        heads = self.raw.shape[1] // (3 * size)
        return [
            pltpu.make_async_copy(
                self.raw.at[:, pl.ds(pl.multiple_of((part * heads + head) * size, size), size)],
                self.wide.at[slot, part],
                self.sems.at[slot, 5 + part],
            )
            for part in range(2)
        ]

    def lows(self, head):
        slot, size = lax.rem(head, 2), self.size
        at = pl.ds(pl.multiple_of(head * size, size), size)
        copies = [
            pltpu.make_async_copy(
                source.at[:, at], self.low.at[slot, index], self.sems.at[slot, index]
            )
            for index, source in enumerate(self.sources)
        ]
        return copies + [
            pltpu.make_async_copy(
                self.log_total.at[head], self.logs.at[slot], self.sems.at[slot, 4]
            )
        ]


def exact_nt(a, b):
    return lax.dot_general(
        a, b, (((1,), (1,)), ((), ())), preferred_element_type=jnp.float32,
        precision=lax.Precision.HIGHEST,
    )


def exact_tn(a, b):
    return lax.dot_general(
        a, b, (((0,), (0,)), ((), ())), preferred_element_type=jnp.float32,
        precision=lax.Precision.HIGHEST,
    )


def finish_kernel(
    queries, keys, values, head_grad, log_total, raw, weight, cosine, signed, q_factor, k_factor,
    q_gain, k_gain, token_gains, whole, gate, up, out_grad,
    out, gains, gate_rows, up_rows, line_out, first_chunks, second_chunks, total_chunks,
    low, logs, wide, q_turned, k_turned, k_sum, v_sum, joined, stat, stat_in, gain, gain_in,
    part, grads, placed,
    mated, landed, first_in, second_in, swapped,
    head_sem, weight_sem, stat_s, stat_r, gain_s, gain_r,
    local, sem_s, sem_r, grad_s, grad_r, *line_scratch
):
    seq, shard = place()
    core, half, quarter = lax.rem(shard, 2), lax.div(seq, 2), lax.rem(seq, 2)
    chip = lax.div(shard, 2)
    base = shard - core
    group = 2 * quarter + core
    rows = out.shape[0] // 2
    mate = (seq, flip(shard, 1))
    bit = 1 + core
    first, second, diagonal = flip_bit(chip, bit), flip_bit(chip, 3 - bit), 3 - chip
    first_device, second_device = (seq, 2 * first + core), (seq, 2 * second + core)
    greet(column_others(seq, shard) + plane_others(seq, shard)[1:])
    late = [
        out_grad.at[start : start + LINE_ROWS] for start in range(0, out_grad.shape[0], LINE_ROWS)
    ] + [
        placed.at[index, start : start + LINE_ROWS]
        for index in range(3)
        for start in range(0, placed.shape[1], LINE_ROWS)
    ]
    line = LineSums(
        gate, up, late, gate_rows, up_rows, line_out,
        (first_chunks, second_chunks, total_chunks), line_scratch,
    )
    line.begin()

    length, size = cosine.shape
    heads = q_gain.shape[1] // size
    loads = HeadLoads(
        (queries, keys, values, head_grad), log_total, raw, low, logs, wide, head_sem
    )
    for copy in loads.lows(0) + loads.raws(0):
        copy.start()
    blocks = grads.shape[1]
    weight_loads = [
        pltpu.make_async_copy(
            weight.at[index * blocks : (index + 1) * blocks], grads.at[index],
            weight_sem.at[index],
        )
        for index in range(4)
    ]
    for copy in weight_loads:
        copy.start()
    stat[...] = jnp.zeros_like(stat)
    gain[...] = jnp.zeros_like(gain)
    gain[2:4] = token_gains[...]
    ones = jnp.ones((8, size), jnp.float32)

    def columns(head):
        return pl.ds(pl.multiple_of(head * size, size), size)

    def back(head, carry):
        slot, at = lax.rem(head, 2), columns(head)
        for copy in loads.lows(head):
            copy.wait()

        @pl.when(head + 1 < heads)
        def _():
            for copy in loads.lows(head + 1) + loads.raws(head + 1):
                copy.start()

        attend_back_kernel(
            low.at[slot, 0], low.at[slot, 1], low.at[slot, 2], low.at[slot, 3],
            logs.at[pl.ds(slot, 1)], cosine, signed,
            q_turned.at[:, at], k_turned.at[:, at],
            joined.at[:, columns(2 * heads + head)],
            k_sum, v_sum,
        )
        for copy in loads.raws(head):
            copy.wait()
        for index, (turned, factor, gain_part) in enumerate(
            ((q_turned, q_factor, q_gain), (k_turned, k_factor, k_gain))
        ):
            along = turned[:, at].astype(jnp.float32) * wide[slot, index]
            stat[8 * index : 8 * index + 8] += exact_nt(ones, along * gain_part[:, at])
            spot = pl.multiple_of(group * heads * size + head * size, size)
            gain[index : index + 1, pl.ds(spot, size)] = jnp.sum(
                along * factor[...], axis=0, keepdims=True
            )

        @pl.when(lax.rem(head, 2) == 1)
        def _():
            line.step(lax.div(head, 2))

        return carry

    lax.fori_loop(0, heads, back, 0)
    partners = [mate, (flip(seq, 1), shard), (flip(seq, 1), flip(shard, 1))]
    stat_copies = [
        remote(stat, stat_in.at[index], stat_s.at[index], stat_r.at[index], partner)
        for index, partner in enumerate(partners)
    ]
    for copy in stat_copies:
        copy.start()
    own_gain = pltpu.make_async_copy(gain, gain_in.at[shard], gain_s.at[0])
    own_gain.start()
    gain_copies = [
        remote(
            gain, gain_in.at[shard], gain_s.at[mask], gain_r.at[mask],
            (seq, flip_mask(shard, mask)),
        )
        for mask in range(1, 8)
    ]
    for copy in gain_copies:
        copy.start()
    for copy in loads.raws(0):
        copy.start()
    line.run(heads // 2, heads // 2 + 1)
    for copy in stat_copies:
        copy.wait()
    stat[...] = (stat[...] + stat_in[0]) + (stat_in[1] + stat_in[2])
    spreading = jnp.full((8, size), 0.125 / whole.shape[1], jnp.float32)

    def norm_back(head, carry):
        slot, at = lax.rem(head, 2), columns(head)
        for copy in loads.raws(head):
            copy.wait()

        @pl.when(head + 1 < heads)
        def _():
            for copy in loads.raws(head + 1):
                copy.start()

        for index, (turned, factor, gain_part) in enumerate(
            ((q_turned, q_factor, q_gain), (k_turned, k_factor, k_gain))
        ):
            inner = exact_tn(stat[8 * index : 8 * index + 8], spreading)
            scale = factor[...]
            joined[:, columns(index * heads + head)] = (
                scale * (turned[:, at].astype(jnp.float32) * gain_part[:, at])
                - wide[slot, index] * (scale * scale * scale * inner)
            ).astype(jnp.bfloat16)
        return carry

    lax.fori_loop(0, heads, norm_back, 0)
    line.run(heads // 2 + 1, heads // 2 + 2)

    mine = pl.ds(pl.multiple_of(core * rows, rows), rows)
    other = pl.ds(pl.multiple_of((1 - core) * rows, rows), rows)
    here = core == half
    order = [2 * (1 - half) + 1 - quarter, 2 * (1 - half) + quarter, flip(seq, 1), seq]
    long = grads.shape[1] // 2

    def project(target):
        span = pl.ds(pl.multiple_of(target * 2 * long, 2 * long), 2 * long)

        def tile(at):
            grads[target, :, at] = dot_tn(whole[:, span], joined[:, at]).astype(jnp.bfloat16)

        tiles(grads.shape[2], tile)

    for copy in weight_loads:
        copy.wait()
    swaps = []
    for slot, block in enumerate(order):
        tokens = pl.ds(pl.multiple_of(block * 2 * rows, 2 * rows), 2 * rows)

        def tile(index, carry, block=block, tokens=tokens):
            at = pl.ds(pl.multiple_of(index * blocks, blocks), blocks)
            part[block, :, at] = dot_nt(joined[tokens], grads[index]).astype(jnp.bfloat16)
            return carry

        lax.fori_loop(0, 4, tile, 0)
        copy = remote(
            part.at[block, other], mated.at[slot], sem_s.at[0, slot], sem_r.at[0, slot], mate
        )
        copy.start()
        swaps.append(copy)
    firsts = []
    for slot, target in ((0, diagonal), (1, first)):
        project(target)
        for index in range(2):
            span = slice(index * long, (index + 1) * long)
            copy = remote(
                grads.at[target, span],
                first_in.at[slot, span],
                grad_s.at[slot, index],
                grad_r.at[slot, index],
                first_device,
            )
            copy.start()
            firsts.append(copy)
    line.run(4, 5)
    project(second)
    project(chip)
    own_gain.wait()
    for copy in gain_copies:
        copy.wait()
    plane_gain = gain_in[0]
    for index in range(1, 8):
        plane_gain = plane_gain + gain_in[index]
    gain[...] = plane_gain
    own_gain = pltpu.make_async_copy(gain, gain_in.at[8 + seq], gain_s.at[8])
    own_gain.start()
    gain_copies = [
        remote(
            gain, gain_in.at[8 + seq], gain_s.at[8 + step], gain_r.at[7 + step],
            (lax.rem(seq + step, 4), shard),
        )
        for step in (1, 2, 3)
    ]
    for copy in gain_copies:
        copy.start()
    placed[...] = jnp.zeros_like(placed)

    sends = []
    for slot, block in enumerate(order):
        swaps[slot].wait_recv()

        def add(span, slot=slot, block=block):
            source = pl.ds(pl.multiple_of(span.start + core * rows, 32), span.size)
            mated[slot, span] = (
                part[block, source].astype(jnp.float32) + mated[slot, span].astype(jnp.float32)
            ).astype(jnp.bfloat16)

        add_rows(rows, add)
        copy = remote(
            mated.at[slot],
            landed.at[quarter, core],
            sem_s.at[1, slot],
            sem_r.at[1, 2 * quarter + core],
            (block, base + half),
        )
        if slot < 3:
            copy.start()
        else:
            own = pltpu.make_async_copy(mated.at[slot], landed.at[quarter, core], local)

            @pl.when(here)
            def _():
                own.start()

            @pl.when(jnp.logical_not(here))
            def _():
                copy.start()

        sends.append(copy)
    line.run(5, 7)

    seconds = []
    for index in range(2):
        firsts[index].wait_recv()

        def add(span, index=index):
            span = pl.ds(span.start + index * long, span.size)
            first_in[0, span] = (
                grads[second, span].astype(jnp.float32) + first_in[0, span].astype(jnp.float32)
            ).astype(jnp.bfloat16)

        add_rows(long, add)
        span = slice(index * long, (index + 1) * long)
        copy = remote(
            first_in.at[0, span], second_in.at[span], grad_s.at[2, index], grad_r.at[2, index],
            second_device,
        )
        copy.start()
        seconds.append(copy)
    line.run(7, 10)
    for turn in range(2):
        start = pl.multiple_of((1 - core if turn == 0 else core) * long, long)
        if turn == 0:
            for copy in (firsts[2], firsts[3], seconds[0], seconds[1]):
                copy.wait_recv()

        def add(span, start=start):
            span = pl.ds(pl.multiple_of(span.start + start, 32), span.size)
            first_in[1, span] = (
                (grads[chip, span].astype(jnp.float32) + first_in[1, span].astype(jnp.float32))
                + second_in[span].astype(jnp.float32)
            ).astype(jnp.bfloat16)

        add_rows(long, add)
        if turn == 0:
            swap = remote(
                first_in.at[1, pl.ds(start, long)], swapped, grad_s.at[3, 0], grad_r.at[3, 0], mate
            )
            swap.start()
    part_width = out.shape[1] // 4
    own_rows = pl.ds(pl.multiple_of(core * long, long), long)
    for index in range(3):
        spot = pl.multiple_of(group * part_width, part_width)
        placed[index, :, pl.ds(spot, part_width)] = first_in[
            1, own_rows, index * part_width : (index + 1) * part_width
        ]
    swap.wait_recv()
    for index in range(3):
        spot = pl.multiple_of((2 * quarter + 1 - core) * part_width, part_width)
        placed[index, :, pl.ds(spot, part_width)] = swapped[
            :, index * part_width : (index + 1) * part_width
        ]
    line.run(10, 12)

    for slot in range(3):
        sends[slot].wait_send()

    @pl.when(here)
    def _():
        own.wait()

    @pl.when(jnp.logical_not(here))
    def _():
        sends[3].wait_send()

    for source in range(4):
        arrival = remote(
            mated.at[0],
            landed.at[source // 2, source % 2],
            sem_s.at[1, 0],
            sem_r.at[1, source],
            mate,
        )

        @pl.when(jnp.logical_not(jnp.logical_and(here, 2 * quarter + core == source)))
        def _():
            arrival.wait_recv()

    for side in range(2):

        def add(span, side=side):
            target = pl.ds(span.start + side * rows, span.size)
            out[target] = landed[0, side, span].astype(jnp.float32) + landed[
                1, side, span
            ].astype(jnp.float32)

        add_rows(rows, add)
    for copy in swaps + firsts + seconds + [swap]:
        copy.wait_send()
    own_gain.wait()
    for copy in gain_copies:
        copy.wait()
    gains[...] = (gain_in[8] + gain_in[9]) + (gain_in[10] + gain_in[11])
    line.run(12, line.early)
    line.finish()


def finish(
    heads_in, log_total, raw, weight, tables, factors, head_gains, token_gains, whole, gate, up,
    out_grad, number, after=()
):
    length, width = whole.shape
    rows, long, wide = length // 4, weight.shape[0] // 4, weight.shape[1]
    size, group_width = tables[0].shape[1], wide // 3
    low = whole.dtype
    hidden_width = gate.shape[1]
    tail = out_grad.shape[0] + 3 * long // 2
    early, late = gate.shape[0] // LINE_ROWS, tail // LINE_ROWS
    count = early + late
    block = (LINE_ROWS, 2 * hidden_width)
    owned = jax.ShapeDtypeStruct((gate.shape[0] // 8, 8 * hidden_width), low)
    chunks = jax.ShapeDtypeStruct((count,) + block, low)
    results = comm_call(
        finish_kernel,
        (
            jax.ShapeDtypeStruct((rows, width), jnp.float32),
            jax.ShapeDtypeStruct((8, width), jnp.float32),
            owned,
            owned,
            jax.ShapeDtypeStruct((tail, width), low),
            chunks,
            chunks,
            chunks,
        ),
        (*heads_in, log_total, raw, weight, *tables, *factors, *head_gains, token_gains)
        + (whole, gate, up, out_grad),
        [ANY] * 7 + [VM] * 8 + [ANY] * 3,
        (VM, VM) + (ANY,) * 6,
        [
            pltpu.VMEM((2, 4, length, size), low),
            pltpu.VMEM((2, length, 1), jnp.float32),
            pltpu.VMEM((2, 2, length, size), jnp.float32),
            pltpu.VMEM((length, group_width), low),
            pltpu.VMEM((length, group_width), low),
            pltpu.VMEM((length, size), jnp.float32),
            pltpu.VMEM((length, size), jnp.float32),
            pltpu.VMEM((length, wide), low),
            pltpu.VMEM((16, length), jnp.float32),
            pltpu.VMEM((3, 16, length), jnp.float32),
            pltpu.VMEM((8, width), jnp.float32),
            pltpu.VMEM((12, 8, width), jnp.float32),
            pltpu.VMEM((4, rows, width), low),
            pltpu.VMEM((4, long, wide), low),
            pltpu.VMEM((3, long // 2, width), low),
            pltpu.VMEM((4, rows // 2, width), low),
            pltpu.VMEM((2, 2, rows // 2, width), low),
            pltpu.VMEM((2, long, wide), low),
            pltpu.VMEM((long, wide), low),
            pltpu.VMEM((long // 2, wide), low),
            DMA((2, 7)),
            DMA((4,)),
            DMA((3,)),
            DMA((3,)),
            DMA((12,)),
            DMA((11,)),
            DMA,
            DMA((2, 4)),
            DMA((2, 4)),
            DMA((4, 2)),
            DMA((4, 2)),
            pltpu.VMEM((2,) + block, low),
            pltpu.VMEM((RING,) + block, low),
            pltpu.VMEM(block, low),
            pltpu.VMEM((RING,) + block, low),
            DMA((2, 2)),
            DMA((2,)),
            DMA((count,)),
            DMA((4, count)),
            DMA((4, count)),
            DMA((2, early)),
            DMA((2, early)),
        ],
        "finish",
        number,
        after,
    )
    return results[:5]


def turn_heads(values, cosine, signed):
    middle = values.shape[-1] // 2
    return values * cosine + jnp.concatenate(
        [values[:, middle:], values[:, :middle]], axis=1
    ) * signed


def dot_nt(a, b):
    return lax.dot_general(a, b, (((1,), (1,)), ((), ())), preferred_element_type=jnp.float32)


def dot_tn(a, b):
    return lax.dot_general(a, b, (((0,), (0,)), ((), ())), preferred_element_type=jnp.float32)


def dot_nn(a, b):
    return jnp.dot(a, b, preferred_element_type=jnp.float32)


ATTENTION_ROWS = 256


def causal(scores, start):
    query = start + lax.broadcasted_iota(jnp.int32, scores.shape, 0)
    key = lax.broadcasted_iota(jnp.int32, scores.shape, 1)
    return jnp.where(key <= query, scores, masked_value)


def attend_kernel(
    q_raw, k_raw, v_raw, q_factor, k_factor, q_gain, k_gain, cosine, signed,
    q_out, k_out, v_out, attended, log_total
):
    length, size = q_raw.shape
    scale = size ** (-0.5)
    cos, sin = cosine[...], signed[...]
    q_out[...] = turn_heads(
        q_raw[...] * q_factor[...] * q_gain[...], cos, sin
    ).astype(jnp.bfloat16)
    k_out[...] = turn_heads(
        k_raw[...] * k_factor[...] * k_gain[...], cos, sin
    ).astype(jnp.bfloat16)
    v_out[...] = v_raw[...].astype(jnp.bfloat16)
    rows = min(ATTENTION_ROWS, length)
    for start in range(0, length, rows):
        stop = start + rows
        scores = dot_nt(q_out[start:stop], k_out[:stop]) * scale
        scores = causal(scores, start)
        maximum = jnp.max(scores, axis=-1, keepdims=True)
        exponent = jnp.exp(scores - maximum)
        total = jnp.sum(exponent, axis=-1, keepdims=True)
        weights = (exponent * (1.0 / total)).astype(jnp.bfloat16)
        attended[start:stop] = dot_nn(weights, v_out[:stop]).astype(jnp.bfloat16)
        log_total[0, start:stop] = maximum + jnp.log(total)


def attend(raw, q_factor, k_factor, q_gain, k_gain, cosine, signed, size, after=()):
    length, width = raw.shape[0], raw.shape[1] // 3
    heads = width // size
    by_head = pl.BlockSpec((length, size), lambda h: (0, h))
    parts = [
        pl.BlockSpec((length, size), lambda h, start=index * heads: (0, start + h))
        for index in range(3)
    ]
    fixed = pl.BlockSpec((length, size), lambda h: (0, 0))
    factor = pl.BlockSpec((length, 1), lambda h: (0, 0))
    gain = pl.BlockSpec((1, size), lambda h: (0, h))
    low = jax.ShapeDtypeStruct((length, width), jnp.bfloat16)
    flops = heads * length * length * size * 2
    inputs = (raw, raw, raw, q_factor, k_factor, q_gain, k_gain, cosine, signed)
    return pl.pallas_call(
        ordered(attend_kernel, inputs, after),
        grid=(heads,),
        out_shape=(low, low, low, low, jax.ShapeDtypeStruct((heads, length, 1), jnp.float32)),
        in_specs=parts + [factor] * 2 + [gain] * 2 + [fixed] * 2 + [ANY] * len(after),
        out_specs=[by_head] * 4 + [pl.BlockSpec((1, length, 1), lambda h: (h, 0, 0))],
        name="attend",
        compiler_params=pltpu.CompilerParams(vmem_limit_bytes=VMEM_LIMIT),
        cost_estimate=pl.CostEstimate(
            flops=flops, bytes_accessed=20 * length * width, transcendentals=flops // (4 * size)
        ),
    )(*inputs, *after)


def attend_back_kernel(
    queries, keys, values, grads, log_total, cosine, signed, q_grad, k_grad, v_grad, k_sum, v_sum
):
    length, size = queries.shape
    scale = size ** (-0.5)
    rows = min(ATTENTION_ROWS, length)
    k_sum[...] = jnp.zeros_like(k_sum)
    v_sum[...] = jnp.zeros_like(v_sum)
    for start in range(0, length, rows):
        stop = start + rows
        query, grad = queries[start:stop], grads[start:stop]
        scores = causal(dot_nt(query, keys[:stop]) * scale, start)
        weights = jnp.exp(scores - log_total[0, start:stop])
        v_sum[:stop] += dot_tn(weights.astype(jnp.bfloat16), grad)
        weight_grad = dot_nt(grad, values[:stop])
        inner = jnp.sum(weights * weight_grad, axis=-1, keepdims=True)
        score_grad = (weights * (weight_grad - inner)).astype(jnp.bfloat16)
        q_low = (dot_nn(score_grad, keys[:stop]) * scale).astype(jnp.bfloat16)
        q_grad[start:stop] = turn_heads(
            q_low.astype(jnp.float32), cosine[start:stop], -signed[start:stop]
        ).astype(q_grad.dtype)
        k_sum[:stop] += dot_tn(score_grad, query)
    k_low = (k_sum[...] * scale).astype(jnp.bfloat16)
    k_grad[...] = turn_heads(k_low.astype(jnp.float32), cosine[...], -signed[...]).astype(
        k_grad.dtype
    )
    v_grad[...] = v_sum[...].astype(jnp.bfloat16)


def split_layer(
    block_input, query_weight, key_weight, value_weight, out_weight, gate_weight, up_weight,
    down_weight, query_gain, key_gain, attention_gain, swiglu_gain, cotangent
):
    tokens, width = block_input.shape[1:]
    head_size = width // HEADS
    seq, shard = lax.axis_index("seq"), lax.axis_index("fsdp")
    core, chip = lax.rem(shard, 2), lax.div(shard, 2)
    half, quarter = lax.div(seq, 2), lax.rem(seq, 2)
    rows = query_weight.shape[0]
    hidden_width = gate_weight.shape[1] // 8
    group_width = width // 4
    group = 2 * quarter + core
    length = 4 * tokens
    low = jnp.bfloat16
    sequence = block_input.reshape(tokens, width)

    whole, qkv = entry(sequence, query_weight, key_weight, value_weight, 1)
    whole = whole.reshape(length, width)
    out_full = lax.all_gather(
        keep(out_weight, (qkv,)), "fsdp", axis=0, tiled=True
    )
    raw = dot_nn(whole, qkv)
    q_raw, k_raw = raw[:, :group_width], raw[:, group_width : 2 * group_width]

    def reduced(first, second, number, after=()):
        part = jnp.stack([first, second]).reshape(2 * length // 128, 128)
        total = stats_sum(part, number, after).reshape(2, length, 1)
        return total[0] / width, total[1] / width

    q_mean, k_mean = reduced(
        jnp.sum(q_raw * q_raw, axis=-1), jnp.sum(k_raw * k_raw, axis=-1), 2
    )
    q_factor, k_factor = lax.rsqrt(q_mean + epsilon), lax.rsqrt(k_mean + epsilon)
    cosine, sine = rotary_tables(length, 0, head_size)
    cosine = jnp.concatenate([cosine[:, 0], cosine[:, 0]], axis=1)
    signed = jnp.concatenate([-sine[:, 0], sine[:, 0]], axis=1)
    q_gain_part = lax.dynamic_slice_in_dim(query_gain, group * group_width, group_width)[None]
    k_gain_part = lax.dynamic_slice_in_dim(key_gain, group * group_width, group_width)[None]
    queries, keys, values, attended_heads, log_total = attend(
        raw, q_factor, k_factor, q_gain_part, k_gain_part, cosine, signed, head_size
    )
    attended, gate_cols = to_tokens(
        attended_heads.reshape(4, tokens, group_width), gate_weight, 3
    )
    gate_cols = gate_cols.reshape(width, hidden_width)
    branch = dot_nn(attended, out_full)
    branch_factor = norm_factor(branch)
    residual = sequence.astype(jnp.float32) + branch * branch_factor * attention_gain

    plane, up_cols, gate, upward, hidden = gather_hidden(
        residual.astype(low), gate_cols, up_weight, 4
    )
    plane, up_cols = plane.reshape(8 * tokens, width), up_cols.reshape(width, hidden_width)
    mixed_out = plane_scatter(
        out_scatter_kernel, (hidden, down_weight), tokens, width, "out_scatter", 5
    )
    mixed_factor = norm_factor(mixed_out)
    output = residual + mixed_out * mixed_factor * swiglu_gain
    upstream = cotangent.reshape(tokens, width).astype(jnp.float32)
    mixed_float, swiglu_gain_grad = norm_backward(mixed_out, mixed_factor, swiglu_gain, upstream)
    mixed_plane, gate_grad, up_grad = gather_hidden_grad(
        mixed_float.astype(low), down_weight, gate, upward, 6
    )
    mixed_plane = mixed_plane.reshape(8 * tokens, width)
    down_grad = transposed_times(
        hidden.reshape(8 * tokens, hidden_width), mixed_plane
    ).astype(low)
    down_sum = lax.psum(down_grad, "seq")
    gate_sum = transposed_times(plane, gate_grad.reshape(8 * tokens, hidden_width)).astype(low)
    up_sum = transposed_times(plane, up_grad.reshape(8 * tokens, hidden_width)).astype(low)

    residual_grad = upstream + plane_scatter(
        back_scatter_kernel,
        (gate_grad, up_grad, gate_cols, up_cols),
        tokens,
        width,
        "back_scatter",
        7,
        (gate_sum, up_sum),
    )

    branch_float, attention_gain_grad = norm_backward(
        branch, branch_factor, attention_gain, residual_grad
    )
    branch_grad = branch_float.astype(low)
    attended_grad = times_transposed(branch_grad, out_full).astype(low)
    head_grad, out_grad = to_heads(attended_grad, attended, branch_grad, 8)
    head_grad, out_grad = head_grad.reshape(length, group_width), out_grad.astype(low)
    input_sum, gain_totals, gate_rows, up_rows, late = finish(
        (queries, keys, values, head_grad),
        log_total,
        raw,
        qkv,
        (cosine, signed),
        (q_factor, k_factor),
        (q_gain_part, k_gain_part),
        jnp.stack([attention_gain_grad, swiglu_gain_grad]),
        whole,
        gate_sum,
        up_sum,
        out_grad,
        10,
        (down_sum,),
    )
    input_grad = residual_grad + input_sum

    down_total = down_sum.astype(jnp.float32)
    gate_total, up_total = gate_rows.astype(jnp.float32), up_rows.astype(jnp.float32)
    out_total, query_total, key_total, value_total = (
        late[index * rows : (index + 1) * rows].astype(jnp.float32) for index in range(4)
    )

    return (
        output.reshape(1, tokens, width),
        input_grad.reshape(1, tokens, width),
        query_total,
        key_total,
        value_total,
        out_total,
        gate_total,
        up_total,
        down_total,
        gain_totals[0],
        gain_totals[1],
        gain_totals[2],
        gain_totals[3],
    )


def fits(mesh):
    return mesh.shape["seq"] == 4 and mesh.shape["fsdp"] == 8


def solution(mesh):
    placed = (
        P("fsdp", "seq", None),
        P("fsdp", None),
        P("fsdp", None),
        P("fsdp", None),
        P("fsdp", None),
        P("fsdp", None),
        P("fsdp", None),
        P("fsdp", None),
        P(),
        P(),
        P(),
        P(),
        P("fsdp", "seq", None),
    )
    return jax.shard_map(
        split_layer if fits(mesh) else local,
        mesh=mesh,
        in_specs=placed,
        out_specs=(
            P("fsdp", "seq", None),
            P("fsdp", "seq", None),
            P("fsdp", None),
            P("fsdp", None),
            P("fsdp", None),
            P("fsdp", None),
            P("fsdp", None),
            P("fsdp", None),
            P("fsdp", None),
            P(),
            P(),
            P(),
            P(),
        ),
        check_vma=False,
    )
```

```python
import jax
import jax.numpy as jnp
from jax import lax
from jax.experimental import pallas as pl
from jax.experimental.pallas import tpu as pltpu
from jax.sharding import PartitionSpec as P

HEADS = 16


epsilon = 1e-06
rotary_base = 500000.0
masked_value = -1e30


def norm_factor(values):
    return lax.rsqrt(jnp.mean(values * values, axis=-1, keepdims=True) + epsilon)


def norm_backward(values, factor, gain_vector, upstream):
    scaled = upstream * gain_vector
    inner_mean = jnp.mean(scaled * values, axis=-1, keepdims=True)
    value_grad = factor * scaled - values * factor * factor * factor * inner_mean
    gain_grad = jnp.sum(upstream * values * factor, axis=0)
    return (value_grad, gain_grad)


def rotary_tables(count, offset, head_size):
    positions = (offset + jnp.arange(count, dtype=jnp.int32)).astype(jnp.float32)
    middle = head_size // 2
    frequency = rotary_base ** (-2.0 * jnp.arange(middle, dtype=jnp.float32) / head_size)
    angles = positions[:, None] * frequency[None, :]
    return (jnp.cos(angles)[:, None, :], jnp.sin(angles)[:, None, :])


def rotate(values, cosine, sine_table, direction_sign):
    middle = values.shape[-1] // 2
    leading = values[..., :middle]
    trailing = values[..., middle:]
    signed = sine_table * direction_sign
    return jnp.concatenate(
        [leading * cosine - trailing * signed, trailing * cosine + leading * signed], axis=-1
    )


def times_transposed(operand, matrix):
    return lax.dot_general(
        operand, matrix, (((1,), (1,)), ((), ())), preferred_element_type=jnp.float32
    )


def transposed_times(operand, matrix):
    return lax.dot_general(
        operand, matrix, (((0,), (0,)), ((), ())), preferred_element_type=jnp.float32
    )


def masked_scores(query_block, keys, row_start, block_rows, score_scale):
    length = keys.shape[0]
    scores = (
        jnp.einsum("qhd,khd->hqk", query_block, keys, preferred_element_type=jnp.float32)
        * score_scale
    )
    query_positions = row_start + jnp.arange(block_rows, dtype=jnp.int32)
    key_positions = jnp.arange(length, dtype=jnp.int32)
    allowed = key_positions[None, :] <= query_positions[:, None]
    return jnp.where(allowed[None], scores, masked_value)


def attention_forward(queries, keys, values):
    length = queries.shape[0]
    block_rows = min(512, length)
    blocks = length // block_rows
    score_scale = queries.shape[-1] ** (-0.5)

    def one_block(block_index):
        row_start = block_index * block_rows
        query_block = lax.dynamic_slice_in_dim(queries, row_start, block_rows, 0)
        scores = masked_scores(query_block, keys, row_start, block_rows, score_scale)
        maximum = jnp.max(scores, axis=-1, keepdims=True)
        exponent = jnp.exp(scores - maximum)
        row_total = jnp.sum(exponent, axis=-1, keepdims=True)
        log_total = maximum[..., 0] + jnp.log(row_total[..., 0])
        weights_low = (exponent / row_total).astype(jnp.bfloat16)
        attended = jnp.einsum(
            "hqk,khd->qhd", weights_low, values, preferred_element_type=jnp.float32
        )
        return (attended.astype(jnp.bfloat16), log_total)

    attended, log_total = lax.map(one_block, jnp.arange(blocks, dtype=jnp.int32))
    return (attended.reshape(length, -1), log_total)


def attention_backward(queries, keys, values, attended_grad, log_total):
    length = queries.shape[0]
    block_rows = min(512, length)
    blocks = length // block_rows
    score_scale = queries.shape[-1] ** (-0.5)
    empty = jnp.zeros(keys.shape, jnp.float32)

    def one_block(carried, operands):
        key_sum, value_sum = carried
        block_index, block_total = operands
        row_start = block_index * block_rows
        query_block = lax.dynamic_slice_in_dim(queries, row_start, block_rows, 0)
        grad_block = lax.dynamic_slice_in_dim(attended_grad, row_start, block_rows, 0)
        scores = masked_scores(query_block, keys, row_start, block_rows, score_scale)
        probabilities = jnp.exp(scores - block_total[..., None])
        weights_low = probabilities.astype(jnp.bfloat16)
        value_sum = value_sum + jnp.einsum(
            "hqk,qhd->khd", weights_low, grad_block, preferred_element_type=jnp.float32
        )
        probability_grad = jnp.einsum(
            "qhd,khd->hqk", grad_block, values, preferred_element_type=jnp.float32
        )
        inner_sum = jnp.sum(probabilities * probability_grad, axis=-1, keepdims=True)
        score_grad = (probabilities * (probability_grad - inner_sum)).astype(jnp.bfloat16)
        query_grad = (
            jnp.einsum("hqk,khd->qhd", score_grad, keys, preferred_element_type=jnp.float32)
            * score_scale
        )
        key_sum = (
            key_sum
            + jnp.einsum(
                "hqk,qhd->khd", score_grad, query_block, preferred_element_type=jnp.float32
            )
            * score_scale
        )
        return ((key_sum, value_sum), query_grad.astype(jnp.bfloat16))

    (key_sum, value_sum), query_grads = lax.scan(
        one_block, (empty, empty), (jnp.arange(blocks, dtype=jnp.int32), log_total)
    )
    return (
        query_grads.reshape(keys.shape),
        key_sum.astype(jnp.bfloat16),
        value_sum.astype(jnp.bfloat16),
    )


def local(
    block_input,
    query_weight,
    key_weight,
    value_weight,
    out_weight,
    gate_weight,
    up_weight,
    down_weight,
    query_gain,
    key_gain,
    attention_gain,
    swiglu_gain,
    cotangent,
):
    tokens = block_input.shape[1]
    model_width = block_input.shape[2]
    head_size = model_width // HEADS
    groups = lax.axis_size("seq")
    local_heads = HEADS // groups
    sequence = block_input.reshape(tokens, model_width)
    query_full, key_full, value_full, out_full = (
        lax.all_gather(query_weight, "fsdp", axis=0, tiled=True),
        lax.all_gather(key_weight, "fsdp", axis=0, tiled=True),
        lax.all_gather(value_weight, "fsdp", axis=0, tiled=True),
        lax.all_gather(out_weight, "fsdp", axis=0, tiled=True),
    )
    query_raw = jnp.dot(sequence, query_full, preferred_element_type=jnp.float32)
    key_raw = jnp.dot(sequence, key_full, preferred_element_type=jnp.float32)
    value_raw = jnp.dot(sequence, value_full, preferred_element_type=jnp.float32)
    query_factor = norm_factor(query_raw)
    key_factor = norm_factor(key_raw)
    cosine, sine_table = rotary_tables(tokens, lax.axis_index("seq") * tokens, head_size)
    query_rot = rotate(
        (query_raw * query_factor * query_gain).reshape(tokens, HEADS, head_size),
        cosine,
        sine_table,
        1.0,
    )
    key_rot = rotate(
        (key_raw * key_factor * key_gain).reshape(tokens, HEADS, head_size), cosine, sine_table, 1.0
    )
    stacked = jnp.stack(
        [
            query_rot.reshape(tokens, model_width).astype(jnp.bfloat16),
            key_rot.reshape(tokens, model_width).astype(jnp.bfloat16),
            value_raw.astype(jnp.bfloat16),
        ]
    )
    grouped = lax.all_to_all(stacked, "seq", split_axis=2, concat_axis=1, tiled=True)
    length = grouped.shape[1]
    head_queries = grouped[0].reshape(length, local_heads, head_size)
    head_keys = grouped[1].reshape(length, local_heads, head_size)
    head_values = grouped[2].reshape(length, local_heads, head_size)
    attended_heads, log_total = attention_forward(head_queries, head_keys, head_values)
    attended = lax.all_to_all(attended_heads, "seq", split_axis=0, concat_axis=1, tiled=True)
    branch = jnp.dot(attended, out_full, preferred_element_type=jnp.float32)
    branch_factor = norm_factor(branch)
    residual = sequence.astype(jnp.float32) + branch * branch_factor * attention_gain
    residual_low = residual.astype(jnp.bfloat16)
    gate_full, up_full, down_full = (
        lax.all_gather(gate_weight, "fsdp", axis=0, tiled=True),
        lax.all_gather(up_weight, "fsdp", axis=0, tiled=True),
        lax.all_gather(down_weight, "fsdp", axis=0, tiled=True),
    )
    gate_value = jnp.dot(residual_low, gate_full, preferred_element_type=jnp.float32)
    upward = jnp.dot(residual_low, up_full, preferred_element_type=jnp.float32)
    sigmoid_gate = jax.nn.sigmoid(gate_value)
    activated = gate_value * sigmoid_gate
    hidden = (activated * upward).astype(jnp.bfloat16)
    mixed_out = jnp.dot(hidden, down_full, preferred_element_type=jnp.float32)
    mixed_factor = norm_factor(mixed_out)
    output = residual + mixed_out * mixed_factor * swiglu_gain
    upstream = cotangent.reshape(tokens, model_width).astype(jnp.float32)
    mixed_float, swiglu_gain_grad = norm_backward(mixed_out, mixed_factor, swiglu_gain, upstream)
    mixed_grad = mixed_float.astype(jnp.bfloat16)
    gate_back, up_back, down_back = (
        lax.all_gather(gate_weight, "fsdp", axis=0, tiled=True),
        lax.all_gather(up_weight, "fsdp", axis=0, tiled=True),
        lax.all_gather(down_weight, "fsdp", axis=0, tiled=True),
    )
    hidden_grad = times_transposed(mixed_grad, down_back)
    gate_grad = (
        hidden_grad * upward * sigmoid_gate * (1.0 + gate_value * (1.0 - sigmoid_gate))
    ).astype(jnp.bfloat16)
    up_grad = (hidden_grad * activated).astype(jnp.bfloat16)
    residual_grad = (
        upstream + times_transposed(gate_grad, gate_back) + times_transposed(up_grad, up_back)
    )
    joined = jnp.concatenate([gate_grad, up_grad], axis=1)
    branch_float, attention_gain_grad = norm_backward(
        branch, branch_factor, attention_gain, residual_grad
    )
    branch_grad = branch_float.astype(jnp.bfloat16)
    query_back, key_back, value_back, out_back = (
        lax.all_gather(query_weight, "fsdp", axis=0, tiled=True),
        lax.all_gather(key_weight, "fsdp", axis=0, tiled=True),
        lax.all_gather(value_weight, "fsdp", axis=0, tiled=True),
        lax.all_gather(out_weight, "fsdp", axis=0, tiled=True),
    )
    attended_grad = times_transposed(branch_grad, out_back).astype(jnp.bfloat16)
    head_grad = lax.all_to_all(attended_grad, "seq", split_axis=1, concat_axis=0, tiled=True)
    query_grads, key_grads, value_grads = attention_backward(
        head_queries,
        head_keys,
        head_values,
        head_grad.reshape(length, local_heads, head_size),
        log_total,
    )
    back_stack = jnp.stack([query_grads, key_grads, value_grads]).reshape(
        3, length, local_heads * head_size
    )
    token_grads = lax.all_to_all(back_stack, "seq", split_axis=1, concat_axis=2, tiled=True)
    query_norm_grad = rotate(
        token_grads[0].astype(jnp.float32).reshape(tokens, HEADS, head_size),
        cosine,
        sine_table,
        -1.0,
    )
    key_norm_grad = rotate(
        token_grads[1].astype(jnp.float32).reshape(tokens, HEADS, head_size),
        cosine,
        sine_table,
        -1.0,
    )
    query_float, query_gain_grad = norm_backward(
        query_raw, query_factor, query_gain, query_norm_grad.reshape(tokens, model_width)
    )
    key_float, key_gain_grad = norm_backward(
        key_raw, key_factor, key_gain, key_norm_grad.reshape(tokens, model_width)
    )
    query_raw_grad = query_float.astype(jnp.bfloat16)
    key_raw_grad = key_float.astype(jnp.bfloat16)
    value_tokens = token_grads[2]
    input_grad = (
        residual_grad
        + times_transposed(query_raw_grad, query_back)
        + times_transposed(key_raw_grad, key_back)
        + times_transposed(value_tokens, value_back)
    )
    projected = jnp.concatenate([query_raw_grad, key_raw_grad, value_tokens], axis=1)
    hidden_width = gate_weight.shape[1]
    columns = hidden
    down_shard = lax.psum_scatter(
        transposed_times(columns, mixed_grad).astype(jnp.bfloat16),
        "fsdp",
        scatter_dimension=0,
        tiled=True,
    )
    columns = residual_low
    gate_up_shard = lax.psum_scatter(
        transposed_times(columns, joined).astype(jnp.bfloat16),
        "fsdp",
        scatter_dimension=0,
        tiled=True,
    )
    attention_shard = lax.psum_scatter(
        jnp.concatenate(
            [transposed_times(sequence, projected), transposed_times(attended, branch_grad)], axis=1
        ).astype(jnp.bfloat16),
        "fsdp",
        scatter_dimension=0,
        tiled=True,
    )
    attention_total, gate_up_total, down_total = (
        lax.psum(attention_shard, "seq").astype(jnp.float32),
        lax.psum(gate_up_shard, "seq").astype(jnp.float32),
        lax.psum(down_shard, "seq").astype(jnp.float32),
    )
    gain_totals = lax.psum(
        jnp.stack([query_gain_grad, key_gain_grad, attention_gain_grad, swiglu_gain_grad]),
        ("seq", "fsdp"),
    )
    return (
        output.reshape(1, tokens, model_width),
        input_grad.reshape(1, tokens, model_width),
        attention_total[:, :model_width],
        attention_total[:, model_width : 2 * model_width],
        attention_total[:, 2 * model_width : 3 * model_width],
        attention_total[:, 3 * model_width :],
        gate_up_total[:, :hidden_width],
        gate_up_total[:, hidden_width:],
        down_total,
        gain_totals[0],
        gain_totals[1],
        gain_totals[2],
        gain_totals[3],
    )


MESH = pl.DeviceIdType.MESH
ANY = pl.BlockSpec(memory_space=pl.ANY)
VM = pl.BlockSpec(memory_space=pltpu.VMEM)
DMA = pltpu.SemaphoreType.DMA
VMEM_LIMIT = 60 * 1024 * 1024


def flip(value, bit):
    return value + bit - 2 * bit * lax.rem(lax.div(value, bit), 2)


def flip_mask(value, mask):
    for bit in (1, 2, 4):
        if mask & bit:
            value = flip(value, bit)
    return value


def place():
    seq, shard = lax.axis_index("seq"), lax.axis_index("fsdp")
    return seq, shard


def greet(targets):
    barrier = pltpu.get_barrier_semaphore()
    for target in targets:
        pl.semaphore_signal(barrier, inc=1, device_id=target, device_id_type=MESH)
    pl.semaphore_wait(barrier, len(targets))


def remote(source, target_ref, send, receive, device):
    return pltpu.make_async_remote_copy(
        src_ref=source,
        dst_ref=target_ref,
        send_sem=send,
        recv_sem=receive,
        device_id=device,
        device_id_type=MESH,
    )


def column_others(seq, shard):
    mate = flip(shard, 1)
    others = [(lax.rem(seq + step, 4), shard) for step in (1, 2, 3)]
    return others + [(lax.rem(seq + step, 4), mate) for step in (0, 1, 2, 3)]


def ordered(kernel, inputs, after):
    count, extra = len(inputs), len(after)
    return lambda *refs: kernel(*refs[:count], *refs[count + extra :])


def comm_call(kernel, out_shape, inputs, in_specs, out_specs, scratch, name, number, after=()):
    return pl.pallas_call(
        ordered(kernel, inputs, after),
        out_shape=out_shape,
        in_specs=list(in_specs) + [ANY] * len(after),
        out_specs=out_specs,
        scratch_shapes=scratch,
        name=name,
        compiler_params=pltpu.CompilerParams(
            collective_id=number, has_side_effects=True, vmem_limit_bytes=VMEM_LIMIT
        ),
        cost_estimate=pl.CostEstimate(flops=1, bytes_accessed=1, transcendentals=0),
    )(*inputs, *after)


def entry_kernel(
    x, wq, wk, wv, out_weight, xo, wo, out_kept,
    local, x_send, x_recv, fwd_send, w_send, w_recv
):
    seq, shard = place()
    core, half = lax.rem(shard, 2), lax.div(seq, 2)
    quarter = lax.rem(seq, 2)
    rows, width = wq.shape[0], wo.shape[1] // 3
    weights = (wq, wk, wv)
    greet(
        [(seq, flip_mask(shard, mask)) for mask in range(1, 8)]
        + [(lax.rem(seq + step, 4), shard) for step in (1, 2, 3)]
    )
    mine = pl.ds(pl.multiple_of(shard * rows, rows), rows)

    def columns(index):
        return slice(index * width, (index + 1) * width)

    def block(index, target):
        group = 2 * quarter + lax.rem(target, 2)
        return weights[index].at[:, pl.ds(pl.multiple_of(group * width, width), width)]

    near = 1 + core
    x_copies = []
    for which in (0, 1):
        target = 2 * core + which
        wanted = jnp.logical_and(
            target != seq, jnp.logical_or(core == half, target == near)
        )
        copy = remote(x, xo.at[seq], x_send.at[which], x_recv.at[seq], (target, shard))

        @pl.when(wanted)
        def _():
            copy.start()

        @pl.when(target == seq)
        def _():
            pltpu.make_async_copy(x, xo.at[seq], local.at[3]).start()

        x_copies.append((wanted, copy))
    kept = pltpu.make_async_copy(out_weight, out_kept, local.at[4])
    kept.start()
    copies = []
    for index in range(3):
        for mask in (2, 4, 3, 5, 1):
            target = flip_mask(shard, mask)
            copy = remote(
                block(index, target),
                wo.at[mine, columns(index)],
                w_send.at[index, mask - 1],
                w_recv.at[index, mask - 1],
                (seq, target),
            )
            copy.start()
            copies.append(copy)
    own = [
        pltpu.make_async_copy(block(index, shard), wo.at[mine, columns(index)], local.at[index])
        for index in range(3)
    ]
    for copy in own:
        copy.start()

    mate = (seq, flip(shard, 1))
    relays = []
    places = (seq, flip(seq, 1), 2 * (1 - half) + half, 2 * (1 - half) + 1 - half)

    def pass_input(turn):
        source = places[turn]
        forward = remote(
            xo.at[source], xo.at[source], fwd_send.at[turn], x_recv.at[source], mate
        )
        if turn > 1:
            relay = remote(
                xo.at[source], xo.at[source], fwd_send.at[turn + 2], x_recv.at[source],
                (flip(seq, 1), shard),
            )
            relays.append(relay)

        @pl.when(core == half)
        def _():
            if turn == 0:
                pltpu.make_async_copy(x, xo.at[seq], local.at[3]).wait()
            else:
                forward.wait_recv()
            if turn > 1:

                @pl.when(seq == near)
                def _():
                    relay.start()

            forward.start()

    def arrival(index, origin, mask):
        spot = wo.at[pl.ds(pl.multiple_of(origin * rows, rows), rows), columns(index)]
        return remote(spot, spot, w_send.at[index, 0], w_recv.at[index, mask - 1], mate)

    base = shard - core
    side, above = flip(base, 2), flip(base, 4)
    onward = []
    for index in range(3):
        pass_input(index)
        for origin, mask, slot, target in (
            (side, 2 + core, 6 + core, flip(shard, 4)),
            (above + 1, 5 - core, 7 - core, flip(shard, 2)),
        ):
            arrival(index, origin, mask).wait_recv()
            spot = wo.at[pl.ds(pl.multiple_of(origin * rows, rows), rows), columns(index)]
            copy = remote(
                spot,
                spot,
                w_send.at[index, 5 + len(onward) % 2],
                w_recv.at[index, slot - 1],
                (seq, target),
            )
            copy.start()
            onward.append(copy)
    pass_input(3)
    for relay in relays:

        @pl.when(jnp.logical_and(core == half, seq == near))
        def _():
            relay.wait_send()

    for turn, source in enumerate(places):
        forward = remote(
            xo.at[source], xo.at[source], fwd_send.at[turn], x_recv.at[source], mate
        )

        @pl.when(core == half)
        def _():
            forward.wait_send()

        @pl.when(core != half)
        def _():
            forward.wait_recv()

    kept.wait()
    for wanted, copy in x_copies:

        @pl.when(wanted)
        def _():
            copy.wait_send()

    for copy in own:
        copy.wait()
    for copy in copies + onward:
        copy.wait_send()
    far = flip_mask(base, 6)
    for index in range(3):
        arrival(index, flip(shard, 1), 1).wait_recv()
        arrival(index, side + 1, 3 - core).wait_recv()
        arrival(index, above, 4 + core).wait_recv()
        arrival(index, far, 6 + core).wait_recv()
        arrival(index, far + 1, 7 - core).wait_recv()


def entry(x, wq, wk, wv, out_weight, number):
    rows, width = wq.shape
    group = width // 4
    return comm_call(
        entry_kernel,
        (
            jax.ShapeDtypeStruct((4,) + x.shape, x.dtype),
            jax.ShapeDtypeStruct((8 * rows, 3 * group), wq.dtype),
            jax.ShapeDtypeStruct(out_weight.shape, out_weight.dtype),
        ),
        (x, wq, wk, wv, out_weight),
        [VM] * 5,
        (ANY,) * 3,
        [DMA((5,)), DMA((2,)), DMA((4,)), DMA((6,)), DMA((3, 7)), DMA((3, 7))],
        "entry",
        number,
    )


def stats_kernel(part, total, held, send, receive):
    seq, shard = place()
    partners = [
        (seq, flip(shard, 1)),
        (flip(seq, 1), shard),
        (flip(seq, 1), flip(shard, 1)),
    ]
    greet(partners)
    copies = [
        remote(part, held.at[index], send.at[index], receive.at[index], partner)
        for index, partner in enumerate(partners)
    ]
    for copy in copies:
        copy.start()
    for copy in copies:
        copy.wait()
    total[...] = (part[...] + held[0]) + (held[1] + held[2])


def stats_sum(part, number, after=()):
    return comm_call(
        stats_kernel,
        jax.ShapeDtypeStruct(part.shape, part.dtype),
        (part,),
        [VM],
        VM,
        [pltpu.VMEM((3,) + part.shape, part.dtype), DMA((3,)), DMA((3,))],
        "stats",
        number,
        after,
    )


def plane_others(seq, shard):
    return [(seq, flip_mask(shard, mask)) for mask in range(1, 8)]


class ColumnExchange:
    def __init__(self, weight, cols, local, send, receive):
        self.parts = (weight, cols, local, send, receive)
        self.seq, self.shard = place()
        self.width = cols.shape[2]

    def block(self, target):
        weight = self.parts[0]
        return weight.at[:, pl.ds(pl.multiple_of(target * self.width, self.width), self.width)]

    def copies(self):
        _, cols, local, send, receive = self.parts
        spot = cols.at[self.shard]
        for mask in (2, 4, 3, 5, 6, 7, 1):
            target = flip_mask(self.shard, mask)
            yield remote(
                self.block(target), spot, send.at[mask], receive.at[mask], (self.seq, target)
            )

    def start(self):
        _, cols, local, _, _ = self.parts
        self.started = list(self.copies())
        for copy in self.started:
            copy.start()
        self.own = pltpu.make_async_copy(self.block(self.shard), cols.at[self.shard], local)
        self.own.start()

    def wait(self):
        self.own.wait()
        for copy in self.started:
            copy.wait()


EXCHANGE = [DMA, DMA((8,)), DMA((8,))]


class PairExchange(ColumnExchange):
    def start(self):
        _, cols, local, send, receive = self.parts
        seq, shard = self.seq, self.shard
        self.sender = lax.rem(shard, 2) == lax.rem(seq, 2)
        copies = {
            mask: remote(
                self.block(flip_mask(shard, mask)),
                cols.at[shard],
                send.at[mask],
                receive.at[mask],
                (seq, flip_mask(shard, mask)),
            )
            for mask in range(1, 8)
        }
        copies[1].start()
        self.started = [copies[1]]
        self.sent = [copies[mask] for mask in (2, 4, 3, 5, 6, 7)]

        @pl.when(self.sender)
        def _():
            for copy in self.sent:
                copy.start()

        self.own = pltpu.make_async_copy(self.block(shard), cols.at[shard], local)
        self.own.start()

    def turn(self, bits):
        _, cols, _, send, receive = self.parts
        parity = lax.rem(lax.rem(self.shard, 2) + lax.rem(self.seq, 2), 2)
        here, there = bits + parity, bits + 1 - parity
        spot, came = cols.at[flip_by(self.shard, here)], cols.at[flip_by(self.shard, there)]
        pair = (flip(self.seq, 1), self.shard)
        arrival = remote(spot, spot, send.at[here], receive.at[here], pair)
        onward = remote(spot, spot, send.at[8 + bits // 2], receive.at[here], pair)
        swapped = remote(came, came, send.at[8 + bits // 2], receive.at[there], pair)
        return arrival, onward, swapped

    def relay(self, bits):
        arrival, onward, _ = self.turn(bits)
        arrival.wait_recv()
        onward.start()

    def wait(self):
        self.own.wait()
        for copy in self.started:
            copy.wait()

        @pl.when(self.sender)
        def _():
            for copy in self.sent:
                copy.wait_send()

        for bits in (2, 4, 6):
            _, onward, swapped = self.turn(bits)
            onward.wait_send()
            swapped.wait_recv()


PAIR_EXCHANGE = [DMA, DMA((12,)), DMA((8,))]


def columns_shape(weight):
    rows, width = weight.shape
    return jax.ShapeDtypeStruct((8, rows, width // 8), weight.dtype)


def to_tokens_kernel(
    heads, weight, tokens, cols, local, send, receive, cols_local, cols_send, cols_receive
):
    seq, shard = place()
    core, half = lax.rem(shard, 2), lax.div(seq, 2)
    base = shard - core
    width = heads.shape[2]
    group = 2 * lax.rem(seq, 2) + core
    greet(column_others(seq, shard) + plane_others(seq, shard)[1:])
    mine = tokens.at[:, pl.ds(pl.multiple_of(group * width, width), width)]
    steps = []
    for turn in range(4):
        target = lax.rem(seq + turn, 4)
        remote_copy = remote(
            heads.at[target], mine, send.at[turn], receive.at[group], (target, base + half)
        )
        if turn == 0:
            here = core == half
            own = pltpu.make_async_copy(heads.at[target], mine, local)

            @pl.when(here)
            def _():
                own.start()

            @pl.when(jnp.logical_not(here))
            def _():
                remote_copy.start()

        else:
            remote_copy.start()
        steps.append(remote_copy)
    exchange = ColumnExchange(weight, cols, cols_local, cols_send, cols_receive)
    exchange.start()
    for turn in range(4):
        if turn == 0:

            @pl.when(here)
            def _():
                own.wait()

            @pl.when(jnp.logical_not(here))
            def _():
                steps[0].wait_send()

        else:
            steps[turn].wait_send()
    for source in range(4):
        slot = tokens.at[:, source * width : (source + 1) * width]
        arrival = remote(heads.at[0], slot, send.at[0], receive.at[source], (seq, shard))

        @pl.when(jnp.logical_not(jnp.logical_and(here, group == source)))
        def _():
            arrival.wait_recv()

    exchange.wait()


def to_tokens(heads, weight, number, after=()):
    blocks, rows, width = heads.shape
    return comm_call(
        to_tokens_kernel,
        (jax.ShapeDtypeStruct((rows, 4 * width), heads.dtype), columns_shape(weight)),
        (heads, weight),
        [ANY] * 2,
        (ANY, ANY),
        [DMA, DMA((4,)), DMA((4,))] + EXCHANGE,
        "to_tokens",
        number,
        after,
    )


def to_heads_kernel(
    tokens, attended, grads, heads, out, part, *scratch
):
    local, send, receive = scratch[-3:]
    scratch = scratch[:-3]
    seq, shard = place()
    greet(column_others(seq, shard) + plane_others(seq, shard)[1:])
    core, half = lax.rem(shard, 2), lax.div(seq, 2)
    base = shard - core
    width = heads.shape[2]
    here = core == half
    mine = 2 * lax.rem(seq, 2) + core
    copies = []
    for group in range(4):
        target = (2 * core + group // 2, base + group % 2)
        source = tokens.at[:, group * width : (group + 1) * width]
        copy = remote(source, heads.at[seq], send.at[group], receive.at[seq], target)
        own = pltpu.make_async_copy(source, heads.at[seq], local)
        self_copy = jnp.logical_and(here, mine == group)

        @pl.when(self_copy)
        def _():
            own.start()

        @pl.when(jnp.logical_not(self_copy))
        def _():
            copy.start()

        copies.append((self_copy, own, copy))
    def produce(block):
        rows = out.shape[0]
        span = pl.ds(pl.multiple_of(block * rows, rows), rows)

        def tile(at):
            part[block, :, at] = dot_tn(attended[:, span], grads[:, at]).astype(jnp.bfloat16)

        tiles(grads.shape[1], tile)

    scatter_products(produce, part, out, *scratch, meet=False)
    for self_copy, own, copy in copies:

        @pl.when(self_copy)
        def _():
            own.wait()

        @pl.when(jnp.logical_not(self_copy))
        def _():
            copy.wait_send()

    for source in range(4):
        arrival = remote(
            tokens.at[:, 0:width], heads.at[source], send.at[0], receive.at[source], (seq, shard)
        )

        @pl.when(jnp.logical_not(jnp.logical_and(here, seq == source)))
        def _():
            arrival.wait_recv()


def to_heads(tokens, attended, grads, number, after=()):
    rows, width = tokens.shape
    low = tokens.dtype
    return comm_call(
        to_heads_kernel,
        (
            jax.ShapeDtypeStruct((4, rows, width // 4), low),
            jax.ShapeDtypeStruct((rows, width), jnp.float32),
        ),
        (tokens, attended, grads),
        [ANY, VM, VM],
        (ANY, VM),
        scatter_scratch(rows, width) + [DMA, DMA((4,)), DMA((4,))],
        "to_heads",
        number,
        after,
    )


def gather_plane(x, out, local, send, receive, ready, exchange=None):
    seq, shard = place()
    core = lax.rem(shard, 2)
    near = [(seq, flip(shard, bit)) for bit in (2, 4, 1)]
    greet(plane_others(seq, shard) + [(flip(seq, 1), shard)] if exchange else near)
    own = pltpu.make_async_copy(x, out.at[shard], local)
    own.start()
    firsts = [
        remote(x, out.at[shard], send.at[index], receive.at[index], device)
        for index, device in enumerate(near)
    ]
    for copy in firsts:
        copy.start()
    if exchange:
        exchange.start()
    mate = near[2]
    mate_shard = flip(shard, 1)

    def pass_on(slot, index, device):
        return remote(out.at[slot], out.at[slot], send.at[index], receive.at[index], device)

    first_bit = 2 + 2 * core
    second_bit = 4 - 2 * core
    first, second = flip_bit(shard, first_bit), flip_bit(shard, second_bit)
    diagonal = flip_mask(shard, 6)

    def arrival(slot, index):
        return remote(out.at[slot], out.at[slot], send.at[0], receive.at[index], mate)

    own.wait()
    ready(shard)
    arrival(mate_shard, 2).wait_recv()
    ready(mate_shard)
    arrival(first, core).wait_recv()
    across = pass_on(first, 3, (seq, second))
    across.start()
    one = remote(out.at[first], out.at[first], send.at[4], receive.at[4 + core], mate)
    one.start()
    arrival(second, 1 - core).wait_recv()
    two = remote(out.at[second], out.at[second], send.at[5], receive.at[5 - core], mate)
    two.start()
    ready(first)
    ready(second)
    if exchange:
        exchange.relay(2)
        exchange.relay(4)
    arrival(flip(mate_shard, 2), 4).wait_recv()
    ready(flip(mate_shard, 2))
    arrival(diagonal, 3).wait_recv()
    three = pass_on(diagonal, 6, mate)
    three.start()
    arrival(flip(mate_shard, 4), 5).wait_recv()
    ready(flip(mate_shard, 4))
    ready(diagonal)
    arrival(flip_mask(mate_shard, 6), 6).wait_recv()
    ready(flip_mask(mate_shard, 6))
    if exchange:
        exchange.relay(6)
    for copy in firsts + [across, one, two, three]:
        copy.wait_send()


class Stores:
    def __init__(self, pairs, sems):
        self.pairs, self.sems = pairs, sems

    def copies(self, slot):
        return [
            pltpu.make_async_copy(source.at[slot], target.at[slot], self.sems.at[index, slot])
            for index, (source, target) in enumerate(self.pairs)
        ]

    def start(self, slot):
        for copy in self.copies(slot):
            copy.start()

    def wait(self):
        def one(slot, carry):
            for copy in self.copies(slot):
                copy.wait()
            return carry

        lax.fori_loop(0, 8, one, 0)


TILE = 512


def tiles(width, body):
    def one(index, carry):
        body(pl.ds(pl.multiple_of(index * TILE, TILE), TILE))
        return carry

    lax.fori_loop(0, width // TILE, one, 0)


def hidden_kernel(
    x, weight, gate_cols, plane, up_cols, gate, upward, hidden,
    plane_in, up_in, gate_wide, gate_low, up_low, hidden_low, local, send, receive, store,
    up_store, cols_local, cols_send, cols_receive
):
    exchange = PairExchange(weight, up_in, cols_local, cols_send, cols_receive)
    width = gate_wide.shape[2]
    early = Stores([(plane_in, plane), (gate_low, gate)], store.at[0])
    late = Stores([(up_low, upward), (hidden_low, hidden)], store.at[1])

    def ready(slot):
        def tile(at):
            value = dot_nn(plane_in[slot], gate_cols[:, at])
            gate_wide[slot, :, at] = value
            gate_low[slot, :, at] = value.astype(jnp.bfloat16)

        tiles(width, tile)
        early.start(slot)

    gather_plane(x, plane_in, local, send, receive, ready, exchange)
    exchange.wait()
    kept = pltpu.make_async_copy(up_in, up_cols, up_store)
    kept.start()

    def last(slot, carry):
        def tile(at):
            value = dot_nn(plane_in[slot], up_in[:, :, at].reshape(-1, TILE))
            gated = gate_wide[slot, :, at]
            up_low[slot, :, at] = value.astype(jnp.bfloat16)
            hidden_low[slot, :, at] = (
                gated * (1.0 / (1.0 + jnp.exp(-gated))) * value
            ).astype(jnp.bfloat16)

        tiles(width, tile)
        late.start(slot)
        return carry

    lax.fori_loop(0, 8, last, 0)
    early.wait()
    late.wait()
    kept.wait()


def gather_hidden(x, gate_cols, weight, number, after=()):
    rows, wide = x.shape
    width = weight.shape[1] // 8
    low = x.dtype
    narrow = (8, rows, width)
    result = jax.ShapeDtypeStruct(narrow, low)
    return comm_call(
        hidden_kernel,
        (jax.ShapeDtypeStruct((8, rows, wide), low), columns_shape(weight)) + (result,) * 3,
        (x, weight, gate_cols),
        [VM, ANY, VM],
        (ANY,) * 5,
        [
            pltpu.VMEM((8, rows, wide), low),
            pltpu.VMEM(columns_shape(weight).shape, low),
            pltpu.VMEM(narrow, jnp.float32),
        ]
        + [pltpu.VMEM(narrow, low)] * 3
        + [DMA, DMA((7,)), DMA((7,)), DMA((2, 2, 8)), DMA]
        + PAIR_EXCHANGE,
        "gather_hidden",
        number,
        after,
    )


def hidden_grad_kernel(
    x, down, gate, upward, plane, gate_grad, up_grad,
    plane_in, gate_low, up_low, local, send, receive, store
):
    width = gate.shape[2]
    stores = Stores([(plane_in, plane), (gate_low, gate_grad), (up_low, up_grad)], store)

    def ready(slot):
        def tile(at):
            grad = dot_nt(plane_in[slot], down[at])
            gated = gate[slot, :, at].astype(jnp.float32)
            sigmoid = 1.0 / (1.0 + jnp.exp(-gated))
            part = grad * sigmoid
            gate_low[slot, :, at] = (
                part * upward[slot, :, at].astype(jnp.float32) * (1.0 + gated * (1.0 - sigmoid))
            ).astype(jnp.bfloat16)
            up_low[slot, :, at] = (part * gated).astype(jnp.bfloat16)

        tiles(width, tile)
        stores.start(slot)

    gather_plane(x, plane_in, local, send, receive, ready)
    stores.wait()


def gather_hidden_grad(x, down, gate, upward, number, after=()):
    rows, wide = x.shape
    low = x.dtype
    narrow = gate.shape
    result = jax.ShapeDtypeStruct(narrow, low)
    return comm_call(
        hidden_grad_kernel,
        (jax.ShapeDtypeStruct((8, rows, wide), low), result, result),
        (x, down, gate, upward),
        [VM] * 4,
        (ANY,) * 3,
        [pltpu.VMEM((8, rows, wide), low)]
        + [pltpu.VMEM(narrow, low)] * 2
        + [DMA, DMA((7,)), DMA((7,)), DMA((3, 8))],
        "gather_hidden_grad",
        number,
        after,
    )


def flip_bit(value, bit):
    return value + bit - 2 * bit * lax.rem(lax.div(value, bit), 2)


PIECES = 2


def add_rows(rows, body):
    step = 32

    def one(index, carry):
        body(pl.ds(pl.multiple_of(index * step, step), step))
        return carry

    lax.fori_loop(0, rows // step, one, 0)


def scatter_products(
    produce, part, out, mated, first_in, second_in, sums, sem_s, sem_r, meet=True
):
    seq, shard = place()
    core, chip = lax.rem(shard, 2), lax.div(shard, 2)
    rows = out.shape[0] // PIECES
    mate = (seq, flip(shard, 1))
    bit = 1 + core
    first, second = flip_bit(chip, bit), flip_bit(chip, 3 - bit)
    diagonal = 3 - chip
    first_device, second_device = (seq, 2 * first + core), (seq, 2 * second + core)
    if meet:
        greet([mate, first_device, second_device])

    def piece(index):
        return pl.ds(index * rows, rows)

    order, mate_order = (diagonal, first, second, chip), (diagonal, second, first, chip)
    swaps = {}

    def make(slot):
        target = mate_order[slot]
        produce(2 * target + 1 - core)
        for index in range(PIECES):
            copy = remote(
                part.at[2 * target + 1 - core, piece(index)],
                mated.at[target, piece(index)],
                sem_s.at[0, slot, index],
                sem_r.at[0, target, index],
                mate,
            )
            copy.start()
            swaps[slot, index] = copy
        produce(2 * order[slot] + core)

    make(0)
    make(1)

    def came(target, index):
        remote(
            part.at[0, piece(index)],
            mated.at[target, piece(index)],
            sem_s.at[0, 0, index],
            sem_r.at[0, target, index],
            mate,
        ).wait_recv()

    sends = []
    for index in range(PIECES):
        for slot, target in ((0, diagonal), (1, first)):
            came(target, index)

            def add(span, slot=slot, target=target, index=index):
                span = pl.ds(span.start + index * rows, span.size)
                sums[slot, span] = (
                    part[2 * target + core, span].astype(jnp.float32)
                    + mated[target, span].astype(jnp.float32)
                ).astype(jnp.bfloat16)

            add_rows(rows, add)
            copy = remote(
                sums.at[slot, piece(index)],
                first_in.at[slot, piece(index)],
                sem_s.at[1, slot, index],
                sem_r.at[1, slot, index],
                first_device,
            )
            copy.start()
            sends.append(copy)
    make(2)
    make(3)
    finals = []
    for index in range(PIECES):
        came(second, index)
        sends[2 * index].wait_recv()

        def add(span, index=index):
            span = pl.ds(span.start + index * rows, span.size)
            sums[2, span] = (
                part[2 * second + core, span].astype(jnp.float32)
                + mated[second, span].astype(jnp.float32)
                + first_in[0, span].astype(jnp.float32)
            ).astype(jnp.bfloat16)

        add_rows(rows, add)
        copy = remote(
            sums.at[2, piece(index)],
            second_in.at[piece(index)],
            sem_s.at[2, 0, index],
            sem_r.at[2, 0, index],
            second_device,
        )
        copy.start()
        finals.append(copy)
    for index in range(PIECES):
        came(chip, index)
        sends[2 * index + 1].wait_recv()
        finals[index].wait_recv()

        def add(span, index=index):
            span = pl.ds(span.start + index * rows, span.size)
            out[span] = (
                part[shard, span].astype(jnp.float32) + mated[chip, span].astype(jnp.float32)
            ) + (first_in[1, span].astype(jnp.float32) + second_in[span].astype(jnp.float32))

        add_rows(rows, add)
    for copy in list(swaps.values()) + sends + finals:
        copy.wait_send()


def out_scatter_kernel(hidden, down, out, part, *scratch):
    def produce(block):
        def tile(at):
            part[block, :, at] = dot_nn(hidden[block], down[:, at]).astype(jnp.bfloat16)

        tiles(down.shape[1], tile)

    scatter_products(produce, part, out, *scratch)


def back_scatter_kernel(gate_grad, up_grad, gate_cols, up_cols, out, part, *scratch):
    def produce(block):
        def tile(at):
            part[block, :, at] = (
                dot_nt(gate_grad[block], gate_cols[at]) + dot_nt(up_grad[block], up_cols[at])
            ).astype(jnp.bfloat16)

        tiles(gate_cols.shape[0], tile)

    scatter_products(produce, part, out, *scratch)


def scatter_scratch(rows, width):
    low = jnp.bfloat16
    return [
        pltpu.VMEM((8, rows, width), low),
        pltpu.VMEM((4, rows, width), low),
        pltpu.VMEM((2, rows, width), low),
        pltpu.VMEM((rows, width), low),
        pltpu.VMEM((3, rows, width), low),
        DMA((3, 4, PIECES)),
        DMA((3, 4, PIECES)),
    ]


def plane_scatter(kernel, inputs, rows, width, name, number, after=()):
    return comm_call(
        kernel,
        jax.ShapeDtypeStruct((rows, width), jnp.float32),
        inputs,
        [VM] * len(inputs),
        VM,
        scatter_scratch(rows, width),
        name,
        number,
        after,
    )


LINE_ROWS = 128
RING = 4
CLOSE_LAG = 2
TAKE_LAG = 5


def flip_by(value, mask):
    for bit in (1, 2, 4):
        here, there = lax.rem(lax.div(value, bit), 2), lax.rem(lax.div(mask, bit), 2)
        value = value + bit * (lax.rem(here + there, 2) - here)
    return value


class LineSums:
    def __init__(self, gate, up, late, gate_rows, up_rows, out, landed, scratch):
        self.gate, self.up, self.late = gate, up, late
        self.rows_out, self.out = (gate_rows, up_rows), out
        self.first_in, self.second_in, self.total_in = landed
        (
            self.own, self.sums, self.others, self.totals,
            self.own_sem, self.load_sem, self.keep_sem, self.send, self.receive,
            self.spread_send, self.spread_receive,
        ) = scratch
        self.seq, self.shard = place()
        self.inner = jnp.logical_or(self.seq == 1, self.seq == 2)
        self.outer = jnp.logical_not(self.inner)
        self.beside = (self.seq + 1 - 2 * lax.rem(self.seq, 2), self.shard)
        self.across = (3 - self.seq, self.shard)
        self.rows, self.width = gate_rows.shape[0], gate.shape[1]
        self.cuts = self.rows // LINE_ROWS
        self.early = 8 * self.cuts
        self.count = self.early + len(late)
        self.away = 7 * self.cuts
        self.halves = (slice(0, self.width), slice(self.width, 2 * self.width))

    def is_late(self, index):
        return isinstance(index, int) and index >= self.early

    def owner(self, index):
        return flip_by(self.shard, 7 - lax.div(index, self.cuts))

    def sources(self, index):
        if self.is_late(index):
            return [(self.late[index - self.early], slice(0, 2 * self.width))]
        start = self.owner(index) * self.rows + lax.rem(index, self.cuts) * LINE_ROWS
        span = pl.ds(pl.multiple_of(start, LINE_ROWS), LINE_ROWS)
        return list(zip((self.gate.at[span], self.up.at[span]), self.halves))

    def inward(self, index):
        return [
            remote(
                source,
                self.first_in.at[index, :, half],
                self.send.at[side, index],
                self.receive.at[side, index],
                self.beside,
            )
            for side, (source, half) in enumerate(self.sources(index))
        ]

    def swap(self, index):
        return remote(
            self.sums.at[lax.rem(index, RING)],
            self.second_in.at[index],
            self.send.at[2, index],
            self.receive.at[2, index],
            self.across,
        )

    def result(self, index):
        if self.is_late(index):
            start = (index - self.early) * LINE_ROWS
            return self.out.at[start : start + LINE_ROWS]
        return self.total_in.at[index]

    def outward(self, index):
        return remote(
            self.totals.at[lax.rem(index, RING)],
            self.result(index),
            self.send.at[3, index],
            self.receive.at[3, index],
            self.beside,
        )

    def keep(self, index):
        return pltpu.make_async_copy(
            self.totals.at[lax.rem(index, RING)], self.result(index), self.keep_sem.at[index]
        )

    def own_loads(self, index):
        slot = lax.rem(index, 2)
        return [
            pltpu.make_async_copy(
                source, self.own.at[slot, :, half], self.own_sem.at[slot, side]
            )
            for side, (source, half) in enumerate(self.sources(index))
        ]

    def spread(self, index, side, source, away):
        down = pl.ds(
            pl.multiple_of(lax.rem(index, self.cuts) * LINE_ROWS, LINE_ROWS), LINE_ROWS
        )
        along = pl.ds(pl.multiple_of(self.shard * self.width, self.width), self.width)
        source = source.at[:, self.halves[side]]
        spot = self.rows_out[side].at[down, along]
        if not away:
            return pltpu.make_async_copy(source, spot, self.spread_send.at[side, index])
        return remote(
            source,
            spot,
            self.spread_send.at[side, index],
            self.spread_receive.at[side, index],
            (self.seq, self.owner(index)),
        )

    def spread_each(self, index, source, there, here):
        for side in range(2):

            @pl.when(index < self.away)
            def _():
                there(self.spread(index, side, source, True))

            @pl.when(index >= self.away)
            def _():
                here(self.spread(index, side, source, False))

    def spread_start(self, index, source):
        self.spread_each(index, source, lambda copy: copy.start(), lambda copy: copy.start())

    def spread_sent(self, index, source):
        self.spread_each(index, source, lambda copy: copy.wait_send(), lambda copy: copy.wait())

    def add_up(self, target, first, second):
        def add(at):
            target[at] = (
                first[at].astype(jnp.float32) + second[at].astype(jnp.float32)
            ).astype(jnp.bfloat16)

        add_rows(LINE_ROWS, add)

    def begin(self):
        @pl.when(self.outer)
        def _():
            for copy in self.inward(0):
                copy.start()

        @pl.when(self.inner)
        def _():
            for copy in self.own_loads(0):
                copy.start()

    def retire(self, index):
        self.outward(index).wait_send()
        if self.is_late(index):
            self.keep(index).wait()
        else:
            self.spread_sent(index, self.totals.at[lax.rem(index, RING)])

    def close(self, index):
        slot = lax.rem(index, RING)
        self.swap(index).wait_recv()
        load = pltpu.make_async_copy(
            self.second_in.at[index], self.others, self.load_sem.at[1]
        )
        load.start()
        if isinstance(index, int):
            self.retire(index - RING)
        else:

            @pl.when(index >= RING)
            def _():
                self.retire(index - RING)

        load.wait()
        self.add_up(self.totals.at[slot], self.sums.at[slot], self.others)
        self.outward(index).start()
        if self.is_late(index):
            self.keep(index).start()
        else:
            self.spread_start(index, self.totals.at[slot])

    def inner_step(self, index, following):
        slot = lax.rem(index, RING)
        if following:
            for copy in self.own_loads(index + 1):
                copy.start()
        for copy in self.inward(index):
            copy.wait_recv()
        if isinstance(index, int):
            self.swap(index - RING).wait_send()
        else:

            @pl.when(index >= RING)
            def _():
                self.swap(index - RING).wait_send()

        load = pltpu.make_async_copy(
            self.first_in.at[index], self.sums.at[slot], self.load_sem.at[0]
        )
        load.start()
        for copy in self.own_loads(index):
            copy.wait()
        load.wait()
        self.add_up(self.sums.at[slot], self.sums.at[slot], self.own.at[lax.rem(index, 2)])
        self.swap(index).start()
        if isinstance(index, int):
            self.close(index - CLOSE_LAG)
        else:

            @pl.when(index >= CLOSE_LAG)
            def _():
                self.close(index - CLOSE_LAG)

    def outer_take(self, index):
        self.outward(index).wait_recv()
        if not self.is_late(index):
            self.spread_start(index, self.total_in.at[index])

    def outer_step(self, index, following):
        if following:
            for copy in self.inward(index + 1):
                copy.start()
        if isinstance(index, int):
            self.outer_take(index - TAKE_LAG)
        else:

            @pl.when(index >= TAKE_LAG)
            def _():
                self.outer_take(index - TAKE_LAG)

    def step(self, index, following=True):
        @pl.when(self.inner)
        def _():
            self.inner_step(index, following)

        @pl.when(self.outer)
        def _():
            self.outer_step(index, following)

    def run(self, start, stop):
        def one(index, carry):
            self.step(index)
            return carry

        lax.fori_loop(start, min(stop, self.early - 1), one, 0)

    def finish(self):
        early, count = self.early, self.count
        for index in range(early - 1, count):
            self.step(index, index + 1 < count)

        @pl.when(self.inner)
        def _():
            for index in range(count - CLOSE_LAG, count):
                self.close(index)
            for index in range(count - RING, count):
                self.swap(index).wait_send()
                self.retire(index)

        def each(body):
            def one(index, carry):
                body(index)
                return carry

            lax.fori_loop(0, early, one, 0)

        @pl.when(self.outer)
        def _():
            for index in range(count - TAKE_LAG, count):
                self.outer_take(index)

            def sent(index):
                for copy in self.inward(index):
                    copy.wait_send()
                self.spread_sent(index, self.total_in.at[index])

            each(sent)
            for index in range(early, count):
                for copy in self.inward(index):
                    copy.wait_send()

        def received(index):
            for side in range(2):

                @pl.when(index < self.away)
                def _():
                    self.spread(index, side, self.total_in.at[index], True).wait_recv()

        each(received)


class HeadLoads:
    def __init__(self, sources, log_total, raw, low, logs, wide, sems):
        self.sources, self.log_total, self.raw = sources, log_total, raw
        self.low, self.logs, self.wide, self.sems = low, logs, wide, sems
        self.size = low.shape[3]

    def raws(self, head):
        slot, size = lax.rem(head, 2), self.size
        heads = self.raw.shape[1] // (3 * size)
        return [
            pltpu.make_async_copy(
                self.raw.at[:, pl.ds(pl.multiple_of((part * heads + head) * size, size), size)],
                self.wide.at[slot, part],
                self.sems.at[slot, 5 + part],
            )
            for part in range(2)
        ]

    def lows(self, head):
        slot, size = lax.rem(head, 2), self.size
        at = pl.ds(pl.multiple_of(head * size, size), size)
        copies = [
            pltpu.make_async_copy(
                source.at[:, at], self.low.at[slot, index], self.sems.at[slot, index]
            )
            for index, source in enumerate(self.sources)
        ]
        return copies + [
            pltpu.make_async_copy(
                self.log_total.at[head], self.logs.at[slot], self.sems.at[slot, 4]
            )
        ]


def exact_nt(a, b):
    return lax.dot_general(
        a, b, (((1,), (1,)), ((), ())), preferred_element_type=jnp.float32,
        precision=lax.Precision.HIGHEST,
    )


def exact_tn(a, b):
    return lax.dot_general(
        a, b, (((0,), (0,)), ((), ())), preferred_element_type=jnp.float32,
        precision=lax.Precision.HIGHEST,
    )


def finish_kernel(
    queries, keys, values, head_grad, log_total, raw, weight, cosine, signed, q_factor, k_factor,
    q_gain, k_gain, token_gains, whole, gate, up, out_grad,
    out, gains, gate_rows, up_rows, line_out, first_chunks, second_chunks, total_chunks,
    low, logs, wide, q_turned, k_turned, k_sum, v_sum, joined, stat, stat_in, gain, gain_in,
    part, grads, placed,
    mated, relayed, landed, first_in, second_in, swapped,
    head_sem, weight_sem, stat_s, stat_r, gain_s, gain_r,
    local, sem_s, sem_r, relay_r, grad_s, grad_r, *line_scratch
):
    seq, shard = place()
    core, half, quarter = lax.rem(shard, 2), lax.div(seq, 2), lax.rem(seq, 2)
    chip = lax.div(shard, 2)
    base = shard - core
    group = 2 * quarter + core
    rows = out.shape[0] // 2
    mate = (seq, flip(shard, 1))
    bit = 1 + core
    first, second, diagonal = flip_bit(chip, bit), flip_bit(chip, 3 - bit), 3 - chip
    first_device, second_device = (seq, 2 * first + core), (seq, 2 * second + core)
    greet(column_others(seq, shard) + plane_others(seq, shard)[1:])
    late = [
        out_grad.at[start : start + LINE_ROWS] for start in range(0, out_grad.shape[0], LINE_ROWS)
    ] + [
        placed.at[index, start : start + LINE_ROWS]
        for index in range(3)
        for start in range(0, placed.shape[1], LINE_ROWS)
    ]
    line = LineSums(
        gate, up, late, gate_rows, up_rows, line_out,
        (first_chunks, second_chunks, total_chunks), line_scratch,
    )
    line.begin()

    length, size = cosine.shape
    heads = q_gain.shape[1] // size
    loads = HeadLoads(
        (queries, keys, values, head_grad), log_total, raw, low, logs, wide, head_sem
    )
    for copy in loads.lows(0) + loads.raws(0):
        copy.start()
    blocks = grads.shape[1]
    weight_loads = [
        pltpu.make_async_copy(
            weight.at[index * blocks : (index + 1) * blocks], grads.at[index],
            weight_sem.at[index],
        )
        for index in range(4)
    ]
    for copy in weight_loads:
        copy.start()
    stat[...] = jnp.zeros_like(stat)
    gain[...] = jnp.zeros_like(gain)
    gain[2:4] = token_gains[...]
    ones = jnp.ones((8, size), jnp.float32)

    def columns(head):
        return pl.ds(pl.multiple_of(head * size, size), size)

    def back(head, carry):
        slot, at = lax.rem(head, 2), columns(head)
        for copy in loads.lows(head):
            copy.wait()

        @pl.when(head + 1 < heads)
        def _():
            for copy in loads.lows(head + 1) + loads.raws(head + 1):
                copy.start()

        attend_back_kernel(
            low.at[slot, 0], low.at[slot, 1], low.at[slot, 2], low.at[slot, 3],
            logs.at[pl.ds(slot, 1)], cosine, signed,
            q_turned.at[:, at], k_turned.at[:, at],
            joined.at[:, columns(2 * heads + head)],
            k_sum, v_sum,
        )
        for copy in loads.raws(head):
            copy.wait()
        for index, (turned, factor, gain_part) in enumerate(
            ((q_turned, q_factor, q_gain), (k_turned, k_factor, k_gain))
        ):
            along = turned[:, at].astype(jnp.float32) * wide[slot, index]
            stat[8 * index : 8 * index + 8] += exact_nt(ones, along * gain_part[:, at])
            spot = pl.multiple_of(group * heads * size + head * size, size)
            gain[index : index + 1, pl.ds(spot, size)] = jnp.sum(
                along * factor[...], axis=0, keepdims=True
            )

        @pl.when(lax.rem(head, 2) == 1)
        def _():
            line.step(lax.div(head, 2))

        return carry

    lax.fori_loop(0, heads, back, 0)
    partners = [mate, (flip(seq, 1), shard), (flip(seq, 1), flip(shard, 1))]
    stat_copies = [
        remote(stat, stat_in.at[index], stat_s.at[index], stat_r.at[index], partner)
        for index, partner in enumerate(partners)
    ]
    for copy in stat_copies:
        copy.start()
    own_gain = pltpu.make_async_copy(gain, gain_in.at[shard], gain_s.at[0])
    own_gain.start()
    gain_copies = [
        remote(
            gain, gain_in.at[shard], gain_s.at[mask], gain_r.at[mask],
            (seq, flip_mask(shard, mask)),
        )
        for mask in range(1, 8)
    ]
    for copy in gain_copies:
        copy.start()
    for copy in loads.raws(0):
        copy.start()
    line.run(heads // 2, heads // 2 + 1)
    for copy in stat_copies:
        copy.wait()
    stat[...] = (stat[...] + stat_in[0]) + (stat_in[1] + stat_in[2])
    spreading = jnp.full((8, size), 0.125 / whole.shape[1], jnp.float32)

    def norm_back(head, carry):
        slot, at = lax.rem(head, 2), columns(head)
        for copy in loads.raws(head):
            copy.wait()

        @pl.when(head + 1 < heads)
        def _():
            for copy in loads.raws(head + 1):
                copy.start()

        for index, (turned, factor, gain_part) in enumerate(
            ((q_turned, q_factor, q_gain), (k_turned, k_factor, k_gain))
        ):
            inner = exact_tn(stat[8 * index : 8 * index + 8], spreading)
            scale = factor[...]
            joined[:, columns(index * heads + head)] = (
                scale * (turned[:, at].astype(jnp.float32) * gain_part[:, at])
                - wide[slot, index] * (scale * scale * scale * inner)
            ).astype(jnp.bfloat16)
        return carry

    lax.fori_loop(0, heads, norm_back, 0)
    line.run(heads // 2 + 1, heads // 2 + 2)

    mine = pl.ds(pl.multiple_of(core * rows, rows), rows)
    other = pl.ds(pl.multiple_of((1 - core) * rows, rows), rows)
    here = core == half
    order = [2 * (1 - half), 2 * (1 - half) + 1, flip(seq, 1), seq]
    long = grads.shape[1] // 2

    def project(target):
        span = pl.ds(pl.multiple_of(target * 2 * long, 2 * long), 2 * long)

        def tile(at):
            grads[target, :, at] = dot_tn(whole[:, span], joined[:, at]).astype(jnp.bfloat16)

        tiles(grads.shape[2], tile)

    for copy in weight_loads:
        copy.wait()
    swaps = []
    for slot, block in enumerate(order):
        tokens = pl.ds(pl.multiple_of(block * 2 * rows, 2 * rows), 2 * rows)

        def tile(index, carry, block=block, tokens=tokens):
            at = pl.ds(pl.multiple_of(index * blocks, blocks), blocks)
            part[block, :, at] = dot_nt(joined[tokens], grads[index]).astype(jnp.bfloat16)
            return carry

        lax.fori_loop(0, 4, tile, 0)
        copy = remote(
            part.at[block, other], mated.at[slot], sem_s.at[0, slot], sem_r.at[0, slot], mate
        )
        copy.start()
        swaps.append(copy)
    firsts = []
    for slot, target in ((0, diagonal), (1, first)):
        project(target)
        for index in range(2):
            span = slice(index * long, (index + 1) * long)
            copy = remote(
                grads.at[target, span],
                first_in.at[slot, span],
                grad_s.at[slot, index],
                grad_r.at[slot, index],
                first_device,
            )
            copy.start()
            firsts.append(copy)
    line.run(4, 5)
    project(second)
    project(chip)
    own_gain.wait()
    for copy in gain_copies:
        copy.wait()
    plane_gain = gain_in[0]
    for index in range(1, 8):
        plane_gain = plane_gain + gain_in[index]
    gain[...] = plane_gain
    own_gain = pltpu.make_async_copy(gain, gain_in.at[8 + seq], gain_s.at[8])
    own_gain.start()
    gain_copies = [
        remote(
            gain, gain_in.at[8 + seq], gain_s.at[8 + step], gain_r.at[7 + step],
            (lax.rem(seq + step, 4), shard),
        )
        for step in (1, 2, 3)
    ]
    for copy in gain_copies:
        copy.start()
    placed[...] = jnp.zeros_like(placed)

    near = quarter + half == 1
    far = jnp.logical_not(near)
    sends = []

    def to_target(slot, block):
        return remote(
            mated.at[slot],
            landed.at[quarter, core],
            sem_s.at[1, slot],
            sem_r.at[1, 2 * quarter + core],
            (block, base + half),
        )

    def to_near(slot):
        return remote(
            mated.at[slot], relayed.at[slot], sem_s.at[1, slot], relay_r.at[slot],
            (flip(seq, 1), shard),
        )

    for slot, block in enumerate(order):
        swaps[slot].wait_recv()

        def add(span, slot=slot, block=block):
            source = pl.ds(pl.multiple_of(span.start + core * rows, 32), span.size)
            mated[slot, span] = (
                part[block, source].astype(jnp.float32) + mated[slot, span].astype(jnp.float32)
            ).astype(jnp.bfloat16)

        add_rows(rows, add)
        copy = to_target(slot, block)
        if slot < 2:

            @pl.when(far)
            def _():
                to_near(slot).start()

        elif slot == 2:
            copy.start()
        else:
            own = pltpu.make_async_copy(mated.at[slot], landed.at[quarter, core], local)

            @pl.when(here)
            def _():
                own.start()

            @pl.when(jnp.logical_not(here))
            def _():
                copy.start()

        sends.append(copy)

    @pl.when(near)
    def _():
        for slot in range(2):
            to_near(slot).wait_recv()

            def add(span, slot=slot):
                mated[slot, span] = (
                    mated[slot, span].astype(jnp.float32)
                    + relayed[slot, span].astype(jnp.float32)
                ).astype(jnp.bfloat16)

            add_rows(rows, add)
            sends[slot].start()

    line.run(5, 7)

    seconds = []
    for index in range(2):
        firsts[index].wait_recv()

        def add(span, index=index):
            span = pl.ds(span.start + index * long, span.size)
            first_in[0, span] = (
                grads[second, span].astype(jnp.float32) + first_in[0, span].astype(jnp.float32)
            ).astype(jnp.bfloat16)

        add_rows(long, add)
        span = slice(index * long, (index + 1) * long)
        copy = remote(
            first_in.at[0, span], second_in.at[span], grad_s.at[2, index], grad_r.at[2, index],
            second_device,
        )
        copy.start()
        seconds.append(copy)
    line.run(7, 10)
    for turn in range(2):
        start = pl.multiple_of((1 - core if turn == 0 else core) * long, long)
        if turn == 0:
            for copy in (firsts[2], firsts[3], seconds[0], seconds[1]):
                copy.wait_recv()

        def add(span, start=start):
            span = pl.ds(pl.multiple_of(span.start + start, 32), span.size)
            first_in[1, span] = (
                (grads[chip, span].astype(jnp.float32) + first_in[1, span].astype(jnp.float32))
                + second_in[span].astype(jnp.float32)
            ).astype(jnp.bfloat16)

        add_rows(long, add)
        if turn == 0:
            swap = remote(
                first_in.at[1, pl.ds(start, long)], swapped, grad_s.at[3, 0], grad_r.at[3, 0], mate
            )
            swap.start()
    part_width = out.shape[1] // 4
    own_rows = pl.ds(pl.multiple_of(core * long, long), long)
    for index in range(3):
        spot = pl.multiple_of(group * part_width, part_width)
        placed[index, :, pl.ds(spot, part_width)] = first_in[
            1, own_rows, index * part_width : (index + 1) * part_width
        ]
    swap.wait_recv()
    for index in range(3):
        spot = pl.multiple_of((2 * quarter + 1 - core) * part_width, part_width)
        placed[index, :, pl.ds(spot, part_width)] = swapped[
            :, index * part_width : (index + 1) * part_width
        ]
    line.run(10, 12)

    for slot in range(2):

        @pl.when(near)
        def _():
            sends[slot].wait_send()

        @pl.when(far)
        def _():
            to_near(slot).wait_send()

    sends[2].wait_send()

    @pl.when(here)
    def _():
        own.wait()

    @pl.when(jnp.logical_not(here))
    def _():
        sends[3].wait_send()

    for source in range(4):
        arrival = remote(
            mated.at[0],
            landed.at[source // 2, source % 2],
            sem_s.at[1, 0],
            sem_r.at[1, source],
            mate,
        )
        expected = jnp.where(here, 2 * quarter + core != source, source // 2 == 1 - core)

        @pl.when(expected)
        def _():
            arrival.wait_recv()

    for side in range(2):

        def add_both(span, side=side):
            target = pl.ds(span.start + side * rows, span.size)
            out[target] = landed[0, side, span].astype(jnp.float32) + landed[
                1, side, span
            ].astype(jnp.float32)

        def take_one(span, side=side):
            target = pl.ds(span.start + side * rows, span.size)
            out[target] = landed[1 - core, side, span].astype(jnp.float32)

        @pl.when(here)
        def _():
            add_rows(rows, add_both)

        @pl.when(jnp.logical_not(here))
        def _():
            add_rows(rows, take_one)

    for copy in swaps + firsts + seconds + [swap]:
        copy.wait_send()
    own_gain.wait()
    for copy in gain_copies:
        copy.wait()
    gains[...] = (gain_in[8] + gain_in[9]) + (gain_in[10] + gain_in[11])
    line.run(12, line.early)
    line.finish()


def finish(
    heads_in, log_total, raw, weight, tables, factors, head_gains, token_gains, whole, gate, up,
    out_grad, number, after=()
):
    length, width = whole.shape
    rows, long, wide = length // 4, weight.shape[0] // 4, weight.shape[1]
    size, group_width = tables[0].shape[1], wide // 3
    low = whole.dtype
    hidden_width = gate.shape[1]
    tail = out_grad.shape[0] + 3 * long // 2
    early, late = gate.shape[0] // LINE_ROWS, tail // LINE_ROWS
    count = early + late
    block = (LINE_ROWS, 2 * hidden_width)
    owned = jax.ShapeDtypeStruct((gate.shape[0] // 8, 8 * hidden_width), low)
    chunks = jax.ShapeDtypeStruct((count,) + block, low)
    results = comm_call(
        finish_kernel,
        (
            jax.ShapeDtypeStruct((rows, width), jnp.float32),
            jax.ShapeDtypeStruct((8, width), jnp.float32),
            owned,
            owned,
            jax.ShapeDtypeStruct((tail, width), low),
            chunks,
            chunks,
            chunks,
        ),
        (*heads_in, log_total, raw, weight, *tables, *factors, *head_gains, token_gains)
        + (whole, gate, up, out_grad),
        [ANY] * 7 + [VM] * 8 + [ANY] * 3,
        (VM, VM) + (ANY,) * 6,
        [
            pltpu.VMEM((2, 4, length, size), low),
            pltpu.VMEM((2, length, 1), jnp.float32),
            pltpu.VMEM((2, 2, length, size), jnp.float32),
            pltpu.VMEM((length, group_width), low),
            pltpu.VMEM((length, group_width), low),
            pltpu.VMEM((length, size), jnp.float32),
            pltpu.VMEM((length, size), jnp.float32),
            pltpu.VMEM((length, wide), low),
            pltpu.VMEM((16, length), jnp.float32),
            pltpu.VMEM((3, 16, length), jnp.float32),
            pltpu.VMEM((8, width), jnp.float32),
            pltpu.VMEM((12, 8, width), jnp.float32),
            pltpu.VMEM((4, rows, width), low),
            pltpu.VMEM((4, long, wide), low),
            pltpu.VMEM((3, long // 2, width), low),
            pltpu.VMEM((4, rows // 2, width), low),
            pltpu.VMEM((2, rows // 2, width), low),
            pltpu.VMEM((2, 2, rows // 2, width), low),
            pltpu.VMEM((2, long, wide), low),
            pltpu.VMEM((long, wide), low),
            pltpu.VMEM((long // 2, wide), low),
            DMA((2, 7)),
            DMA((4,)),
            DMA((3,)),
            DMA((3,)),
            DMA((12,)),
            DMA((11,)),
            DMA,
            DMA((2, 4)),
            DMA((2, 4)),
            DMA((2,)),
            DMA((4, 2)),
            DMA((4, 2)),
            pltpu.VMEM((2,) + block, low),
            pltpu.VMEM((RING,) + block, low),
            pltpu.VMEM(block, low),
            pltpu.VMEM((RING,) + block, low),
            DMA((2, 2)),
            DMA((2,)),
            DMA((count,)),
            DMA((4, count)),
            DMA((4, count)),
            DMA((2, early)),
            DMA((2, early)),
        ],
        "finish",
        number,
        after,
    )
    return results[:5]


def turn_heads(values, cosine, signed):
    middle = values.shape[-1] // 2
    return values * cosine + jnp.concatenate(
        [values[:, middle:], values[:, :middle]], axis=1
    ) * signed


def dot_nt(a, b):
    return lax.dot_general(a, b, (((1,), (1,)), ((), ())), preferred_element_type=jnp.float32)


def dot_tn(a, b):
    return lax.dot_general(a, b, (((0,), (0,)), ((), ())), preferred_element_type=jnp.float32)


def dot_nn(a, b):
    return jnp.dot(a, b, preferred_element_type=jnp.float32)


ATTENTION_ROWS = 256


def causal(scores, start):
    query = start + lax.broadcasted_iota(jnp.int32, scores.shape, 0)
    key = lax.broadcasted_iota(jnp.int32, scores.shape, 1)
    return jnp.where(key <= query, scores, masked_value)


def attend_kernel(
    q_raw, k_raw, v_raw, q_factor, k_factor, q_gain, k_gain, cosine, signed,
    q_out, k_out, v_out, attended, log_total
):
    length, size = q_raw.shape
    scale = size ** (-0.5)
    cos, sin = cosine[...], signed[...]
    q_out[...] = turn_heads(
        q_raw[...] * q_factor[...] * q_gain[...], cos, sin
    ).astype(jnp.bfloat16)
    k_out[...] = turn_heads(
        k_raw[...] * k_factor[...] * k_gain[...], cos, sin
    ).astype(jnp.bfloat16)
    v_out[...] = v_raw[...].astype(jnp.bfloat16)
    rows = min(ATTENTION_ROWS, length)
    for start in range(0, length, rows):
        stop = start + rows
        scores = dot_nt(q_out[start:stop], k_out[:stop]) * scale
        scores = causal(scores, start)
        maximum = jnp.max(scores, axis=-1, keepdims=True)
        exponent = jnp.exp(scores - maximum)
        total = jnp.sum(exponent, axis=-1, keepdims=True)
        weights = (exponent * (1.0 / total)).astype(jnp.bfloat16)
        attended[start:stop] = dot_nn(weights, v_out[:stop]).astype(jnp.bfloat16)
        log_total[0, start:stop] = maximum + jnp.log(total)


def attend(raw, q_factor, k_factor, q_gain, k_gain, cosine, signed, size, after=()):
    length, width = raw.shape[0], raw.shape[1] // 3
    heads = width // size
    by_head = pl.BlockSpec((length, size), lambda h: (0, h))
    parts = [
        pl.BlockSpec((length, size), lambda h, start=index * heads: (0, start + h))
        for index in range(3)
    ]
    fixed = pl.BlockSpec((length, size), lambda h: (0, 0))
    factor = pl.BlockSpec((length, 1), lambda h: (0, 0))
    gain = pl.BlockSpec((1, size), lambda h: (0, h))
    low = jax.ShapeDtypeStruct((length, width), jnp.bfloat16)
    flops = heads * length * length * size * 2
    inputs = (raw, raw, raw, q_factor, k_factor, q_gain, k_gain, cosine, signed)
    return pl.pallas_call(
        ordered(attend_kernel, inputs, after),
        grid=(heads,),
        out_shape=(low, low, low, low, jax.ShapeDtypeStruct((heads, length, 1), jnp.float32)),
        in_specs=parts + [factor] * 2 + [gain] * 2 + [fixed] * 2 + [ANY] * len(after),
        out_specs=[by_head] * 4 + [pl.BlockSpec((1, length, 1), lambda h: (h, 0, 0))],
        name="attend",
        compiler_params=pltpu.CompilerParams(vmem_limit_bytes=VMEM_LIMIT),
        cost_estimate=pl.CostEstimate(
            flops=flops, bytes_accessed=20 * length * width, transcendentals=flops // (4 * size)
        ),
    )(*inputs, *after)


def attend_back_kernel(
    queries, keys, values, grads, log_total, cosine, signed, q_grad, k_grad, v_grad, k_sum, v_sum
):
    length, size = queries.shape
    scale = size ** (-0.5)
    rows = min(ATTENTION_ROWS, length)
    k_sum[...] = jnp.zeros_like(k_sum)
    v_sum[...] = jnp.zeros_like(v_sum)
    for start in range(0, length, rows):
        stop = start + rows
        query, grad = queries[start:stop], grads[start:stop]
        scores = causal(dot_nt(query, keys[:stop]) * scale, start)
        weights = jnp.exp(scores - log_total[0, start:stop])
        v_sum[:stop] += dot_tn(weights.astype(jnp.bfloat16), grad)
        weight_grad = dot_nt(grad, values[:stop])
        inner = jnp.sum(weights * weight_grad, axis=-1, keepdims=True)
        score_grad = (weights * (weight_grad - inner)).astype(jnp.bfloat16)
        q_low = (dot_nn(score_grad, keys[:stop]) * scale).astype(jnp.bfloat16)
        q_grad[start:stop] = turn_heads(
            q_low.astype(jnp.float32), cosine[start:stop], -signed[start:stop]
        ).astype(q_grad.dtype)
        k_sum[:stop] += dot_tn(score_grad, query)
    k_low = (k_sum[...] * scale).astype(jnp.bfloat16)
    k_grad[...] = turn_heads(k_low.astype(jnp.float32), cosine[...], -signed[...]).astype(
        k_grad.dtype
    )
    v_grad[...] = v_sum[...].astype(jnp.bfloat16)


def split_layer(
    block_input, query_weight, key_weight, value_weight, out_weight, gate_weight, up_weight,
    down_weight, query_gain, key_gain, attention_gain, swiglu_gain, cotangent
):
    tokens, width = block_input.shape[1:]
    head_size = width // HEADS
    seq, shard = lax.axis_index("seq"), lax.axis_index("fsdp")
    core, chip = lax.rem(shard, 2), lax.div(shard, 2)
    half, quarter = lax.div(seq, 2), lax.rem(seq, 2)
    rows = query_weight.shape[0]
    hidden_width = gate_weight.shape[1] // 8
    group_width = width // 4
    group = 2 * quarter + core
    length = 4 * tokens
    low = jnp.bfloat16
    sequence = block_input.reshape(tokens, width)

    whole, qkv, out_rows = entry(
        sequence, query_weight, key_weight, value_weight, out_weight, 1
    )
    whole = whole.reshape(length, width)
    out_full = lax.all_gather(out_rows, "fsdp", axis=0, tiled=True)
    raw = dot_nn(whole, qkv)
    q_raw, k_raw = raw[:, :group_width], raw[:, group_width : 2 * group_width]

    def reduced(first, second, number, after=()):
        part = jnp.stack([first, second]).reshape(2 * length // 128, 128)
        total = stats_sum(part, number, after).reshape(2, length, 1)
        return total[0] / width, total[1] / width

    q_mean, k_mean = reduced(
        jnp.sum(q_raw * q_raw, axis=-1), jnp.sum(k_raw * k_raw, axis=-1), 2
    )
    q_factor, k_factor = lax.rsqrt(q_mean + epsilon), lax.rsqrt(k_mean + epsilon)
    cosine, sine = rotary_tables(length, 0, head_size)
    cosine = jnp.concatenate([cosine[:, 0], cosine[:, 0]], axis=1)
    signed = jnp.concatenate([-sine[:, 0], sine[:, 0]], axis=1)
    q_gain_part = lax.dynamic_slice_in_dim(query_gain, group * group_width, group_width)[None]
    k_gain_part = lax.dynamic_slice_in_dim(key_gain, group * group_width, group_width)[None]
    queries, keys, values, attended_heads, log_total = attend(
        raw, q_factor, k_factor, q_gain_part, k_gain_part, cosine, signed, head_size
    )
    attended, gate_cols = to_tokens(
        attended_heads.reshape(4, tokens, group_width), gate_weight, 3
    )
    gate_cols = gate_cols.reshape(width, hidden_width)
    branch = dot_nn(attended, out_full)
    branch_factor = norm_factor(branch)
    residual = sequence.astype(jnp.float32) + branch * branch_factor * attention_gain

    plane, up_cols, gate, upward, hidden = gather_hidden(
        residual.astype(low), gate_cols, up_weight, 4
    )
    plane, up_cols = plane.reshape(8 * tokens, width), up_cols.reshape(width, hidden_width)
    mixed_out = plane_scatter(
        out_scatter_kernel, (hidden, down_weight), tokens, width, "out_scatter", 5
    )
    mixed_factor = norm_factor(mixed_out)
    output = residual + mixed_out * mixed_factor * swiglu_gain
    upstream = cotangent.reshape(tokens, width).astype(jnp.float32)
    mixed_float, swiglu_gain_grad = norm_backward(mixed_out, mixed_factor, swiglu_gain, upstream)
    mixed_plane, gate_grad, up_grad = gather_hidden_grad(
        mixed_float.astype(low), down_weight, gate, upward, 6
    )
    mixed_plane = mixed_plane.reshape(8 * tokens, width)
    down_grad = transposed_times(
        hidden.reshape(8 * tokens, hidden_width), mixed_plane
    ).astype(low)
    down_sum = lax.psum(down_grad, "seq")
    gate_sum = transposed_times(plane, gate_grad.reshape(8 * tokens, hidden_width)).astype(low)
    up_sum = transposed_times(plane, up_grad.reshape(8 * tokens, hidden_width)).astype(low)

    residual_grad = upstream + plane_scatter(
        back_scatter_kernel,
        (gate_grad, up_grad, gate_cols, up_cols),
        tokens,
        width,
        "back_scatter",
        7,
        (gate_sum, up_sum),
    )

    branch_float, attention_gain_grad = norm_backward(
        branch, branch_factor, attention_gain, residual_grad
    )
    branch_grad = branch_float.astype(low)
    attended_grad = times_transposed(branch_grad, out_full).astype(low)
    head_grad, out_grad = to_heads(attended_grad, attended, branch_grad, 8)
    head_grad, out_grad = head_grad.reshape(length, group_width), out_grad.astype(low)
    input_sum, gain_totals, gate_rows, up_rows, late = finish(
        (queries, keys, values, head_grad),
        log_total,
        raw,
        qkv,
        (cosine, signed),
        (q_factor, k_factor),
        (q_gain_part, k_gain_part),
        jnp.stack([attention_gain_grad, swiglu_gain_grad]),
        whole,
        gate_sum,
        up_sum,
        out_grad,
        10,
        (down_sum,),
    )
    input_grad = residual_grad + input_sum

    down_total = down_sum.astype(jnp.float32)
    gate_total, up_total = gate_rows.astype(jnp.float32), up_rows.astype(jnp.float32)
    out_total, query_total, key_total, value_total = (
        late[index * rows : (index + 1) * rows].astype(jnp.float32) for index in range(4)
    )

    return (
        output.reshape(1, tokens, width),
        input_grad.reshape(1, tokens, width),
        query_total,
        key_total,
        value_total,
        out_total,
        gate_total,
        up_total,
        down_total,
        gain_totals[0],
        gain_totals[1],
        gain_totals[2],
        gain_totals[3],
    )


def fits(mesh):
    return mesh.shape["seq"] == 4 and mesh.shape["fsdp"] == 8


def solution(mesh):
    placed = (
        P("fsdp", "seq", None),
        P("fsdp", None),
        P("fsdp", None),
        P("fsdp", None),
        P("fsdp", None),
        P("fsdp", None),
        P("fsdp", None),
        P("fsdp", None),
        P(),
        P(),
        P(),
        P(),
        P("fsdp", "seq", None),
    )
    return jax.shard_map(
        split_layer if fits(mesh) else local,
        mesh=mesh,
        in_specs=placed,
        out_specs=(
            P("fsdp", "seq", None),
            P("fsdp", "seq", None),
            P("fsdp", None),
            P("fsdp", None),
            P("fsdp", None),
            P("fsdp", None),
            P("fsdp", None),
            P("fsdp", None),
            P("fsdp", None),
            P(),
            P(),
            P(),
            P(),
        ),
        check_vma=False,
    )
```

```python
import jax
import jax.numpy as jnp
from jax import lax
from jax.experimental import pallas as pl
from jax.experimental.pallas import tpu as pltpu
from jax.sharding import PartitionSpec as P

HEADS = 16


epsilon = 1e-06
rotary_base = 500000.0
masked_value = -1e30


def norm_factor(values):
    return lax.rsqrt(jnp.mean(values * values, axis=-1, keepdims=True) + epsilon)


def norm_backward(values, factor, gain_vector, upstream):
    scaled = upstream * gain_vector
    inner_mean = jnp.mean(scaled * values, axis=-1, keepdims=True)
    value_grad = factor * scaled - values * factor * factor * factor * inner_mean
    gain_grad = jnp.sum(upstream * values * factor, axis=0)
    return (value_grad, gain_grad)


def rotary_tables(count, offset, head_size):
    positions = (offset + jnp.arange(count, dtype=jnp.int32)).astype(jnp.float32)
    middle = head_size // 2
    frequency = rotary_base ** (-2.0 * jnp.arange(middle, dtype=jnp.float32) / head_size)
    angles = positions[:, None] * frequency[None, :]
    return (jnp.cos(angles)[:, None, :], jnp.sin(angles)[:, None, :])


def rotate(values, cosine, sine_table, direction_sign):
    middle = values.shape[-1] // 2
    leading = values[..., :middle]
    trailing = values[..., middle:]
    signed = sine_table * direction_sign
    return jnp.concatenate(
        [leading * cosine - trailing * signed, trailing * cosine + leading * signed], axis=-1
    )


def times_transposed(operand, matrix):
    return lax.dot_general(
        operand, matrix, (((1,), (1,)), ((), ())), preferred_element_type=jnp.float32
    )


def transposed_times(operand, matrix):
    return lax.dot_general(
        operand, matrix, (((0,), (0,)), ((), ())), preferred_element_type=jnp.float32
    )


def masked_scores(query_block, keys, row_start, block_rows, score_scale):
    length = keys.shape[0]
    scores = (
        jnp.einsum("qhd,khd->hqk", query_block, keys, preferred_element_type=jnp.float32)
        * score_scale
    )
    query_positions = row_start + jnp.arange(block_rows, dtype=jnp.int32)
    key_positions = jnp.arange(length, dtype=jnp.int32)
    allowed = key_positions[None, :] <= query_positions[:, None]
    return jnp.where(allowed[None], scores, masked_value)


def attention_forward(queries, keys, values):
    length = queries.shape[0]
    block_rows = min(512, length)
    blocks = length // block_rows
    score_scale = queries.shape[-1] ** (-0.5)

    def one_block(block_index):
        row_start = block_index * block_rows
        query_block = lax.dynamic_slice_in_dim(queries, row_start, block_rows, 0)
        scores = masked_scores(query_block, keys, row_start, block_rows, score_scale)
        maximum = jnp.max(scores, axis=-1, keepdims=True)
        exponent = jnp.exp(scores - maximum)
        row_total = jnp.sum(exponent, axis=-1, keepdims=True)
        log_total = maximum[..., 0] + jnp.log(row_total[..., 0])
        weights_low = (exponent / row_total).astype(jnp.bfloat16)
        attended = jnp.einsum(
            "hqk,khd->qhd", weights_low, values, preferred_element_type=jnp.float32
        )
        return (attended.astype(jnp.bfloat16), log_total)

    attended, log_total = lax.map(one_block, jnp.arange(blocks, dtype=jnp.int32))
    return (attended.reshape(length, -1), log_total)


def attention_backward(queries, keys, values, attended_grad, log_total):
    length = queries.shape[0]
    block_rows = min(512, length)
    blocks = length // block_rows
    score_scale = queries.shape[-1] ** (-0.5)
    empty = jnp.zeros(keys.shape, jnp.float32)

    def one_block(carried, operands):
        key_sum, value_sum = carried
        block_index, block_total = operands
        row_start = block_index * block_rows
        query_block = lax.dynamic_slice_in_dim(queries, row_start, block_rows, 0)
        grad_block = lax.dynamic_slice_in_dim(attended_grad, row_start, block_rows, 0)
        scores = masked_scores(query_block, keys, row_start, block_rows, score_scale)
        probabilities = jnp.exp(scores - block_total[..., None])
        weights_low = probabilities.astype(jnp.bfloat16)
        value_sum = value_sum + jnp.einsum(
            "hqk,qhd->khd", weights_low, grad_block, preferred_element_type=jnp.float32
        )
        probability_grad = jnp.einsum(
            "qhd,khd->hqk", grad_block, values, preferred_element_type=jnp.float32
        )
        inner_sum = jnp.sum(probabilities * probability_grad, axis=-1, keepdims=True)
        score_grad = (probabilities * (probability_grad - inner_sum)).astype(jnp.bfloat16)
        query_grad = (
            jnp.einsum("hqk,khd->qhd", score_grad, keys, preferred_element_type=jnp.float32)
            * score_scale
        )
        key_sum = (
            key_sum
            + jnp.einsum(
                "hqk,qhd->khd", score_grad, query_block, preferred_element_type=jnp.float32
            )
            * score_scale
        )
        return ((key_sum, value_sum), query_grad.astype(jnp.bfloat16))

    (key_sum, value_sum), query_grads = lax.scan(
        one_block, (empty, empty), (jnp.arange(blocks, dtype=jnp.int32), log_total)
    )
    return (
        query_grads.reshape(keys.shape),
        key_sum.astype(jnp.bfloat16),
        value_sum.astype(jnp.bfloat16),
    )


def local(
    block_input,
    query_weight,
    key_weight,
    value_weight,
    out_weight,
    gate_weight,
    up_weight,
    down_weight,
    query_gain,
    key_gain,
    attention_gain,
    swiglu_gain,
    cotangent,
):
    tokens = block_input.shape[1]
    model_width = block_input.shape[2]
    head_size = model_width // HEADS
    groups = lax.axis_size("seq")
    local_heads = HEADS // groups
    sequence = block_input.reshape(tokens, model_width)
    query_full, key_full, value_full, out_full = (
        lax.all_gather(query_weight, "fsdp", axis=0, tiled=True),
        lax.all_gather(key_weight, "fsdp", axis=0, tiled=True),
        lax.all_gather(value_weight, "fsdp", axis=0, tiled=True),
        lax.all_gather(out_weight, "fsdp", axis=0, tiled=True),
    )
    query_raw = jnp.dot(sequence, query_full, preferred_element_type=jnp.float32)
    key_raw = jnp.dot(sequence, key_full, preferred_element_type=jnp.float32)
    value_raw = jnp.dot(sequence, value_full, preferred_element_type=jnp.float32)
    query_factor = norm_factor(query_raw)
    key_factor = norm_factor(key_raw)
    cosine, sine_table = rotary_tables(tokens, lax.axis_index("seq") * tokens, head_size)
    query_rot = rotate(
        (query_raw * query_factor * query_gain).reshape(tokens, HEADS, head_size),
        cosine,
        sine_table,
        1.0,
    )
    key_rot = rotate(
        (key_raw * key_factor * key_gain).reshape(tokens, HEADS, head_size), cosine, sine_table, 1.0
    )
    stacked = jnp.stack(
        [
            query_rot.reshape(tokens, model_width).astype(jnp.bfloat16),
            key_rot.reshape(tokens, model_width).astype(jnp.bfloat16),
            value_raw.astype(jnp.bfloat16),
        ]
    )
    grouped = lax.all_to_all(stacked, "seq", split_axis=2, concat_axis=1, tiled=True)
    length = grouped.shape[1]
    head_queries = grouped[0].reshape(length, local_heads, head_size)
    head_keys = grouped[1].reshape(length, local_heads, head_size)
    head_values = grouped[2].reshape(length, local_heads, head_size)
    attended_heads, log_total = attention_forward(head_queries, head_keys, head_values)
    attended = lax.all_to_all(attended_heads, "seq", split_axis=0, concat_axis=1, tiled=True)
    branch = jnp.dot(attended, out_full, preferred_element_type=jnp.float32)
    branch_factor = norm_factor(branch)
    residual = sequence.astype(jnp.float32) + branch * branch_factor * attention_gain
    residual_low = residual.astype(jnp.bfloat16)
    gate_full, up_full, down_full = (
        lax.all_gather(gate_weight, "fsdp", axis=0, tiled=True),
        lax.all_gather(up_weight, "fsdp", axis=0, tiled=True),
        lax.all_gather(down_weight, "fsdp", axis=0, tiled=True),
    )
    gate_value = jnp.dot(residual_low, gate_full, preferred_element_type=jnp.float32)
    upward = jnp.dot(residual_low, up_full, preferred_element_type=jnp.float32)
    sigmoid_gate = jax.nn.sigmoid(gate_value)
    activated = gate_value * sigmoid_gate
    hidden = (activated * upward).astype(jnp.bfloat16)
    mixed_out = jnp.dot(hidden, down_full, preferred_element_type=jnp.float32)
    mixed_factor = norm_factor(mixed_out)
    output = residual + mixed_out * mixed_factor * swiglu_gain
    upstream = cotangent.reshape(tokens, model_width).astype(jnp.float32)
    mixed_float, swiglu_gain_grad = norm_backward(mixed_out, mixed_factor, swiglu_gain, upstream)
    mixed_grad = mixed_float.astype(jnp.bfloat16)
    gate_back, up_back, down_back = (
        lax.all_gather(gate_weight, "fsdp", axis=0, tiled=True),
        lax.all_gather(up_weight, "fsdp", axis=0, tiled=True),
        lax.all_gather(down_weight, "fsdp", axis=0, tiled=True),
    )
    hidden_grad = times_transposed(mixed_grad, down_back)
    gate_grad = (
        hidden_grad * upward * sigmoid_gate * (1.0 + gate_value * (1.0 - sigmoid_gate))
    ).astype(jnp.bfloat16)
    up_grad = (hidden_grad * activated).astype(jnp.bfloat16)
    residual_grad = (
        upstream + times_transposed(gate_grad, gate_back) + times_transposed(up_grad, up_back)
    )
    joined = jnp.concatenate([gate_grad, up_grad], axis=1)
    branch_float, attention_gain_grad = norm_backward(
        branch, branch_factor, attention_gain, residual_grad
    )
    branch_grad = branch_float.astype(jnp.bfloat16)
    query_back, key_back, value_back, out_back = (
        lax.all_gather(query_weight, "fsdp", axis=0, tiled=True),
        lax.all_gather(key_weight, "fsdp", axis=0, tiled=True),
        lax.all_gather(value_weight, "fsdp", axis=0, tiled=True),
        lax.all_gather(out_weight, "fsdp", axis=0, tiled=True),
    )
    attended_grad = times_transposed(branch_grad, out_back).astype(jnp.bfloat16)
    head_grad = lax.all_to_all(attended_grad, "seq", split_axis=1, concat_axis=0, tiled=True)
    query_grads, key_grads, value_grads = attention_backward(
        head_queries,
        head_keys,
        head_values,
        head_grad.reshape(length, local_heads, head_size),
        log_total,
    )
    back_stack = jnp.stack([query_grads, key_grads, value_grads]).reshape(
        3, length, local_heads * head_size
    )
    token_grads = lax.all_to_all(back_stack, "seq", split_axis=1, concat_axis=2, tiled=True)
    query_norm_grad = rotate(
        token_grads[0].astype(jnp.float32).reshape(tokens, HEADS, head_size),
        cosine,
        sine_table,
        -1.0,
    )
    key_norm_grad = rotate(
        token_grads[1].astype(jnp.float32).reshape(tokens, HEADS, head_size),
        cosine,
        sine_table,
        -1.0,
    )
    query_float, query_gain_grad = norm_backward(
        query_raw, query_factor, query_gain, query_norm_grad.reshape(tokens, model_width)
    )
    key_float, key_gain_grad = norm_backward(
        key_raw, key_factor, key_gain, key_norm_grad.reshape(tokens, model_width)
    )
    query_raw_grad = query_float.astype(jnp.bfloat16)
    key_raw_grad = key_float.astype(jnp.bfloat16)
    value_tokens = token_grads[2]
    input_grad = (
        residual_grad
        + times_transposed(query_raw_grad, query_back)
        + times_transposed(key_raw_grad, key_back)
        + times_transposed(value_tokens, value_back)
    )
    projected = jnp.concatenate([query_raw_grad, key_raw_grad, value_tokens], axis=1)
    hidden_width = gate_weight.shape[1]
    columns = hidden
    down_shard = lax.psum_scatter(
        transposed_times(columns, mixed_grad).astype(jnp.bfloat16),
        "fsdp",
        scatter_dimension=0,
        tiled=True,
    )
    columns = residual_low
    gate_up_shard = lax.psum_scatter(
        transposed_times(columns, joined).astype(jnp.bfloat16),
        "fsdp",
        scatter_dimension=0,
        tiled=True,
    )
    attention_shard = lax.psum_scatter(
        jnp.concatenate(
            [transposed_times(sequence, projected), transposed_times(attended, branch_grad)], axis=1
        ).astype(jnp.bfloat16),
        "fsdp",
        scatter_dimension=0,
        tiled=True,
    )
    attention_total, gate_up_total, down_total = (
        lax.psum(attention_shard, "seq").astype(jnp.float32),
        lax.psum(gate_up_shard, "seq").astype(jnp.float32),
        lax.psum(down_shard, "seq").astype(jnp.float32),
    )
    gain_totals = lax.psum(
        jnp.stack([query_gain_grad, key_gain_grad, attention_gain_grad, swiglu_gain_grad]),
        ("seq", "fsdp"),
    )
    return (
        output.reshape(1, tokens, model_width),
        input_grad.reshape(1, tokens, model_width),
        attention_total[:, :model_width],
        attention_total[:, model_width : 2 * model_width],
        attention_total[:, 2 * model_width : 3 * model_width],
        attention_total[:, 3 * model_width :],
        gate_up_total[:, :hidden_width],
        gate_up_total[:, hidden_width:],
        down_total,
        gain_totals[0],
        gain_totals[1],
        gain_totals[2],
        gain_totals[3],
    )


MESH = pl.DeviceIdType.MESH
ANY = pl.BlockSpec(memory_space=pl.ANY)
VM = pl.BlockSpec(memory_space=pltpu.VMEM)
DMA = pltpu.SemaphoreType.DMA
VMEM_LIMIT = 60 * 1024 * 1024


def flip(value, bit):
    return value + bit - 2 * bit * lax.rem(lax.div(value, bit), 2)


def flip_mask(value, mask):
    for bit in (1, 2, 4):
        if mask & bit:
            value = flip(value, bit)
    return value


def place():
    seq, shard = lax.axis_index("seq"), lax.axis_index("fsdp")
    return seq, shard


def greet(targets):
    barrier = pltpu.get_barrier_semaphore()
    for target in targets:
        pl.semaphore_signal(barrier, inc=1, device_id=target, device_id_type=MESH)
    pl.semaphore_wait(barrier, len(targets))


def remote(source, target_ref, send, receive, device):
    return pltpu.make_async_remote_copy(
        src_ref=source,
        dst_ref=target_ref,
        send_sem=send,
        recv_sem=receive,
        device_id=device,
        device_id_type=MESH,
    )


def column_others(seq, shard):
    mate = flip(shard, 1)
    others = [(lax.rem(seq + step, 4), shard) for step in (1, 2, 3)]
    return others + [(lax.rem(seq + step, 4), mate) for step in (0, 1, 2, 3)]


def ordered(kernel, inputs, after):
    count, extra = len(inputs), len(after)
    return lambda *refs: kernel(*refs[:count], *refs[count + extra :])


def comm_call(kernel, out_shape, inputs, in_specs, out_specs, scratch, name, number, after=()):
    return pl.pallas_call(
        ordered(kernel, inputs, after),
        out_shape=out_shape,
        in_specs=list(in_specs) + [ANY] * len(after),
        out_specs=out_specs,
        scratch_shapes=scratch,
        name=name,
        compiler_params=pltpu.CompilerParams(
            collective_id=number, has_side_effects=True, vmem_limit_bytes=VMEM_LIMIT
        ),
        cost_estimate=pl.CostEstimate(flops=1, bytes_accessed=1, transcendentals=0),
    )(*inputs, *after)


def entry_kernel(
    x, wq, wk, wv, out_weight, xo, wo, out_kept,
    local, x_send, x_recv, fwd_send, w_send, w_recv
):
    seq, shard = place()
    core, half = lax.rem(shard, 2), lax.div(seq, 2)
    quarter = lax.rem(seq, 2)
    rows, width = wq.shape[0], wo.shape[1] // 3
    weights = (wq, wk, wv)
    greet(
        [(seq, flip_mask(shard, mask)) for mask in range(1, 8)]
        + [(lax.rem(seq + step, 4), shard) for step in (1, 2, 3)]
    )
    mine = pl.ds(pl.multiple_of(shard * rows, rows), rows)

    def columns(index):
        return slice(index * width, (index + 1) * width)

    def block(index, target):
        group = 2 * quarter + lax.rem(target, 2)
        return weights[index].at[:, pl.ds(pl.multiple_of(group * width, width), width)]

    near = 1 + core
    x_copies = []
    for which in (0, 1):
        target = 2 * core + which
        wanted = jnp.logical_and(
            target != seq, jnp.logical_or(core == half, target == near)
        )
        copy = remote(x, xo.at[seq], x_send.at[which], x_recv.at[seq], (target, shard))

        @pl.when(wanted)
        def _():
            copy.start()

        @pl.when(target == seq)
        def _():
            pltpu.make_async_copy(x, xo.at[seq], local.at[3]).start()

        x_copies.append((wanted, copy))
    kept = pltpu.make_async_copy(out_weight, out_kept, local.at[4])
    kept.start()
    copies = []
    for index in range(3):
        for mask in (2, 4, 3, 5, 1):
            target = flip_mask(shard, mask)
            copy = remote(
                block(index, target),
                wo.at[mine, columns(index)],
                w_send.at[index, mask - 1],
                w_recv.at[index, mask - 1],
                (seq, target),
            )
            copy.start()
            copies.append(copy)
    own = [
        pltpu.make_async_copy(block(index, shard), wo.at[mine, columns(index)], local.at[index])
        for index in range(3)
    ]
    for copy in own:
        copy.start()

    mate = (seq, flip(shard, 1))
    relays = []
    places = (seq, flip(seq, 1), 2 * (1 - half) + half, 2 * (1 - half) + 1 - half)

    def pass_input(turn):
        source = places[turn]
        forward = remote(
            xo.at[source], xo.at[source], fwd_send.at[turn], x_recv.at[source], mate
        )
        if turn > 1:
            relay = remote(
                xo.at[source], xo.at[source], fwd_send.at[turn + 2], x_recv.at[source],
                (flip(seq, 1), shard),
            )
            relays.append(relay)

        @pl.when(core == half)
        def _():
            if turn == 0:
                pltpu.make_async_copy(x, xo.at[seq], local.at[3]).wait()
            else:
                forward.wait_recv()
            if turn > 1:

                @pl.when(seq == near)
                def _():
                    relay.start()

            forward.start()

    def arrival(index, origin, mask):
        spot = wo.at[pl.ds(pl.multiple_of(origin * rows, rows), rows), columns(index)]
        return remote(spot, spot, w_send.at[index, 0], w_recv.at[index, mask - 1], mate)

    base = shard - core
    side, above = flip(base, 2), flip(base, 4)
    onward = []
    for index in range(3):
        pass_input(index)
        for origin, mask, slot, target in (
            (side, 2 + core, 6 + core, flip(shard, 4)),
            (above + 1, 5 - core, 7 - core, flip(shard, 2)),
        ):
            arrival(index, origin, mask).wait_recv()
            spot = wo.at[pl.ds(pl.multiple_of(origin * rows, rows), rows), columns(index)]
            copy = remote(
                spot,
                spot,
                w_send.at[index, 5 + len(onward) % 2],
                w_recv.at[index, slot - 1],
                (seq, target),
            )
            copy.start()
            onward.append(copy)
    pass_input(3)
    for relay in relays:

        @pl.when(jnp.logical_and(core == half, seq == near))
        def _():
            relay.wait_send()

    for turn, source in enumerate(places):
        forward = remote(
            xo.at[source], xo.at[source], fwd_send.at[turn], x_recv.at[source], mate
        )

        @pl.when(core == half)
        def _():
            forward.wait_send()

        @pl.when(core != half)
        def _():
            forward.wait_recv()

    kept.wait()
    for wanted, copy in x_copies:

        @pl.when(wanted)
        def _():
            copy.wait_send()

    for copy in own:
        copy.wait()
    for copy in copies + onward:
        copy.wait_send()
    far = flip_mask(base, 6)
    for index in range(3):
        arrival(index, flip(shard, 1), 1).wait_recv()
        arrival(index, side + 1, 3 - core).wait_recv()
        arrival(index, above, 4 + core).wait_recv()
        arrival(index, far, 6 + core).wait_recv()
        arrival(index, far + 1, 7 - core).wait_recv()


def entry(x, wq, wk, wv, out_weight, number):
    rows, width = wq.shape
    group = width // 4
    return comm_call(
        entry_kernel,
        (
            jax.ShapeDtypeStruct((4,) + x.shape, x.dtype),
            jax.ShapeDtypeStruct((8 * rows, 3 * group), wq.dtype),
            jax.ShapeDtypeStruct(out_weight.shape, out_weight.dtype),
        ),
        (x, wq, wk, wv, out_weight),
        [VM] * 5,
        (ANY,) * 3,
        [DMA((5,)), DMA((2,)), DMA((4,)), DMA((6,)), DMA((3, 7)), DMA((3, 7))],
        "entry",
        number,
    )


def stats_kernel(part, total, held, send, receive):
    seq, shard = place()
    partners = [
        (seq, flip(shard, 1)),
        (flip(seq, 1), shard),
        (flip(seq, 1), flip(shard, 1)),
    ]
    greet(partners)
    copies = [
        remote(part, held.at[index], send.at[index], receive.at[index], partner)
        for index, partner in enumerate(partners)
    ]
    for copy in copies:
        copy.start()
    for copy in copies:
        copy.wait()
    total[...] = (part[...] + held[0]) + (held[1] + held[2])


def stats_sum(part, number, after=()):
    return comm_call(
        stats_kernel,
        jax.ShapeDtypeStruct(part.shape, part.dtype),
        (part,),
        [VM],
        VM,
        [pltpu.VMEM((3,) + part.shape, part.dtype), DMA((3,)), DMA((3,))],
        "stats",
        number,
        after,
    )


def plane_others(seq, shard):
    return [(seq, flip_mask(shard, mask)) for mask in range(1, 8)]


class ColumnExchange:
    def __init__(self, weight, cols, local, send, receive):
        self.parts = (weight, cols, local, send, receive)
        self.seq, self.shard = place()
        self.width = cols.shape[2]

    def block(self, target):
        weight = self.parts[0]
        return weight.at[:, pl.ds(pl.multiple_of(target * self.width, self.width), self.width)]

    def copies(self):
        _, cols, local, send, receive = self.parts
        spot = cols.at[self.shard]
        for mask in (2, 4, 3, 5, 6, 7, 1):
            target = flip_mask(self.shard, mask)
            yield remote(
                self.block(target), spot, send.at[mask], receive.at[mask], (self.seq, target)
            )

    def start(self):
        _, cols, local, _, _ = self.parts
        self.started = list(self.copies())
        for copy in self.started:
            copy.start()
        self.own = pltpu.make_async_copy(self.block(self.shard), cols.at[self.shard], local)
        self.own.start()

    def wait(self):
        self.own.wait()
        for copy in self.started:
            copy.wait()


EXCHANGE = [DMA, DMA((8,)), DMA((8,))]


class PairExchange(ColumnExchange):
    def start(self):
        _, cols, local, send, receive = self.parts
        seq, shard = self.seq, self.shard
        self.sender = lax.rem(shard, 2) == lax.rem(seq, 2)
        copies = {
            mask: remote(
                self.block(flip_mask(shard, mask)),
                cols.at[shard],
                send.at[mask],
                receive.at[mask],
                (seq, flip_mask(shard, mask)),
            )
            for mask in range(1, 8)
        }
        copies[1].start()
        self.started = [copies[1]]
        self.sent = [copies[mask] for mask in (2, 4, 3, 5, 6, 7)]

        @pl.when(self.sender)
        def _():
            for copy in self.sent:
                copy.start()

        self.own = pltpu.make_async_copy(self.block(shard), cols.at[shard], local)
        self.own.start()

    def turn(self, bits):
        _, cols, _, send, receive = self.parts
        parity = lax.rem(lax.rem(self.shard, 2) + lax.rem(self.seq, 2), 2)
        here, there = bits + parity, bits + 1 - parity
        spot, came = cols.at[flip_by(self.shard, here)], cols.at[flip_by(self.shard, there)]
        pair = (flip(self.seq, 1), self.shard)
        arrival = remote(spot, spot, send.at[here], receive.at[here], pair)
        onward = remote(spot, spot, send.at[8 + bits // 2], receive.at[here], pair)
        swapped = remote(came, came, send.at[8 + bits // 2], receive.at[there], pair)
        return arrival, onward, swapped

    def relay(self, bits):
        arrival, onward, _ = self.turn(bits)
        arrival.wait_recv()
        onward.start()

    def wait(self):
        self.own.wait()
        for copy in self.started:
            copy.wait()

        @pl.when(self.sender)
        def _():
            for copy in self.sent:
                copy.wait_send()

        for bits in (2, 4, 6):
            _, onward, swapped = self.turn(bits)
            onward.wait_send()
            swapped.wait_recv()


PAIR_EXCHANGE = [DMA, DMA((12,)), DMA((8,))]


def columns_shape(weight):
    rows, width = weight.shape
    return jax.ShapeDtypeStruct((8, rows, width // 8), weight.dtype)


def to_tokens_kernel(
    heads, weight, tokens, cols, local, send, receive, cols_local, cols_send, cols_receive
):
    seq, shard = place()
    core, half = lax.rem(shard, 2), lax.div(seq, 2)
    base = shard - core
    width = heads.shape[2]
    group = 2 * lax.rem(seq, 2) + core
    greet(column_others(seq, shard) + plane_others(seq, shard)[1:])
    mine = tokens.at[:, pl.ds(pl.multiple_of(group * width, width), width)]
    steps = []
    for turn in range(4):
        target = lax.rem(seq + turn, 4)
        remote_copy = remote(
            heads.at[target], mine, send.at[turn], receive.at[group], (target, base + half)
        )
        if turn == 0:
            here = core == half
            own = pltpu.make_async_copy(heads.at[target], mine, local)

            @pl.when(here)
            def _():
                own.start()

            @pl.when(jnp.logical_not(here))
            def _():
                remote_copy.start()

        else:
            remote_copy.start()
        steps.append(remote_copy)
    exchange = ColumnExchange(weight, cols, cols_local, cols_send, cols_receive)
    exchange.start()
    for turn in range(4):
        if turn == 0:

            @pl.when(here)
            def _():
                own.wait()

            @pl.when(jnp.logical_not(here))
            def _():
                steps[0].wait_send()

        else:
            steps[turn].wait_send()
    for source in range(4):
        slot = tokens.at[:, source * width : (source + 1) * width]
        arrival = remote(heads.at[0], slot, send.at[0], receive.at[source], (seq, shard))

        @pl.when(jnp.logical_not(jnp.logical_and(here, group == source)))
        def _():
            arrival.wait_recv()

    exchange.wait()


def to_tokens(heads, weight, number, after=()):
    blocks, rows, width = heads.shape
    return comm_call(
        to_tokens_kernel,
        (jax.ShapeDtypeStruct((rows, 4 * width), heads.dtype), columns_shape(weight)),
        (heads, weight),
        [ANY] * 2,
        (ANY, ANY),
        [DMA, DMA((4,)), DMA((4,))] + EXCHANGE,
        "to_tokens",
        number,
        after,
    )


def to_heads_kernel(
    tokens, attended, grads, heads, out, part, *scratch
):
    local, send, receive = scratch[-3:]
    scratch = scratch[:-3]
    seq, shard = place()
    greet(column_others(seq, shard) + plane_others(seq, shard)[1:])
    core, half = lax.rem(shard, 2), lax.div(seq, 2)
    base = shard - core
    width = heads.shape[2]
    here = core == half
    mine = 2 * lax.rem(seq, 2) + core
    copies = []
    for group in range(4):
        target = (2 * core + group // 2, base + group % 2)
        source = tokens.at[:, group * width : (group + 1) * width]
        copy = remote(source, heads.at[seq], send.at[group], receive.at[seq], target)
        own = pltpu.make_async_copy(source, heads.at[seq], local)
        self_copy = jnp.logical_and(here, mine == group)

        @pl.when(self_copy)
        def _():
            own.start()

        @pl.when(jnp.logical_not(self_copy))
        def _():
            copy.start()

        copies.append((self_copy, own, copy))
    def produce(block):
        rows = out.shape[0]
        span = pl.ds(pl.multiple_of(block * rows, rows), rows)

        def tile(at):
            part[block, :, at] = dot_tn(attended[:, span], grads[:, at]).astype(jnp.bfloat16)

        tiles(grads.shape[1], tile)

    scatter_products(produce, part, out, *scratch, meet=False)
    for self_copy, own, copy in copies:

        @pl.when(self_copy)
        def _():
            own.wait()

        @pl.when(jnp.logical_not(self_copy))
        def _():
            copy.wait_send()

    for source in range(4):
        arrival = remote(
            tokens.at[:, 0:width], heads.at[source], send.at[0], receive.at[source], (seq, shard)
        )

        @pl.when(jnp.logical_not(jnp.logical_and(here, seq == source)))
        def _():
            arrival.wait_recv()


def to_heads(tokens, attended, grads, number, after=()):
    rows, width = tokens.shape
    low = tokens.dtype
    return comm_call(
        to_heads_kernel,
        (
            jax.ShapeDtypeStruct((4, rows, width // 4), low),
            jax.ShapeDtypeStruct((rows, width), jnp.float32),
        ),
        (tokens, attended, grads),
        [ANY, VM, VM],
        (ANY, VM),
        scatter_scratch(rows, width) + [DMA, DMA((4,)), DMA((4,))],
        "to_heads",
        number,
        after,
    )


def gather_plane(x, out, local, send, receive, ready, exchange=None):
    seq, shard = place()
    core = lax.rem(shard, 2)
    near = [(seq, flip(shard, bit)) for bit in (2, 4, 1)]
    greet(plane_others(seq, shard) + [(flip(seq, 1), shard)] if exchange else near)
    own = pltpu.make_async_copy(x, out.at[shard], local)
    own.start()
    firsts = [
        remote(x, out.at[shard], send.at[index], receive.at[index], device)
        for index, device in enumerate(near)
    ]
    for copy in firsts:
        copy.start()
    if exchange:
        exchange.start()
    mate = near[2]
    mate_shard = flip(shard, 1)

    def pass_on(slot, index, device):
        return remote(out.at[slot], out.at[slot], send.at[index], receive.at[index], device)

    first_bit = 2 + 2 * core
    second_bit = 4 - 2 * core
    first, second = flip_bit(shard, first_bit), flip_bit(shard, second_bit)
    diagonal = flip_mask(shard, 6)

    def arrival(slot, index):
        return remote(out.at[slot], out.at[slot], send.at[0], receive.at[index], mate)

    own.wait()
    ready(shard)
    arrival(mate_shard, 2).wait_recv()
    ready(mate_shard)
    arrival(first, core).wait_recv()
    across = pass_on(first, 3, (seq, second))
    across.start()
    one = remote(out.at[first], out.at[first], send.at[4], receive.at[4 + core], mate)
    one.start()
    arrival(second, 1 - core).wait_recv()
    two = remote(out.at[second], out.at[second], send.at[5], receive.at[5 - core], mate)
    two.start()
    ready(first)
    ready(second)
    if exchange:
        exchange.relay(2)
        exchange.relay(4)
    arrival(flip(mate_shard, 2), 4).wait_recv()
    ready(flip(mate_shard, 2))
    arrival(diagonal, 3).wait_recv()
    three = pass_on(diagonal, 6, mate)
    three.start()
    arrival(flip(mate_shard, 4), 5).wait_recv()
    ready(flip(mate_shard, 4))
    ready(diagonal)
    arrival(flip_mask(mate_shard, 6), 6).wait_recv()
    ready(flip_mask(mate_shard, 6))
    if exchange:
        exchange.relay(6)
    for copy in firsts + [across, one, two, three]:
        copy.wait_send()


class Stores:
    def __init__(self, pairs, sems):
        self.pairs, self.sems = pairs, sems

    def copies(self, slot):
        return [
            pltpu.make_async_copy(source.at[slot], target.at[slot], self.sems.at[index, slot])
            for index, (source, target) in enumerate(self.pairs)
        ]

    def start(self, slot):
        for copy in self.copies(slot):
            copy.start()

    def wait(self):
        def one(slot, carry):
            for copy in self.copies(slot):
                copy.wait()
            return carry

        lax.fori_loop(0, 8, one, 0)


TILE = 512


def tiles(width, body):
    def one(index, carry):
        body(pl.ds(pl.multiple_of(index * TILE, TILE), TILE))
        return carry

    lax.fori_loop(0, width // TILE, one, 0)


def hidden_kernel(
    x, weight, gate_cols, plane, up_cols, gate, upward, hidden,
    plane_in, up_in, gate_wide, gate_low, up_low, hidden_low, local, send, receive, store,
    up_store, cols_local, cols_send, cols_receive
):
    exchange = PairExchange(weight, up_in, cols_local, cols_send, cols_receive)
    width = gate_wide.shape[2]
    early = Stores([(plane_in, plane), (gate_low, gate)], store.at[0])
    late = Stores([(up_low, upward), (hidden_low, hidden)], store.at[1])

    def ready(slot):
        def tile(at):
            value = dot_nn(plane_in[slot], gate_cols[:, at])
            gate_wide[slot, :, at] = value
            gate_low[slot, :, at] = value.astype(jnp.bfloat16)

        tiles(width, tile)
        early.start(slot)

    gather_plane(x, plane_in, local, send, receive, ready, exchange)
    exchange.wait()
    kept = pltpu.make_async_copy(up_in, up_cols, up_store)
    kept.start()

    def last(slot, carry):
        def tile(at):
            value = dot_nn(plane_in[slot], up_in[:, :, at].reshape(-1, TILE))
            gated = gate_wide[slot, :, at]
            up_low[slot, :, at] = value.astype(jnp.bfloat16)
            hidden_low[slot, :, at] = (
                gated * (1.0 / (1.0 + jnp.exp(-gated))) * value
            ).astype(jnp.bfloat16)

        tiles(width, tile)
        late.start(slot)
        return carry

    lax.fori_loop(0, 8, last, 0)
    early.wait()
    late.wait()
    kept.wait()


def gather_hidden(x, gate_cols, weight, number, after=()):
    rows, wide = x.shape
    width = weight.shape[1] // 8
    low = x.dtype
    narrow = (8, rows, width)
    result = jax.ShapeDtypeStruct(narrow, low)
    return comm_call(
        hidden_kernel,
        (jax.ShapeDtypeStruct((8, rows, wide), low), columns_shape(weight)) + (result,) * 3,
        (x, weight, gate_cols),
        [VM, ANY, VM],
        (ANY,) * 5,
        [
            pltpu.VMEM((8, rows, wide), low),
            pltpu.VMEM(columns_shape(weight).shape, low),
            pltpu.VMEM(narrow, jnp.float32),
        ]
        + [pltpu.VMEM(narrow, low)] * 3
        + [DMA, DMA((7,)), DMA((7,)), DMA((2, 2, 8)), DMA]
        + PAIR_EXCHANGE,
        "gather_hidden",
        number,
        after,
    )


def hidden_grad_kernel(
    x, down, gate, upward, plane, gate_grad, up_grad,
    plane_in, gate_low, up_low, local, send, receive, store
):
    width = gate.shape[2]
    stores = Stores([(plane_in, plane), (gate_low, gate_grad), (up_low, up_grad)], store)

    def ready(slot):
        def tile(at):
            grad = dot_nt(plane_in[slot], down[at])
            gated = gate[slot, :, at].astype(jnp.float32)
            sigmoid = 1.0 / (1.0 + jnp.exp(-gated))
            part = grad * sigmoid
            gate_low[slot, :, at] = (
                part * upward[slot, :, at].astype(jnp.float32) * (1.0 + gated * (1.0 - sigmoid))
            ).astype(jnp.bfloat16)
            up_low[slot, :, at] = (part * gated).astype(jnp.bfloat16)

        tiles(width, tile)
        stores.start(slot)

    gather_plane(x, plane_in, local, send, receive, ready)
    stores.wait()


def gather_hidden_grad(x, down, gate, upward, number, after=()):
    rows, wide = x.shape
    low = x.dtype
    narrow = gate.shape
    result = jax.ShapeDtypeStruct(narrow, low)
    return comm_call(
        hidden_grad_kernel,
        (jax.ShapeDtypeStruct((8, rows, wide), low), result, result),
        (x, down, gate, upward),
        [VM] * 4,
        (ANY,) * 3,
        [pltpu.VMEM((8, rows, wide), low)]
        + [pltpu.VMEM(narrow, low)] * 2
        + [DMA, DMA((7,)), DMA((7,)), DMA((3, 8))],
        "gather_hidden_grad",
        number,
        after,
    )


def flip_bit(value, bit):
    return value + bit - 2 * bit * lax.rem(lax.div(value, bit), 2)


PIECES = 2


def add_rows(rows, body):
    step = 32

    def one(index, carry):
        body(pl.ds(pl.multiple_of(index * step, step), step))
        return carry

    lax.fori_loop(0, rows // step, one, 0)


def scatter_products(
    produce, part, out, mated, first_in, second_in, sums, sem_s, sem_r, meet=True
):
    seq, shard = place()
    core, chip = lax.rem(shard, 2), lax.div(shard, 2)
    rows = out.shape[0] // PIECES
    mate = (seq, flip(shard, 1))
    bit = 1 + core
    first, second = flip_bit(chip, bit), flip_bit(chip, 3 - bit)
    diagonal = 3 - chip
    first_device, second_device = (seq, 2 * first + core), (seq, 2 * second + core)
    if meet:
        greet([mate, first_device, second_device])

    def piece(index):
        return pl.ds(index * rows, rows)

    order, mate_order = (diagonal, first, second, chip), (diagonal, second, first, chip)
    swaps = {}

    def make(slot):
        target = mate_order[slot]
        produce(2 * target + 1 - core)
        for index in range(PIECES):
            copy = remote(
                part.at[2 * target + 1 - core, piece(index)],
                mated.at[target, piece(index)],
                sem_s.at[0, slot, index],
                sem_r.at[0, target, index],
                mate,
            )
            copy.start()
            swaps[slot, index] = copy
        produce(2 * order[slot] + core)

    make(0)
    make(1)

    def came(target, index):
        remote(
            part.at[0, piece(index)],
            mated.at[target, piece(index)],
            sem_s.at[0, 0, index],
            sem_r.at[0, target, index],
            mate,
        ).wait_recv()

    sends = []
    for index in range(PIECES):
        for slot, target in ((0, diagonal), (1, first)):
            came(target, index)

            def add(span, slot=slot, target=target, index=index):
                span = pl.ds(span.start + index * rows, span.size)
                sums[slot, span] = (
                    part[2 * target + core, span].astype(jnp.float32)
                    + mated[target, span].astype(jnp.float32)
                ).astype(jnp.bfloat16)

            add_rows(rows, add)
            copy = remote(
                sums.at[slot, piece(index)],
                first_in.at[slot, piece(index)],
                sem_s.at[1, slot, index],
                sem_r.at[1, slot, index],
                first_device,
            )
            copy.start()
            sends.append(copy)
    make(2)
    make(3)
    finals = []
    for index in range(PIECES):
        came(second, index)
        sends[2 * index].wait_recv()

        def add(span, index=index):
            span = pl.ds(span.start + index * rows, span.size)
            sums[2, span] = (
                part[2 * second + core, span].astype(jnp.float32)
                + mated[second, span].astype(jnp.float32)
                + first_in[0, span].astype(jnp.float32)
            ).astype(jnp.bfloat16)

        add_rows(rows, add)
        copy = remote(
            sums.at[2, piece(index)],
            second_in.at[piece(index)],
            sem_s.at[2, 0, index],
            sem_r.at[2, 0, index],
            second_device,
        )
        copy.start()
        finals.append(copy)
    for index in range(PIECES):
        came(chip, index)
        sends[2 * index + 1].wait_recv()
        finals[index].wait_recv()

        def add(span, index=index):
            span = pl.ds(span.start + index * rows, span.size)
            out[span] = (
                part[shard, span].astype(jnp.float32) + mated[chip, span].astype(jnp.float32)
            ) + (first_in[1, span].astype(jnp.float32) + second_in[span].astype(jnp.float32))

        add_rows(rows, add)
    for copy in list(swaps.values()) + sends + finals:
        copy.wait_send()


def out_scatter_kernel(hidden, down, out, part, *scratch):
    def produce(block):
        def tile(at):
            part[block, :, at] = dot_nn(hidden[block], down[:, at]).astype(jnp.bfloat16)

        tiles(down.shape[1], tile)

    scatter_products(produce, part, out, *scratch)


def back_scatter_kernel(gate_grad, up_grad, gate_cols, up_cols, out, part, *scratch):
    def produce(block):
        def tile(at):
            part[block, :, at] = (
                dot_nt(gate_grad[block], gate_cols[at]) + dot_nt(up_grad[block], up_cols[at])
            ).astype(jnp.bfloat16)

        tiles(gate_cols.shape[0], tile)

    scatter_products(produce, part, out, *scratch)


def scatter_scratch(rows, width):
    low = jnp.bfloat16
    return [
        pltpu.VMEM((8, rows, width), low),
        pltpu.VMEM((4, rows, width), low),
        pltpu.VMEM((2, rows, width), low),
        pltpu.VMEM((rows, width), low),
        pltpu.VMEM((3, rows, width), low),
        DMA((3, 4, PIECES)),
        DMA((3, 4, PIECES)),
    ]


def plane_scatter(kernel, inputs, rows, width, name, number, after=()):
    return comm_call(
        kernel,
        jax.ShapeDtypeStruct((rows, width), jnp.float32),
        inputs,
        [VM] * len(inputs),
        VM,
        scatter_scratch(rows, width),
        name,
        number,
        after,
    )


LINE_ROWS = 128
RING = 4
CLOSE_LAG = 2
TAKE_LAG = 5
AHEAD = 3


def flip_by(value, mask):
    for bit in (1, 2, 4):
        here, there = lax.rem(lax.div(value, bit), 2), lax.rem(lax.div(mask, bit), 2)
        value = value + bit * (lax.rem(here + there, 2) - here)
    return value


class LineSums:
    def __init__(self, gate, up, late, gate_rows, up_rows, out, landed, scratch):
        self.gate, self.up, self.late = gate, up, late
        self.rows_out, self.out = (gate_rows, up_rows), out
        self.first_in, self.second_in, self.total_in = landed
        (
            self.own, self.sums, self.others, self.totals,
            self.own_sem, self.load_sem, self.keep_sem, self.send, self.receive,
            self.spread_send, self.spread_receive,
        ) = scratch
        self.seq, self.shard = place()
        self.inner = jnp.logical_or(self.seq == 1, self.seq == 2)
        self.outer = jnp.logical_not(self.inner)
        self.beside = (self.seq + 1 - 2 * lax.rem(self.seq, 2), self.shard)
        self.across = (3 - self.seq, self.shard)
        self.rows, self.width = gate_rows.shape[0], gate.shape[1]
        self.cuts = self.rows // LINE_ROWS
        self.early = 8 * self.cuts
        self.count = self.early + len(late)
        self.away = 7 * self.cuts
        self.halves = (slice(0, self.width), slice(self.width, 2 * self.width))

    def is_late(self, index):
        return isinstance(index, int) and index >= self.early

    def owner(self, index):
        return flip_by(self.shard, 7 - lax.div(index, self.cuts))

    def sources(self, index):
        if self.is_late(index):
            return [(self.late[index - self.early], slice(0, 2 * self.width))]
        start = self.owner(index) * self.rows + lax.rem(index, self.cuts) * LINE_ROWS
        span = pl.ds(pl.multiple_of(start, LINE_ROWS), LINE_ROWS)
        return list(zip((self.gate.at[span], self.up.at[span]), self.halves))

    def inward(self, index):
        return [
            remote(
                source,
                self.first_in.at[index, :, half],
                self.send.at[side, index],
                self.receive.at[side, index],
                self.beside,
            )
            for side, (source, half) in enumerate(self.sources(index))
        ]

    def swap(self, index):
        return remote(
            self.sums.at[lax.rem(index, RING)],
            self.second_in.at[index],
            self.send.at[2, index],
            self.receive.at[2, index],
            self.across,
        )

    def result(self, index):
        if self.is_late(index):
            start = (index - self.early) * LINE_ROWS
            return self.out.at[start : start + LINE_ROWS]
        return self.total_in.at[index]

    def outward(self, index):
        return remote(
            self.totals.at[lax.rem(index, RING)],
            self.result(index),
            self.send.at[3, index],
            self.receive.at[3, index],
            self.beside,
        )

    def keep(self, index):
        return pltpu.make_async_copy(
            self.totals.at[lax.rem(index, RING)], self.result(index), self.keep_sem.at[index]
        )

    def own_loads(self, index):
        slot = lax.rem(index, 2)
        return [
            pltpu.make_async_copy(
                source, self.own.at[slot, :, half], self.own_sem.at[slot, side]
            )
            for side, (source, half) in enumerate(self.sources(index))
        ]

    def spread(self, index, side, source, away):
        down = pl.ds(
            pl.multiple_of(lax.rem(index, self.cuts) * LINE_ROWS, LINE_ROWS), LINE_ROWS
        )
        along = pl.ds(pl.multiple_of(self.shard * self.width, self.width), self.width)
        source = source.at[:, self.halves[side]]
        spot = self.rows_out[side].at[down, along]
        if not away:
            return pltpu.make_async_copy(source, spot, self.spread_send.at[side, index])
        return remote(
            source,
            spot,
            self.spread_send.at[side, index],
            self.spread_receive.at[side, index],
            (self.seq, self.owner(index)),
        )

    def spread_each(self, index, source, there, here):
        for side in range(2):

            @pl.when(index < self.away)
            def _():
                there(self.spread(index, side, source, True))

            @pl.when(index >= self.away)
            def _():
                here(self.spread(index, side, source, False))

    def spread_start(self, index, source):
        self.spread_each(index, source, lambda copy: copy.start(), lambda copy: copy.start())

    def spread_sent(self, index, source):
        self.spread_each(index, source, lambda copy: copy.wait_send(), lambda copy: copy.wait())

    def add_up(self, target, first, second):
        def add(at):
            target[at] = (
                first[at].astype(jnp.float32) + second[at].astype(jnp.float32)
            ).astype(jnp.bfloat16)

        add_rows(LINE_ROWS, add)

    def begin(self):
        @pl.when(self.outer)
        def _():
            for index in range(AHEAD):
                for copy in self.inward(index):
                    copy.start()

        @pl.when(self.inner)
        def _():
            for copy in self.own_loads(0):
                copy.start()

    def retire(self, index):
        self.outward(index).wait_send()
        if self.is_late(index):
            self.keep(index).wait()
        else:
            self.spread_sent(index, self.totals.at[lax.rem(index, RING)])

    def close(self, index):
        slot = lax.rem(index, RING)
        self.swap(index).wait_recv()
        load = pltpu.make_async_copy(
            self.second_in.at[index], self.others, self.load_sem.at[1]
        )
        load.start()
        if isinstance(index, int):
            self.retire(index - RING)
        else:

            @pl.when(index >= RING)
            def _():
                self.retire(index - RING)

        load.wait()
        self.add_up(self.totals.at[slot], self.sums.at[slot], self.others)
        self.outward(index).start()
        if self.is_late(index):
            self.keep(index).start()
        else:
            self.spread_start(index, self.totals.at[slot])

    def inner_step(self, index, following):
        slot = lax.rem(index, RING)
        if following:
            for copy in self.own_loads(index + 1):
                copy.start()
        for copy in self.inward(index):
            copy.wait_recv()
        if isinstance(index, int):
            self.swap(index - RING).wait_send()
        else:

            @pl.when(index >= RING)
            def _():
                self.swap(index - RING).wait_send()

        load = pltpu.make_async_copy(
            self.first_in.at[index], self.sums.at[slot], self.load_sem.at[0]
        )
        load.start()
        for copy in self.own_loads(index):
            copy.wait()
        load.wait()
        self.add_up(self.sums.at[slot], self.sums.at[slot], self.own.at[lax.rem(index, 2)])
        self.swap(index).start()
        if isinstance(index, int):
            self.close(index - CLOSE_LAG)
        else:

            @pl.when(index >= CLOSE_LAG)
            def _():
                self.close(index - CLOSE_LAG)

    def outer_take(self, index):
        self.outward(index).wait_recv()
        if not self.is_late(index):
            self.spread_start(index, self.total_in.at[index])

    def outer_step(self, index):
        if isinstance(index, int):
            if index + AHEAD < self.count:
                for copy in self.inward(index + AHEAD):
                    copy.start()
        else:

            @pl.when(index + AHEAD < self.early)
            def _():
                for copy in self.inward(index + AHEAD):
                    copy.start()

        if isinstance(index, int):
            self.outer_take(index - TAKE_LAG)
        else:

            @pl.when(index >= TAKE_LAG)
            def _():
                self.outer_take(index - TAKE_LAG)

    def step(self, index, following=True):
        @pl.when(self.inner)
        def _():
            self.inner_step(index, following)

        @pl.when(self.outer)
        def _():
            self.outer_step(index)

    def run(self, start, stop):
        def one(index, carry):
            self.step(index)
            return carry

        lax.fori_loop(start, min(stop, self.early - 1), one, 0)

    def finish(self):
        early, count = self.early, self.count

        @pl.when(self.outer)
        def _():
            for index in range(early, early - 1 + AHEAD):
                for copy in self.inward(index):
                    copy.start()

        for index in range(early - 1, count):
            self.step(index, index + 1 < count)

        @pl.when(self.inner)
        def _():
            for index in range(count - CLOSE_LAG, count):
                self.close(index)
            for index in range(count - RING, count):
                self.swap(index).wait_send()
                self.retire(index)

        def each(body):
            def one(index, carry):
                body(index)
                return carry

            lax.fori_loop(0, early, one, 0)

        @pl.when(self.outer)
        def _():
            for index in range(count - TAKE_LAG, count):
                self.outer_take(index)

            def sent(index):
                for copy in self.inward(index):
                    copy.wait_send()
                self.spread_sent(index, self.total_in.at[index])

            each(sent)
            for index in range(early, count):
                for copy in self.inward(index):
                    copy.wait_send()

        def received(index):
            for side in range(2):

                @pl.when(index < self.away)
                def _():
                    self.spread(index, side, self.total_in.at[index], True).wait_recv()

        each(received)


class HeadLoads:
    def __init__(self, sources, log_total, raw, low, logs, wide, sems):
        self.sources, self.log_total, self.raw = sources, log_total, raw
        self.low, self.logs, self.wide, self.sems = low, logs, wide, sems
        self.size = low.shape[3]

    def raws(self, head):
        slot, size = lax.rem(head, 2), self.size
        heads = self.raw.shape[1] // (3 * size)
        return [
            pltpu.make_async_copy(
                self.raw.at[:, pl.ds(pl.multiple_of((part * heads + head) * size, size), size)],
                self.wide.at[slot, part],
                self.sems.at[slot, 5 + part],
            )
            for part in range(2)
        ]

    def lows(self, head):
        slot, size = lax.rem(head, 2), self.size
        at = pl.ds(pl.multiple_of(head * size, size), size)
        copies = [
            pltpu.make_async_copy(
                source.at[:, at], self.low.at[slot, index], self.sems.at[slot, index]
            )
            for index, source in enumerate(self.sources)
        ]
        return copies + [
            pltpu.make_async_copy(
                self.log_total.at[head], self.logs.at[slot], self.sems.at[slot, 4]
            )
        ]


def exact_nt(a, b):
    return lax.dot_general(
        a, b, (((1,), (1,)), ((), ())), preferred_element_type=jnp.float32,
        precision=lax.Precision.HIGHEST,
    )


def exact_tn(a, b):
    return lax.dot_general(
        a, b, (((0,), (0,)), ((), ())), preferred_element_type=jnp.float32,
        precision=lax.Precision.HIGHEST,
    )


def finish_kernel(
    queries, keys, values, head_grad, log_total, raw, weight, cosine, signed, q_factor, k_factor,
    q_gain, k_gain, token_gains, whole, gate, up, out_grad,
    out, gains, gate_rows, up_rows, line_out, first_chunks, second_chunks, total_chunks,
    low, logs, wide, q_turned, k_turned, k_sum, v_sum, joined, stat, stat_in, gain, gain_in,
    part, grads, placed,
    mated, relayed, landed, first_in, second_in, swapped,
    head_sem, weight_sem, stat_s, stat_r, gain_s, gain_r,
    local, sem_s, sem_r, relay_r, grad_s, grad_r, *line_scratch
):
    seq, shard = place()
    core, half, quarter = lax.rem(shard, 2), lax.div(seq, 2), lax.rem(seq, 2)
    chip = lax.div(shard, 2)
    base = shard - core
    group = 2 * quarter + core
    rows = out.shape[0] // 2
    mate = (seq, flip(shard, 1))
    bit = 1 + core
    first, second, diagonal = flip_bit(chip, bit), flip_bit(chip, 3 - bit), 3 - chip
    first_device, second_device = (seq, 2 * first + core), (seq, 2 * second + core)
    greet(column_others(seq, shard) + plane_others(seq, shard)[1:])
    late = [
        out_grad.at[start : start + LINE_ROWS] for start in range(0, out_grad.shape[0], LINE_ROWS)
    ] + [
        placed.at[index, start : start + LINE_ROWS]
        for index in range(3)
        for start in range(0, placed.shape[1], LINE_ROWS)
    ]
    line = LineSums(
        gate, up, late, gate_rows, up_rows, line_out,
        (first_chunks, second_chunks, total_chunks), line_scratch,
    )
    line.begin()

    length, size = cosine.shape
    heads = q_gain.shape[1] // size
    loads = HeadLoads(
        (queries, keys, values, head_grad), log_total, raw, low, logs, wide, head_sem
    )
    for copy in loads.lows(0) + loads.raws(0):
        copy.start()
    blocks = grads.shape[1]
    weight_loads = [
        pltpu.make_async_copy(
            weight.at[index * blocks : (index + 1) * blocks], grads.at[index],
            weight_sem.at[index],
        )
        for index in range(4)
    ]
    for copy in weight_loads:
        copy.start()
    stat[...] = jnp.zeros_like(stat)
    gain[...] = jnp.zeros_like(gain)
    gain[2:4] = token_gains[...]
    ones = jnp.ones((8, size), jnp.float32)

    def columns(head):
        return pl.ds(pl.multiple_of(head * size, size), size)

    def back(head, carry):
        slot, at = lax.rem(head, 2), columns(head)
        for copy in loads.lows(head):
            copy.wait()

        @pl.when(head + 1 < heads)
        def _():
            for copy in loads.lows(head + 1) + loads.raws(head + 1):
                copy.start()

        attend_back_kernel(
            low.at[slot, 0], low.at[slot, 1], low.at[slot, 2], low.at[slot, 3],
            logs.at[pl.ds(slot, 1)], cosine, signed,
            q_turned.at[:, at], k_turned.at[:, at],
            joined.at[:, columns(2 * heads + head)],
            k_sum, v_sum,
        )
        for copy in loads.raws(head):
            copy.wait()
        for index, (turned, factor, gain_part) in enumerate(
            ((q_turned, q_factor, q_gain), (k_turned, k_factor, k_gain))
        ):
            along = turned[:, at].astype(jnp.float32) * wide[slot, index]
            stat[8 * index : 8 * index + 8] += exact_nt(ones, along * gain_part[:, at])
            spot = pl.multiple_of(group * heads * size + head * size, size)
            gain[index : index + 1, pl.ds(spot, size)] = jnp.sum(
                along * factor[...], axis=0, keepdims=True
            )

        @pl.when(lax.rem(head, 2) == 1)
        def _():
            line.step(lax.div(head, 2))

        return carry

    lax.fori_loop(0, heads, back, 0)
    partners = [mate, (flip(seq, 1), shard), (flip(seq, 1), flip(shard, 1))]
    stat_copies = [
        remote(stat, stat_in.at[index], stat_s.at[index], stat_r.at[index], partner)
        for index, partner in enumerate(partners)
    ]
    for copy in stat_copies:
        copy.start()
    own_gain = pltpu.make_async_copy(gain, gain_in.at[shard], gain_s.at[0])
    own_gain.start()
    gain_copies = [
        remote(
            gain, gain_in.at[shard], gain_s.at[mask], gain_r.at[mask],
            (seq, flip_mask(shard, mask)),
        )
        for mask in range(1, 8)
    ]
    for copy in gain_copies:
        copy.start()
    for copy in loads.raws(0):
        copy.start()
    line.run(heads // 2, heads // 2 + 1)
    for copy in stat_copies:
        copy.wait()
    stat[...] = (stat[...] + stat_in[0]) + (stat_in[1] + stat_in[2])
    spreading = jnp.full((8, size), 0.125 / whole.shape[1], jnp.float32)

    def norm_back(head, carry):
        slot, at = lax.rem(head, 2), columns(head)
        for copy in loads.raws(head):
            copy.wait()

        @pl.when(head + 1 < heads)
        def _():
            for copy in loads.raws(head + 1):
                copy.start()

        for index, (turned, factor, gain_part) in enumerate(
            ((q_turned, q_factor, q_gain), (k_turned, k_factor, k_gain))
        ):
            inner = exact_tn(stat[8 * index : 8 * index + 8], spreading)
            scale = factor[...]
            joined[:, columns(index * heads + head)] = (
                scale * (turned[:, at].astype(jnp.float32) * gain_part[:, at])
                - wide[slot, index] * (scale * scale * scale * inner)
            ).astype(jnp.bfloat16)
        return carry

    lax.fori_loop(0, heads, norm_back, 0)
    line.run(heads // 2 + 1, heads // 2 + 2)

    mine = pl.ds(pl.multiple_of(core * rows, rows), rows)
    other = pl.ds(pl.multiple_of((1 - core) * rows, rows), rows)
    here = core == half
    order = [2 * (1 - half), 2 * (1 - half) + 1, flip(seq, 1), seq]
    long = grads.shape[1] // 2

    def project(target):
        span = pl.ds(pl.multiple_of(target * 2 * long, 2 * long), 2 * long)

        def tile(at):
            grads[target, :, at] = dot_tn(whole[:, span], joined[:, at]).astype(jnp.bfloat16)

        tiles(grads.shape[2], tile)

    for copy in weight_loads:
        copy.wait()
    swaps = []
    for slot, block in enumerate(order):
        tokens = pl.ds(pl.multiple_of(block * 2 * rows, 2 * rows), 2 * rows)

        def tile(index, carry, block=block, tokens=tokens):
            at = pl.ds(pl.multiple_of(index * blocks, blocks), blocks)
            part[block, :, at] = dot_nt(joined[tokens], grads[index]).astype(jnp.bfloat16)
            return carry

        lax.fori_loop(0, 4, tile, 0)
        copy = remote(
            part.at[block, other], mated.at[slot], sem_s.at[0, slot], sem_r.at[0, slot], mate
        )
        copy.start()
        swaps.append(copy)
    firsts = []
    for slot, target in ((0, diagonal), (1, first)):
        project(target)
        for index in range(2):
            span = slice(index * long, (index + 1) * long)
            copy = remote(
                grads.at[target, span],
                first_in.at[slot, span],
                grad_s.at[slot, index],
                grad_r.at[slot, index],
                first_device,
            )
            copy.start()
            firsts.append(copy)
    line.run(4, 5)
    project(second)
    project(chip)
    own_gain.wait()
    for copy in gain_copies:
        copy.wait()
    plane_gain = gain_in[0]
    for index in range(1, 8):
        plane_gain = plane_gain + gain_in[index]
    gain[...] = plane_gain
    own_gain = pltpu.make_async_copy(gain, gain_in.at[8 + seq], gain_s.at[8])
    own_gain.start()
    gain_copies = [
        remote(
            gain, gain_in.at[8 + seq], gain_s.at[8 + step], gain_r.at[7 + step],
            (lax.rem(seq + step, 4), shard),
        )
        for step in (1, 2, 3)
    ]
    for copy in gain_copies:
        copy.start()
    placed[...] = jnp.zeros_like(placed)

    near = quarter + half == 1
    far = jnp.logical_not(near)
    sends = []

    def to_target(slot, block):
        return remote(
            mated.at[slot],
            landed.at[quarter, core],
            sem_s.at[1, slot],
            sem_r.at[1, 2 * quarter + core],
            (block, base + half),
        )

    def to_near(slot):
        return remote(
            mated.at[slot], relayed.at[slot], sem_s.at[1, slot], relay_r.at[slot],
            (flip(seq, 1), shard),
        )

    for slot, block in enumerate(order):
        swaps[slot].wait_recv()

        def add(span, slot=slot, block=block):
            source = pl.ds(pl.multiple_of(span.start + core * rows, 32), span.size)
            mated[slot, span] = (
                part[block, source].astype(jnp.float32) + mated[slot, span].astype(jnp.float32)
            ).astype(jnp.bfloat16)

        add_rows(rows, add)
        copy = to_target(slot, block)
        if slot < 2:

            @pl.when(far)
            def _():
                to_near(slot).start()

        elif slot == 2:
            copy.start()
        else:
            own = pltpu.make_async_copy(mated.at[slot], landed.at[quarter, core], local)

            @pl.when(here)
            def _():
                own.start()

            @pl.when(jnp.logical_not(here))
            def _():
                copy.start()

        sends.append(copy)

    @pl.when(near)
    def _():
        for slot in range(2):
            to_near(slot).wait_recv()

            def add(span, slot=slot):
                mated[slot, span] = (
                    mated[slot, span].astype(jnp.float32)
                    + relayed[slot, span].astype(jnp.float32)
                ).astype(jnp.bfloat16)

            add_rows(rows, add)
            sends[slot].start()

    line.run(5, 7)

    seconds = []
    for index in range(2):
        firsts[index].wait_recv()

        def add(span, index=index):
            span = pl.ds(span.start + index * long, span.size)
            first_in[0, span] = (
                grads[second, span].astype(jnp.float32) + first_in[0, span].astype(jnp.float32)
            ).astype(jnp.bfloat16)

        add_rows(long, add)
        span = slice(index * long, (index + 1) * long)
        copy = remote(
            first_in.at[0, span], second_in.at[span], grad_s.at[2, index], grad_r.at[2, index],
            second_device,
        )
        copy.start()
        seconds.append(copy)
    line.run(7, 10)
    for turn in range(2):
        start = pl.multiple_of((1 - core if turn == 0 else core) * long, long)
        if turn == 0:
            for copy in (firsts[2], firsts[3], seconds[0], seconds[1]):
                copy.wait_recv()

        def add(span, start=start):
            span = pl.ds(pl.multiple_of(span.start + start, 32), span.size)
            first_in[1, span] = (
                (grads[chip, span].astype(jnp.float32) + first_in[1, span].astype(jnp.float32))
                + second_in[span].astype(jnp.float32)
            ).astype(jnp.bfloat16)

        add_rows(long, add)
        if turn == 0:
            swap = remote(
                first_in.at[1, pl.ds(start, long)], swapped, grad_s.at[3, 0], grad_r.at[3, 0], mate
            )
            swap.start()
    part_width = out.shape[1] // 4
    own_rows = pl.ds(pl.multiple_of(core * long, long), long)
    for index in range(3):
        spot = pl.multiple_of(group * part_width, part_width)
        placed[index, :, pl.ds(spot, part_width)] = first_in[
            1, own_rows, index * part_width : (index + 1) * part_width
        ]
    swap.wait_recv()
    for index in range(3):
        spot = pl.multiple_of((2 * quarter + 1 - core) * part_width, part_width)
        placed[index, :, pl.ds(spot, part_width)] = swapped[
            :, index * part_width : (index + 1) * part_width
        ]
    line.run(10, 12)

    for slot in range(2):

        @pl.when(near)
        def _():
            sends[slot].wait_send()

        @pl.when(far)
        def _():
            to_near(slot).wait_send()

    sends[2].wait_send()

    @pl.when(here)
    def _():
        own.wait()

    @pl.when(jnp.logical_not(here))
    def _():
        sends[3].wait_send()

    for source in range(4):
        arrival = remote(
            mated.at[0],
            landed.at[source // 2, source % 2],
            sem_s.at[1, 0],
            sem_r.at[1, source],
            mate,
        )
        expected = jnp.where(here, 2 * quarter + core != source, source // 2 == 1 - core)

        @pl.when(expected)
        def _():
            arrival.wait_recv()

    for side in range(2):

        def add_both(span, side=side):
            target = pl.ds(span.start + side * rows, span.size)
            out[target] = landed[0, side, span].astype(jnp.float32) + landed[
                1, side, span
            ].astype(jnp.float32)

        def take_one(span, side=side):
            target = pl.ds(span.start + side * rows, span.size)
            out[target] = landed[1 - core, side, span].astype(jnp.float32)

        @pl.when(here)
        def _():
            add_rows(rows, add_both)

        @pl.when(jnp.logical_not(here))
        def _():
            add_rows(rows, take_one)

    for copy in swaps + firsts + seconds + [swap]:
        copy.wait_send()
    own_gain.wait()
    for copy in gain_copies:
        copy.wait()
    gains[...] = (gain_in[8] + gain_in[9]) + (gain_in[10] + gain_in[11])
    line.run(12, line.early)
    line.finish()


def finish(
    heads_in, log_total, raw, weight, tables, factors, head_gains, token_gains, whole, gate, up,
    out_grad, number, after=()
):
    length, width = whole.shape
    rows, long, wide = length // 4, weight.shape[0] // 4, weight.shape[1]
    size, group_width = tables[0].shape[1], wide // 3
    low = whole.dtype
    hidden_width = gate.shape[1]
    tail = out_grad.shape[0] + 3 * long // 2
    early, late = gate.shape[0] // LINE_ROWS, tail // LINE_ROWS
    count = early + late
    block = (LINE_ROWS, 2 * hidden_width)
    owned = jax.ShapeDtypeStruct((gate.shape[0] // 8, 8 * hidden_width), low)
    chunks = jax.ShapeDtypeStruct((count,) + block, low)
    results = comm_call(
        finish_kernel,
        (
            jax.ShapeDtypeStruct((rows, width), jnp.float32),
            jax.ShapeDtypeStruct((8, width), jnp.float32),
            owned,
            owned,
            jax.ShapeDtypeStruct((tail, width), low),
            chunks,
            chunks,
            chunks,
        ),
        (*heads_in, log_total, raw, weight, *tables, *factors, *head_gains, token_gains)
        + (whole, gate, up, out_grad),
        [ANY] * 7 + [VM] * 8 + [ANY] * 3,
        (VM, VM) + (ANY,) * 6,
        [
            pltpu.VMEM((2, 4, length, size), low),
            pltpu.VMEM((2, length, 1), jnp.float32),
            pltpu.VMEM((2, 2, length, size), jnp.float32),
            pltpu.VMEM((length, group_width), low),
            pltpu.VMEM((length, group_width), low),
            pltpu.VMEM((length, size), jnp.float32),
            pltpu.VMEM((length, size), jnp.float32),
            pltpu.VMEM((length, wide), low),
            pltpu.VMEM((16, length), jnp.float32),
            pltpu.VMEM((3, 16, length), jnp.float32),
            pltpu.VMEM((8, width), jnp.float32),
            pltpu.VMEM((12, 8, width), jnp.float32),
            pltpu.VMEM((4, rows, width), low),
            pltpu.VMEM((4, long, wide), low),
            pltpu.VMEM((3, long // 2, width), low),
            pltpu.VMEM((4, rows // 2, width), low),
            pltpu.VMEM((2, rows // 2, width), low),
            pltpu.VMEM((2, 2, rows // 2, width), low),
            pltpu.VMEM((2, long, wide), low),
            pltpu.VMEM((long, wide), low),
            pltpu.VMEM((long // 2, wide), low),
            DMA((2, 7)),
            DMA((4,)),
            DMA((3,)),
            DMA((3,)),
            DMA((12,)),
            DMA((11,)),
            DMA,
            DMA((2, 4)),
            DMA((2, 4)),
            DMA((2,)),
            DMA((4, 2)),
            DMA((4, 2)),
            pltpu.VMEM((2,) + block, low),
            pltpu.VMEM((RING,) + block, low),
            pltpu.VMEM(block, low),
            pltpu.VMEM((RING,) + block, low),
            DMA((2, 2)),
            DMA((2,)),
            DMA((count,)),
            DMA((4, count)),
            DMA((4, count)),
            DMA((2, early)),
            DMA((2, early)),
        ],
        "finish",
        number,
        after,
    )
    return results[:5]


def turn_heads(values, cosine, signed):
    middle = values.shape[-1] // 2
    return values * cosine + jnp.concatenate(
        [values[:, middle:], values[:, :middle]], axis=1
    ) * signed


def dot_nt(a, b):
    return lax.dot_general(a, b, (((1,), (1,)), ((), ())), preferred_element_type=jnp.float32)


def dot_tn(a, b):
    return lax.dot_general(a, b, (((0,), (0,)), ((), ())), preferred_element_type=jnp.float32)


def dot_nn(a, b):
    return jnp.dot(a, b, preferred_element_type=jnp.float32)


ATTENTION_ROWS = 256


def causal(scores, start):
    query = start + lax.broadcasted_iota(jnp.int32, scores.shape, 0)
    key = lax.broadcasted_iota(jnp.int32, scores.shape, 1)
    return jnp.where(key <= query, scores, masked_value)


def attend_kernel(
    q_raw, k_raw, v_raw, q_factor, k_factor, q_gain, k_gain, cosine, signed,
    q_out, k_out, v_out, attended, log_total
):
    length, size = q_raw.shape
    scale = size ** (-0.5)
    cos, sin = cosine[...], signed[...]
    q_out[...] = turn_heads(
        q_raw[...] * q_factor[...] * q_gain[...], cos, sin
    ).astype(jnp.bfloat16)
    k_out[...] = turn_heads(
        k_raw[...] * k_factor[...] * k_gain[...], cos, sin
    ).astype(jnp.bfloat16)
    v_out[...] = v_raw[...].astype(jnp.bfloat16)
    rows = min(ATTENTION_ROWS, length)
    for start in range(0, length, rows):
        stop = start + rows
        scores = dot_nt(q_out[start:stop], k_out[:stop]) * scale
        scores = causal(scores, start)
        maximum = jnp.max(scores, axis=-1, keepdims=True)
        exponent = jnp.exp(scores - maximum)
        total = jnp.sum(exponent, axis=-1, keepdims=True)
        weights = (exponent * (1.0 / total)).astype(jnp.bfloat16)
        attended[start:stop] = dot_nn(weights, v_out[:stop]).astype(jnp.bfloat16)
        log_total[0, start:stop] = maximum + jnp.log(total)


def attend(raw, q_factor, k_factor, q_gain, k_gain, cosine, signed, size, after=()):
    length, width = raw.shape[0], raw.shape[1] // 3
    heads = width // size
    by_head = pl.BlockSpec((length, size), lambda h: (0, h))
    parts = [
        pl.BlockSpec((length, size), lambda h, start=index * heads: (0, start + h))
        for index in range(3)
    ]
    fixed = pl.BlockSpec((length, size), lambda h: (0, 0))
    factor = pl.BlockSpec((length, 1), lambda h: (0, 0))
    gain = pl.BlockSpec((1, size), lambda h: (0, h))
    low = jax.ShapeDtypeStruct((length, width), jnp.bfloat16)
    flops = heads * length * length * size * 2
    inputs = (raw, raw, raw, q_factor, k_factor, q_gain, k_gain, cosine, signed)
    return pl.pallas_call(
        ordered(attend_kernel, inputs, after),
        grid=(heads,),
        out_shape=(low, low, low, low, jax.ShapeDtypeStruct((heads, length, 1), jnp.float32)),
        in_specs=parts + [factor] * 2 + [gain] * 2 + [fixed] * 2 + [ANY] * len(after),
        out_specs=[by_head] * 4 + [pl.BlockSpec((1, length, 1), lambda h: (h, 0, 0))],
        name="attend",
        compiler_params=pltpu.CompilerParams(vmem_limit_bytes=VMEM_LIMIT),
        cost_estimate=pl.CostEstimate(
            flops=flops, bytes_accessed=20 * length * width, transcendentals=flops // (4 * size)
        ),
    )(*inputs, *after)


def attend_back_kernel(
    queries, keys, values, grads, log_total, cosine, signed, q_grad, k_grad, v_grad, k_sum, v_sum
):
    length, size = queries.shape
    scale = size ** (-0.5)
    rows = min(ATTENTION_ROWS, length)
    k_sum[...] = jnp.zeros_like(k_sum)
    v_sum[...] = jnp.zeros_like(v_sum)
    for start in range(0, length, rows):
        stop = start + rows
        query, grad = queries[start:stop], grads[start:stop]
        scores = causal(dot_nt(query, keys[:stop]) * scale, start)
        weights = jnp.exp(scores - log_total[0, start:stop])
        v_sum[:stop] += dot_tn(weights.astype(jnp.bfloat16), grad)
        weight_grad = dot_nt(grad, values[:stop])
        inner = jnp.sum(weights * weight_grad, axis=-1, keepdims=True)
        score_grad = (weights * (weight_grad - inner)).astype(jnp.bfloat16)
        q_low = (dot_nn(score_grad, keys[:stop]) * scale).astype(jnp.bfloat16)
        q_grad[start:stop] = turn_heads(
            q_low.astype(jnp.float32), cosine[start:stop], -signed[start:stop]
        ).astype(q_grad.dtype)
        k_sum[:stop] += dot_tn(score_grad, query)
    k_low = (k_sum[...] * scale).astype(jnp.bfloat16)
    k_grad[...] = turn_heads(k_low.astype(jnp.float32), cosine[...], -signed[...]).astype(
        k_grad.dtype
    )
    v_grad[...] = v_sum[...].astype(jnp.bfloat16)


def split_layer(
    block_input, query_weight, key_weight, value_weight, out_weight, gate_weight, up_weight,
    down_weight, query_gain, key_gain, attention_gain, swiglu_gain, cotangent
):
    tokens, width = block_input.shape[1:]
    head_size = width // HEADS
    seq, shard = lax.axis_index("seq"), lax.axis_index("fsdp")
    core, chip = lax.rem(shard, 2), lax.div(shard, 2)
    half, quarter = lax.div(seq, 2), lax.rem(seq, 2)
    rows = query_weight.shape[0]
    hidden_width = gate_weight.shape[1] // 8
    group_width = width // 4
    group = 2 * quarter + core
    length = 4 * tokens
    low = jnp.bfloat16
    sequence = block_input.reshape(tokens, width)

    whole, qkv, out_rows = entry(
        sequence, query_weight, key_weight, value_weight, out_weight, 1
    )
    whole = whole.reshape(length, width)
    out_full = lax.all_gather(out_rows, "fsdp", axis=0, tiled=True)
    raw = dot_nn(whole, qkv)
    q_raw, k_raw = raw[:, :group_width], raw[:, group_width : 2 * group_width]

    def reduced(first, second, number, after=()):
        part = jnp.stack([first, second]).reshape(2 * length // 128, 128)
        total = stats_sum(part, number, after).reshape(2, length, 1)
        return total[0] / width, total[1] / width

    q_mean, k_mean = reduced(
        jnp.sum(q_raw * q_raw, axis=-1), jnp.sum(k_raw * k_raw, axis=-1), 2
    )
    q_factor, k_factor = lax.rsqrt(q_mean + epsilon), lax.rsqrt(k_mean + epsilon)
    cosine, sine = rotary_tables(length, 0, head_size)
    cosine = jnp.concatenate([cosine[:, 0], cosine[:, 0]], axis=1)
    signed = jnp.concatenate([-sine[:, 0], sine[:, 0]], axis=1)
    q_gain_part = lax.dynamic_slice_in_dim(query_gain, group * group_width, group_width)[None]
    k_gain_part = lax.dynamic_slice_in_dim(key_gain, group * group_width, group_width)[None]
    queries, keys, values, attended_heads, log_total = attend(
        raw, q_factor, k_factor, q_gain_part, k_gain_part, cosine, signed, head_size
    )
    attended, gate_cols = to_tokens(
        attended_heads.reshape(4, tokens, group_width), gate_weight, 3
    )
    gate_cols = gate_cols.reshape(width, hidden_width)
    branch = dot_nn(attended, out_full)
    branch_factor = norm_factor(branch)
    residual = sequence.astype(jnp.float32) + branch * branch_factor * attention_gain

    plane, up_cols, gate, upward, hidden = gather_hidden(
        residual.astype(low), gate_cols, up_weight, 4
    )
    plane, up_cols = plane.reshape(8 * tokens, width), up_cols.reshape(width, hidden_width)
    mixed_out = plane_scatter(
        out_scatter_kernel, (hidden, down_weight), tokens, width, "out_scatter", 5
    )
    mixed_factor = norm_factor(mixed_out)
    output = residual + mixed_out * mixed_factor * swiglu_gain
    upstream = cotangent.reshape(tokens, width).astype(jnp.float32)
    mixed_float, swiglu_gain_grad = norm_backward(mixed_out, mixed_factor, swiglu_gain, upstream)
    mixed_plane, gate_grad, up_grad = gather_hidden_grad(
        mixed_float.astype(low), down_weight, gate, upward, 6
    )
    mixed_plane = mixed_plane.reshape(8 * tokens, width)
    down_grad = transposed_times(
        hidden.reshape(8 * tokens, hidden_width), mixed_plane
    ).astype(low)
    down_sum = lax.psum(down_grad, "seq")
    gate_sum = transposed_times(plane, gate_grad.reshape(8 * tokens, hidden_width)).astype(low)
    up_sum = transposed_times(plane, up_grad.reshape(8 * tokens, hidden_width)).astype(low)

    residual_grad = upstream + plane_scatter(
        back_scatter_kernel,
        (gate_grad, up_grad, gate_cols, up_cols),
        tokens,
        width,
        "back_scatter",
        7,
        (gate_sum, up_sum),
    )

    branch_float, attention_gain_grad = norm_backward(
        branch, branch_factor, attention_gain, residual_grad
    )
    branch_grad = branch_float.astype(low)
    attended_grad = times_transposed(branch_grad, out_full).astype(low)
    head_grad, out_grad = to_heads(attended_grad, attended, branch_grad, 8)
    head_grad, out_grad = head_grad.reshape(length, group_width), out_grad.astype(low)
    input_sum, gain_totals, gate_rows, up_rows, late = finish(
        (queries, keys, values, head_grad),
        log_total,
        raw,
        qkv,
        (cosine, signed),
        (q_factor, k_factor),
        (q_gain_part, k_gain_part),
        jnp.stack([attention_gain_grad, swiglu_gain_grad]),
        whole,
        gate_sum,
        up_sum,
        out_grad,
        10,
        (down_sum,),
    )
    input_grad = residual_grad + input_sum

    down_total = down_sum.astype(jnp.float32)
    gate_total, up_total = gate_rows.astype(jnp.float32), up_rows.astype(jnp.float32)
    out_total, query_total, key_total, value_total = (
        late[index * rows : (index + 1) * rows].astype(jnp.float32) for index in range(4)
    )

    return (
        output.reshape(1, tokens, width),
        input_grad.reshape(1, tokens, width),
        query_total,
        key_total,
        value_total,
        out_total,
        gate_total,
        up_total,
        down_total,
        gain_totals[0],
        gain_totals[1],
        gain_totals[2],
        gain_totals[3],
    )


def fits(mesh):
    return mesh.shape["seq"] == 4 and mesh.shape["fsdp"] == 8


def solution(mesh):
    placed = (
        P("fsdp", "seq", None),
        P("fsdp", None),
        P("fsdp", None),
        P("fsdp", None),
        P("fsdp", None),
        P("fsdp", None),
        P("fsdp", None),
        P("fsdp", None),
        P(),
        P(),
        P(),
        P(),
        P("fsdp", "seq", None),
    )
    return jax.shard_map(
        split_layer if fits(mesh) else local,
        mesh=mesh,
        in_specs=placed,
        out_specs=(
            P("fsdp", "seq", None),
            P("fsdp", "seq", None),
            P("fsdp", None),
            P("fsdp", None),
            P("fsdp", None),
            P("fsdp", None),
            P("fsdp", None),
            P("fsdp", None),
            P("fsdp", None),
            P(),
            P(),
            P(),
            P(),
        ),
        check_vma=False,
    )
```
